32 devices in a mesh: dp: 8 (over z, y), seq: 4 (over x, core).
Axes of the slice: x: 2, y: 2, z: 4, core: 2. Of those that a mesh axis runs over, the one named last changes fastest.
Arguments:
- inputs: bfloat16 [8, 2048, 512], P('dp', 'seq'), may hold values from -6 to 6
- grad_out: bfloat16 [8, 2048, 512], P('dp', 'seq'), may hold values from -6 to 6
- ln_gain: float32 [512], P(('dp', 'seq')), may hold values from 0.1 to 1.9
- ln_bias: float32 [512], P(('dp', 'seq')), may hold values from -1.5 to 1.5
- skip_scale: float32 [512], P(('dp', 'seq')), may hold values from -4 to 4
- w_glu: float32 [512, 1024], P(('dp', 'seq')), may hold values from -0.25 to 0.25
- b_glu: float32 [1024], P(('dp', 'seq')), may hold values from -1.5 to 1.5
- log_dt: float32 [512], P(('dp', 'seq')), may hold values from -6.9 to -2.3
- log_a_real: float32 [512, 64], P(('dp', 'seq')), may hold values from -1.2 to 0
- a_imag: float32 [512, 64], P(('dp', 'seq')), may hold values from 0 to 60
- c_coef: float32 [512, 128], P(('dp', 'seq')), may hold values from -3 to 3
Outputs:
- result: bfloat16 [8, 2048, 512], P('dp', 'seq')
- grad_in: bfloat16 [8, 2048, 512], P('dp', 'seq')
- d_ln_gain: float32 [512], P(('dp', 'seq'))
- d_ln_bias: float32 [512], P(('dp', 'seq'))
- d_skip_scale: float32 [512], P(('dp', 'seq'))
- d_w_glu: float32 [512, 1024], P(('dp', 'seq'))
- d_b_glu: float32 [1024], P(('dp', 'seq'))
- d_log_dt: float32 [512], P(('dp', 'seq'))
- d_log_a_real: float32 [512, 64], P(('dp', 'seq'))
- d_a_imag: float32 [512, 64], P(('dp', 'seq'))
- d_c_coef: float32 [512, 128], P(('dp', 'seq'))
The draws below stay inside these ranges and needn't reach their ends.
All inputs are finite; a program needn't handle non-finite values.
Results may differ from the reference program's by a relative error of at most 0.0098.
Values may be sent and summed in bfloat16 or wider, within the bound.
A program may use at most 512 MiB of HBM per device.

```python
import jax
import jax.numpy as jnp
from jax import lax

D = 512
N_MODES = 64
GLU = 1024
KTAPS = 512
SEQS = 8
LENGTH = 2048


def strengthened(array, rng, source, target, parts, factor):
    owner, partner = [(jnp.arange(array.shape[axis_at]) // (array.shape[axis_at] // parts)).reshape([-1 if axis == axis_at else 1 for axis in range(array.ndim)]) for axis_at in (source, target)]
    chosen = jax.random.permutation(rng, parts)[partner]
    strong = (owner == chosen) | (owner == (partner + parts // 2) % parts)
    return jnp.where(strong, factor * array, array)


def shard_levels(own_key, extent, split, least, top_value):
    level, own = 1.0, jax.random.fold_in(own_key, 6)
    for dim, parts in split:
        heights = jnp.exp(jax.random.uniform(jax.random.fold_in(own, dim), (parts,), jnp.float32, least / len(split), top_value / len(split)))
        level = level * jnp.repeat(heights, extent[dim] // parts).reshape([-1 if axis == dim else 1 for axis in range(len(extent))])
    return level


def bell_draw(own_key, shape, scale, reach, shards=(), kind=jnp.bfloat16):
    array = scale * jax.random.normal(own_key, shape, jnp.float32)
    if shards:
        array = array * shard_levels(own_key, shape, shards, -0.22, 0.18)
    return jnp.clip(array, -reach, reach).astype(kind)


def heavy_noise(rng, dims, spread, bound, cuts, heavy, held_as=jnp.bfloat16):
    entries = spread * jax.random.normal(rng, dims, jnp.float32)
    if cuts:
        entries = entries * shard_levels(rng, dims, cuts, -0.22, 0.18)
    return jnp.clip(strengthened(entries, jax.random.fold_in(rng, 3), *heavy), -bound, bound).astype(held_as)


def setup_inputs(seed: int = 0) -> dict:
    seeds = jax.random.split(jax.random.key(seed), 12)
    return {
        "inputs": bell_draw(seeds[0], (SEQS, LENGTH, D), 1.0, 6.0, ((0, 8), (1, 4))),
        "grad_out": heavy_noise(seeds[1], (SEQS, LENGTH, D), 1.0, 6.0, ((0, 8), (1, 4)), (0, 2, 8, 2.0)),
        "ln_gain": jnp.clip(1.0 + 0.18 * jax.random.normal(seeds[2], (D,), jnp.float32), 0.1, 1.9),
        "ln_bias": bell_draw(seeds[3], (D,), 0.3, 1.5, ((0, 32),), jnp.float32),
        "skip_scale": bell_draw(seeds[4], (D,), 1.0, 4.0, ((0, 32),), jnp.float32),
        "w_glu": bell_draw(seeds[5], (D, GLU), D ** -0.5, 0.25, ((0, 32),), jnp.float32),
        "b_glu": bell_draw(seeds[6], (GLU,), 0.3, 1.5, ((0, 32),), jnp.float32),
        "log_dt": jnp.clip(-6.9 + 4.6000001430511475 * jax.random.uniform(seeds[7], (D,), jnp.float32) ** shard_levels(seeds[7], (D,), ((0, 32),), -0.2, 0.2), -6.9, -2.3),
        "log_a_real": jnp.clip(-1.2 + 1.2 * jax.random.uniform(seeds[8], (D, N_MODES), jnp.float32) ** shard_levels(seeds[8], (D, N_MODES), ((0, 32),), -0.2, 0.2), -1.2, 0.0),
        "a_imag": jnp.clip(60.0 * jax.random.uniform(seeds[9], (D, N_MODES), jnp.float32) ** shard_levels(seeds[9], (D, N_MODES), ((0, 32),), -0.2, 0.2), 0.0, 60.0),
        "c_coef": bell_draw(seeds[10], (D, 2 * N_MODES), 0.5, 3.0, ((0, 32),), jnp.float32),
    }


EPS = 1e-05
HIGH = lax.Precision.HIGHEST

@jax.custom_vjp
def low(v):
    return lax.optimization_barrier(v.astype(jnp.bfloat16)).astype(jnp.float32)

@jax.custom_vjp
def low_back(v):
    return v

def low_keep(v):
    return (low(v), None)

def low_pass(kept, grad):
    return (grad,)

def back_keep(v):
    return (v, None)

def back_low(kept, grad):
    return (low(grad),)
low.defvjp(low_keep, low_pass)
low_back.defvjp(back_keep, back_low)

def kernel_block(log_dt, log_a_real, a_imag, c_coef, start, count):
    mode_count = log_a_real.shape[1]
    step_size = jnp.exp(log_dt)[:, None]
    a_real = -jnp.exp(log_a_real)
    decay = a_real * step_size
    turn = a_imag * step_size
    growth = jnp.exp(decay)
    ex_re = growth * jnp.cos(turn) - 1.0
    ex_im = growth * jnp.sin(turn)
    norm_sq = a_real * a_real + a_imag * a_imag
    ratio_re = (ex_re * a_real + ex_im * a_imag) / norm_sq
    ratio_im = (ex_im * a_real - ex_re * a_imag) / norm_sq
    c_re = c_coef[:, :mode_count]
    c_im = c_coef[:, mode_count:]
    coef_re = c_re * ratio_re - c_im * ratio_im
    coef_im = c_re * ratio_im + c_im * ratio_re
    places = (start + jnp.arange(count)).astype(jnp.float32)
    phase = turn[:, :, None] * places
    damping = jnp.exp(decay[:, :, None] * places)
    terms = damping * (coef_re[:, :, None] * jnp.cos(phase) - coef_im[:, :, None] * jnp.sin(phase))
    return 2.0 * lax.optimization_barrier(jnp.sum(terms, axis=1))

def toeplitz_blocks(kernel, lag_block):
    tap_count = kernel.shape[1]
    span_len = tap_count // 4
    row_ids = jnp.arange(span_len)[:, None]
    col_ids = jnp.arange(span_len)[None, :]
    lag_ids = span_len * lag_block + col_ids - row_ids
    valid = (lag_ids >= 0) & (lag_ids < tap_count)
    picked = jnp.take(kernel, jnp.clip(lag_ids, 0, tap_count - 1), axis=1)
    return jnp.where(valid[None], picked, jnp.zeros((), kernel.dtype))

def causal_mix(signal, blocks):
    seq_count, seq_len, channels = signal.shape
    span_len = blocks.shape[2]
    tap_count = 4 * span_len
    extended = jnp.concatenate([jnp.zeros((seq_count, tap_count, channels), jnp.float32), signal], axis=1)
    total = jnp.zeros((seq_count, seq_len // span_len, span_len, channels), jnp.float32)
    for lag_block in range(5):
        begin = span_len * (4 - lag_block)
        piece = extended[:, begin:begin + seq_len].reshape(seq_count, seq_len // span_len, span_len, channels)
        total = total + jnp.einsum('btch,hcr->btrh', piece, blocks[lag_block], precision=HIGH)
    return total.reshape(seq_count, seq_len, channels)

def full_layer(x_groups, ln_gain, ln_bias, skip_scale, w_glu, b_glu, log_dt, log_a_real, a_imag, c_coef):
    kernel = low(kernel_block(log_dt, log_a_real, a_imag, c_coef, 0, KTAPS))
    blocks = jnp.stack([toeplitz_blocks(kernel, lag_block) for lag_block in range(5)])
    gain_r = low(ln_gain)
    shift_r = low(ln_bias)
    skip_r = low(skip_scale)
    weight_r = low(w_glu)
    glu_bias = low(b_glu)

    def one_group(seq_group):
        row_mean = lax.optimization_barrier(jnp.mean(seq_group, axis=-1, keepdims=True))
        centered = seq_group - row_mean
        row_var = lax.optimization_barrier(jnp.mean(centered * centered, axis=-1, keepdims=True))
        normed = centered * lax.rsqrt(row_var + EPS) * gain_r + shift_r
        mixed_pre = low_back(causal_mix(low(normed), blocks) + skip_r * normed)
        activ = low(jax.nn.gelu(mixed_pre, approximate=False))
        glu_pre = low_back(jnp.einsum('slh,hg->slg', activ, weight_r, precision=HIGH) + glu_bias)
        half_dim = glu_pre.shape[-1] // 2
        return seq_group + glu_pre[..., :half_dim] * jax.nn.sigmoid(glu_pre[..., half_dim:])
    return lax.map(jax.checkpoint(one_group), x_groups)

def reference(inputs, grad_out, ln_gain, ln_bias, skip_scale, w_glu, b_glu, log_dt, log_a_real, a_imag, c_coef):
    group_size = 2 if SEQS % 2 == 0 else 1
    group_shape = (SEQS // group_size, group_size, LENGTH, D)
    x_full = inputs.astype(jnp.float32).reshape(group_shape)
    g_full = grad_out.astype(jnp.float32).reshape(group_shape)
    result, pull_back = jax.vjp(full_layer, x_full, ln_gain, ln_bias, skip_scale, w_glu, b_glu, log_dt, log_a_real, a_imag, c_coef)
    grad_list = pull_back(g_full)
    return (result.reshape(SEQS, LENGTH, D).astype(jnp.bfloat16), grad_list[0].reshape(SEQS, LENGTH, D).astype(jnp.bfloat16), grad_list[1], grad_list[2], grad_list[3], grad_list[4], grad_list[5], grad_list[6], grad_list[7], grad_list[8], grad_list[9])
```

```python
from functools import partial

import jax
import jax.numpy as jnp
import numpy as np
from jax import lax
from jax.sharding import PartitionSpec as P

KTAPS = 512


EPS = 1e-05


def passed_along(value, axis, steps):
    count = lax.axis_size(axis)
    first, last = (max(0, -steps), min(count, count - steps))
    return lax.ppermute(value, axis, [(source, source + steps) for source in range(first, last)])


def kernel_block(log_dt, log_a_real, a_imag, c_coef, start, count):
    mode_count = log_a_real.shape[1]
    step_size = jnp.exp(log_dt)[:, None]
    a_real = -jnp.exp(log_a_real)
    decay = a_real * step_size
    turn = a_imag * step_size
    growth = jnp.exp(decay)
    ex_re = growth * jnp.cos(turn) - 1.0
    ex_im = growth * jnp.sin(turn)
    norm_sq = a_real * a_real + a_imag * a_imag
    ratio_re = (ex_re * a_real + ex_im * a_imag) / norm_sq
    ratio_im = (ex_im * a_real - ex_re * a_imag) / norm_sq
    c_re = c_coef[:, :mode_count]
    c_im = c_coef[:, mode_count:]
    coef_re = c_re * ratio_re - c_im * ratio_im
    coef_im = c_re * ratio_im + c_im * ratio_re
    places = (start + jnp.arange(count)).astype(jnp.float32)
    phase = turn[:, :, None] * places
    damping = jnp.exp(decay[:, :, None] * places)
    terms = damping * (coef_re[:, :, None] * jnp.cos(phase) - coef_im[:, :, None] * jnp.sin(phase))
    return 2.0 * jnp.sum(terms, axis=1)


def transforms(taps):
    angle = np.outer(np.arange(taps) + 0.5, np.arange(taps)) * (np.pi / taps)
    forward = np.concatenate([np.cos(angle), -np.sin(angle)], axis=0)
    inverse = forward.T / taps
    return forward.astype(jnp.bfloat16), inverse.astype(jnp.bfloat16)


def body(
    inputs, grad_out, ln_gain, ln_bias, skip_scale, w_glu, b_glu, log_dt, log_a_real, a_imag, c_coef
):
    seq_count, own_len, channels = inputs.shape
    gain_low = ln_gain.astype(jnp.bfloat16)
    shift_low = ln_bias.astype(jnp.bfloat16)
    skip_low = skip_scale.astype(jnp.bfloat16)
    weight_low = w_glu.astype(jnp.bfloat16)
    bias_low = b_glu.astype(jnp.bfloat16)
    mode_own = (log_dt, log_a_real, a_imag, c_coef)
    own_kernel = kernel_block(*mode_own, 0, KTAPS).astype(jnp.bfloat16)
    gathered = (
        lax.all_gather(gain_low, ("dp", "seq"), axis=0, tiled=True),
        lax.all_gather(shift_low, ("dp", "seq"), axis=0, tiled=True),
        lax.all_gather(skip_low, ("dp", "seq"), axis=0, tiled=True),
        lax.all_gather(weight_low, ("dp", "seq"), axis=0, tiled=True),
        lax.all_gather(bias_low, ("dp", "seq"), axis=0, tiled=True),
        lax.all_gather(own_kernel, ("dp", "seq"), axis=0, tiled=True),
    )
    kernel_b = gathered[5]
    taps = own_len
    forward, inverse = transforms(taps)
    sign = jnp.where(jnp.arange(taps) % 2 == 0, 1.0, -1.0).astype(jnp.float32)[:, None]

    def to_spectrum(block):
        both = jnp.dot(forward, block, preferred_element_type=jnp.float32)
        return both[:taps], both[taps:]

    def from_spectrum(real, imag):
        both = jnp.concatenate([real, imag], axis=0).astype(jnp.bfloat16)
        return jnp.dot(inverse, both, preferred_element_type=jnp.float32)

    kernel_re, kernel_im = to_spectrum(kernel_b.T)
    gain_full = gathered[0].astype(jnp.float32)
    shift_full = gathered[1].astype(jnp.float32)
    skip_full = gathered[2].astype(jnp.float32)
    weight_b = gathered[3]
    glu_bias = gathered[4].astype(jnp.float32)
    x_float = inputs.astype(jnp.float32)
    row_mean = jnp.mean(x_float, axis=-1, keepdims=True)
    centered = x_float - row_mean
    row_var = jnp.mean(centered * centered, axis=-1, keepdims=True)
    inv_std = lax.rsqrt(row_var + EPS)
    x_hat = centered * inv_std
    normed = x_hat * gain_full + shift_full
    normed_b = normed.astype(jnp.bfloat16)
    own_re, own_im = to_spectrum(normed_b[0])
    left_re, left_im = to_spectrum(passed_along(normed_b, "seq", 1)[0])
    source_re = own_re - sign * left_im
    source_im = own_im + sign * left_re
    conv = from_spectrum(
        kernel_re * source_re - kernel_im * source_im,
        kernel_re * source_im + kernel_im * source_re,
    )
    mixed_pre = conv[None] + skip_full * normed
    activ, gelu_pull = jax.vjp(partial(jax.nn.gelu, approximate=False), mixed_pre)
    activ_b = activ.astype(jnp.bfloat16)
    glu_pre = (
        jnp.einsum("slh,hg->slg", activ_b, weight_b, preferred_element_type=jnp.float32) + glu_bias
    )
    half_dim = glu_pre.shape[-1] // 2
    lin_part = glu_pre[..., :half_dim]
    gate_sig = jax.nn.sigmoid(glu_pre[..., half_dim:])
    result = (x_float + lin_part * gate_sig).astype(jnp.bfloat16)
    grad_f = grad_out.astype(jnp.float32)
    d_pre = jnp.concatenate(
        [grad_f * gate_sig, grad_f * lin_part * gate_sig * (1.0 - gate_sig)], axis=-1
    ).astype(jnp.bfloat16)
    d_weight = jnp.einsum("slh,slg->hg", activ_b, d_pre, preferred_element_type=jnp.float32)
    d_glu_bias = jnp.sum(d_pre.astype(jnp.float32), axis=(0, 1))
    d_act = jnp.einsum("slg,hg->slh", d_pre, weight_b, preferred_element_type=jnp.float32)
    d_mix = gelu_pull(d_act)[0].astype(jnp.bfloat16)
    d_mix_f = d_mix.astype(jnp.float32)
    d_skip = jnp.sum(d_mix_f * normed, axis=(0, 1))
    mix_re, mix_im = to_spectrum(d_mix[0])
    d_kernel = from_spectrum(
        source_re * mix_re + source_im * mix_im, source_re * mix_im - source_im * mix_re
    ).T
    right_re, right_im = to_spectrum(passed_along(d_mix, "seq", -1)[0])
    sum_re = mix_re + sign * right_im
    sum_im = mix_im - sign * right_re
    d_conv = from_spectrum(
        kernel_re * sum_re + kernel_im * sum_im, kernel_re * sum_im - kernel_im * sum_re
    )[None]
    d_normed = d_conv + skip_full * d_mix_f
    d_gain = jnp.sum(d_normed * x_hat, axis=(0, 1))
    d_shift = jnp.sum(d_normed, axis=(0, 1))
    scaled = d_normed * gain_full
    d_input = (
        inv_std
        * (
            scaled
            - jnp.mean(scaled, axis=-1, keepdims=True)
            - x_hat * jnp.mean(scaled * x_hat, axis=-1, keepdims=True)
        )
        + grad_f
    )
    grad_in = d_input.astype(jnp.bfloat16)
    summed = (
        lax.psum_scatter(d_gain, ("dp", "seq"), scatter_dimension=0, tiled=True),
        lax.psum_scatter(d_shift, ("dp", "seq"), scatter_dimension=0, tiled=True),
        lax.psum_scatter(d_skip, ("dp", "seq"), scatter_dimension=0, tiled=True),
        lax.psum_scatter(d_weight, ("dp", "seq"), scatter_dimension=0, tiled=True),
        lax.psum_scatter(d_glu_bias, ("dp", "seq"), scatter_dimension=0, tiled=True),
        lax.psum_scatter(d_kernel, ("dp", "seq"), scatter_dimension=0, tiled=True),
    )
    _, own_pull = jax.vjp(partial(kernel_block, start=0, count=KTAPS), *mode_own)
    mode_grads = own_pull(summed[5])
    return (
        result,
        grad_in,
        summed[0],
        summed[1],
        summed[2],
        summed[3],
        summed[4],
        mode_grads[0],
        mode_grads[1],
        mode_grads[2],
        mode_grads[3],
    )


def solution(mesh):
    in_specs = (
        P("dp", "seq", None),
        P("dp", "seq", None),
        P(("dp", "seq")),
        P(("dp", "seq")),
        P(("dp", "seq")),
        P(("dp", "seq"), None),
        P(("dp", "seq")),
        P(("dp", "seq")),
        P(("dp", "seq"), None),
        P(("dp", "seq"), None),
        P(("dp", "seq"), None),
    )
    out_specs = (
        P("dp", "seq", None),
        P("dp", "seq", None),
        P(("dp", "seq")),
        P(("dp", "seq")),
        P(("dp", "seq")),
        P(("dp", "seq"), None),
        P(("dp", "seq")),
        P(("dp", "seq")),
        P(("dp", "seq"), None),
        P(("dp", "seq"), None),
        P(("dp", "seq"), None),
    )
    return jax.shard_map(body, mesh=mesh, in_specs=in_specs, out_specs=out_specs, check_vma=False)
```

```python
from functools import partial

import jax
import jax.numpy as jnp
import numpy as np
from jax import lax
from jax.experimental import pallas as pl
from jax.experimental.pallas import tpu as pltpu
from jax.sharding import PartitionSpec as P

KTAPS = 512


EPS = 1e-05


def passed_along(value, axis, steps):
    count = lax.axis_size(axis)
    first, last = (max(0, -steps), min(count, count - steps))
    return lax.ppermute(value, axis, [(source, source + steps) for source in range(first, last)])


def kernel_block(log_dt, log_a_real, a_imag, c_coef, start, count):
    mode_count = log_a_real.shape[1]
    step_size = jnp.exp(log_dt)[:, None]
    a_real = -jnp.exp(log_a_real)
    decay = a_real * step_size
    turn = a_imag * step_size
    growth = jnp.exp(decay)
    ex_re = growth * jnp.cos(turn) - 1.0
    ex_im = growth * jnp.sin(turn)
    norm_sq = a_real * a_real + a_imag * a_imag
    ratio_re = (ex_re * a_real + ex_im * a_imag) / norm_sq
    ratio_im = (ex_im * a_real - ex_re * a_imag) / norm_sq
    c_re = c_coef[:, :mode_count]
    c_im = c_coef[:, mode_count:]
    coef_re = c_re * ratio_re - c_im * ratio_im
    coef_im = c_re * ratio_im + c_im * ratio_re
    places = (start + jnp.arange(count)).astype(jnp.float32)
    phase = turn[:, :, None] * places
    damping = jnp.exp(decay[:, :, None] * places)
    terms = damping * (coef_re[:, :, None] * jnp.cos(phase) - coef_im[:, :, None] * jnp.sin(phase))
    return 2.0 * jnp.sum(terms, axis=1)


def transforms(taps):
    angle = np.outer(np.arange(taps) + 0.5, np.arange(taps)) * (np.pi / taps)
    forward = np.concatenate([np.cos(angle), -np.sin(angle)], axis=0)
    inverse = forward.T / taps
    return forward.astype(jnp.bfloat16), inverse.astype(jnp.bfloat16)


def body(
    inputs, grad_out, ln_gain, ln_bias, skip_scale, w_glu, b_glu, log_dt, log_a_real, a_imag, c_coef
):
    seq_count, own_len, channels = inputs.shape
    gain_low = ln_gain.astype(jnp.bfloat16)
    shift_low = ln_bias.astype(jnp.bfloat16)
    skip_low = skip_scale.astype(jnp.bfloat16)
    weight_low = w_glu.astype(jnp.bfloat16)
    bias_low = b_glu.astype(jnp.bfloat16)
    mode_own = (log_dt, log_a_real, a_imag, c_coef)
    own_kernel = kernel_block(*mode_own, 0, KTAPS).astype(jnp.bfloat16)
    gathered = (
        lax.all_gather(gain_low, ("dp", "seq"), axis=0, tiled=True),
        lax.all_gather(shift_low, ("dp", "seq"), axis=0, tiled=True),
        lax.all_gather(skip_low, ("dp", "seq"), axis=0, tiled=True),
        lax.all_gather(weight_low, ("dp", "seq"), axis=0, tiled=True),
        lax.all_gather(bias_low, ("dp", "seq"), axis=0, tiled=True),
        lax.all_gather(own_kernel, ("dp", "seq"), axis=0, tiled=True),
    )
    kernel_b = gathered[5]
    taps = own_len
    forward, inverse = transforms(taps)
    sign = jnp.where(jnp.arange(taps) % 2 == 0, 1.0, -1.0).astype(jnp.float32)[:, None]

    def to_spectrum(block):
        both = jnp.dot(forward, block, preferred_element_type=jnp.float32)
        return both[:taps], both[taps:]

    def from_spectrum(real, imag):
        both = jnp.concatenate([real, imag], axis=0).astype(jnp.bfloat16)
        return jnp.dot(inverse, both, preferred_element_type=jnp.float32)

    kernel_re, kernel_im = to_spectrum(kernel_b.T)
    gain_full = gathered[0].astype(jnp.float32)
    shift_full = gathered[1].astype(jnp.float32)
    skip_full = gathered[2].astype(jnp.float32)
    weight_b = gathered[3]
    glu_bias = gathered[4].astype(jnp.float32)
    x_float = inputs.astype(jnp.float32)
    row_mean = jnp.mean(x_float, axis=-1, keepdims=True)
    centered = x_float - row_mean
    row_var = jnp.mean(centered * centered, axis=-1, keepdims=True)
    inv_std = lax.rsqrt(row_var + EPS)
    x_hat = centered * inv_std
    normed = x_hat * gain_full + shift_full
    normed_b = normed.astype(jnp.bfloat16)
    own_re, own_im = to_spectrum(normed_b[0])
    left_re, left_im = to_spectrum(passed_along(normed_b, "seq", 1)[0])
    source_re = own_re - sign * left_im
    source_im = own_im + sign * left_re
    conv = from_spectrum(
        kernel_re * source_re - kernel_im * source_im,
        kernel_re * source_im + kernel_im * source_re,
    )
    mixed_pre = conv[None] + skip_full * normed
    activ, gelu_pull = jax.vjp(partial(jax.nn.gelu, approximate=False), mixed_pre)
    activ_b = activ.astype(jnp.bfloat16)
    glu_pre = (
        jnp.einsum("slh,hg->slg", activ_b, weight_b, preferred_element_type=jnp.float32) + glu_bias
    )
    half_dim = glu_pre.shape[-1] // 2
    lin_part = glu_pre[..., :half_dim]
    gate_sig = jax.nn.sigmoid(glu_pre[..., half_dim:])
    result = (x_float + lin_part * gate_sig).astype(jnp.bfloat16)
    grad_f = grad_out.astype(jnp.float32)
    d_pre = jnp.concatenate(
        [grad_f * gate_sig, grad_f * lin_part * gate_sig * (1.0 - gate_sig)], axis=-1
    ).astype(jnp.bfloat16)
    d_weight = jnp.einsum("slh,slg->hg", activ_b, d_pre, preferred_element_type=jnp.float32)
    d_glu_bias = jnp.sum(d_pre.astype(jnp.float32), axis=(0, 1))
    d_act = jnp.einsum("slg,hg->slh", d_pre, weight_b, preferred_element_type=jnp.float32)
    d_mix = gelu_pull(d_act)[0].astype(jnp.bfloat16)
    d_mix_f = d_mix.astype(jnp.float32)
    d_skip = jnp.sum(d_mix_f * normed, axis=(0, 1))
    mix_re, mix_im = to_spectrum(d_mix[0])
    d_kernel = from_spectrum(
        source_re * mix_re + source_im * mix_im, source_re * mix_im - source_im * mix_re
    ).T
    right_re, right_im = to_spectrum(passed_along(d_mix, "seq", -1)[0])
    sum_re = mix_re + sign * right_im
    sum_im = mix_im - sign * right_re
    d_conv = from_spectrum(
        kernel_re * sum_re + kernel_im * sum_im, kernel_re * sum_im - kernel_im * sum_re
    )[None]
    d_normed = d_conv + skip_full * d_mix_f
    d_gain = jnp.sum(d_normed * x_hat, axis=(0, 1))
    d_shift = jnp.sum(d_normed, axis=(0, 1))
    scaled = d_normed * gain_full
    d_input = (
        inv_std
        * (
            scaled
            - jnp.mean(scaled, axis=-1, keepdims=True)
            - x_hat * jnp.mean(scaled * x_hat, axis=-1, keepdims=True)
        )
        + grad_f
    )
    grad_in = d_input.astype(jnp.bfloat16)
    summed = (
        lax.psum_scatter(d_gain, ("dp", "seq"), scatter_dimension=0, tiled=True),
        lax.psum_scatter(d_shift, ("dp", "seq"), scatter_dimension=0, tiled=True),
        lax.psum_scatter(d_skip, ("dp", "seq"), scatter_dimension=0, tiled=True),
        lax.psum_scatter(d_weight, ("dp", "seq"), scatter_dimension=0, tiled=True),
        lax.psum_scatter(d_glu_bias, ("dp", "seq"), scatter_dimension=0, tiled=True),
        lax.psum_scatter(d_kernel, ("dp", "seq"), scatter_dimension=0, tiled=True),
    )
    _, own_pull = jax.vjp(partial(kernel_block, start=0, count=KTAPS), *mode_own)
    mode_grads = own_pull(summed[5])
    return (
        result,
        grad_in,
        summed[0],
        summed[1],
        summed[2],
        summed[3],
        summed[4],
        mode_grads[0],
        mode_grads[1],
        mode_grads[2],
        mode_grads[3],
    )


MESH = pl.DeviceIdType.MESH
ROWS = 16


def pair_lanes(value):
    return jnp.concatenate([value[:8], value[8:]], axis=1)


def unpair_lanes(value):
    half = value.shape[1] // 2
    return jnp.concatenate([value[:, :half], value[:, half:]], axis=0)


def column_of(row):
    n = row.shape[1]
    at = lax.broadcasted_iota(jnp.int32, (n, n), 0) == lax.broadcasted_iota(jnp.int32, (n, n), 1)
    return jnp.sum(jnp.where(at, jnp.broadcast_to(row, (n, n)), 0.0), axis=1, keepdims=True)


def row_of(column):
    n = column.shape[0]
    at = lax.broadcasted_iota(jnp.int32, (n, n), 0) == lax.broadcasted_iota(jnp.int32, (n, n), 1)
    return jnp.sum(jnp.where(at, jnp.broadcast_to(column, (n, n)), 0.0), axis=0, keepdims=True)


def mode_terms(ldt, lar, ai, cc):
    n_modes = lar.shape[1]
    dt = column_of(jnp.exp(ldt))
    dt = jnp.concatenate(
        [jnp.broadcast_to(dt[:8], (8, n_modes)), jnp.broadcast_to(dt[8:], (8, n_modes))], axis=1
    )
    a_re, a_im = -jnp.exp(pair_lanes(lar)), pair_lanes(ai)
    decay, turn = a_re * dt, a_im * dt
    growth = jnp.exp(decay)
    z_re, z_im = growth * jnp.cos(turn), growth * jnp.sin(turn)
    ex_re, ex_im = z_re - 1.0, z_im
    norm_sq = a_re * a_re + a_im * a_im
    r_re = (ex_re * a_re + ex_im * a_im) / norm_sq
    r_im = (ex_im * a_re - ex_re * a_im) / norm_sq
    c_re, c_im = pair_lanes(cc[:, :n_modes]), pair_lanes(cc[:, n_modes:])
    w_re, w_im = c_re * r_re - c_im * r_im, c_re * r_im + c_im * r_re
    return dt, (a_re, a_im), (z_re, z_im), norm_sq, (r_re, r_im), (c_re, c_im), (w_re, w_im)


def times(a, b):
    return a[0] * b[0] - a[1] * b[1], a[0] * b[1] + a[1] * b[0]


def split_low(value):
    high = value.astype(jnp.bfloat16)
    return high, (value - high.astype(jnp.float32)).astype(jnp.bfloat16)


def dot_nn(a, b):
    return lax.dot_general(a, b, (((1,), (0,)), ((), ())), preferred_element_type=jnp.float32)


def dot_nt(a, b):
    return lax.dot_general(a, b, (((1,), (1,)), ((), ())), preferred_element_type=jnp.float32)


def layer_kernel(
    x_hbm, g_hbm, fwd_hbm, inv_hbm, pick_hbm, mask_hbm, fold_hbm, turn_hbm,
    w_hbm, gain_hbm, shift_hbm, skip_hbm, bias_hbm, ldt_hbm, lar_hbm, ai_hbm, cc_hbm,
    res_v, gin_v, dgain_ref, dshift_ref, dskip_ref, dw_ref, dbias_ref, dldt_ref, dlar_ref, dai_ref, dcc_ref,
    w_ref, gain_ref, shift_ref, skip_ref, bias_ref, ldt_ref, lar_ref, ai_ref, cc_ref,
    x_v, g_v, left_v, fwd, inv, pick, mask, fold, turn, kern, weight, powers, e_low, t_all,
    share_in, share_out, share_in1, share_mid, share_in2, share_end, share_in3, rows_f, x_hat, inv_std, left_hat, normed, own_b, left_b,
    k_spec, u_spec, mixed, slope, activ, activ_t, d_act, d_mix, right_v, d_spec, d_norm,
    dw_own, dw_in1, dw_mid, dw_in2, dw_low, dw_in3, dw_end, dw_in4,
    dk_own, dk_low, dk_in1, dk_mid, dk_cut, dk_in2, dk_end, dk_in3,
    local, sends, recvs,
):
    f32, bf16 = jnp.float32, jnp.bfloat16
    tokens, channels = x_v.shape
    taps = KTAPS
    half, fourth = taps // 2, taps // 4
    dp, seq = lax.axis_index("dp"), lax.axis_index("seq")
    index = dp * 4 + seq
    z, y, x, c = lax.div(dp, 2), lax.rem(dp, 2), lax.div(seq, 2), lax.rem(seq, 2)
    flip_y, flip_x, flip_c = 1 - y, 1 - x, 1 - c

    def device(z, y, x, c):
        return (z * 2 + y, x * 2 + c)

    z_peers = [(lax.rem(z + k, 4), y, x, c) for k in (1, 2, 3)]
    plane_peers = [
        (z, lax.rem(y + k // 2, 2), lax.rem(x + k % 2, 2), c) for k in (1, 2, 3)
    ]
    x_peer, y_peer, core_peer = (z, y, flip_x, c), (z, flip_y, x, c), (z, y, x, flip_c)
    used = {"send": 0, "recv": 0}
    departures = []

    def claim(kind):
        used[kind] += 1
        return used[kind] - 1

    def sender(total):
        number = claim("send")
        departures.append((sends.at[number], total))
        return sends.at[number]

    def arrive(semaphore, total):
        pltpu.make_async_copy(total, total, semaphore).wait()

    def start(copies, send_sem, total, recv_sem=None):
        if recv_sem is None:
            recv_sem = recvs.at[claim("recv")]
        for source, target, peer in copies:
            pltpu.make_async_remote_copy(
                src_ref=source, dst_ref=target, send_sem=send_sem, recv_sem=recv_sem,
                device_id=device(*peer), device_id_type=MESH,
            ).start()
        return recv_sem, total

    def finish(arrival):
        arrive(*arrival)

    def load(copies):
        for copy in copies:
            copy.start()
        return copies

    def take(ref, lines, first=0, count=4):
        return jnp.concatenate([ref[first + i, lines, :] for i in range(count)], axis=1)

    def put(ref, lines, value, first=0):
        for i in range(value.shape[1] // 128):
            ref[first + i, lines, :] = value[:, 128 * i : 128 * (i + 1)]

    barrier = pltpu.get_barrier_semaphore()
    peers = z_peers + plane_peers + [core_peer, (z, y, flip_x, flip_c)]
    for peer in peers:
        pl.semaphore_signal(barrier, inc=1, device_id=device(*peer), device_id_type=MESH)
    def fetch(pairs, first):
        return load([pltpu.make_async_copy(source, target, local.at[first + i]) for i, (source, target) in enumerate(pairs)])

    params = fetch([
        (gain_hbm, gain_ref), (shift_hbm, shift_ref), (skip_hbm, skip_ref), (bias_hbm, bias_ref), (w_hbm, w_ref),
        (ldt_hbm, ldt_ref), (lar_hbm, lar_ref), (ai_hbm, ai_ref), (cc_hbm, cc_ref),
    ], 8)
    loads = fetch([
        (fold_hbm, fold), (x_hbm, x_v), (pick_hbm, pick), (mask_hbm, mask), (fwd_hbm, fwd), (inv_hbm, inv), (g_hbm, g_v),
        (turn_hbm, turn),
    ], 0)
    for copy in params:
        copy.wait()
    low = [ref[...].astype(bf16).astype(f32) for ref in (gain_ref, shift_ref, skip_ref, bias_ref)]
    share_in[z, y, x, c] = jnp.concatenate(low + [jnp.zeros((1, 128 - 5 * ROWS), f32)], axis=1)
    for q in range(4):
        weight[q, z, y, x, c] = jnp.concatenate(
            [w_ref[:, 128 * q : 128 * q + 128], w_ref[:, channels + 128 * q : channels + 128 * q + 128]], axis=1
        ).astype(bf16)
    pl.semaphore_wait(barrier, len(peers))
    three = pl.ds(0, 3)

    def same(ref, peers, total, send_sem=None, recv_sem=None):
        return start([(ref, ref, peer) for peer in peers], send_sem or sender(total), total, recv_sem)

    share_plane = same(share_in.at[z, y, x, c], plane_peers, share_in.at[three, 0, 0, 0])
    weight_x = same(weight.at[:, z, y, x, c], [x_peer], weight.at[:, 0, 0, 0, 0])
    right_copy = pltpu.make_async_remote_copy(
        src_ref=x_hbm, dst_ref=left_v, send_sem=sends.at[claim("send")], recv_sem=recvs.at[claim("recv")],
        device_id=(dp, seq + 1), device_id_type=MESH,
    )

    @pl.when(seq < 3)
    def _():
        right_copy.start()

    _, _, unit, _, _, _, coef = mode_terms(ldt_ref[...], lar_ref[...], ai_ref[...], cc_ref[...])
    power = times(unit, unit)
    for bit in range(6):
        powers[bit, 0], powers[bit, 1] = power
        power = times(power, power)
    jumps = taps // 64
    jump = (jnp.ones((8, 128), f32), jnp.zeros((8, 128), f32))
    for m in range(jumps // 2):
        for place, value in ((m, jump), (m + jumps // 2, times(jump, unit))):
            powers[6 + place, 0], powers[6 + place, 1] = value
            powers[6 + jumps + place, 0], powers[6 + jumps + place, 1] = times(coef, value)
        jump = times(jump, power)

    def one_pair(p, _):
        def row(bit):
            return powers[bit, 0, pl.ds(p, 1), :], powers[bit, 1, pl.ds(p, 1), :]

        sub = lax.broadcasted_iota(jnp.int32, (8, 128), 0)
        base = (jnp.ones((8, 128), f32), jnp.zeros((8, 128), f32))
        for bit in range(3):
            r, i = row(bit)
            on = lax.rem(lax.div(sub, 2**bit), 2) == 1
            base = times(base, (jnp.where(on, r, 1.0), jnp.where(on, i, 0.0)))
        for bit in range(3, 6):
            more = times(base, row(bit))
            base = tuple(jnp.concatenate([old, new], axis=0) for old, new in zip(base, more))
        at = pl.ds(pl.multiple_of(p * 256, 256), 256)
        for m in range(jumps):
            lines = slice(64 * m, 64 * m + 64)
            e_low[lines, at] = jnp.concatenate(times(base, row(6 + m)), axis=1).astype(bf16)
            lead = row(6 + jumps + m)
            t_all[lines, at] = jnp.concatenate(split_low(lead[0] * base[0] - lead[1] * base[1]), axis=1)
        return 0

    lax.fori_loop(0, 8, one_pair, 0)
    loads[0].wait()
    kern[z, y, x, c] = (2.0 * dot_nn(t_all[...], fold[...])).T[:ROWS].astype(bf16)
    kern_z = same(kern.at[z, y, x, c], z_peers, kern.at[three, 0, 0, 0])
    finish(share_plane)
    share_z = same(share_in.at[z, :, :, c], z_peers, share_in.at[three, :, :, 0])
    finish(weight_x)
    z_sender, y_sender = sender(weight.at[:, three, 0, :, 0]), sender(weight.at[:, :, 0, :, 0])
    core_sender = sender(weight.at[:, :, :, :, 0])

    def weight_to_z(q):
        return same(weight.at[q, z, y, :, c], z_peers, weight.at[q, three, 0, :, 0], z_sender)

    def weight_to_y(q):
        finish(weight_z[q])
        piece = weight.at[q, :, y, :, c]
        weight_core.append(same(piece, [core_peer], weight.at[q, :, :, :, 0], core_sender))
        return same(piece, [y_peer], weight.at[q, :, 0, :, 0], y_sender)

    def weight_to_core(q):
        finish(weight_y[q])
        same(weight.at[q, :, flip_y, :, c], [core_peer], weight.at[q, :, :, :, 0], core_sender, weight_core[q][0])

    weight_core, weight_z = [], [weight_to_z(0)]

    def normalise(source, hat, keep_std):
        def rows(i, _):
            at = pl.ds(pl.multiple_of(i * 128, 128), 128)
            value = source[at, :].astype(f32)
            centered = value - jnp.mean(value, axis=1, keepdims=True)
            scale = lax.rsqrt(jnp.mean(centered * centered, axis=1, keepdims=True) + EPS)
            put(hat, at, centered * scale)
            if keep_std:
                inv_std[at, :] = jnp.broadcast_to(scale, (128, 128))
            return 0

        lax.fori_loop(0, tokens // 128, rows, 0)

    loads[1].wait()
    normalise(x_v, x_hat, True)
    finish(kern_z)
    halves = [pl.ds(0, 2), pl.ds(2, 2)]
    plane_sender, pair_sender = sender(dk_in2), sender(kern.at[:, :, :, 0])
    kern_plane = [same(kern.at[at, y, x, c], plane_peers, dk_in2.at[:, at], plane_sender) for at in halves]
    for q in range(1, 4):
        weight_z.append(weight_to_z(q))
    finish(share_z)
    share_core = same(share_in.at[:, :, :, c], [core_peer], share_in.at[:, :, :, 0])
    finish(share_core)
    loads[2].wait()
    loads[3].wait()
    shares = share_in[...].reshape(32, 1, 128).reshape(32, 128).astype(bf16)
    spread = dot_nn(shares, pick[...]) * mask[...].astype(f32)
    spread = jnp.sum(spread, axis=0, keepdims=True)
    rows_f[...] = jnp.concatenate(
        [spread[:, channels * i : channels * (i + 1)] for i in range(5)] + [jnp.zeros((3, channels), f32)], axis=0
    )
    gain, shift = rows_f[0:1, :], rows_f[1:2, :]

    def every_other(i, parity):
        return pl.ds(128 * i + parity, 64, stride=2)

    def sixty_four(i):
        return pl.ds(pl.multiple_of(64 * i, 64), 64)

    def shifted(i, _):
        at = pl.ds(pl.multiple_of(i * 128, 128), 128)
        put(normed, at, take(x_hat, at) * gain + shift)
        for parity in range(2):
            own_b[parity, sixty_four(i)] = take(normed, every_other(i, parity)).astype(bf16)
        return 0

    lax.fori_loop(0, tokens // 128, shifted, 0)
    loads[4].wait()
    loads[5].wait()

    loads[7].wait()
    wide = 256

    def lanes(j):
        return pl.ds(pl.multiple_of(j * wide, wide), wide)

    def turned(value, back):
        sine = turn[1]
        return times(value, (jnp.concatenate([turn[0]] * 2, axis=1), jnp.concatenate([-sine if back else sine] * 2, axis=1)))

    def joined(even, odd):
        odd = turned((odd[:half], odd[half:]), False)
        even = (even[:half], even[half:])
        return tuple(jnp.concatenate([a + b, a - b], axis=0) for a, b in zip(even, odd))

    def spectrum(block, exact):
        both = jnp.concatenate([block[0], block[1]], axis=1)
        if exact:
            both = dot_nn(fwd[...], jnp.concatenate([both, both], axis=0))
        else:
            both = dot_nn(fwd[:, :half], both)
        return joined(both[:, :wide], both[:, wide:])

    def signal(spec, exact):
        even = [part[:half] + part[half:] for part in spec]
        odd = turned([part[:half] - part[half:] for part in spec], True)
        both = jnp.concatenate([jnp.concatenate(even, axis=0), jnp.concatenate(odd, axis=0)], axis=1)
        if exact:
            high, low = split_low(both)
            return dot_nn(inv[...], jnp.concatenate([high, high, low], axis=0))
        return dot_nn(inv[:, : 2 * half], both.astype(bf16))

    def quads(value):
        return [value[fourth * i : fourth * (i + 1)] for i in range(4)]

    def signed(value, sign):
        return jnp.concatenate([part if (i % 2 == 0) == (sign > 0) else -part for i, part in enumerate(quads(value))], axis=0)

    def own_spectrum(j, _):
        at = lanes(j)
        u_spec[0:taps, at], u_spec[taps:, at] = spectrum((own_b[0, :, at], own_b[1, :, at]), True)
        return 0

    lax.fori_loop(0, 2, own_spectrum, 0)
    weight_y = [weight_to_y(0)]

    @pl.when(seq < 3)
    def _():
        right_copy.wait_send()

    @pl.when(seq > 0)
    def _():
        right_copy.wait_recv()
        normalise(left_v, left_hat, False)

        def shifted_left(i, _):
            for parity in range(2):
                value = take(left_hat, every_other(i, parity)) * gain + shift
                left_b[parity, sixty_four(i)] = value.astype(bf16)
            return 0

        lax.fori_loop(0, tokens // 128, shifted_left, 0)

        def left_spectrum(j, _):
            at = lanes(j)
            real, imag = spectrum((left_b[0, :, at], left_b[1, :, at]), True)
            u_spec[0:taps, at] += signed(imag, -1)
            u_spec[taps:, at] += signed(real, 1)
            return 0

        lax.fori_loop(0, 2, left_spectrum, 0)

    @pl.when(seq == 0)
    def _():
        left_hat[...] = jnp.zeros_like(left_hat)

    weight_y.append(weight_to_y(1))
    kern_core = []
    for j, at in enumerate(halves):
        finish(kern_plane[j])
        kern_core.append(same(kern.at[at, :, :, c], [core_peer], kern.at[at, :, :, 0], pair_sender))

    def convolve(j):
        at = lanes(j)
        rows = kern[2 * j : 2 * j + 2].reshape(wide, taps)
        even, odd = rows[:, :half], rows[:, half:]
        k = joined(
            dot_nt(fwd[...], jnp.concatenate([even, even], axis=1)), dot_nt(fwd[...], jnp.concatenate([odd, odd], axis=1))
        )
        k_spec[0:taps, at], k_spec[taps:, at] = k
        both = signal(times(k, (u_spec[0:taps, at], u_spec[taps:, at])), True)
        for parity in range(2):
            put(mixed, pl.ds(parity, half, stride=2), both[:, wide * parity : wide * (parity + 1)], 2 * j)

    weight_y.append(weight_to_y(2))
    finish(kern_core[0])
    convolve(0)
    weight_y.append(weight_to_y(3))
    weight_to_core(0)
    finish(kern_core[1])
    convolve(1)
    weight_to_core(1)

    def activate(i, _):
        at = pl.ds(pl.multiple_of(i * 128, 128), 128)
        value = take(mixed, at) + rows_f[2:3, :] * take(normed, at)
        chance = 0.5 * (1.0 + lax.erf(value * (0.5**0.5)))
        slope[at, :] = chance + value * (jnp.exp(value * value * -0.5) * ((2.0 * np.pi) ** -0.5))
        low = (value * chance).astype(bf16)
        activ[at, :] = low
        activ_t[:, at] = low.T
        return 0

    lax.fori_loop(0, tokens // 128, activate, 0)
    loads[6].wait()

    def quarter(q):
        at = slice(128 * q, 128 * q + 128)
        matrix = weight[q].reshape(channels, 256)
        pre = dot_nn(activ[...], matrix)
        lin = pre[:, :128] + rows_f[3:4, at]
        gate = 0.5 + 0.5 * jnp.tanh(0.5 * (pre[:, 128:] + rows_f[4:5, at]))
        grad = g_v[:, at].astype(f32)
        res_v[:, at] = (x_v[:, at].astype(f32) + lin * gate).astype(bf16)
        low_lin = (grad * gate).astype(bf16)
        low_gate = (grad * lin * gate * (1.0 - gate)).astype(bf16)
        low = jnp.concatenate([low_lin, low_gate], axis=1)
        dw_own[q] = dot_nn(activ_t[...], low).astype(bf16).reshape(4, 2, 2, 2, ROWS, 256)
        back = dot_nt(low, matrix)
        if q == 0:
            d_act[...] = back
        elif q < 3:
            d_act[...] += back
        else:
            mix = ((d_act[...] + back) * slope[...]).astype(bf16).astype(f32)
            rows_f[2:3, :] = jnp.sum(mix * take(normed, slice(None)), axis=0, keepdims=True)
            put(mixed, slice(None), mix)
            for parity in range(2):
                d_mix[parity] = take(mixed, pl.ds(parity, half, stride=2)).astype(bf16)
        rows_f[3:4, at] = jnp.sum(low_lin.astype(f32), axis=0, keepdims=True)
        rows_f[4:5, at] = jnp.sum(low_gate.astype(f32), axis=0, keepdims=True)
        return start([(dw_own.at[q, :, :, :, flip_c], dw_in1.at[q], core_peer)], dw_senders[0], dw_in1.at[q])

    def to_y(q):
        finish(dw_core[q])
        dw_mid[q] = (dw_own[q, :, :, :, c].astype(f32) + dw_in1[q].astype(f32)).astype(bf16)
        return start([(dw_mid.at[q, :, flip_y], dw_in2.at[q], y_peer)], dw_senders[1], dw_in2.at[q])

    def to_z(q):
        finish(dw_y[q])
        dw_low[q] = (dw_mid[q, :, y].astype(f32) + dw_in2[q].astype(f32)).astype(bf16)
        copies = [(dw_low.at[q, peer[0]], dw_in3.at[q, i], peer) for i, peer in enumerate(z_peers)]
        return start(copies, dw_senders[2], dw_in3.at[q])

    def to_x(q):
        finish(dw_z[q])
        total = dw_low[q, z].astype(f32)
        for i in range(3):
            total = total + dw_in3[q, i].astype(f32)
        dw_end[q] = total.astype(bf16)
        return start([(dw_end.at[q, flip_x], dw_in4.at[q], x_peer)], dw_senders[3], dw_in4.at[q])

    def to_end(q):
        finish(dw_x[q])
        total = dw_end[q, x].astype(f32) + dw_in4[q].astype(f32)
        dw_ref[:, 128 * q : 128 * q + 128] = total[:, :128]
        dw_ref[:, channels + 128 * q : channels + 128 * q + 128] = total[:, 128:]

    skip = rows_f[2:3, :]
    dw_core, dw_y, dw_z, dw_x = [], [], [], []
    dw_senders = [sender(ref) for ref in (dw_in1, dw_in2, dw_in3, dw_in4)]
    for q in range(4):
        finish(weight_core[q])
        if q < 2:
            weight_to_core(q + 2)
        dw_core.append(quarter(q))
        if q >= 2:
            dw_y.append(to_y(q - 2))
    left_sender = sends.at[claim("send")]
    left_copies = [
        pltpu.make_async_remote_copy(
            src_ref=d_mix.at[:, :, pl.ds(wide * j, wide)], dst_ref=right_v.at[j], send_sem=left_sender,
            recv_sem=recvs.at[claim("recv")], device_id=(dp, seq - 1), device_id_type=MESH,
        )
        for j in range(2)
    ]
    dk_senders = [sender(ref) for ref in (dk_in1, dk_in2, dk_in3)]

    @pl.when(seq > 0)
    def _():
        left_copies[0].start()

    dw_y.append(to_y(2))

    def kernel_grad(j):
        at = lanes(j)
        d = spectrum((d_mix[0, :, at], d_mix[1, :, at]), False)
        d_spec[0:taps, at], d_spec[taps:, at] = d
        both = signal(times(d, (u_spec[0:taps, at], -u_spec[taps:, at])), False)
        grad = jnp.concatenate([both[:, :wide].T, both[:, wide:].T], axis=1).reshape(2, 2, 2, 2, ROWS, taps)
        dk_own[2 * j : 2 * j + 2] = grad
        dk_low[2 * j : 2 * j + 2] = grad.astype(bf16)
        part = halves[j]
        return start([(dk_low.at[part, :, :, flip_c], dk_in1.at[part], core_peer)], dk_senders[0], dk_in1.at[part])

    def kernel_middle(j):
        finish(dk_core[j])
        for i in (2 * j, 2 * j + 1):
            total = dk_own[i, :, :, c] + dk_in1[i].astype(f32)
            dk_mid[i] = total
            dk_cut[i] = total.astype(bf16)
        part = halves[j]
        copies = [(dk_cut.at[part, peer[1], peer[2]], dk_in2.at[i, part], peer) for i, peer in enumerate(plane_peers)]
        return start(copies, dk_senders[1], dk_in2.at[:, part])

    def kernel_end(j):
        finish(dk_plane[j])
        for i in (2 * j, 2 * j + 1):
            total = dk_mid[i, y, x]
            for k in range(3):
                total = total + dk_in2[k, i].astype(f32)
            dk_end[i] = total

    def own_grad(j):
        at = lanes(j)
        k = (k_spec[0:taps, at], -k_spec[taps:, at])
        real, imag = times(k, (d_spec[0:taps, at], d_spec[taps:, at]))
        own = signal((real, imag), False)
        back = signal((signed(imag, 1), signed(real, -1)), False)
        d_gain, d_shift = jnp.zeros((1, wide), f32), jnp.zeros((1, wide), f32)
        for parity in range(2):
            lines = pl.ds(parity, half, stride=2)
            columns = slice(wide * parity, wide * (parity + 1))
            grad = own[:, columns] + rows_f[5:6, at] * d_mix[parity, :, at].astype(f32)
            put(d_norm, lines, grad, 2 * j)
            before = jnp.where(seq > 0, back[:, columns], 0.0)
            d_gain += jnp.sum(
                grad * take(x_hat, lines, 2 * j, 2) + before * take(left_hat, lines, 2 * j, 2), axis=0, keepdims=True
            )
            d_shift += jnp.sum(grad + before, axis=0, keepdims=True)
        rows_f[6:7, at], rows_f[7:8, at] = d_gain, d_shift

    def right_grad(j):
        at = lanes(j)
        real, imag = spectrum((right_v[j, 0], right_v[j, 1]), False)
        k = (k_spec[0:taps, at], -k_spec[taps:, at])
        both = signal(times(k, (signed(imag, 1), signed(real, -1))), False)
        for parity in range(2):
            lines = pl.ds(parity, half, stride=2)
            more = both[:, wide * parity : wide * (parity + 1)]
            put(d_norm, lines, take(d_norm, lines, 2 * j, 2) + more, 2 * j)

    rows_f[5:6, :] = skip
    dk_core = [kernel_grad(0)]
    dw_y.append(to_y(3))
    dk_core.append(kernel_grad(1))
    dk_plane = [kernel_middle(0)]
    dw_z.append(to_z(0))
    own_grad(0)
    dk_plane.append(kernel_middle(1))

    @pl.when(seq > 0)
    def _():
        left_copies[1].start()

    dw_z.append(to_z(1))
    own_grad(1)
    vector = jnp.concatenate([rows_f[6:7, :], rows_f[7:8, :], rows_f[2:3, :], rows_f[3:4, :], rows_f[4:5, :]], axis=1)
    high, low = split_low(jnp.broadcast_to(vector, mask.shape) * mask[...].astype(f32))
    shares = dot_nt(high, pick[...]) + dot_nt(low, pick[...])
    share_out[...] = shares.reshape(32, 1, 128).reshape(4, 2, 2, 2, 1, 128)
    share_core = start([(share_out.at[:, :, :, flip_c], share_in1, core_peer)], sender(share_in1), share_in1)
    dw_z.append(to_z(2))
    finish(share_core)
    share_mid[...] = share_out[:, :, :, c] + share_in1[...]
    copies = [(share_mid.at[:, peer[1], peer[2]], share_in2.at[i], peer) for i, peer in enumerate(plane_peers)]
    share_plane = start(copies, sender(share_in2), share_in2)
    dw_z.append(to_z(3))

    @pl.when(seq < 3)
    def _():
        left_copies[0].wait_recv()
        right_grad(0)

    kernel_end(0)
    kernel_end(1)
    dk_z = start([(dk_end.at[peer[0]], dk_in3.at[i], peer) for i, peer in enumerate(z_peers)], dk_senders[2], dk_in3)
    dw_x.append(to_x(0))
    dw_x.append(to_x(1))
    finish(share_plane)
    share_end[...] = share_mid[:, y, x] + share_in2[0] + share_in2[1] + share_in2[2]
    copies = [(share_end.at[peer[0]], share_in3.at[i], peer) for i, peer in enumerate(z_peers)]
    share_z = start(copies, sender(share_in3), share_in3)
    dw_x.append(to_x(2))
    dw_x.append(to_x(3))

    @pl.when(seq < 3)
    def _():
        left_copies[1].wait_recv()
        right_grad(1)

    @pl.when(seq > 0)
    def _():
        arrive(left_sender, d_mix)

    def input_grad(i, _):
        at = pl.ds(pl.multiple_of(i * 128, 128), 128)
        grad, hat = take(d_norm, at), take(x_hat, at)
        scaled = grad * rows_f[0:1, :]
        inner = (
            scaled
            - jnp.mean(scaled, axis=1, keepdims=True)
            - hat * jnp.mean(scaled * hat, axis=1, keepdims=True)
        )
        gin_v[at, :] = (inv_std[at, 0:1] * inner + g_v[at, :].astype(f32)).astype(bf16)
        return 0

    lax.fori_loop(0, tokens // 128, input_grad, 0)
    finish(dk_z)
    d_kernel = dk_end[z]
    for k in range(3):
        d_kernel = d_kernel + dk_in3[k]

    place = lax.broadcasted_iota(jnp.int32, (ROWS, taps), 1)
    place = jnp.where(place < half, 2 * place, 2 * (place - half) + 1)
    weighted = d_kernel * place.astype(f32)
    stack = jnp.concatenate(split_low(d_kernel) + split_low(weighted), axis=0)
    sums = dot_nn(stack, e_low[...])
    plain, ramp = sums[0:16] + sums[16:32], sums[32:48] + sums[48:64]
    at_row = lax.broadcasted_iota(jnp.int32, (8, 128), 0)
    first = lax.broadcasted_iota(jnp.int32, (8, 128), 1) < 64

    def gathered(value, part):
        total = jnp.zeros((8, 128), f32)
        for p in range(8):
            block = value[:, 256 * p + 128 * part : 256 * p + 128 * part + 128]
            total = jnp.where(at_row == p, jnp.where(first, block[:8], block[8:]), total)
        return total

    s0 = (gathered(plain, 0), gathered(plain, 1))
    s1 = (gathered(ramp, 0), gathered(ramp, 1))
    dt, a, unit, norm_sq, ratio, coef, scaled = mode_terms(ldt_ref[...], lar_ref[...], ai_ref[...], cc_ref[...])
    inverse_a = (a[0] / norm_sq, -a[1] / norm_sq)
    d_coef = times(s0, ratio)
    half_g = times(times(coef, s0), times(unit, inverse_a))
    ramp_part = times(scaled, s1)
    half_g = (half_g[0] + ramp_part[0], half_g[1] + ramp_part[1])
    back = times(times(scaled, s0), inverse_a)
    q = (half_g[0] * dt - back[0], half_g[1] * dt - back[1])
    d_dt = 2.0 * dt * times(half_g, a)[0]
    dldt_ref[...] = row_of(jnp.sum(unpair_lanes(d_dt), axis=1, keepdims=True))[0]
    dlar_ref[...] = unpair_lanes(2.0 * q[0] * a[0])
    dai_ref[...] = unpair_lanes(-2.0 * q[1])
    dcc_ref[...] = jnp.concatenate([unpair_lanes(2.0 * d_coef[0]), unpair_lanes(-2.0 * d_coef[1])], axis=1)

    for q in range(4):
        to_end(q)
    finish(share_z)
    small = share_end[z] + share_in3[0] + share_in3[1] + share_in3[2]
    for i, target in enumerate([dgain_ref, dshift_ref, dskip_ref]):
        target[...] = small[0, ROWS * i : ROWS * (i + 1)]
    dbias_ref[...] = small[0, 3 * ROWS : 5 * ROWS]
    for departure in departures:
        arrive(*departure)


def finish_kernel(*refs):
    count = len(refs) // 2
    sems = refs[-1]
    copies = [pltpu.make_async_copy(refs[i], refs[count + i], sems.at[i]) for i in range(count)]
    for copy in copies:
        copy.start()
    for copy in copies:
        copy.wait()


def kernel_body(
    inputs, grad_out, ln_gain, ln_bias, skip_scale, w_glu, b_glu, log_dt, log_a_real, a_imag, c_coef
):
    _, tokens, channels = inputs.shape
    taps = KTAPS
    glu = w_glu.shape[1]
    f32, bf16 = jnp.float32, jnp.bfloat16
    order = np.concatenate([np.arange(0, taps // 2, 2), np.arange(1, taps // 2, 2)]) + 0.5
    angle = np.outer(order, np.arange(taps // 2)) * (2 * np.pi / taps)
    matrix = np.concatenate([np.cos(angle), -np.sin(angle)], axis=0)
    high = matrix.astype(bf16)
    low = (matrix - high.astype(np.float64)).astype(bf16)
    forward = np.concatenate([high, low], axis=1)
    scale = np.asarray(1.0 / taps, bf16)
    inverse = np.concatenate([high.T, low.T, high.T], axis=1) * scale
    turns = np.stack([np.cos(order * (np.pi / taps)), -np.sin(order * (np.pi / taps))])
    turns = np.ascontiguousarray(np.broadcast_to(turns[:, :, None], (2, taps // 2, 128))).astype(np.float32)
    device_at, lane = np.arange(32)[:, None], np.arange(channels)[None, :]
    bias_lane = np.arange(2 * channels)[None, :]
    row = np.arange(128)[:, None]
    pick = np.concatenate(
        [row == i * ROWS + lane % ROWS for i in range(3)] + [row == 3 * ROWS + bias_lane % (2 * ROWS)], axis=1
    ).astype(bf16)
    mask = np.concatenate(
        [device_at == lane // ROWS] * 3 + [device_at == bias_lane // (2 * ROWS)], axis=1
    ).astype(bf16)
    line = np.arange(2048)[:, None]
    fold = (np.arange(128)[None, :] == line // 256 + 8 * (line % 128 >= 64)).astype(bf16)
    hbm, vmem = pl.BlockSpec(memory_space=pl.ANY), pl.BlockSpec(memory_space=pltpu.VMEM)
    block = (tokens, channels)
    spec, tall = (2 * taps, channels), (channels // 128, tokens, 128)

    def space(*dims, kind=f32):
        return pltpu.VMEM(dims, kind)

    results = (
        (block, bf16), (block, bf16), ((ROWS,), f32), ((ROWS,), f32), ((ROWS,), f32), (w_glu.shape, f32),
        ((2 * ROWS,), f32), ((ROWS,), f32), (log_a_real.shape, f32), (a_imag.shape, f32), (c_coef.shape, f32),
    )
    outs = pl.pallas_call(
        layer_kernel,
        name="layer",
        out_shape=tuple(pltpu.VMEM(dims, kind) for dims, kind in results),
        in_specs=[hbm] * 17,
        out_specs=(vmem,) * len(results),
        scratch_shapes=[
            space(*w_glu.shape), space(1, ROWS), space(1, ROWS), space(1, ROWS), space(1, 2 * ROWS), space(1, ROWS),
            space(*log_a_real.shape), space(*a_imag.shape), space(*c_coef.shape),
            space(*block, kind=bf16), space(*block, kind=bf16), space(*block, kind=bf16),
            space(*forward.shape, kind=bf16), space(*inverse.shape, kind=bf16),
            space(*pick.shape, kind=bf16), space(*mask.shape, kind=bf16), space(*fold.shape, kind=bf16), space(*turns.shape),
            space(4, 2, 2, 2, ROWS, taps, kind=bf16), space(4, 4, 2, 2, 2, ROWS, 256, kind=bf16),
            space(22, 2, 8, 128), space(taps, 2048, kind=bf16), space(taps, 2048, kind=bf16),
            space(4, 2, 2, 2, 1, 128), space(4, 2, 2, 2, 1, 128), space(4, 2, 2, 1, 128), space(4, 2, 2, 1, 128),
            space(3, 4, 1, 128), space(4, 1, 128), space(3, 1, 128), space(8, channels),
            space(*tall), space(tokens, 128), space(*tall), space(*tall),
            space(2, tokens // 2, channels, kind=bf16), space(2, tokens // 2, channels, kind=bf16),
            space(*spec), space(*spec), space(*tall), space(*block),
            space(*block, kind=bf16), space(channels, tokens, kind=bf16),
            space(*block), space(2, tokens // 2, channels, kind=bf16), space(2, 2, tokens // 2, 256, kind=bf16),
            space(*spec), space(*tall),
            space(4, 4, 2, 2, 2, ROWS, 256, kind=bf16), space(4, 4, 2, 2, ROWS, 256, kind=bf16),
            space(4, 4, 2, 2, ROWS, 256, kind=bf16), space(4, 4, 2, ROWS, 256, kind=bf16),
            space(4, 4, 2, ROWS, 256, kind=bf16), space(4, 3, 2, ROWS, 256, kind=bf16),
            space(4, 2, ROWS, 256, kind=bf16), space(4, ROWS, 256, kind=bf16),
            space(4, 2, 2, 2, ROWS, taps), space(4, 2, 2, 2, ROWS, taps, kind=bf16), space(4, 2, 2, ROWS, taps, kind=bf16),
            space(4, 2, 2, ROWS, taps), space(4, 2, 2, ROWS, taps, kind=bf16), space(3, 4, ROWS, taps, kind=bf16),
            space(4, ROWS, taps), space(3, ROWS, taps),
            pltpu.SemaphoreType.DMA((17,)), pltpu.SemaphoreType.DMA((22,)), pltpu.SemaphoreType.DMA((48,)),
        ],
        compiler_params=pltpu.CompilerParams(
            collective_id=0, has_side_effects=True, vmem_limit_bytes=48 * 2**20
        ),
    )(*[
        pltpu.with_memory_space_constraint(value, pltpu.HBM)
        for value in (
            inputs.reshape(block), grad_out.reshape(block), forward, inverse, pick, mask, fold, turns, w_glu,
            ln_gain.reshape(1, -1), ln_bias.reshape(1, -1), skip_scale.reshape(1, -1), b_glu.reshape(1, -1),
            log_dt.reshape(1, -1), log_a_real, a_imag, c_coef,
        )
    ])
    ended = pl.pallas_call(
        finish_kernel,
        name="finish",
        out_shape=tuple(jax.ShapeDtypeStruct(dims, kind) for dims, kind in results),
        in_specs=[vmem] * len(results),
        out_specs=(hbm,) * len(results),
        scratch_shapes=[pltpu.SemaphoreType.DMA((len(results),))],
    )(*[pltpu.with_memory_space_constraint(value, pltpu.VMEM) for value in outs])
    return (ended[0].reshape(inputs.shape), ended[1].reshape(inputs.shape)) + tuple(ended[2:])


def solution(mesh):
    in_specs = (
        P("dp", "seq", None),
        P("dp", "seq", None),
        P(("dp", "seq")),
        P(("dp", "seq")),
        P(("dp", "seq")),
        P(("dp", "seq"), None),
        P(("dp", "seq")),
        P(("dp", "seq")),
        P(("dp", "seq"), None),
        P(("dp", "seq"), None),
        P(("dp", "seq"), None),
    )
    out_specs = (
        P("dp", "seq", None),
        P("dp", "seq", None),
        P(("dp", "seq")),
        P(("dp", "seq")),
        P(("dp", "seq")),
        P(("dp", "seq"), None),
        P(("dp", "seq")),
        P(("dp", "seq")),
        P(("dp", "seq"), None),
        P(("dp", "seq"), None),
        P(("dp", "seq"), None),
    )
    quick = mesh.shape["dp"] == 8 and mesh.shape["seq"] == 4
    return jax.shard_map(kernel_body if quick else body, mesh=mesh, in_specs=in_specs, out_specs=out_specs, check_vma=False)
```

```python
from functools import partial

import jax
import jax.numpy as jnp
import numpy as np
from jax import lax
from jax.experimental import pallas as pl
from jax.experimental.pallas import tpu as pltpu
from jax.sharding import PartitionSpec as P

KTAPS = 512


EPS = 1e-05


def passed_along(value, axis, steps):
    count = lax.axis_size(axis)
    first, last = (max(0, -steps), min(count, count - steps))
    return lax.ppermute(value, axis, [(source, source + steps) for source in range(first, last)])


def kernel_block(log_dt, log_a_real, a_imag, c_coef, start, count):
    mode_count = log_a_real.shape[1]
    step_size = jnp.exp(log_dt)[:, None]
    a_real = -jnp.exp(log_a_real)
    decay = a_real * step_size
    turn = a_imag * step_size
    growth = jnp.exp(decay)
    ex_re = growth * jnp.cos(turn) - 1.0
    ex_im = growth * jnp.sin(turn)
    norm_sq = a_real * a_real + a_imag * a_imag
    ratio_re = (ex_re * a_real + ex_im * a_imag) / norm_sq
    ratio_im = (ex_im * a_real - ex_re * a_imag) / norm_sq
    c_re = c_coef[:, :mode_count]
    c_im = c_coef[:, mode_count:]
    coef_re = c_re * ratio_re - c_im * ratio_im
    coef_im = c_re * ratio_im + c_im * ratio_re
    places = (start + jnp.arange(count)).astype(jnp.float32)
    phase = turn[:, :, None] * places
    damping = jnp.exp(decay[:, :, None] * places)
    terms = damping * (coef_re[:, :, None] * jnp.cos(phase) - coef_im[:, :, None] * jnp.sin(phase))
    return 2.0 * jnp.sum(terms, axis=1)


def transforms(taps):
    angle = np.outer(np.arange(taps) + 0.5, np.arange(taps)) * (np.pi / taps)
    forward = np.concatenate([np.cos(angle), -np.sin(angle)], axis=0)
    inverse = forward.T / taps
    return forward.astype(jnp.bfloat16), inverse.astype(jnp.bfloat16)


def body(
    inputs, grad_out, ln_gain, ln_bias, skip_scale, w_glu, b_glu, log_dt, log_a_real, a_imag, c_coef
):
    seq_count, own_len, channels = inputs.shape
    gain_low = ln_gain.astype(jnp.bfloat16)
    shift_low = ln_bias.astype(jnp.bfloat16)
    skip_low = skip_scale.astype(jnp.bfloat16)
    weight_low = w_glu.astype(jnp.bfloat16)
    bias_low = b_glu.astype(jnp.bfloat16)
    mode_own = (log_dt, log_a_real, a_imag, c_coef)
    own_kernel = kernel_block(*mode_own, 0, KTAPS).astype(jnp.bfloat16)
    gathered = (
        lax.all_gather(gain_low, ("dp", "seq"), axis=0, tiled=True),
        lax.all_gather(shift_low, ("dp", "seq"), axis=0, tiled=True),
        lax.all_gather(skip_low, ("dp", "seq"), axis=0, tiled=True),
        lax.all_gather(weight_low, ("dp", "seq"), axis=0, tiled=True),
        lax.all_gather(bias_low, ("dp", "seq"), axis=0, tiled=True),
        lax.all_gather(own_kernel, ("dp", "seq"), axis=0, tiled=True),
    )
    kernel_b = gathered[5]
    taps = own_len
    forward, inverse = transforms(taps)
    sign = jnp.where(jnp.arange(taps) % 2 == 0, 1.0, -1.0).astype(jnp.float32)[:, None]

    def to_spectrum(block):
        both = jnp.dot(forward, block, preferred_element_type=jnp.float32)
        return both[:taps], both[taps:]

    def from_spectrum(real, imag):
        both = jnp.concatenate([real, imag], axis=0).astype(jnp.bfloat16)
        return jnp.dot(inverse, both, preferred_element_type=jnp.float32)

    kernel_re, kernel_im = to_spectrum(kernel_b.T)
    gain_full = gathered[0].astype(jnp.float32)
    shift_full = gathered[1].astype(jnp.float32)
    skip_full = gathered[2].astype(jnp.float32)
    weight_b = gathered[3]
    glu_bias = gathered[4].astype(jnp.float32)
    x_float = inputs.astype(jnp.float32)
    row_mean = jnp.mean(x_float, axis=-1, keepdims=True)
    centered = x_float - row_mean
    row_var = jnp.mean(centered * centered, axis=-1, keepdims=True)
    inv_std = lax.rsqrt(row_var + EPS)
    x_hat = centered * inv_std
    normed = x_hat * gain_full + shift_full
    normed_b = normed.astype(jnp.bfloat16)
    own_re, own_im = to_spectrum(normed_b[0])
    left_re, left_im = to_spectrum(passed_along(normed_b, "seq", 1)[0])
    source_re = own_re - sign * left_im
    source_im = own_im + sign * left_re
    conv = from_spectrum(
        kernel_re * source_re - kernel_im * source_im,
        kernel_re * source_im + kernel_im * source_re,
    )
    mixed_pre = conv[None] + skip_full * normed
    activ, gelu_pull = jax.vjp(partial(jax.nn.gelu, approximate=False), mixed_pre)
    activ_b = activ.astype(jnp.bfloat16)
    glu_pre = (
        jnp.einsum("slh,hg->slg", activ_b, weight_b, preferred_element_type=jnp.float32) + glu_bias
    )
    half_dim = glu_pre.shape[-1] // 2
    lin_part = glu_pre[..., :half_dim]
    gate_sig = jax.nn.sigmoid(glu_pre[..., half_dim:])
    result = (x_float + lin_part * gate_sig).astype(jnp.bfloat16)
    grad_f = grad_out.astype(jnp.float32)
    d_pre = jnp.concatenate(
        [grad_f * gate_sig, grad_f * lin_part * gate_sig * (1.0 - gate_sig)], axis=-1
    ).astype(jnp.bfloat16)
    d_weight = jnp.einsum("slh,slg->hg", activ_b, d_pre, preferred_element_type=jnp.float32)
    d_glu_bias = jnp.sum(d_pre.astype(jnp.float32), axis=(0, 1))
    d_act = jnp.einsum("slg,hg->slh", d_pre, weight_b, preferred_element_type=jnp.float32)
    d_mix = gelu_pull(d_act)[0].astype(jnp.bfloat16)
    d_mix_f = d_mix.astype(jnp.float32)
    d_skip = jnp.sum(d_mix_f * normed, axis=(0, 1))
    mix_re, mix_im = to_spectrum(d_mix[0])
    d_kernel = from_spectrum(
        source_re * mix_re + source_im * mix_im, source_re * mix_im - source_im * mix_re
    ).T
    right_re, right_im = to_spectrum(passed_along(d_mix, "seq", -1)[0])
    sum_re = mix_re + sign * right_im
    sum_im = mix_im - sign * right_re
    d_conv = from_spectrum(
        kernel_re * sum_re + kernel_im * sum_im, kernel_re * sum_im - kernel_im * sum_re
    )[None]
    d_normed = d_conv + skip_full * d_mix_f
    d_gain = jnp.sum(d_normed * x_hat, axis=(0, 1))
    d_shift = jnp.sum(d_normed, axis=(0, 1))
    scaled = d_normed * gain_full
    d_input = (
        inv_std
        * (
            scaled
            - jnp.mean(scaled, axis=-1, keepdims=True)
            - x_hat * jnp.mean(scaled * x_hat, axis=-1, keepdims=True)
        )
        + grad_f
    )
    grad_in = d_input.astype(jnp.bfloat16)
    summed = (
        lax.psum_scatter(d_gain, ("dp", "seq"), scatter_dimension=0, tiled=True),
        lax.psum_scatter(d_shift, ("dp", "seq"), scatter_dimension=0, tiled=True),
        lax.psum_scatter(d_skip, ("dp", "seq"), scatter_dimension=0, tiled=True),
        lax.psum_scatter(d_weight, ("dp", "seq"), scatter_dimension=0, tiled=True),
        lax.psum_scatter(d_glu_bias, ("dp", "seq"), scatter_dimension=0, tiled=True),
        lax.psum_scatter(d_kernel, ("dp", "seq"), scatter_dimension=0, tiled=True),
    )
    _, own_pull = jax.vjp(partial(kernel_block, start=0, count=KTAPS), *mode_own)
    mode_grads = own_pull(summed[5])
    return (
        result,
        grad_in,
        summed[0],
        summed[1],
        summed[2],
        summed[3],
        summed[4],
        mode_grads[0],
        mode_grads[1],
        mode_grads[2],
        mode_grads[3],
    )


MESH = pl.DeviceIdType.MESH
ROWS = 16


def pair_lanes(value):
    return jnp.concatenate([value[:8], value[8:]], axis=1)


def unpair_lanes(value):
    half = value.shape[1] // 2
    return jnp.concatenate([value[:, :half], value[:, half:]], axis=0)


def column_of(row):
    n = row.shape[1]
    at = lax.broadcasted_iota(jnp.int32, (n, n), 0) == lax.broadcasted_iota(jnp.int32, (n, n), 1)
    return jnp.sum(jnp.where(at, jnp.broadcast_to(row, (n, n)), 0.0), axis=1, keepdims=True)


def row_of(column):
    n = column.shape[0]
    at = lax.broadcasted_iota(jnp.int32, (n, n), 0) == lax.broadcasted_iota(jnp.int32, (n, n), 1)
    return jnp.sum(jnp.where(at, jnp.broadcast_to(column, (n, n)), 0.0), axis=0, keepdims=True)


def mode_terms(ldt, lar, ai, cc):
    n_modes = lar.shape[1]
    dt = column_of(jnp.exp(ldt))
    dt = jnp.concatenate(
        [jnp.broadcast_to(dt[:8], (8, n_modes)), jnp.broadcast_to(dt[8:], (8, n_modes))], axis=1
    )
    a_re, a_im = -jnp.exp(pair_lanes(lar)), pair_lanes(ai)
    decay, turn = a_re * dt, a_im * dt
    growth = jnp.exp(decay)
    z_re, z_im = growth * jnp.cos(turn), growth * jnp.sin(turn)
    ex_re, ex_im = z_re - 1.0, z_im
    norm_sq = a_re * a_re + a_im * a_im
    r_re = (ex_re * a_re + ex_im * a_im) / norm_sq
    r_im = (ex_im * a_re - ex_re * a_im) / norm_sq
    c_re, c_im = pair_lanes(cc[:, :n_modes]), pair_lanes(cc[:, n_modes:])
    w_re, w_im = c_re * r_re - c_im * r_im, c_re * r_im + c_im * r_re
    return dt, (a_re, a_im), (z_re, z_im), norm_sq, (r_re, r_im), (c_re, c_im), (w_re, w_im)


def times(a, b):
    return a[0] * b[0] - a[1] * b[1], a[0] * b[1] + a[1] * b[0]


def conj_times(a, b):
    return a[0] * b[0] + a[1] * b[1], a[0] * b[1] - a[1] * b[0]


def split_low(value):
    high = value.astype(jnp.bfloat16)
    return high, (value - high.astype(jnp.float32)).astype(jnp.bfloat16)


def dot_nn(a, b):
    return lax.dot_general(a, b, (((1,), (0,)), ((), ())), preferred_element_type=jnp.float32)


def dot_nt(a, b):
    return lax.dot_general(a, b, (((1,), (1,)), ((), ())), preferred_element_type=jnp.float32)


def layer_kernel(
    x_hbm, g_hbm, fwd_hbm, inv_hbm, pick_hbm, mask_hbm, turn_hbm,
    w_hbm, gain_hbm, shift_hbm, skip_hbm, bias_hbm, ldt_hbm, lar_hbm, ai_hbm, cc_hbm,
    res_v, gin_v, dgain_ref, dshift_ref, dskip_ref, dw_ref, dbias_ref, dldt_ref, dlar_ref, dai_ref, dcc_ref,
    w_ref, gain_ref, shift_ref, skip_ref, bias_ref, ldt_ref, lar_ref, ai_ref, cc_ref,
    x_v, g_v, left_v, fwd, inv, pick, mask, turn, kern, weight, base_high, base_low, leaps, lines_f,
    share_in, share_out, share_in1, share_mid, share_in2, rows_f, x_hat, inv_std, left_hat, normed, own_b, left_b,
    k_spec, u_spec, mixed, slope, activ, activ_t, d_mix, right_v, d_spec, d_norm,
    dw_own, dw_in1, dw_mid, dw_in2, dw_low, dw_in3, dw_end, dw_in4, end_in1, end_mid, end_in2,
    dk_own, dk_low, dk_in1, dk_mid, dk_cut, dk_in2, dk_end, dk_out, dk_in3,
    local, sends, recvs,
):
    f32, bf16 = jnp.float32, jnp.bfloat16
    tokens, channels = x_v.shape
    taps = KTAPS
    half, fourth = taps // 2, taps // 4
    dp, seq = lax.axis_index("dp"), lax.axis_index("seq")
    index = dp * 4 + seq
    z, y, x, c = lax.div(dp, 2), lax.rem(dp, 2), lax.div(seq, 2), lax.rem(seq, 2)
    flip_y, flip_x, flip_c = 1 - y, 1 - x, 1 - c

    def device(z, y, x, c):
        return (z * 2 + y, x * 2 + c)

    z_peers = [(lax.rem(z + k, 4), y, x, c) for k in (1, 2, 3)]
    plane_peers = [
        (z, lax.rem(y + k // 2, 2), lax.rem(x + k % 2, 2), c) for k in (1, 2, 3)
    ]
    x_peer, y_peer, core_peer = (z, y, flip_x, c), (z, flip_y, x, c), (z, y, x, flip_c)
    other_peers = [core_peer] + [(peer[0], peer[1], peer[2], flip_c) for peer in plane_peers]
    used = {"send": 0, "recv": 0}
    departures = []

    def claim(kind):
        used[kind] += 1
        return used[kind] - 1

    def sender(total):
        number = claim("send")
        departures.append((sends.at[number], total))
        return sends.at[number]

    def arrive(semaphore, total):
        pltpu.make_async_copy(total, total, semaphore).wait()

    def start(copies, send_sem, total, recv_sem=None):
        if recv_sem is None:
            recv_sem = recvs.at[claim("recv")]
        for source, target, peer in copies:
            pltpu.make_async_remote_copy(
                src_ref=source, dst_ref=target, send_sem=send_sem, recv_sem=recv_sem,
                device_id=device(*peer), device_id_type=MESH,
            ).start()
        return recv_sem, total

    def finish(arrival):
        arrive(*arrival)

    def load(copies):
        for copy in copies:
            copy.start()
        return copies

    def take(ref, lines, first=0, count=4):
        return jnp.concatenate([ref[first + i, lines, :] for i in range(count)], axis=1)

    def put(ref, lines, value, first=0):
        for i in range(value.shape[1] // 128):
            ref[first + i, lines, :] = value[:, 128 * i : 128 * (i + 1)]

    barrier = pltpu.get_barrier_semaphore()
    peers = z_peers + plane_peers + other_peers
    for peer in peers:
        pl.semaphore_signal(barrier, inc=1, device_id=device(*peer), device_id_type=MESH)
    def fetch(pairs, first):
        return load([pltpu.make_async_copy(source, target, local.at[first + i]) for i, (source, target) in enumerate(pairs)])

    params = fetch([
        (gain_hbm, gain_ref), (shift_hbm, shift_ref), (skip_hbm, skip_ref), (bias_hbm, bias_ref), (w_hbm, w_ref),
        (ldt_hbm, ldt_ref), (lar_hbm, lar_ref), (ai_hbm, ai_ref), (cc_hbm, cc_ref),
    ], 7)
    loads = fetch([
        (x_hbm, x_v), (pick_hbm, pick), (mask_hbm, mask), (fwd_hbm, fwd), (inv_hbm, inv), (g_hbm, g_v),
        (turn_hbm, turn),
    ], 0)
    three, place = pl.ds(0, 3), (y * 2 + x) * 2 + c

    def same(ref, peers, total, send_sem=None, recv_sem=None):
        return start([(ref, ref, peer) for peer in peers], send_sem or sender(total), total, recv_sem)

    right_copy = pltpu.make_async_remote_copy(
        src_ref=x_hbm, dst_ref=left_v, send_sem=sends.at[claim("send")], recv_sem=recvs.at[claim("recv")],
        device_id=(dp, seq + 1), device_id_type=MESH,
    )

    def prepare_shares():
        for copy in params:
            copy.wait()
        low = [ref[...].astype(bf16).astype(f32) for ref in (gain_ref, shift_ref, skip_ref, bias_ref)]
        share_in[z, place] = jnp.concatenate(low + [jnp.zeros((1, 128 - 5 * ROWS), f32)], axis=1)
        for q in range(4):
            weight[q, z, y, x, c] = jnp.concatenate(
                [w_ref[:, 128 * q : 128 * q + 128], w_ref[:, channels + 128 * q : channels + 128 * q + 128]], axis=1
            ).astype(bf16)

    def prepare_taps():
        _, _, unit, _, _, _, coef = mode_terms(ldt_ref[...], lar_ref[...], ai_ref[...], cc_ref[...])
        steps, power = [], times(unit, unit)
        for _ in range(8):
            steps.append(power)
            power = times(power, power)
        for p in range(8):
            def row(value):
                return value[0][p : p + 1], value[1][p : p + 1]

            def table(factors):
                sub = lax.broadcasted_iota(jnp.int32, (8, 128), 0)
                tile = None
                for bit, factor in enumerate(factors):
                    on = lax.rem(lax.div(sub, 2**bit), 2) == 1
                    factor = tuple(jnp.where(on, part, rest) for part, rest in zip(row(factor), (1.0, 0.0)))
                    tile = factor if tile is None else times(tile, factor)
                return tile

            base = table(steps[:3])
            for step in steps[3:6]:
                more = times(base, row(step))
                base = tuple(jnp.concatenate([old, new], axis=0) for old, new in zip(base, more))
            leap = table([steps[6], steps[7], unit])
            leaps[p, 0], leaps[p, 1] = leap
            at = slice(256 * p, 256 * p + 256)
            high, low = split_low(jnp.concatenate(base, axis=1))
            base_high[:, at], base_low[:, at] = high, low
            lead = times(row(coef), leap)
            lead = jnp.concatenate([lead[0], -lead[1]], axis=1)
            first = lax.rem(lax.broadcasted_iota(jnp.int32, (8, 256), 1), 128) < 64
            lead = jnp.concatenate([jnp.where(first, lead, 0.0), jnp.where(first, 0.0, lead)], axis=0)
            lead_high, lead_low = split_low(lead)
            taps_of = dot_nt(
                jnp.concatenate([lead_high, lead_low, lead_high], axis=1), jnp.concatenate([high, high, low], axis=1)
            )
            taps_of = jnp.concatenate([taps_of, taps_of], axis=1)
            lines_f[8 * p : 8 * p + 8], lines_f[8 * p + 64 : 8 * p + 72] = taps_of[:8], taps_of[8:]
        own = jnp.concatenate([lines_f[pl.ds(m, ROWS, stride=8), :][:, :64] for m in range(8)], axis=1)
        kern[z, y, x, c] = (2.0 * own).astype(bf16)

    late = z == 3

    @pl.when(jnp.logical_not(late))
    def _():
        prepare_shares()
        prepare_taps()

    pl.semaphore_wait(barrier, len(peers))

    @pl.when(late)
    def _():
        prepare_shares()

    share_plane = same(share_in.at[z, place], plane_peers + other_peers, share_in.at[0, pl.ds(0, 7)])
    weight_x = same(weight.at[:, z, y, x, c], [x_peer], weight.at[:, 0, 0, 0, 0])

    @pl.when(seq < 3)
    def _():
        right_copy.start()

    @pl.when(late)
    def _():
        prepare_taps()

    kern_z = same(kern.at[z, y, x, c], z_peers, kern.at[three, 0, 0, 0])
    finish(share_plane)
    share_z = same(share_in.at[z], z_peers, share_in.at[three])
    finish(weight_x)
    z_sender, y_sender = sender(weight.at[three, three, 0, :, 0]), sender(weight.at[three, :, 0, :, 0])
    core_sender = sender(weight.at[:, :, :, :, 0])

    def weight_to_z(q):
        return same(weight.at[q, z, y, :, c], z_peers, weight.at[q, three, 0, :, 0], z_sender)

    def weight_to_y(q):
        finish(weight_z[q])
        piece = weight.at[q, :, y, :, c]
        weight_core.append(same(piece, [core_peer], weight.at[q, :, :, :, 0], core_sender))
        return same(piece, [y_peer], weight.at[q, :, 0, :, 0], y_sender)

    def weight_to_core(q):
        finish(weight_y[q])
        same(weight.at[q, :, flip_y, :, c], [core_peer], weight.at[q, :, :, :, 0], core_sender, weight_core[q][0])

    weight_core = []
    weight_z = [weight_to_z(q) for q in range(3)]
    last_y = same(weight.at[3, z, y, :, c], [y_peer], weight.at[3, 0, 0, :, 0])

    def last_to_z():
        finish(last_y)
        return same(weight.at[3, z, :, :, c], z_peers, weight.at[3, three, :, :, 0])

    def last_to_core():
        finish(last_z)
        weight_core.append(same(weight.at[3, :, :, :, c], [core_peer], weight.at[3, :, :, :, 0], core_sender))

    def normalise(source, hat, keep_std):
        def rows(i, _):
            at = pl.ds(pl.multiple_of(i * 128, 128), 128)
            value = source[at, :].astype(f32)
            centered = value - jnp.mean(value, axis=1, keepdims=True)
            scale = lax.rsqrt(jnp.mean(centered * centered, axis=1, keepdims=True) + EPS)
            put(hat, at, centered * scale)
            if keep_std:
                inv_std[at, :] = jnp.broadcast_to(scale, (128, 128))
            return 0

        lax.fori_loop(0, tokens // 128, rows, 0)

    loads[0].wait()
    normalise(x_v, x_hat, True)
    finish(kern_z)
    halves = [pl.ds(0, 2), pl.ds(2, 2)]
    plane_sender, pair_sender = sender(dk_in2), sender(kern.at[:, :, :, 0])
    kern_plane = [same(kern.at[at, y, x, c], plane_peers, dk_in2.at[:, at], plane_sender) for at in halves]
    finish(share_z)
    last_z = last_to_z()
    loads[1].wait()
    loads[2].wait()
    shares = share_in[...].reshape(32, 1, 128).reshape(32, 128).astype(bf16)
    spread = dot_nn(shares, pick[...]) * mask[...].astype(f32)
    spread = jnp.sum(spread, axis=0, keepdims=True)
    rows_f[...] = jnp.concatenate(
        [spread[:, channels * i : channels * (i + 1)] for i in range(5)] + [jnp.zeros((3, channels), f32)], axis=0
    )
    gain, shift = rows_f[0:1, :], rows_f[1:2, :]

    def every_other(i, parity):
        return pl.ds(128 * i + parity, 64, stride=2)

    def sixty_four(i):
        return pl.ds(pl.multiple_of(64 * i, 64), 64)

    def shifted(i, _):
        at = pl.ds(pl.multiple_of(i * 128, 128), 128)
        put(normed, at, take(x_hat, at) * gain + shift)
        for parity in range(2):
            own_b[parity, sixty_four(i)] = take(normed, every_other(i, parity)).astype(bf16)
        return 0

    lax.fori_loop(0, tokens // 128, shifted, 0)
    loads[3].wait()
    loads[4].wait()

    loads[6].wait()
    wide = 256

    def lanes(j):
        return pl.ds(pl.multiple_of(j * wide, wide), wide)

    few = 16

    def sign_of(r):
        return 1 if r < half // 2 else -1

    def turned(value, r, back):
        cosine, sine = (jnp.concatenate([turn[i, r : r + few]] * 2, axis=1) for i in range(2))
        return conj_times((cosine, sine), value) if back else times(value, (cosine, sine))

    def transform(block, exact):
        both = jnp.concatenate([block[0], block[1]], axis=1)
        if exact:
            return dot_nn(fwd[...], jnp.concatenate([both, both], axis=0))
        return dot_nn(fwd[:, :half], both)

    def joined(both, r):
        parts = both[r : r + few], both[half + r : half + r + few]
        even, odd = [part[:, :wide] for part in parts], turned([part[:, wide:] for part in parts], r, False)
        return tuple(a + b for a, b in zip(even, odd)), tuple(a - b for a, b in zip(even, odd))

    def places(r):
        return [pl.ds(first + r, few) for first in (0, taps, half, taps + half)]

    def keep(ref, at, r, pair):
        for lines, part in zip(places(r), pair[0] + pair[1]):
            ref[lines, at] = part

    def kept(ref, at, r):
        parts = [ref[lines, at] for lines in places(r)]
        return parts[:2], parts[2:]

    def signal(pair_at, exact):
        real, imag = [], []
        for r in range(0, half, few):
            a, b = pair_at(r)
            even = [x + y for x, y in zip(a, b)]
            odd = turned([x - y for x, y in zip(a, b)], r, True)
            for lines, x, y in zip((real, imag), even, odd):
                both = jnp.concatenate([x, y], axis=1)
                lines.append(split_low(both) if exact else (both.astype(bf16),))
        lines = real + imag
        if exact:
            high, low = (jnp.concatenate([line[i] for line in lines], axis=0) for i in range(2))
            return dot_nn(inv[...], jnp.concatenate([high, high, low], axis=0))
        return dot_nn(inv[:, : 2 * half], jnp.concatenate([line[0] for line in lines], axis=0))

    def each(function, pairs):
        return tuple(function(*values) for values in zip(*pairs))

    def swung(value, sign):
        return (value[1], -value[0]) if sign > 0 else (-value[1], value[0])

    def own_spectrum(j, _):
        at = lanes(j)
        both = transform((own_b[0, :, at], own_b[1, :, at]), True)
        for r in range(0, half, few):
            keep(u_spec, at, r, joined(both, r))
        return 0

    lax.fori_loop(0, 2, own_spectrum, 0)
    weight_y = [weight_to_y(0)]

    @pl.when(seq < 3)
    def _():
        right_copy.wait_send()

    @pl.when(seq > 0)
    def _():
        right_copy.wait_recv()
        normalise(left_v, left_hat, False)

        def shifted_left(i, _):
            for parity in range(2):
                value = take(left_hat, every_other(i, parity)) * gain + shift
                left_b[parity, sixty_four(i)] = value.astype(bf16)
            return 0

        lax.fori_loop(0, tokens // 128, shifted_left, 0)

    @pl.when(seq == 0)
    def _():
        left_hat[...] = jnp.zeros_like(left_hat)

    def kern_to_core(j):
        finish(kern_plane[j])
        return same(kern.at[halves[j], :, :, c], [core_peer], kern.at[halves[j], :, :, 0], pair_sender)

    weight_y.append(weight_to_y(1))
    kern_core = [kern_to_core(0)]

    @pl.when(seq > 0)
    def _():
        def left_spectrum(j, _):
            at = lanes(j)
            both = transform((left_b[0, :, at], left_b[1, :, at]), True)
            for r in range(0, half, few):
                turns = [swung(value, -sign_of(r)) for value in joined(both, r)]
                old = kept(u_spec, at, r)
                keep(u_spec, at, r, tuple(tuple(a + b for a, b in zip(x, y)) for x, y in zip(old, turns)))
            return 0

        lax.fori_loop(0, 2, left_spectrum, 0)

    kern_core.append(kern_to_core(1))
    weight_y.append(weight_to_y(2))
    weight_to_core(0)

    def kernel_transform(j):
        rows = kern[2 * j : 2 * j + 2].reshape(wide, taps)
        rows = [jnp.concatenate([rows[:, at]] * 2, axis=1) for at in (slice(0, half), slice(half, taps))]
        return dot_nt(fwd[...], jnp.concatenate(rows, axis=0))

    def convolve(j, both):
        at = lanes(j)

        def product(r):
            k = joined(both, r)
            keep(k_spec, at, r, k)
            return each(times, (k, kept(u_spec, at, r)))

        both = signal(product, True)
        for parity in range(2):
            put(mixed, pl.ds(parity, half, stride=2), both[:, wide * parity : wide * (parity + 1)], 2 * j)

    def activate(j):
        for tile in (2 * j, 2 * j + 1):
            at = slice(128 * tile, 128 * tile + 128)
            for start_at in range(0, tokens, 128):
                lines = slice(start_at, start_at + 128)
                value = mixed[tile, lines, :] + rows_f[2:3, at] * normed[tile, lines, :]
                chance = 0.5 + 0.5 * lax.erf(value * (0.5**0.5))
                slope[lines, at] = chance + value * jnp.exp(value * value * -0.5 - 0.5 * float(np.log(2.0 * np.pi)))
                low = (value * chance).astype(bf16)
                activ[lines, at] = low
                activ_t[at, lines] = low.T

    finish(kern_core[0])
    first_half = kernel_transform(0)
    finish(kern_core[1])
    second_half = kernel_transform(1)
    convolve(0, first_half)
    weight_to_core(1)
    last_to_core()
    convolve(1, second_half)
    activate(0)
    activate(1)
    weight_to_core(2)
    loads[5].wait()

    def matrix_of(h):
        return jnp.concatenate([weight[q].reshape(channels, 256) for q in (2 * h, 2 * h + 1)], axis=1)

    def gates(h, pre):
        lines_out = []
        sums = [jnp.zeros((32, 128), f32) for _ in range(4)]
        for start_at in range(0, tokens, 32):
            lines = slice(start_at, start_at + 32)
            low = []
            for i, q in enumerate((2 * h, 2 * h + 1)):
                at = slice(128 * q, 128 * q + 128)
                lin = pre[lines, 256 * i : 256 * i + 128] + rows_f[3:4, at]
                gate = 0.5 + 0.5 * jnp.tanh(0.5 * (pre[lines, 256 * i + 128 : 256 * i + 256] + rows_f[4:5, at]))
                grad = g_v[lines, at].astype(f32)
                product = lin * gate
                res_v[lines, at] = (x_v[lines, at].astype(f32) + product).astype(bf16)
                low += [(grad * gate).astype(bf16), (grad * (product - product * gate)).astype(bf16)]
            sums = [total + part.astype(f32) for total, part in zip(sums, low)]
            lines_out.append(jnp.concatenate(low, axis=1))
        for i, q in enumerate((2 * h, 2 * h + 1)):
            for k in range(2):
                rows_f[3 + k : 4 + k, 128 * q : 128 * q + 128] = jnp.sum(sums[2 * i + k], axis=0, keepdims=True)
        return jnp.concatenate(lines_out, axis=0)

    def weight_grad(h, low):
        grad = dot_nn(activ_t[...], low).astype(bf16)
        for i, q in enumerate((2 * h, 2 * h + 1)):
            dw_own[q] = grad[:, 256 * i : 256 * i + 256].reshape(4, 2, 2, 2, ROWS, 256)
            arrival = start([(dw_own.at[q, :, :, :, flip_c], dw_in1.at[q], core_peer)], dw_senders[0], dw_in1.at[q])
            dw_core.append(arrival)

    def mix_grad(d_act):
        total = jnp.zeros((32, channels), f32)
        for start_at in range(0, tokens, 32):
            lines = slice(start_at, start_at + 32)
            mix = (d_act[lines] * slope[lines, :]).astype(bf16).astype(f32)
            total += mix * take(normed, lines)
            put(mixed, lines, mix)
        rows_f[2:3, :] = jnp.sum(total, axis=0, keepdims=True)
        for parity in range(2):
            for start_at in range(0, half, 64):
                part = take(mixed, pl.ds(2 * start_at + parity, 64, stride=2))
                d_mix[parity, start_at : start_at + 64] = part.astype(bf16)

    def core_sum(q):
        finish(dw_core[q])
        dw_mid[q] = (dw_own[q, :, :, :, c].astype(f32) + dw_in1[q].astype(f32)).astype(bf16)

    def to_y(q):
        core_sum(q)
        return start([(dw_mid.at[q, :, flip_y], dw_in2.at[q], y_peer)], dw_senders[1], dw_in2.at[q])

    def end_to_z():
        core_sum(3)
        copies = [(dw_mid.at[3, peer[0]], end_in1.at[i], peer) for i, peer in enumerate(z_peers)]
        return start(copies, sender(end_in1), end_in1)

    def end_to_y():
        finish(end_z)
        total = dw_mid[3, z].astype(f32)
        for i in range(3):
            total = total + end_in1[i].astype(f32)
        end_mid[...] = total.astype(bf16)
        return start([(end_mid.at[flip_y], end_in2, y_peer)], sender(end_in2), end_in2)

    def end_to_x():
        finish(end_y)
        dw_end[3] = (end_mid[y].astype(f32) + end_in2[...].astype(f32)).astype(bf16)
        return start([(dw_end.at[3, flip_x], dw_in4.at[3], x_peer)], dw_senders[3], dw_in4.at[3])

    def to_z(q):
        finish(dw_y[q])
        dw_low[q] = (dw_mid[q, :, y].astype(f32) + dw_in2[q].astype(f32)).astype(bf16)
        copies = [(dw_low.at[q, peer[0]], dw_in3.at[q, i], peer) for i, peer in enumerate(z_peers)]
        return start(copies, dw_senders[2], dw_in3.at[q])

    def to_x(q):
        finish(dw_z[q])
        total = dw_low[q, z].astype(f32)
        for i in range(3):
            total = total + dw_in3[q, i].astype(f32)
        dw_end[q] = total.astype(bf16)
        return start([(dw_end.at[q, flip_x], dw_in4.at[q], x_peer)], dw_senders[3], dw_in4.at[q])

    def to_end(q):
        finish(dw_x[q])
        total = dw_end[q, x].astype(f32) + dw_in4[q].astype(f32)
        dw_ref[:, 128 * q : 128 * q + 128] = total[:, :128]
        dw_ref[:, channels + 128 * q : channels + 128 * q + 128] = total[:, 128:]

    skip = rows_f[2:3, :]
    dw_core, dw_y, dw_z, dw_x = [], [], [], []
    dw_senders = [sender(ref) for ref in (dw_in1, dw_in2.at[three], dw_in3.at[three], dw_in4)]
    finish(weight_core[0])
    finish(weight_core[1])
    first_pre = dot_nn(activ[...], matrix_of(0))
    first_low = gates(0, first_pre)
    finish(weight_core[2])
    finish(weight_core[3])
    second_pre = dot_nn(activ[...], matrix_of(1))
    weight_grad(0, first_low)
    second_low = gates(1, second_pre)
    weight_grad(1, second_low)
    d_act = dot_nt(
        jnp.concatenate([first_low, second_low], axis=1), jnp.concatenate([matrix_of(0), matrix_of(1)], axis=1)
    )
    mix_grad(d_act)
    left_sender = sends.at[claim("send")]
    left_copies = [
        pltpu.make_async_remote_copy(
            src_ref=d_mix.at[:, :, pl.ds(wide * j, wide)], dst_ref=right_v.at[j], send_sem=left_sender,
            recv_sem=recvs.at[claim("recv")], device_id=(dp, seq - 1), device_id_type=MESH,
        )
        for j in range(2)
    ]
    dk_senders = [sender(ref) for ref in (dk_in1, dk_in2, dk_in3)]

    @pl.when(seq > 0)
    def _():
        left_copies[0].start()

    dw_y.append(to_y(0))
    dw_y.append(to_y(1))

    def mix_transform(j):
        at = lanes(j)
        return transform((d_mix[0, :, at], d_mix[1, :, at]), False)

    def kernel_grad(j, both):
        at = lanes(j)

        def product(r):
            d = joined(both, r)
            keep(d_spec, at, r, d)
            return each(conj_times, (kept(u_spec, at, r), d))

        both = signal(product, False)
        grad = jnp.concatenate([both[:, :wide].T, both[:, wide:].T], axis=1).reshape(2, 2, 2, 2, ROWS, taps)
        dk_own[2 * j : 2 * j + 2] = grad
        dk_low[2 * j : 2 * j + 2] = grad.astype(bf16)
        part = halves[j]
        return start([(dk_low.at[part, :, :, flip_c], dk_in1.at[part], core_peer)], dk_senders[0], dk_in1.at[part])

    def kernel_middle(j):
        finish(dk_core[j])
        for i in (2 * j, 2 * j + 1):
            total = dk_own[i, :, :, c] + dk_in1[i].astype(f32)
            dk_mid[i] = total
            dk_cut[i] = total.astype(bf16)
        part = halves[j]
        copies = [(dk_cut.at[part, peer[1], peer[2]], dk_in2.at[i, part], peer) for i, peer in enumerate(plane_peers)]
        return start(copies, dk_senders[1], dk_in2.at[:, part])

    def kernel_end(j):
        finish(dk_plane[j])
        for i in (2 * j, 2 * j + 1):
            total = dk_mid[i, y, x]
            for k in range(3):
                total = total + dk_in2[k, i].astype(f32)
            dk_end[i] = total
            dk_out[i] = total.astype(bf16)

    def own_grad(j):
        at = lanes(j)

        def product(r):
            return each(conj_times, (kept(k_spec, at, r), kept(d_spec, at, r)))

        def shifted_product(r):
            return tuple(swung(value, sign_of(r)) for value in product(r))

        own, back = signal(product, False), signal(shifted_product, False)
        d_gain, d_shift = jnp.zeros((1, wide), f32), jnp.zeros((1, wide), f32)
        for parity in range(2):
            lines = pl.ds(parity, half, stride=2)
            columns = slice(wide * parity, wide * (parity + 1))
            grad = own[:, columns] + rows_f[5:6, at] * d_mix[parity, :, at].astype(f32)
            put(d_norm, lines, grad, 2 * j)
            before = jnp.where(seq > 0, back[:, columns], 0.0)
            d_gain += jnp.sum(
                grad * take(x_hat, lines, 2 * j, 2) + before * take(left_hat, lines, 2 * j, 2), axis=0, keepdims=True
            )
            d_shift += jnp.sum(grad + before, axis=0, keepdims=True)
        rows_f[6:7, at], rows_f[7:8, at] = d_gain, d_shift

    def right_grad(j):
        at = lanes(j)
        both = transform((right_v[j, 0], right_v[j, 1]), False)

        def product(r):
            turns = [swung(value, sign_of(r)) for value in joined(both, r)]
            return each(conj_times, (kept(k_spec, at, r), turns))

        both = signal(product, False)
        for parity in range(2):
            lines = pl.ds(parity, half, stride=2)
            more = both[:, wide * parity : wide * (parity + 1)]
            put(d_norm, lines, take(d_norm, lines, 2 * j, 2) + more, 2 * j)

    rows_f[5:6, :] = skip
    first_half, second_half = mix_transform(0), mix_transform(1)
    dk_core = [kernel_grad(0, first_half)]
    dw_y.append(to_y(2))
    end_z = end_to_z()
    dk_core.append(kernel_grad(1, second_half))
    dk_plane = [kernel_middle(0)]
    own_grad(0)
    dk_plane.append(kernel_middle(1))

    @pl.when(seq > 0)
    def _():
        left_copies[1].start()

    own_grad(1)
    dw_z.append(to_z(0))
    dw_z.append(to_z(1))
    vector = jnp.concatenate([rows_f[6:7, :], rows_f[7:8, :], rows_f[2:3, :], rows_f[3:4, :], rows_f[4:5, :]], axis=1)
    high, low = split_low(jnp.broadcast_to(vector, mask.shape) * mask[...].astype(f32))
    shares = dot_nt(high, pick[...]) + dot_nt(low, pick[...])
    share_out[...] = shares.reshape(32, 1, 128).reshape(4, 8, 1, 128)
    copies = [(share_out.at[peer[0]], share_in1.at[i], peer) for i, peer in enumerate(z_peers)]
    share_z = start(copies, sender(share_in1), share_in1)
    @pl.when(seq < 3)
    def _():
        left_copies[0].wait_recv()
        right_grad(0)

    dw_z.append(to_z(2))
    end_y = end_to_y()
    kernel_end(0)
    kernel_end(1)
    dk_z = start([(dk_out.at[peer[0]], dk_in3.at[i], peer) for i, peer in enumerate(z_peers)], dk_senders[2], dk_in3)
    finish(share_z)
    share_mid[...] = share_out[z] + share_in1[0] + share_in1[1] + share_in1[2]
    copies = [
        (share_mid.at[(peer[1] * 2 + peer[2]) * 2 + peer[3]], share_in2.at[i], peer)
        for i, peer in enumerate(plane_peers + other_peers)
    ]
    share_plane = start(copies, sender(share_in2), share_in2)

    @pl.when(seq < 3)
    def _():
        left_copies[1].wait_recv()
        right_grad(1)

    dw_x.append(to_x(0))
    dw_x.append(to_x(1))
    end_x = end_to_x()
    dw_x.append(to_x(2))
    dw_x.append(end_x)

    @pl.when(seq > 0)
    def _():
        arrive(left_sender, d_mix)

    def input_grad(i, _):
        at = pl.ds(pl.multiple_of(i * 128, 128), 128)
        grad, hat = take(d_norm, at), take(x_hat, at)
        scaled = grad * rows_f[0:1, :]
        inner = (
            scaled
            - jnp.mean(scaled, axis=1, keepdims=True)
            - hat * jnp.mean(scaled * hat, axis=1, keepdims=True)
        )
        gin_v[at, :] = (inv_std[at, 0:1] * inner + g_v[at, :].astype(f32)).astype(bf16)
        return 0

    lax.fori_loop(0, tokens // 128, input_grad, 0)
    finish(dk_z)
    d_kernel = dk_end[z]
    for k in range(3):
        d_kernel = d_kernel + dk_in3[k].astype(f32)

    for m in range(8):
        block = d_kernel[:, 64 * m : 64 * m + 64]
        lines_f[pl.ds(m, ROWS, stride=8), :] = jnp.concatenate([block, block], axis=1)
    plain = lines_f[...][:, :64]
    ramp = plain * (2 * lax.broadcasted_iota(jnp.int32, (8 * ROWS, 64), 1)).astype(f32)
    high, low = split_low(jnp.concatenate([plain, ramp], axis=0))
    table = jnp.concatenate([base_high[...], base_low[...], base_high[...]], axis=0)
    sums = dot_nn(jnp.concatenate([high, high, low], axis=1), table)
    at_row = lax.broadcasted_iota(jnp.int32, (8, 128), 0)
    first = lax.broadcasted_iota(jnp.int32, (8, 128), 1) < 64
    leap_of = (128 * lax.rem(at_row, 4) + lax.div(at_row, 4)).astype(f32)
    zero = jnp.zeros((8, 128), f32)
    s0, s1 = [zero, zero], [zero, zero]
    for p in range(8):
        def pair(start, part):
            block = sums[start : start + 128, 256 * p + 128 * part : 256 * p + 128 * part + 128]
            return jnp.where(first, block[8 * p : 8 * p + 8], block[8 * p + 64 : 8 * p + 72])

        value, slope_of = [pair(0, part) for part in range(2)], [pair(128, part) for part in range(2)]
        leap = (leaps[p, 0], leaps[p, 1])
        slope_of = [one + leap_of * other for one, other in zip(slope_of, value)]
        for total, terms in ((s0, value), (s1, slope_of)):
            for part, product in enumerate(times(leap, terms)):
                total[part] = jnp.where(at_row == p, jnp.sum(product, axis=0, keepdims=True), total[part])
    dt, a, unit, norm_sq, ratio, coef, scaled = mode_terms(ldt_ref[...], lar_ref[...], ai_ref[...], cc_ref[...])
    inverse_a = (a[0] / norm_sq, -a[1] / norm_sq)
    d_coef = times(s0, ratio)
    half_g = times(times(coef, s0), times(unit, inverse_a))
    ramp_part = times(scaled, s1)
    half_g = (half_g[0] + ramp_part[0], half_g[1] + ramp_part[1])
    back = times(times(scaled, s0), inverse_a)
    q = (half_g[0] * dt - back[0], half_g[1] * dt - back[1])
    d_dt = 2.0 * dt * times(half_g, a)[0]
    dldt_ref[...] = row_of(jnp.sum(unpair_lanes(d_dt), axis=1, keepdims=True))[0]
    dlar_ref[...] = unpair_lanes(2.0 * q[0] * a[0])
    dai_ref[...] = unpair_lanes(-2.0 * q[1])
    dcc_ref[...] = jnp.concatenate([unpair_lanes(2.0 * d_coef[0]), unpair_lanes(-2.0 * d_coef[1])], axis=1)

    for q in range(4):
        to_end(q)
    finish(share_plane)
    small = share_mid[place]
    for i in range(7):
        small = small + share_in2[i]
    for i, target in enumerate([dgain_ref, dshift_ref, dskip_ref]):
        target[...] = small[0, ROWS * i : ROWS * (i + 1)]
    dbias_ref[...] = small[0, 3 * ROWS : 5 * ROWS]
    for departure in departures:
        arrive(*departure)


def finish_kernel(*refs):
    count = len(refs) // 2
    sems = refs[-1]
    copies = [pltpu.make_async_copy(refs[i], refs[count + i], sems.at[i]) for i in range(count)]
    for copy in copies:
        copy.start()
    for copy in copies:
        copy.wait()


def kernel_body(
    inputs, grad_out, ln_gain, ln_bias, skip_scale, w_glu, b_glu, log_dt, log_a_real, a_imag, c_coef
):
    _, tokens, channels = inputs.shape
    taps = KTAPS
    glu = w_glu.shape[1]
    f32, bf16 = jnp.float32, jnp.bfloat16
    order = np.concatenate([np.arange(0, taps // 2, 2), np.arange(1, taps // 2, 2)]) + 0.5
    angle = np.outer(order, np.arange(taps // 2)) * (2 * np.pi / taps)
    matrix = np.concatenate([np.cos(angle), -np.sin(angle)], axis=0)
    high = matrix.astype(bf16)
    low = (matrix - high.astype(np.float64)).astype(bf16)
    forward = np.concatenate([high, low], axis=1)
    scale = np.asarray(1.0 / taps, bf16)
    inverse = np.concatenate([high.T, low.T, high.T], axis=1) * scale
    turns = np.stack([np.cos(order * (np.pi / taps)), -np.sin(order * (np.pi / taps))])
    turns = np.ascontiguousarray(np.broadcast_to(turns[:, :, None], (2, taps // 2, 128))).astype(np.float32)
    device_at, lane = np.arange(32)[:, None], np.arange(channels)[None, :]
    bias_lane = np.arange(2 * channels)[None, :]
    row = np.arange(128)[:, None]
    pick = np.concatenate(
        [row == i * ROWS + lane % ROWS for i in range(3)] + [row == 3 * ROWS + bias_lane % (2 * ROWS)], axis=1
    ).astype(bf16)
    mask = np.concatenate(
        [device_at == lane // ROWS] * 3 + [device_at == bias_lane // (2 * ROWS)], axis=1
    ).astype(bf16)
    hbm, vmem = pl.BlockSpec(memory_space=pl.ANY), pl.BlockSpec(memory_space=pltpu.VMEM)
    block = (tokens, channels)
    spec, tall = (2 * taps, channels), (channels // 128, tokens, 128)

    def space(*dims, kind=f32):
        return pltpu.VMEM(dims, kind)

    results = (
        (block, bf16), (block, bf16), ((ROWS,), f32), ((ROWS,), f32), ((ROWS,), f32), (w_glu.shape, f32),
        ((2 * ROWS,), f32), ((ROWS,), f32), (log_a_real.shape, f32), (a_imag.shape, f32), (c_coef.shape, f32),
    )
    outs = pl.pallas_call(
        layer_kernel,
        name="layer",
        out_shape=tuple(pltpu.VMEM(dims, kind) for dims, kind in results),
        in_specs=[hbm] * 16,
        out_specs=(vmem,) * len(results),
        scratch_shapes=[
            space(*w_glu.shape), space(1, ROWS), space(1, ROWS), space(1, ROWS), space(1, 2 * ROWS), space(1, ROWS),
            space(*log_a_real.shape), space(*a_imag.shape), space(*c_coef.shape),
            space(*block, kind=bf16), space(*block, kind=bf16), space(*block, kind=bf16),
            space(*forward.shape, kind=bf16), space(*inverse.shape, kind=bf16),
            space(*pick.shape, kind=bf16), space(*mask.shape, kind=bf16), space(*turns.shape),
            space(4, 2, 2, 2, ROWS, taps, kind=bf16), space(4, 4, 2, 2, 2, ROWS, 256, kind=bf16),
            space(64, 2048, kind=bf16), space(64, 2048, kind=bf16), space(8, 2, 8, 128), space(8 * ROWS, 128),
            space(4, 8, 1, 128), space(4, 8, 1, 128), space(3, 8, 1, 128), space(8, 1, 128), space(7, 1, 128),
            space(8, channels),
            space(*tall), space(tokens, 128), space(*tall), space(*tall),
            space(2, tokens // 2, channels, kind=bf16), space(2, tokens // 2, channels, kind=bf16),
            space(*spec), space(*spec), space(*tall), space(*block),
            space(*block, kind=bf16), space(channels, tokens, kind=bf16),
            space(2, tokens // 2, channels, kind=bf16), space(2, 2, tokens // 2, 256, kind=bf16),
            space(*spec), space(*tall),
            space(4, 4, 2, 2, 2, ROWS, 256, kind=bf16), space(4, 4, 2, 2, ROWS, 256, kind=bf16),
            space(4, 4, 2, 2, ROWS, 256, kind=bf16), space(4, 4, 2, ROWS, 256, kind=bf16),
            space(4, 4, 2, ROWS, 256, kind=bf16), space(4, 3, 2, ROWS, 256, kind=bf16),
            space(4, 2, ROWS, 256, kind=bf16), space(4, ROWS, 256, kind=bf16),
            space(3, 2, 2, ROWS, 256, kind=bf16), space(2, 2, ROWS, 256, kind=bf16), space(2, ROWS, 256, kind=bf16),
            space(4, 2, 2, 2, ROWS, taps), space(4, 2, 2, 2, ROWS, taps, kind=bf16), space(4, 2, 2, ROWS, taps, kind=bf16),
            space(4, 2, 2, ROWS, taps), space(4, 2, 2, ROWS, taps, kind=bf16), space(3, 4, ROWS, taps, kind=bf16),
            space(4, ROWS, taps), space(4, ROWS, taps, kind=bf16), space(3, ROWS, taps, kind=bf16),
            pltpu.SemaphoreType.DMA((16,)), pltpu.SemaphoreType.DMA((24,)), pltpu.SemaphoreType.DMA((46,)),
        ],
        compiler_params=pltpu.CompilerParams(
            collective_id=0, has_side_effects=True, vmem_limit_bytes=48 * 2**20
        ),
    )(*[
        pltpu.with_memory_space_constraint(value, pltpu.HBM)
        for value in (
            inputs.reshape(block), grad_out.reshape(block), forward, inverse, pick, mask, turns, w_glu,
            ln_gain.reshape(1, -1), ln_bias.reshape(1, -1), skip_scale.reshape(1, -1), b_glu.reshape(1, -1),
            log_dt.reshape(1, -1), log_a_real, a_imag, c_coef,
        )
    ])
    ended = pl.pallas_call(
        finish_kernel,
        name="finish",
        out_shape=tuple(jax.ShapeDtypeStruct(dims, kind) for dims, kind in results),
        in_specs=[vmem] * len(results),
        out_specs=(hbm,) * len(results),
        scratch_shapes=[pltpu.SemaphoreType.DMA((len(results),))],
    )(*[pltpu.with_memory_space_constraint(value, pltpu.VMEM) for value in outs])
    return (ended[0].reshape(inputs.shape), ended[1].reshape(inputs.shape)) + tuple(ended[2:])


def solution(mesh):
    in_specs = (
        P("dp", "seq", None),
        P("dp", "seq", None),
        P(("dp", "seq")),
        P(("dp", "seq")),
        P(("dp", "seq")),
        P(("dp", "seq"), None),
        P(("dp", "seq")),
        P(("dp", "seq")),
        P(("dp", "seq"), None),
        P(("dp", "seq"), None),
        P(("dp", "seq"), None),
    )
    out_specs = (
        P("dp", "seq", None),
        P("dp", "seq", None),
        P(("dp", "seq")),
        P(("dp", "seq")),
        P(("dp", "seq")),
        P(("dp", "seq"), None),
        P(("dp", "seq")),
        P(("dp", "seq")),
        P(("dp", "seq"), None),
        P(("dp", "seq"), None),
        P(("dp", "seq"), None),
    )
    quick = mesh.shape["dp"] == 8 and mesh.shape["seq"] == 4
    return jax.shard_map(kernel_body if quick else body, mesh=mesh, in_specs=in_specs, out_specs=out_specs, check_vma=False)
```

```python
from functools import partial

import jax
import jax.numpy as jnp
import numpy as np
from jax import lax
from jax.experimental import pallas as pl
from jax.experimental.pallas import tpu as pltpu
from jax.sharding import PartitionSpec as P

KTAPS = 512


EPS = 1e-05


def passed_along(value, axis, steps):
    count = lax.axis_size(axis)
    first, last = (max(0, -steps), min(count, count - steps))
    return lax.ppermute(value, axis, [(source, source + steps) for source in range(first, last)])


def kernel_block(log_dt, log_a_real, a_imag, c_coef, start, count):
    mode_count = log_a_real.shape[1]
    step_size = jnp.exp(log_dt)[:, None]
    a_real = -jnp.exp(log_a_real)
    decay = a_real * step_size
    turn = a_imag * step_size
    growth = jnp.exp(decay)
    ex_re = growth * jnp.cos(turn) - 1.0
    ex_im = growth * jnp.sin(turn)
    norm_sq = a_real * a_real + a_imag * a_imag
    ratio_re = (ex_re * a_real + ex_im * a_imag) / norm_sq
    ratio_im = (ex_im * a_real - ex_re * a_imag) / norm_sq
    c_re = c_coef[:, :mode_count]
    c_im = c_coef[:, mode_count:]
    coef_re = c_re * ratio_re - c_im * ratio_im
    coef_im = c_re * ratio_im + c_im * ratio_re
    places = (start + jnp.arange(count)).astype(jnp.float32)
    phase = turn[:, :, None] * places
    damping = jnp.exp(decay[:, :, None] * places)
    terms = damping * (coef_re[:, :, None] * jnp.cos(phase) - coef_im[:, :, None] * jnp.sin(phase))
    return 2.0 * jnp.sum(terms, axis=1)


def transforms(taps):
    angle = np.outer(np.arange(taps) + 0.5, np.arange(taps)) * (np.pi / taps)
    forward = np.concatenate([np.cos(angle), -np.sin(angle)], axis=0)
    inverse = forward.T / taps
    return forward.astype(jnp.bfloat16), inverse.astype(jnp.bfloat16)


def body(
    inputs, grad_out, ln_gain, ln_bias, skip_scale, w_glu, b_glu, log_dt, log_a_real, a_imag, c_coef
):
    seq_count, own_len, channels = inputs.shape
    gain_low = ln_gain.astype(jnp.bfloat16)
    shift_low = ln_bias.astype(jnp.bfloat16)
    skip_low = skip_scale.astype(jnp.bfloat16)
    weight_low = w_glu.astype(jnp.bfloat16)
    bias_low = b_glu.astype(jnp.bfloat16)
    mode_own = (log_dt, log_a_real, a_imag, c_coef)
    own_kernel = kernel_block(*mode_own, 0, KTAPS).astype(jnp.bfloat16)
    gathered = (
        lax.all_gather(gain_low, ("dp", "seq"), axis=0, tiled=True),
        lax.all_gather(shift_low, ("dp", "seq"), axis=0, tiled=True),
        lax.all_gather(skip_low, ("dp", "seq"), axis=0, tiled=True),
        lax.all_gather(weight_low, ("dp", "seq"), axis=0, tiled=True),
        lax.all_gather(bias_low, ("dp", "seq"), axis=0, tiled=True),
        lax.all_gather(own_kernel, ("dp", "seq"), axis=0, tiled=True),
    )
    kernel_b = gathered[5]
    taps = own_len
    forward, inverse = transforms(taps)
    sign = jnp.where(jnp.arange(taps) % 2 == 0, 1.0, -1.0).astype(jnp.float32)[:, None]

    def to_spectrum(block):
        both = jnp.dot(forward, block, preferred_element_type=jnp.float32)
        return both[:taps], both[taps:]

    def from_spectrum(real, imag):
        both = jnp.concatenate([real, imag], axis=0).astype(jnp.bfloat16)
        return jnp.dot(inverse, both, preferred_element_type=jnp.float32)

    kernel_re, kernel_im = to_spectrum(kernel_b.T)
    gain_full = gathered[0].astype(jnp.float32)
    shift_full = gathered[1].astype(jnp.float32)
    skip_full = gathered[2].astype(jnp.float32)
    weight_b = gathered[3]
    glu_bias = gathered[4].astype(jnp.float32)
    x_float = inputs.astype(jnp.float32)
    row_mean = jnp.mean(x_float, axis=-1, keepdims=True)
    centered = x_float - row_mean
    row_var = jnp.mean(centered * centered, axis=-1, keepdims=True)
    inv_std = lax.rsqrt(row_var + EPS)
    x_hat = centered * inv_std
    normed = x_hat * gain_full + shift_full
    normed_b = normed.astype(jnp.bfloat16)
    own_re, own_im = to_spectrum(normed_b[0])
    left_re, left_im = to_spectrum(passed_along(normed_b, "seq", 1)[0])
    source_re = own_re - sign * left_im
    source_im = own_im + sign * left_re
    conv = from_spectrum(
        kernel_re * source_re - kernel_im * source_im,
        kernel_re * source_im + kernel_im * source_re,
    )
    mixed_pre = conv[None] + skip_full * normed
    activ, gelu_pull = jax.vjp(partial(jax.nn.gelu, approximate=False), mixed_pre)
    activ_b = activ.astype(jnp.bfloat16)
    glu_pre = (
        jnp.einsum("slh,hg->slg", activ_b, weight_b, preferred_element_type=jnp.float32) + glu_bias
    )
    half_dim = glu_pre.shape[-1] // 2
    lin_part = glu_pre[..., :half_dim]
    gate_sig = jax.nn.sigmoid(glu_pre[..., half_dim:])
    result = (x_float + lin_part * gate_sig).astype(jnp.bfloat16)
    grad_f = grad_out.astype(jnp.float32)
    d_pre = jnp.concatenate(
        [grad_f * gate_sig, grad_f * lin_part * gate_sig * (1.0 - gate_sig)], axis=-1
    ).astype(jnp.bfloat16)
    d_weight = jnp.einsum("slh,slg->hg", activ_b, d_pre, preferred_element_type=jnp.float32)
    d_glu_bias = jnp.sum(d_pre.astype(jnp.float32), axis=(0, 1))
    d_act = jnp.einsum("slg,hg->slh", d_pre, weight_b, preferred_element_type=jnp.float32)
    d_mix = gelu_pull(d_act)[0].astype(jnp.bfloat16)
    d_mix_f = d_mix.astype(jnp.float32)
    d_skip = jnp.sum(d_mix_f * normed, axis=(0, 1))
    mix_re, mix_im = to_spectrum(d_mix[0])
    d_kernel = from_spectrum(
        source_re * mix_re + source_im * mix_im, source_re * mix_im - source_im * mix_re
    ).T
    right_re, right_im = to_spectrum(passed_along(d_mix, "seq", -1)[0])
    sum_re = mix_re + sign * right_im
    sum_im = mix_im - sign * right_re
    d_conv = from_spectrum(
        kernel_re * sum_re + kernel_im * sum_im, kernel_re * sum_im - kernel_im * sum_re
    )[None]
    d_normed = d_conv + skip_full * d_mix_f
    d_gain = jnp.sum(d_normed * x_hat, axis=(0, 1))
    d_shift = jnp.sum(d_normed, axis=(0, 1))
    scaled = d_normed * gain_full
    d_input = (
        inv_std
        * (
            scaled
            - jnp.mean(scaled, axis=-1, keepdims=True)
            - x_hat * jnp.mean(scaled * x_hat, axis=-1, keepdims=True)
        )
        + grad_f
    )
    grad_in = d_input.astype(jnp.bfloat16)
    summed = (
        lax.psum_scatter(d_gain, ("dp", "seq"), scatter_dimension=0, tiled=True),
        lax.psum_scatter(d_shift, ("dp", "seq"), scatter_dimension=0, tiled=True),
        lax.psum_scatter(d_skip, ("dp", "seq"), scatter_dimension=0, tiled=True),
        lax.psum_scatter(d_weight, ("dp", "seq"), scatter_dimension=0, tiled=True),
        lax.psum_scatter(d_glu_bias, ("dp", "seq"), scatter_dimension=0, tiled=True),
        lax.psum_scatter(d_kernel, ("dp", "seq"), scatter_dimension=0, tiled=True),
    )
    _, own_pull = jax.vjp(partial(kernel_block, start=0, count=KTAPS), *mode_own)
    mode_grads = own_pull(summed[5])
    return (
        result,
        grad_in,
        summed[0],
        summed[1],
        summed[2],
        summed[3],
        summed[4],
        mode_grads[0],
        mode_grads[1],
        mode_grads[2],
        mode_grads[3],
    )


MESH = pl.DeviceIdType.MESH
ROWS = 16


def pair_lanes(value):
    return jnp.concatenate([value[:8], value[8:]], axis=1)


def unpair_lanes(value):
    half = value.shape[1] // 2
    return jnp.concatenate([value[:, :half], value[:, half:]], axis=0)


def column_of(row):
    n = row.shape[1]
    at = lax.broadcasted_iota(jnp.int32, (n, n), 0) == lax.broadcasted_iota(jnp.int32, (n, n), 1)
    return jnp.sum(jnp.where(at, jnp.broadcast_to(row, (n, n)), 0.0), axis=1, keepdims=True)


def row_of(column):
    n = column.shape[0]
    at = lax.broadcasted_iota(jnp.int32, (n, n), 0) == lax.broadcasted_iota(jnp.int32, (n, n), 1)
    return jnp.sum(jnp.where(at, jnp.broadcast_to(column, (n, n)), 0.0), axis=0, keepdims=True)


def mode_terms(ldt, lar, ai, cc):
    n_modes = lar.shape[1]
    dt = column_of(jnp.exp(ldt))
    dt = jnp.concatenate(
        [jnp.broadcast_to(dt[:8], (8, n_modes)), jnp.broadcast_to(dt[8:], (8, n_modes))], axis=1
    )
    a_re, a_im = -jnp.exp(pair_lanes(lar)), pair_lanes(ai)
    decay, turn = a_re * dt, a_im * dt
    growth = jnp.exp(decay)
    z_re, z_im = growth * jnp.cos(turn), growth * jnp.sin(turn)
    ex_re, ex_im = z_re - 1.0, z_im
    norm_sq = a_re * a_re + a_im * a_im
    r_re = (ex_re * a_re + ex_im * a_im) / norm_sq
    r_im = (ex_im * a_re - ex_re * a_im) / norm_sq
    c_re, c_im = pair_lanes(cc[:, :n_modes]), pair_lanes(cc[:, n_modes:])
    w_re, w_im = c_re * r_re - c_im * r_im, c_re * r_im + c_im * r_re
    return dt, (a_re, a_im), (z_re, z_im), norm_sq, (r_re, r_im), (c_re, c_im), (w_re, w_im)


def times(a, b):
    return a[0] * b[0] - a[1] * b[1], a[0] * b[1] + a[1] * b[0]


def conj_times(a, b):
    return a[0] * b[0] + a[1] * b[1], a[0] * b[1] - a[1] * b[0]


def split_low(value):
    high = value.astype(jnp.bfloat16)
    return high, (value - high.astype(jnp.float32)).astype(jnp.bfloat16)


def dot_nn(a, b):
    return lax.dot_general(a, b, (((1,), (0,)), ((), ())), preferred_element_type=jnp.float32)


def dot_nt(a, b):
    return lax.dot_general(a, b, (((1,), (1,)), ((), ())), preferred_element_type=jnp.float32)


def layer_kernel(
    x_hbm, g_hbm, fwd_hbm, most_hbm, rest_hbm, inv_hbm, pick_hbm, mask_hbm, turn_hbm,
    w_hbm, gain_hbm, shift_hbm, skip_hbm, bias_hbm, ldt_hbm, lar_hbm, ai_hbm, cc_hbm,
    res_v, gin_v, dgain_ref, dshift_ref, dskip_ref, dw_ref, dbias_ref, dldt_ref, dlar_ref, dai_ref, dcc_ref,
    w_ref, gain_ref, shift_ref, skip_ref, bias_ref, ldt_ref, lar_ref, ai_ref, cc_ref,
    x_v, g_v, left_v, fwd, fwd_most, fwd_rest, inv, pick, mask, turn, kern, weight, base_high, base_low, leaps, lines_f,
    share_in, share_out, share_in1, share_mid, share_in2, rows_f, x_hat, inv_std, left_hat, normed, own_b, left_b,
    k_raw, k_spec, u_spec, mixed, slope, activ, activ_t, d_mix, right_v, d_spec, d_norm,
    dw_own, dw_in1, dw_mid, dw_in2, dw_low, dw_in3, dw_end, dw_in4, end_in1, end_mid, end_in2,
    dk_own, dk_low, dk_in1, dk_mid, dk_cut, dk_in2, dk_end, dk_out, dk_in3,
    local, sends, recvs,
):
    f32, bf16 = jnp.float32, jnp.bfloat16
    tokens, channels = x_v.shape
    taps = KTAPS
    half, fourth = taps // 2, taps // 4
    dp, seq = lax.axis_index("dp"), lax.axis_index("seq")
    index = dp * 4 + seq
    z, y, x, c = lax.div(dp, 2), lax.rem(dp, 2), lax.div(seq, 2), lax.rem(seq, 2)
    flip_y, flip_x, flip_c = 1 - y, 1 - x, 1 - c

    def device(z, y, x, c):
        return (z * 2 + y, x * 2 + c)

    z_peers = [(lax.rem(z + k, 4), y, x, c) for k in (1, 2, 3)]
    plane_peers = [
        (z, lax.rem(y + k // 2, 2), lax.rem(x + k % 2, 2), c) for k in (1, 2, 3)
    ]
    x_peer, y_peer, core_peer = (z, y, flip_x, c), (z, flip_y, x, c), (z, y, x, flip_c)
    other_peers = [core_peer] + [(peer[0], peer[1], peer[2], flip_c) for peer in plane_peers]
    used = {"send": 0, "recv": 0}
    departures = []

    def claim(kind):
        used[kind] += 1
        return used[kind] - 1

    def sender(total):
        number = claim("send")
        departures.append((sends.at[number], total))
        return sends.at[number]

    def arrive(semaphore, total):
        pltpu.make_async_copy(total, total, semaphore).wait()

    def start(copies, send_sem, total, recv_sem=None):
        if recv_sem is None:
            recv_sem = recvs.at[claim("recv")]
        for source, target, peer in copies:
            pltpu.make_async_remote_copy(
                src_ref=source, dst_ref=target, send_sem=send_sem, recv_sem=recv_sem,
                device_id=device(*peer), device_id_type=MESH,
            ).start()
        return recv_sem, total

    def finish(arrival):
        arrive(*arrival)

    def load(copies):
        for copy in copies:
            copy.start()
        return copies

    def take(ref, lines, first=0, count=4):
        return jnp.concatenate([ref[first + i, lines, :] for i in range(count)], axis=1)

    def put(ref, lines, value, first=0):
        for i in range(value.shape[1] // 128):
            ref[first + i, lines, :] = value[:, 128 * i : 128 * (i + 1)]

    barrier = pltpu.get_barrier_semaphore()
    peers = z_peers + plane_peers + other_peers
    for peer in peers:
        pl.semaphore_signal(barrier, inc=1, device_id=device(*peer), device_id_type=MESH)
    def fetch(pairs, first):
        return load([pltpu.make_async_copy(source, target, local.at[first + i]) for i, (source, target) in enumerate(pairs)])

    params = fetch([
        (gain_hbm, gain_ref), (shift_hbm, shift_ref), (skip_hbm, skip_ref), (bias_hbm, bias_ref), (w_hbm, w_ref),
        (ldt_hbm, ldt_ref), (lar_hbm, lar_ref), (ai_hbm, ai_ref), (cc_hbm, cc_ref),
    ], 9)
    loads = fetch([
        (x_hbm, x_v), (pick_hbm, pick), (mask_hbm, mask), (fwd_hbm, fwd), (inv_hbm, inv), (g_hbm, g_v),
        (turn_hbm, turn), (most_hbm, fwd_most), (rest_hbm, fwd_rest),
    ], 0)
    three, place = pl.ds(0, 3), (y * 2 + x) * 2 + c

    def same(ref, peers, total, send_sem=None, recv_sem=None):
        return start([(ref, ref, peer) for peer in peers], send_sem or sender(total), total, recv_sem)

    right_sender = sends.at[claim("send")]
    right_copies = [
        pltpu.make_async_remote_copy(
            src_ref=x_hbm.at[at], dst_ref=left_v.at[at], send_sem=right_sender, recv_sem=recvs.at[claim("recv")],
            device_id=(dp, seq + 1), device_id_type=MESH,
        )
        for at in (pl.ds(0, tokens - fourth), pl.ds(tokens - fourth, fourth))
    ]

    def prepare_shares():
        for copy in params:
            copy.wait()
        low = [ref[...].astype(bf16).astype(f32) for ref in (gain_ref, shift_ref, skip_ref, bias_ref)]
        share_in[z, place] = jnp.concatenate(low + [jnp.zeros((1, 128 - 5 * ROWS), f32)], axis=1)
        for q in range(4):
            weight[q, z, y, x, c] = jnp.concatenate(
                [w_ref[:, 128 * q : 128 * q + 128], w_ref[:, channels + 128 * q : channels + 128 * q + 128]], axis=1
            ).astype(bf16)

    def prepare_taps():
        _, _, unit, _, _, _, coef = mode_terms(ldt_ref[...], lar_ref[...], ai_ref[...], cc_ref[...])
        steps, power = [], times(unit, unit)
        for _ in range(8):
            steps.append(power)
            power = times(power, power)
        for p in range(8):
            def row(value):
                return value[0][p : p + 1], value[1][p : p + 1]

            def table(factors):
                sub = lax.broadcasted_iota(jnp.int32, (8, 128), 0)
                tile = None
                for bit, factor in enumerate(factors):
                    on = lax.rem(lax.div(sub, 2**bit), 2) == 1
                    factor = tuple(jnp.where(on, part, rest) for part, rest in zip(row(factor), (1.0, 0.0)))
                    tile = factor if tile is None else times(tile, factor)
                return tile

            base = table(steps[:3])
            for step in steps[3:6]:
                more = times(base, row(step))
                base = tuple(jnp.concatenate([old, new], axis=0) for old, new in zip(base, more))
            leap = table([steps[6], steps[7], unit])
            leaps[p, 0], leaps[p, 1] = leap
            at = slice(256 * p, 256 * p + 256)
            high, low = split_low(jnp.concatenate(base, axis=1))
            base_high[:, at], base_low[:, at] = high, low
            lead = times(row(coef), leap)
            lead = jnp.concatenate([lead[0], -lead[1]], axis=1)
            first = lax.rem(lax.broadcasted_iota(jnp.int32, (8, 256), 1), 128) < 64
            lead = jnp.concatenate([jnp.where(first, lead, 0.0), jnp.where(first, 0.0, lead)], axis=0)
            lead_high, lead_low = split_low(lead)
            taps_of = dot_nt(
                jnp.concatenate([lead_high, lead_low, lead_high], axis=1), jnp.concatenate([high, high, low], axis=1)
            )
            taps_of = jnp.concatenate([taps_of, taps_of], axis=1)
            lines_f[8 * p : 8 * p + 8], lines_f[8 * p + 64 : 8 * p + 72] = taps_of[:8], taps_of[8:]
        own = jnp.concatenate([lines_f[pl.ds(m, ROWS, stride=8), :][:, :64] for m in range(8)], axis=1)
        kern[z, y, x, c] = (2.0 * own).astype(bf16)

    late = z == 3

    @pl.when(jnp.logical_not(late))
    def _():
        prepare_shares()
        prepare_taps()

    pl.semaphore_wait(barrier, len(peers))

    @pl.when(late)
    def _():
        prepare_shares()

    share_plane = same(share_in.at[z, place], plane_peers + other_peers, share_in.at[0, pl.ds(0, 7)])
    weight_x = same(weight.at[:, z, y, x, c], [x_peer], weight.at[:, 0, 0, 0, 0])

    @pl.when(seq < 3)
    def _():
        right_copies[0].start()

    @pl.when(late)
    def _():
        prepare_taps()

    kern_z = same(kern.at[z, y, x, c], z_peers, kern.at[three, 0, 0, 0])
    finish(share_plane)
    share_z = same(share_in.at[z], z_peers, share_in.at[three])
    finish(weight_x)
    z_sender, y_sender = sender(weight.at[three, three, 0, :, 0]), sender(weight.at[three, :, 0, :, 0])
    core_sender = sender(weight.at[:, :, :, :, 0])

    def weight_to_z(q):
        return same(weight.at[q, z, y, :, c], z_peers, weight.at[q, three, 0, :, 0], z_sender)

    def weight_to_y(q):
        finish(weight_z[q])
        piece = weight.at[q, :, y, :, c]
        weight_core.append(same(piece, [core_peer], weight.at[q, :, :, :, 0], core_sender))
        return same(piece, [y_peer], weight.at[q, :, 0, :, 0], y_sender)

    def weight_to_core(q):
        finish(weight_y[q])
        same(weight.at[q, :, flip_y, :, c], [core_peer], weight.at[q, :, :, :, 0], core_sender, weight_core[q][0])

    weight_core = []
    weight_z = [weight_to_z(q) for q in range(3)]
    last_y = same(weight.at[3, z, y, :, c], [y_peer], weight.at[3, 0, 0, :, 0])

    def last_to_z():
        finish(last_y)
        return same(weight.at[3, z, :, :, c], z_peers, weight.at[3, three, :, :, 0])

    def last_to_core():
        finish(last_z)
        weight_core.append(same(weight.at[3, :, :, :, c], [core_peer], weight.at[3, :, :, :, 0], core_sender))

    def normalise(source, hat, keep_std, begin, end):
        for first in range(begin, end, 32):
            at = slice(first, first + 32)
            value = source[at, :].astype(f32)
            centered = value - jnp.mean(value, axis=1, keepdims=True)
            scale = lax.rsqrt(jnp.mean(centered * centered, axis=1, keepdims=True) + EPS)
            put(hat, at, centered * scale)
            if keep_std:
                inv_std[at, :] = jnp.broadcast_to(scale, (32, 128))

    loads[0].wait()
    normalise(x_v, x_hat, True, 0, tokens)
    finish(kern_z)
    halves = [pl.ds(0, 2), pl.ds(2, 2)]
    plane_sender, pair_sender = sender(dk_in2), sender(kern.at[:, :, :, 0])
    kern_plane = [same(kern.at[at, y, x, c], plane_peers, dk_in2.at[:, at], plane_sender) for at in halves]

    @pl.when(seq < 3)
    def _():
        right_copies[1].start()

    finish(share_z)
    last_z = last_to_z()
    loads[1].wait()
    loads[2].wait()
    shares = share_in[...].reshape(32, 1, 128).reshape(32, 128).astype(bf16)
    spread = dot_nn(shares, pick[...]) * mask[...].astype(f32)
    spread = jnp.sum(spread, axis=0, keepdims=True)
    rows_f[...] = jnp.concatenate(
        [spread[:, channels * i : channels * (i + 1)] for i in range(5)] + [jnp.zeros((3, channels), f32)], axis=0
    )
    gain, shift = rows_f[0:1, :], rows_f[1:2, :]

    def every_other(i, parity):
        return pl.ds(128 * i + parity, 64, stride=2)

    def sixty_four(i):
        return pl.ds(pl.multiple_of(64 * i, 64), 64)

    def shifted(i, _):
        at = pl.ds(pl.multiple_of(i * 128, 128), 128)
        put(normed, at, take(x_hat, at) * gain + shift)
        for parity in range(2):
            own_b[parity, sixty_four(i)] = take(normed, every_other(i, parity)).astype(bf16)
        return 0

    lax.fori_loop(0, tokens // 128, shifted, 0)
    loads[3].wait()
    loads[4].wait()

    for copy in loads[6:]:
        copy.wait()
    wide = 256

    def lanes(j):
        return pl.ds(pl.multiple_of(j * wide, wide), wide)

    few = 16

    def sign_of(r):
        return 1 if r < half // 2 else -1

    def turned(value, r, back):
        cosine, sine = (jnp.concatenate([turn[i, r : r + few]] * 2, axis=1) for i in range(2))
        return conj_times((cosine, sine), value) if back else times(value, (cosine, sine))

    def transform(block, exact):
        both = jnp.concatenate([block[0], block[1]], axis=1)
        if exact:
            return dot_nn(fwd[...], jnp.concatenate([both, both], axis=0))
        return dot_nn(fwd[:, :half], both)

    def joined(both, r):
        parts = both[r : r + few], both[half + r : half + r + few]
        even, odd = [part[:, :wide] for part in parts], turned([part[:, wide:] for part in parts], r, False)
        return tuple(a + b for a, b in zip(even, odd)), tuple(a - b for a, b in zip(even, odd))

    def places(r):
        return [pl.ds(first + r, few) for first in (0, taps, half, taps + half)]

    def keep(ref, at, r, pair):
        for lines, part in zip(places(r), pair[0] + pair[1]):
            ref[lines, at] = part

    def kept(ref, at, r):
        parts = [ref[lines, at] for lines in places(r)]
        return parts[:2], parts[2:]

    def signal(pair_at, exact):
        real, imag = [], []
        for r in range(0, half, few):
            a, b = pair_at(r)
            even = [x + y for x, y in zip(a, b)]
            odd = turned([x - y for x, y in zip(a, b)], r, True)
            for lines, x, y in zip((real, imag), even, odd):
                both = jnp.concatenate([x, y], axis=1)
                lines.append(split_low(both) if exact else (both.astype(bf16),))
        lines = real + imag
        if exact:
            high, low = (jnp.concatenate([line[i] for line in lines], axis=0) for i in range(2))
            return dot_nn(inv[...], jnp.concatenate([high, high, low], axis=0))
        return dot_nn(inv[:, : 2 * half], jnp.concatenate([line[0] for line in lines], axis=0))

    def each(function, pairs):
        return tuple(function(*values) for values in zip(*pairs))

    def swung(value, sign):
        return (value[1], -value[0]) if sign > 0 else (-value[1], value[0])

    def own_spectrum(j):
        at = lanes(j)
        both = transform((own_b[0, :, at], own_b[1, :, at]), True)
        for r in range(0, half, few):
            keep(u_spec, at, r, joined(both, r))

    own_spectrum(0)
    own_spectrum(1)
    weight_y = [weight_to_y(0)]

    def left_block(i):
        first, last = (0, 3) if i == 0 else (3, 4)
        right_copies[i].wait_recv()
        normalise(left_v, left_hat, False, 128 * first, 128 * last)
        for k in range(first, last):
            for parity in range(2):
                value = take(left_hat, pl.ds(128 * k + parity, 64, stride=2)) * gain + shift
                left_b[parity, 64 * k : 64 * k + 64] = value.astype(bf16)
        at = slice(64 * first, 64 * last)
        matrix = (fwd_most if i == 0 else fwd_rest)[...]
        for j in range(2):
            lane = slice(wide * j, wide * (j + 1))
            both = jnp.concatenate([left_b[0, at, lane], left_b[1, at, lane]], axis=1)
            both = dot_nn(matrix, jnp.concatenate([both, both], axis=0))
            lines = slice(taps * j, taps * (j + 1))
            if i == 0:
                d_spec[lines, :] = both
                continue
            both += d_spec[lines, :]
            for r in range(0, half, few):
                turns = [swung(value, -sign_of(r)) for value in joined(both, r)]
                old = kept(u_spec, lanes(j), r)
                keep(u_spec, lanes(j), r, tuple(tuple(a + b for a, b in zip(x, y)) for x, y in zip(old, turns)))

    @pl.when(seq > 0)
    def _():
        left_block(0)

    @pl.when(seq == 0)
    def _():
        left_hat[...] = jnp.zeros_like(left_hat)

    def kern_to_core(j):
        finish(kern_plane[j])
        return same(kern.at[halves[j], :, :, c], [core_peer], kern.at[halves[j], :, :, 0], pair_sender)

    weight_y.append(weight_to_y(1))
    kern_core = [kern_to_core(0), kern_to_core(1)]

    def kernel_transform(j):
        rows = kern[2 * j : 2 * j + 2].reshape(wide, taps)
        rows = [jnp.concatenate([rows[:, at]] * 2, axis=1) for at in (slice(0, half), slice(half, taps))]
        return dot_nt(fwd[...], jnp.concatenate(rows, axis=0))

    def convolve(j, both):
        at = lanes(j)

        def product(r):
            k = joined(both, r)
            keep(k_spec, at, r, k)
            return each(times, (k, kept(u_spec, at, r)))

        both = signal(product, True)
        for parity in range(2):
            put(mixed, pl.ds(parity, half, stride=2), both[:, wide * parity : wide * (parity + 1)], 2 * j)

    def activate(j):
        for tile in (2 * j, 2 * j + 1):
            at = slice(128 * tile, 128 * tile + 128)
            for start_at in range(0, tokens, 128):
                lines = slice(start_at, start_at + 128)
                value = mixed[tile, lines, :] + rows_f[2:3, at] * normed[tile, lines, :]
                chance = 0.5 + 0.5 * lax.erf(value * (0.5**0.5))
                slope[lines, at] = chance + value * jnp.exp(value * value * -0.5 - 0.5 * float(np.log(2.0 * np.pi)))
                low = (value * chance).astype(bf16)
                activ[lines, at] = low
                activ_t[at, lines] = low.T

    for j in range(2):
        finish(kern_core[j])
        k_raw[j] = kernel_transform(j)
        if j == 0:
            weight_y.append(weight_to_y(2))

    @pl.when(seq > 0)
    def _():
        left_block(1)

    weight_to_core(0)
    convolve(0, k_raw[0])
    weight_to_core(1)
    last_to_core()
    convolve(1, k_raw[1])
    activate(0)
    activate(1)
    weight_to_core(2)
    loads[5].wait()

    def matrix_of(h):
        return jnp.concatenate([weight[q].reshape(channels, 256) for q in (2 * h, 2 * h + 1)], axis=1)

    def gates(h, pre):
        lines_out = []
        sums = [jnp.zeros((32, 128), f32) for _ in range(4)]
        for start_at in range(0, tokens, 32):
            lines = slice(start_at, start_at + 32)
            low = []
            for i, q in enumerate((2 * h, 2 * h + 1)):
                at = slice(128 * q, 128 * q + 128)
                lin = pre[lines, 256 * i : 256 * i + 128] + rows_f[3:4, at]
                gate = 0.5 + 0.5 * jnp.tanh(0.5 * (pre[lines, 256 * i + 128 : 256 * i + 256] + rows_f[4:5, at]))
                grad = g_v[lines, at].astype(f32)
                product = lin * gate
                res_v[lines, at] = (x_v[lines, at].astype(f32) + product).astype(bf16)
                low += [(grad * gate).astype(bf16), (grad * (product - product * gate)).astype(bf16)]
            sums = [total + part.astype(f32) for total, part in zip(sums, low)]
            lines_out.append(jnp.concatenate(low, axis=1))
        for i, q in enumerate((2 * h, 2 * h + 1)):
            for k in range(2):
                rows_f[3 + k : 4 + k, 128 * q : 128 * q + 128] = jnp.sum(sums[2 * i + k], axis=0, keepdims=True)
        return jnp.concatenate(lines_out, axis=0)

    def weight_grad(h, low):
        grad = dot_nn(activ_t[...], low).astype(bf16)
        for i, q in enumerate((2 * h, 2 * h + 1)):
            dw_own[q] = grad[:, 256 * i : 256 * i + 256].reshape(4, 2, 2, 2, ROWS, 256)
            arrival = start([(dw_own.at[q, :, :, :, flip_c], dw_in1.at[q], core_peer)], dw_senders[0], dw_in1.at[q])
            dw_core.append(arrival)

    def mix_grad(d_act):
        total = jnp.zeros((32, channels), f32)
        for start_at in range(0, tokens, 32):
            lines = slice(start_at, start_at + 32)
            mix = (d_act[lines] * slope[lines, :]).astype(bf16).astype(f32)
            total += mix * take(normed, lines)
            put(mixed, lines, mix)
        rows_f[2:3, :] = jnp.sum(total, axis=0, keepdims=True)
        for parity in range(2):
            for start_at in range(0, half, 64):
                part = take(mixed, pl.ds(2 * start_at + parity, 64, stride=2))
                d_mix[parity, start_at : start_at + 64] = part.astype(bf16)

    def core_sum(q):
        finish(dw_core[q])
        dw_mid[q] = (dw_own[q, :, :, :, c].astype(f32) + dw_in1[q].astype(f32)).astype(bf16)

    def to_y(q):
        core_sum(q)
        return start([(dw_mid.at[q, :, flip_y], dw_in2.at[q], y_peer)], dw_senders[1], dw_in2.at[q])

    def end_to_z():
        core_sum(3)
        copies = [(dw_mid.at[3, peer[0]], end_in1.at[i], peer) for i, peer in enumerate(z_peers)]
        return start(copies, sender(end_in1), end_in1)

    def end_to_plane():
        finish(end_z)
        total = dw_mid[3, z].astype(f32)
        for i in range(3):
            total = total + end_in1[i].astype(f32)
        end_mid[...] = total.astype(bf16)
        copies = [(end_mid.at[peer[1], peer[2]], end_in2.at[i], peer) for i, peer in enumerate(plane_peers)]
        return start(copies, sender(end_in2), end_in2)

    def write_out(q, total):
        dw_ref[:, 128 * q : 128 * q + 128] = total[:, :128]
        dw_ref[:, channels + 128 * q : channels + 128 * q + 128] = total[:, 128:]

    def end_of_last():
        finish(end_plane)
        total = end_mid[y, x].astype(f32)
        for i in range(3):
            total = total + end_in2[i].astype(f32)
        write_out(3, total)

    def to_z(q):
        finish(dw_y[q])
        dw_low[q] = (dw_mid[q, :, y].astype(f32) + dw_in2[q].astype(f32)).astype(bf16)
        copies = [(dw_low.at[q, peer[0]], dw_in3.at[q, i], peer) for i, peer in enumerate(z_peers)]
        return start(copies, dw_senders[2], dw_in3.at[q])

    def to_x(q):
        finish(dw_z[q])
        total = dw_low[q, z].astype(f32)
        for i in range(3):
            total = total + dw_in3[q, i].astype(f32)
        dw_end[q] = total.astype(bf16)
        return start([(dw_end.at[q, flip_x], dw_in4.at[q], x_peer)], dw_senders[3], dw_in4.at[q])

    def to_end(q):
        finish(dw_x[q])
        write_out(q, dw_end[q, x].astype(f32) + dw_in4[q].astype(f32))

    skip = rows_f[2:3, :]
    dw_core, dw_y, dw_z, dw_x = [], [], [], []
    dw_senders = [sender(ref) for ref in (dw_in1, dw_in2.at[three], dw_in3.at[three], dw_in4.at[three])]
    finish(weight_core[0])
    finish(weight_core[1])
    first_low = gates(0, dot_nn(activ[...], matrix_of(0)))
    weight_grad(0, first_low)
    finish(weight_core[2])
    finish(weight_core[3])
    second_low = gates(1, dot_nn(activ[...], matrix_of(1)))
    weight_grad(1, second_low)
    dw_y.append(to_y(0))
    dw_y.append(to_y(1))
    d_act = dot_nt(
        jnp.concatenate([first_low, second_low], axis=1), jnp.concatenate([matrix_of(0), matrix_of(1)], axis=1)
    )
    mix_grad(d_act)
    left_sender = sends.at[claim("send")]
    left_copies = [
        pltpu.make_async_remote_copy(
            src_ref=d_mix.at[:, :, pl.ds(wide * j, wide)], dst_ref=right_v.at[j], send_sem=left_sender,
            recv_sem=recvs.at[claim("recv")], device_id=(dp, seq - 1), device_id_type=MESH,
        )
        for j in range(2)
    ]
    dk_senders = [sender(ref) for ref in (dk_in1, dk_in2, dk_in3)]

    @pl.when(seq > 0)
    def _():
        left_copies[0].start()


    def mix_transform(j):
        at = lanes(j)
        return transform((d_mix[0, :, at], d_mix[1, :, at]), False)

    def kernel_grad(j, both):
        at = lanes(j)

        def product(r):
            d = joined(both, r)
            keep(d_spec, at, r, d)
            return each(conj_times, (kept(u_spec, at, r), d))

        both = signal(product, False)
        grad = jnp.concatenate([both[:, :wide].T, both[:, wide:].T], axis=1).reshape(2, 2, 2, 2, ROWS, taps)
        dk_own[2 * j : 2 * j + 2] = grad
        dk_low[2 * j : 2 * j + 2] = grad.astype(bf16)

    def kernel_middle(j):
        finish(dk_core[j])
        for i in (2 * j, 2 * j + 1):
            total = dk_own[i, :, :, c] + dk_in1[i].astype(f32)
            dk_mid[i] = total
            dk_cut[i] = total.astype(bf16)
        part = halves[j]
        copies = [(dk_cut.at[part, peer[1], peer[2]], dk_in2.at[i, part], peer) for i, peer in enumerate(plane_peers)]
        return start(copies, dk_senders[1], dk_in2.at[:, part])

    def kernel_end(j):
        finish(dk_plane[j])
        for i in (2 * j, 2 * j + 1):
            total = dk_mid[i, y, x]
            for k in range(3):
                total = total + dk_in2[k, i].astype(f32)
            dk_end[i] = total
            dk_out[i] = total.astype(bf16)

    def own_grad(j):
        at = lanes(j)

        def product(r):
            return each(conj_times, (kept(k_spec, at, r), kept(d_spec, at, r)))

        def shifted_product(r):
            return tuple(swung(value, sign_of(r)) for value in product(r))

        own, back = signal(product, False), signal(shifted_product, False)
        d_gain, d_shift = jnp.zeros((1, wide), f32), jnp.zeros((1, wide), f32)
        for parity in range(2):
            lines = pl.ds(parity, half, stride=2)
            columns = slice(wide * parity, wide * (parity + 1))
            grad = own[:, columns] + rows_f[5:6, at] * d_mix[parity, :, at].astype(f32)
            put(d_norm, lines, grad, 2 * j)
            before = jnp.where(seq > 0, back[:, columns], 0.0)
            d_gain += jnp.sum(
                grad * take(x_hat, lines, 2 * j, 2) + before * take(left_hat, lines, 2 * j, 2), axis=0, keepdims=True
            )
            d_shift += jnp.sum(grad + before, axis=0, keepdims=True)
        rows_f[6:7, at], rows_f[7:8, at] = d_gain, d_shift

    def right_grad(j):
        at = lanes(j)
        both = transform((right_v[j, 0], right_v[j, 1]), False)

        def product(r):
            turns = [swung(value, sign_of(r)) for value in joined(both, r)]
            return each(conj_times, (kept(k_spec, at, r), turns))

        both = signal(product, False)
        for parity in range(2):
            lines = pl.ds(parity, half, stride=2)
            more = both[:, wide * parity : wide * (parity + 1)]
            put(d_norm, lines, take(d_norm, lines, 2 * j, 2) + more, 2 * j)

    rows_f[5:6, :] = skip
    first_half, second_half = mix_transform(0), mix_transform(1)
    kernel_grad(0, first_half)
    kernel_grad(1, second_half)
    dk_core = [
        start([(dk_low.at[part, :, :, flip_c], dk_in1.at[part], core_peer)], dk_senders[0], dk_in1.at[part])
        for part in halves
    ]
    dw_y.append(to_y(2))
    end_z = end_to_z()
    own_grad(0)
    own_grad(1)
    dk_plane = [kernel_middle(0), kernel_middle(1)]

    @pl.when(seq > 0)
    def _():
        left_copies[1].start()

    dw_z.append(to_z(0))
    dw_z.append(to_z(1))
    vector = jnp.concatenate([rows_f[6:7, :], rows_f[7:8, :], rows_f[2:3, :], rows_f[3:4, :], rows_f[4:5, :]], axis=1)
    high, low = split_low(jnp.broadcast_to(vector, mask.shape) * mask[...].astype(f32))
    shares = dot_nt(high, pick[...]) + dot_nt(low, pick[...])
    share_out[...] = shares.reshape(32, 1, 128).reshape(4, 8, 1, 128)
    copies = [(share_out.at[peer[0]], share_in1.at[i], peer) for i, peer in enumerate(z_peers)]
    share_z = start(copies, sender(share_in1), share_in1)
    @pl.when(seq < 3)
    def _():
        left_copies[0].wait_recv()
        right_grad(0)

    dw_z.append(to_z(2))
    end_plane = end_to_plane()
    kernel_end(0)
    kernel_end(1)
    dk_z = start([(dk_out.at[peer[0]], dk_in3.at[i], peer) for i, peer in enumerate(z_peers)], dk_senders[2], dk_in3)
    dw_x.append(to_x(0))
    dw_x.append(to_x(1))
    finish(share_z)
    share_mid[...] = share_out[z] + share_in1[0] + share_in1[1] + share_in1[2]
    copies = [
        (share_mid.at[(peer[1] * 2 + peer[2]) * 2 + peer[3]], share_in2.at[i], peer)
        for i, peer in enumerate(plane_peers + other_peers)
    ]
    share_plane = start(copies, sender(share_in2), share_in2)

    @pl.when(seq < 3)
    def _():
        left_copies[1].wait_recv()
        right_grad(1)

    dw_x.append(to_x(2))

    @pl.when(seq < 3)
    def _():
        arrive(right_sender, x_v)

    @pl.when(seq > 0)
    def _():
        arrive(left_sender, d_mix)

    for first in range(0, tokens, 32):
        at = slice(first, first + 32)
        hat = [x_hat[i, at, :] for i in range(4)]
        grad = [d_norm[i, at, :] * rows_f[0:1, 128 * i : 128 * i + 128] for i in range(4)]
        mean = jnp.sum(sum(grad[1:], grad[0]), axis=1, keepdims=True) * (1.0 / channels)
        along = [one * other for one, other in zip(grad, hat)]
        along = jnp.sum(sum(along[1:], along[0]), axis=1, keepdims=True) * (1.0 / channels)
        for i in range(4):
            lane = slice(128 * i, 128 * i + 128)
            inner = inv_std[at, :] * (grad[i] - mean - hat[i] * along)
            gin_v[at, lane] = (inner + g_v[at, lane].astype(f32)).astype(bf16)
    dt, a, unit, norm_sq, ratio, coef, scaled = mode_terms(ldt_ref[...], lar_ref[...], ai_ref[...], cc_ref[...])
    inverse_a = (a[0] / norm_sq, -a[1] / norm_sq)
    finish(dk_z)
    d_kernel = dk_end[z]
    for k in range(3):
        d_kernel = d_kernel + dk_in3[k].astype(f32)

    for m in range(8):
        block = d_kernel[:, 64 * m : 64 * m + 64]
        lines_f[pl.ds(m, ROWS, stride=8), :] = jnp.concatenate([block, block], axis=1)
    plain = lines_f[...][:, :64]
    ramp = plain * (2 * lax.broadcasted_iota(jnp.int32, (8 * ROWS, 64), 1)).astype(f32)
    high, low = split_low(jnp.concatenate([plain, ramp], axis=0))
    table = jnp.concatenate([base_high[...], base_low[...], base_high[...]], axis=0)
    sums = dot_nn(jnp.concatenate([high, high, low], axis=1), table)
    at_row = lax.broadcasted_iota(jnp.int32, (8, 128), 0)
    first = lax.broadcasted_iota(jnp.int32, (8, 128), 1) < 64
    leap_of = (128 * lax.rem(at_row, 4) + lax.div(at_row, 4)).astype(f32)
    zero = jnp.zeros((8, 128), f32)
    s0, s1 = [zero, zero], [zero, zero]
    for p in range(8):
        def pair(start, part):
            block = sums[start : start + 128, 256 * p + 128 * part : 256 * p + 128 * part + 128]
            return jnp.where(first, block[8 * p : 8 * p + 8], block[8 * p + 64 : 8 * p + 72])

        value, slope_of = [pair(0, part) for part in range(2)], [pair(128, part) for part in range(2)]
        leap = (leaps[p, 0], leaps[p, 1])
        slope_of = [one + leap_of * other for one, other in zip(slope_of, value)]
        for total, terms in ((s0, value), (s1, slope_of)):
            for part, product in enumerate(times(leap, terms)):
                total[part] = jnp.where(at_row == p, jnp.sum(product, axis=0, keepdims=True), total[part])
    d_coef = times(s0, ratio)
    half_g = times(times(coef, s0), times(unit, inverse_a))
    ramp_part = times(scaled, s1)
    half_g = (half_g[0] + ramp_part[0], half_g[1] + ramp_part[1])
    back = times(times(scaled, s0), inverse_a)
    q = (half_g[0] * dt - back[0], half_g[1] * dt - back[1])
    d_dt = 2.0 * dt * times(half_g, a)[0]
    dldt_ref[...] = row_of(jnp.sum(unpair_lanes(d_dt), axis=1, keepdims=True))[0]
    dlar_ref[...] = unpair_lanes(2.0 * q[0] * a[0])
    dai_ref[...] = unpair_lanes(-2.0 * q[1])
    dcc_ref[...] = jnp.concatenate([unpair_lanes(2.0 * d_coef[0]), unpair_lanes(-2.0 * d_coef[1])], axis=1)

    end_of_last()
    for q in range(3):
        to_end(q)
    finish(share_plane)
    small = share_mid[place]
    for i in range(7):
        small = small + share_in2[i]
    for i, target in enumerate([dgain_ref, dshift_ref, dskip_ref]):
        target[...] = small[0, ROWS * i : ROWS * (i + 1)]
    dbias_ref[...] = small[0, 3 * ROWS : 5 * ROWS]
    for departure in departures:
        arrive(*departure)


def finish_kernel(*refs):
    count = len(refs) // 2
    sems = refs[-1]
    copies = [pltpu.make_async_copy(refs[i], refs[count + i], sems.at[i]) for i in range(count)]
    for copy in copies:
        copy.start()
    for copy in copies:
        copy.wait()


def kernel_body(
    inputs, grad_out, ln_gain, ln_bias, skip_scale, w_glu, b_glu, log_dt, log_a_real, a_imag, c_coef
):
    _, tokens, channels = inputs.shape
    taps = KTAPS
    glu = w_glu.shape[1]
    f32, bf16 = jnp.float32, jnp.bfloat16
    order = np.concatenate([np.arange(0, taps // 2, 2), np.arange(1, taps // 2, 2)]) + 0.5
    angle = np.outer(order, np.arange(taps // 2)) * (2 * np.pi / taps)
    matrix = np.concatenate([np.cos(angle), -np.sin(angle)], axis=0)
    high = matrix.astype(bf16)
    low = (matrix - high.astype(np.float64)).astype(bf16)
    forward = np.concatenate([high, low], axis=1)
    cut = 3 * taps // 8
    most, rest = (np.concatenate([part[:, at] for part in (high, low)], axis=1) for at in (slice(0, cut), slice(cut, None)))
    scale = np.asarray(1.0 / taps, bf16)
    inverse = np.concatenate([high.T, low.T, high.T], axis=1) * scale
    turns = np.stack([np.cos(order * (np.pi / taps)), -np.sin(order * (np.pi / taps))])
    turns = np.ascontiguousarray(np.broadcast_to(turns[:, :, None], (2, taps // 2, 128))).astype(np.float32)
    device_at, lane = np.arange(32)[:, None], np.arange(channels)[None, :]
    bias_lane = np.arange(2 * channels)[None, :]
    row = np.arange(128)[:, None]
    pick = np.concatenate(
        [row == i * ROWS + lane % ROWS for i in range(3)] + [row == 3 * ROWS + bias_lane % (2 * ROWS)], axis=1
    ).astype(bf16)
    mask = np.concatenate(
        [device_at == lane // ROWS] * 3 + [device_at == bias_lane // (2 * ROWS)], axis=1
    ).astype(bf16)
    hbm, vmem = pl.BlockSpec(memory_space=pl.ANY), pl.BlockSpec(memory_space=pltpu.VMEM)
    block = (tokens, channels)
    spec, tall = (2 * taps, channels), (channels // 128, tokens, 128)

    def space(*dims, kind=f32):
        return pltpu.VMEM(dims, kind)

    results = (
        (block, bf16), (block, bf16), ((ROWS,), f32), ((ROWS,), f32), ((ROWS,), f32), (w_glu.shape, f32),
        ((2 * ROWS,), f32), ((ROWS,), f32), (log_a_real.shape, f32), (a_imag.shape, f32), (c_coef.shape, f32),
    )
    outs = pl.pallas_call(
        layer_kernel,
        name="layer",
        out_shape=tuple(pltpu.VMEM(dims, kind) for dims, kind in results),
        in_specs=[hbm] * 18,
        out_specs=(vmem,) * len(results),
        scratch_shapes=[
            space(*w_glu.shape), space(1, ROWS), space(1, ROWS), space(1, ROWS), space(1, 2 * ROWS), space(1, ROWS),
            space(*log_a_real.shape), space(*a_imag.shape), space(*c_coef.shape),
            space(*block, kind=bf16), space(*block, kind=bf16), space(*block, kind=bf16),
            space(*forward.shape, kind=bf16), space(*most.shape, kind=bf16), space(*rest.shape, kind=bf16),
            space(*inverse.shape, kind=bf16),
            space(*pick.shape, kind=bf16), space(*mask.shape, kind=bf16), space(*turns.shape),
            space(4, 2, 2, 2, ROWS, taps, kind=bf16), space(4, 4, 2, 2, 2, ROWS, 256, kind=bf16),
            space(64, 2048, kind=bf16), space(64, 2048, kind=bf16), space(8, 2, 8, 128), space(8 * ROWS, 128),
            space(4, 8, 1, 128), space(4, 8, 1, 128), space(3, 8, 1, 128), space(8, 1, 128), space(7, 1, 128),
            space(8, channels),
            space(*tall), space(tokens, 128), space(*tall), space(*tall),
            space(2, tokens // 2, channels, kind=bf16), space(2, tokens // 2, channels, kind=bf16),
            space(2, taps, taps), space(*spec), space(*spec), space(*tall), space(*block),
            space(*block, kind=bf16), space(channels, tokens, kind=bf16),
            space(2, tokens // 2, channels, kind=bf16), space(2, 2, tokens // 2, 256, kind=bf16),
            space(*spec), space(*tall),
            space(4, 4, 2, 2, 2, ROWS, 256, kind=bf16), space(4, 4, 2, 2, ROWS, 256, kind=bf16),
            space(4, 4, 2, 2, ROWS, 256, kind=bf16), space(4, 4, 2, ROWS, 256, kind=bf16),
            space(4, 4, 2, ROWS, 256, kind=bf16), space(4, 3, 2, ROWS, 256, kind=bf16),
            space(4, 2, ROWS, 256, kind=bf16), space(4, ROWS, 256, kind=bf16),
            space(3, 2, 2, ROWS, 256, kind=bf16), space(2, 2, ROWS, 256, kind=bf16), space(3, ROWS, 256, kind=bf16),
            space(4, 2, 2, 2, ROWS, taps), space(4, 2, 2, 2, ROWS, taps, kind=bf16), space(4, 2, 2, ROWS, taps, kind=bf16),
            space(4, 2, 2, ROWS, taps), space(4, 2, 2, ROWS, taps, kind=bf16), space(3, 4, ROWS, taps, kind=bf16),
            space(4, ROWS, taps), space(4, ROWS, taps, kind=bf16), space(3, ROWS, taps, kind=bf16),
            pltpu.SemaphoreType.DMA((18,)), pltpu.SemaphoreType.DMA((24,)), pltpu.SemaphoreType.DMA((46,)),
        ],
        compiler_params=pltpu.CompilerParams(
            collective_id=0, has_side_effects=True, vmem_limit_bytes=48 * 2**20
        ),
    )(*[
        pltpu.with_memory_space_constraint(value, pltpu.HBM)
        for value in (
            inputs.reshape(block), grad_out.reshape(block), forward, most, rest, inverse, pick, mask, turns, w_glu,
            ln_gain.reshape(1, -1), ln_bias.reshape(1, -1), skip_scale.reshape(1, -1), b_glu.reshape(1, -1),
            log_dt.reshape(1, -1), log_a_real, a_imag, c_coef,
        )
    ])
    ended = pl.pallas_call(
        finish_kernel,
        name="finish",
        out_shape=tuple(jax.ShapeDtypeStruct(dims, kind) for dims, kind in results),
        in_specs=[vmem] * len(results),
        out_specs=(hbm,) * len(results),
        scratch_shapes=[pltpu.SemaphoreType.DMA((len(results),))],
    )(*[pltpu.with_memory_space_constraint(value, pltpu.VMEM) for value in outs])
    return (ended[0].reshape(inputs.shape), ended[1].reshape(inputs.shape)) + tuple(ended[2:])


def solution(mesh):
    in_specs = (
        P("dp", "seq", None),
        P("dp", "seq", None),
        P(("dp", "seq")),
        P(("dp", "seq")),
        P(("dp", "seq")),
        P(("dp", "seq"), None),
        P(("dp", "seq")),
        P(("dp", "seq")),
        P(("dp", "seq"), None),
        P(("dp", "seq"), None),
        P(("dp", "seq"), None),
    )
    out_specs = (
        P("dp", "seq", None),
        P("dp", "seq", None),
        P(("dp", "seq")),
        P(("dp", "seq")),
        P(("dp", "seq")),
        P(("dp", "seq"), None),
        P(("dp", "seq")),
        P(("dp", "seq")),
        P(("dp", "seq"), None),
        P(("dp", "seq"), None),
        P(("dp", "seq"), None),
    )
    quick = mesh.shape["dp"] == 8 and mesh.shape["seq"] == 4
    return jax.shard_map(kernel_body if quick else body, mesh=mesh, in_specs=in_specs, out_specs=out_specs, check_vma=False)
```

```python
import math
from functools import partial

import jax
import jax.numpy as jnp
import numpy as np
from jax import lax
from jax.experimental import pallas as pl
from jax.experimental.pallas import tpu as pltpu
from jax.sharding import PartitionSpec as P

KTAPS = 512


EPS = 1e-05


def passed_along(value, axis, steps):
    count = lax.axis_size(axis)
    first, last = (max(0, -steps), min(count, count - steps))
    return lax.ppermute(value, axis, [(source, source + steps) for source in range(first, last)])


def kernel_block(log_dt, log_a_real, a_imag, c_coef, start, count):
    mode_count = log_a_real.shape[1]
    step_size = jnp.exp(log_dt)[:, None]
    a_real = -jnp.exp(log_a_real)
    decay = a_real * step_size
    turn = a_imag * step_size
    growth = jnp.exp(decay)
    ex_re = growth * jnp.cos(turn) - 1.0
    ex_im = growth * jnp.sin(turn)
    norm_sq = a_real * a_real + a_imag * a_imag
    ratio_re = (ex_re * a_real + ex_im * a_imag) / norm_sq
    ratio_im = (ex_im * a_real - ex_re * a_imag) / norm_sq
    c_re = c_coef[:, :mode_count]
    c_im = c_coef[:, mode_count:]
    coef_re = c_re * ratio_re - c_im * ratio_im
    coef_im = c_re * ratio_im + c_im * ratio_re
    places = (start + jnp.arange(count)).astype(jnp.float32)
    phase = turn[:, :, None] * places
    damping = jnp.exp(decay[:, :, None] * places)
    terms = damping * (coef_re[:, :, None] * jnp.cos(phase) - coef_im[:, :, None] * jnp.sin(phase))
    return 2.0 * jnp.sum(terms, axis=1)


def transforms(taps):
    angle = np.outer(np.arange(taps) + 0.5, np.arange(taps)) * (np.pi / taps)
    forward = np.concatenate([np.cos(angle), -np.sin(angle)], axis=0)
    inverse = forward.T / taps
    return forward.astype(jnp.bfloat16), inverse.astype(jnp.bfloat16)


def body(
    inputs, grad_out, ln_gain, ln_bias, skip_scale, w_glu, b_glu, log_dt, log_a_real, a_imag, c_coef
):
    seq_count, own_len, channels = inputs.shape
    gain_low = ln_gain.astype(jnp.bfloat16)
    shift_low = ln_bias.astype(jnp.bfloat16)
    skip_low = skip_scale.astype(jnp.bfloat16)
    weight_low = w_glu.astype(jnp.bfloat16)
    bias_low = b_glu.astype(jnp.bfloat16)
    mode_own = (log_dt, log_a_real, a_imag, c_coef)
    own_kernel = kernel_block(*mode_own, 0, KTAPS).astype(jnp.bfloat16)
    gathered = (
        lax.all_gather(gain_low, ("dp", "seq"), axis=0, tiled=True),
        lax.all_gather(shift_low, ("dp", "seq"), axis=0, tiled=True),
        lax.all_gather(skip_low, ("dp", "seq"), axis=0, tiled=True),
        lax.all_gather(weight_low, ("dp", "seq"), axis=0, tiled=True),
        lax.all_gather(bias_low, ("dp", "seq"), axis=0, tiled=True),
        lax.all_gather(own_kernel, ("dp", "seq"), axis=0, tiled=True),
    )
    kernel_b = gathered[5]
    taps = own_len
    forward, inverse = transforms(taps)
    sign = jnp.where(jnp.arange(taps) % 2 == 0, 1.0, -1.0).astype(jnp.float32)[:, None]

    def to_spectrum(block):
        both = jnp.dot(forward, block, preferred_element_type=jnp.float32)
        return both[:taps], both[taps:]

    def from_spectrum(real, imag):
        both = jnp.concatenate([real, imag], axis=0).astype(jnp.bfloat16)
        return jnp.dot(inverse, both, preferred_element_type=jnp.float32)

    kernel_re, kernel_im = to_spectrum(kernel_b.T)
    gain_full = gathered[0].astype(jnp.float32)
    shift_full = gathered[1].astype(jnp.float32)
    skip_full = gathered[2].astype(jnp.float32)
    weight_b = gathered[3]
    glu_bias = gathered[4].astype(jnp.float32)
    x_float = inputs.astype(jnp.float32)
    row_mean = jnp.mean(x_float, axis=-1, keepdims=True)
    centered = x_float - row_mean
    row_var = jnp.mean(centered * centered, axis=-1, keepdims=True)
    inv_std = lax.rsqrt(row_var + EPS)
    x_hat = centered * inv_std
    normed = x_hat * gain_full + shift_full
    normed_b = normed.astype(jnp.bfloat16)
    own_re, own_im = to_spectrum(normed_b[0])
    left_re, left_im = to_spectrum(passed_along(normed_b, "seq", 1)[0])
    source_re = own_re - sign * left_im
    source_im = own_im + sign * left_re
    conv = from_spectrum(
        kernel_re * source_re - kernel_im * source_im,
        kernel_re * source_im + kernel_im * source_re,
    )
    mixed_pre = conv[None] + skip_full * normed
    activ, gelu_pull = jax.vjp(partial(jax.nn.gelu, approximate=False), mixed_pre)
    activ_b = activ.astype(jnp.bfloat16)
    glu_pre = (
        jnp.einsum("slh,hg->slg", activ_b, weight_b, preferred_element_type=jnp.float32) + glu_bias
    )
    half_dim = glu_pre.shape[-1] // 2
    lin_part = glu_pre[..., :half_dim]
    gate_sig = jax.nn.sigmoid(glu_pre[..., half_dim:])
    result = (x_float + lin_part * gate_sig).astype(jnp.bfloat16)
    grad_f = grad_out.astype(jnp.float32)
    d_pre = jnp.concatenate(
        [grad_f * gate_sig, grad_f * lin_part * gate_sig * (1.0 - gate_sig)], axis=-1
    ).astype(jnp.bfloat16)
    d_weight = jnp.einsum("slh,slg->hg", activ_b, d_pre, preferred_element_type=jnp.float32)
    d_glu_bias = jnp.sum(d_pre.astype(jnp.float32), axis=(0, 1))
    d_act = jnp.einsum("slg,hg->slh", d_pre, weight_b, preferred_element_type=jnp.float32)
    d_mix = gelu_pull(d_act)[0].astype(jnp.bfloat16)
    d_mix_f = d_mix.astype(jnp.float32)
    d_skip = jnp.sum(d_mix_f * normed, axis=(0, 1))
    mix_re, mix_im = to_spectrum(d_mix[0])
    d_kernel = from_spectrum(
        source_re * mix_re + source_im * mix_im, source_re * mix_im - source_im * mix_re
    ).T
    right_re, right_im = to_spectrum(passed_along(d_mix, "seq", -1)[0])
    sum_re = mix_re + sign * right_im
    sum_im = mix_im - sign * right_re
    d_conv = from_spectrum(
        kernel_re * sum_re + kernel_im * sum_im, kernel_re * sum_im - kernel_im * sum_re
    )[None]
    d_normed = d_conv + skip_full * d_mix_f
    d_gain = jnp.sum(d_normed * x_hat, axis=(0, 1))
    d_shift = jnp.sum(d_normed, axis=(0, 1))
    scaled = d_normed * gain_full
    d_input = (
        inv_std
        * (
            scaled
            - jnp.mean(scaled, axis=-1, keepdims=True)
            - x_hat * jnp.mean(scaled * x_hat, axis=-1, keepdims=True)
        )
        + grad_f
    )
    grad_in = d_input.astype(jnp.bfloat16)
    summed = (
        lax.psum_scatter(d_gain, ("dp", "seq"), scatter_dimension=0, tiled=True),
        lax.psum_scatter(d_shift, ("dp", "seq"), scatter_dimension=0, tiled=True),
        lax.psum_scatter(d_skip, ("dp", "seq"), scatter_dimension=0, tiled=True),
        lax.psum_scatter(d_weight, ("dp", "seq"), scatter_dimension=0, tiled=True),
        lax.psum_scatter(d_glu_bias, ("dp", "seq"), scatter_dimension=0, tiled=True),
        lax.psum_scatter(d_kernel, ("dp", "seq"), scatter_dimension=0, tiled=True),
    )
    _, own_pull = jax.vjp(partial(kernel_block, start=0, count=KTAPS), *mode_own)
    mode_grads = own_pull(summed[5])
    return (
        result,
        grad_in,
        summed[0],
        summed[1],
        summed[2],
        summed[3],
        summed[4],
        mode_grads[0],
        mode_grads[1],
        mode_grads[2],
        mode_grads[3],
    )


MESH = pl.DeviceIdType.MESH
ROWS = 16


def pair_lanes(value):
    return jnp.concatenate([value[:8], value[8:]], axis=1)


def unpair_lanes(value):
    half = value.shape[1] // 2
    return jnp.concatenate([value[:, :half], value[:, half:]], axis=0)


def column_of(row):
    n = row.shape[1]
    at = lax.broadcasted_iota(jnp.int32, (n, n), 0) == lax.broadcasted_iota(jnp.int32, (n, n), 1)
    return jnp.sum(jnp.where(at, jnp.broadcast_to(row, (n, n)), 0.0), axis=1, keepdims=True)


def row_of(column):
    n = column.shape[0]
    at = lax.broadcasted_iota(jnp.int32, (n, n), 0) == lax.broadcasted_iota(jnp.int32, (n, n), 1)
    return jnp.sum(jnp.where(at, jnp.broadcast_to(column, (n, n)), 0.0), axis=0, keepdims=True)


def mode_terms(ldt, lar, ai, cc):
    n_modes = lar.shape[1]
    dt = column_of(jnp.exp(ldt))
    dt = jnp.concatenate(
        [jnp.broadcast_to(dt[:8], (8, n_modes)), jnp.broadcast_to(dt[8:], (8, n_modes))], axis=1
    )
    a_re, a_im = -jnp.exp(pair_lanes(lar)), pair_lanes(ai)
    decay, turn = a_re * dt, a_im * dt
    growth = jnp.exp(decay)
    z_re, z_im = growth * jnp.cos(turn), growth * jnp.sin(turn)
    ex_re, ex_im = z_re - 1.0, z_im
    norm_sq = a_re * a_re + a_im * a_im
    r_re = (ex_re * a_re + ex_im * a_im) / norm_sq
    r_im = (ex_im * a_re - ex_re * a_im) / norm_sq
    c_re, c_im = pair_lanes(cc[:, :n_modes]), pair_lanes(cc[:, n_modes:])
    w_re, w_im = c_re * r_re - c_im * r_im, c_re * r_im + c_im * r_re
    return dt, (a_re, a_im), (z_re, z_im), norm_sq, (r_re, r_im), (c_re, c_im), (w_re, w_im)


def times(a, b):
    return a[0] * b[0] - a[1] * b[1], a[0] * b[1] + a[1] * b[0]


def conj_times(a, b):
    return a[0] * b[0] + a[1] * b[1], a[0] * b[1] - a[1] * b[0]


def split_low(value):
    high = value.astype(jnp.bfloat16)
    return high, (value - high.astype(jnp.float32)).astype(jnp.bfloat16)


def dot_nn(a, b):
    return lax.dot_general(a, b, (((1,), (0,)), ((), ())), preferred_element_type=jnp.float32)


def dot_nt(a, b):
    return lax.dot_general(a, b, (((1,), (1,)), ((), ())), preferred_element_type=jnp.float32)


def layer_kernel(
    x_hbm, g_hbm, fwd_hbm, most_hbm, rest_hbm, inv_hbm, pick_hbm, mask_hbm, turn_hbm,
    w_hbm, gain_hbm, shift_hbm, skip_hbm, bias_hbm, ldt_hbm, lar_hbm, ai_hbm, cc_hbm,
    res_v, gin_v, dgain_ref, dshift_ref, dskip_ref, dw_ref, dbias_ref, dldt_ref, dlar_ref, dai_ref, dcc_ref,
    w_ref, gain_ref, shift_ref, skip_ref, bias_ref, ldt_ref, lar_ref, ai_ref, cc_ref,
    x_v, g_v, left_v, fwd, fwd_most, fwd_rest, inv, pick, mask, turn, kern, weight, base_high, base_low, leaps, lines_f,
    share_in, share_out, share_in1, share_mid, share_in2, vector_rows, rows_f, x_hat, inv_std, left_hat, normed, own_b, left_b,
    k_raw, k_spec, u_spec, mixed, slope, activ, activ_t, d_mix, right_v, d_spec, d_norm,
    dw_own, dw_in1, dw_mid, dw_in2, dw_low, dw_in3, dw_end, dw_in4, end_in1, end_mid, end_in2,
    dk_own, dk_low, dk_in1, dk_mid, dk_cut, dk_in2, dk_end, dk_out, dk_in3,
    local, sends, recvs,
):
    f32, bf16 = jnp.float32, jnp.bfloat16
    tokens, channels = x_v.shape
    taps = KTAPS
    half, fourth = taps // 2, taps // 4
    dp, seq = lax.axis_index("dp"), lax.axis_index("seq")
    index = dp * 4 + seq
    z, y, x, c = lax.div(dp, 2), lax.rem(dp, 2), lax.div(seq, 2), lax.rem(seq, 2)
    flip_y, flip_x, flip_c = 1 - y, 1 - x, 1 - c

    def device(z, y, x, c):
        return (z * 2 + y, x * 2 + c)

    z_peers = [(lax.rem(z + k, 4), y, x, c) for k in (1, 2, 3)]
    plane_peers = [
        (z, lax.rem(y + k // 2, 2), lax.rem(x + k % 2, 2), c) for k in (1, 2, 3)
    ]
    x_peer, y_peer, core_peer = (z, y, flip_x, c), (z, flip_y, x, c), (z, y, x, flip_c)
    other_peers = [core_peer] + [(peer[0], peer[1], peer[2], flip_c) for peer in plane_peers]
    groups = ("gather", "reduce", "vector")
    sent = dict.fromkeys(groups, 0)
    phase, used = ["gather"], [0]

    def claim():
        used[0] += 1
        return recvs.at[used[0] - 1]

    def size_of(ref):
        return math.prod(ref.shape) * jnp.dtype(ref.dtype).itemsize

    def arrive(semaphore, total):
        pltpu.make_async_copy(total, total, semaphore).wait()

    def start(copies, total, recv_sem=None):
        if recv_sem is None:
            recv_sem = claim()
        group = "vector" if copies[0][0].shape[-2:] == (1, 128) else phase[0]
        for source, target, peer in copies:
            sent[group] += size_of(source)
            pltpu.make_async_remote_copy(
                src_ref=source, dst_ref=target, send_sem=sends.at[groups.index(group)], recv_sem=recv_sem,
                device_id=device(*peer), device_id_type=MESH,
            ).start()
        return recv_sem, total

    def finish(arrival):
        arrive(*arrival)

    def load(copies):
        for copy in copies:
            copy.start()
        return copies

    def take(ref, lines, first=0, count=4):
        return jnp.concatenate([ref[first + i, lines, :] for i in range(count)], axis=1)

    def put(ref, lines, value, first=0):
        for i in range(value.shape[1] // 128):
            ref[first + i, lines, :] = value[:, 128 * i : 128 * (i + 1)]

    barrier = pltpu.get_barrier_semaphore()
    peers = z_peers + plane_peers + other_peers
    for peer in peers:
        pl.semaphore_signal(barrier, inc=1, device_id=device(*peer), device_id_type=MESH)
    def fetch(pairs, numbers):
        return load([pltpu.make_async_copy(source, target, local.at[i]) for i, (source, target) in zip(numbers, pairs)])

    params = fetch([
        (gain_hbm, gain_ref), (shift_hbm, shift_ref), (skip_hbm, skip_ref), (bias_hbm, bias_ref), (w_hbm, w_ref),
        (ldt_hbm, ldt_ref), (lar_hbm, lar_ref), (ai_hbm, ai_ref), (cc_hbm, cc_ref),
    ], range(9))
    loads = fetch([
        (x_hbm, x_v), (pick_hbm, pick), (mask_hbm, mask), (fwd_hbm, fwd), (most_hbm, fwd_most), (rest_hbm, fwd_rest),
        (inv_hbm, inv), (turn_hbm, turn), (g_hbm, g_v),
    ], (9, 10, 10, 11, 11, 11, 11, 11, 12))
    three, place = pl.ds(0, 3), (y * 2 + x) * 2 + c

    def same(ref, peers, total, recv_sem=None):
        return start([(ref, ref, peer) for peer in peers], total, recv_sem)

    def load_all(number, refs):
        arrive(local.at[number], u_spec.at[pl.ds(0, sum(size_of(ref) for ref in refs) // (4 * channels)), :])

    right_sender, left_sender = sends.at[3], sends.at[4]
    right_copies = [
        pltpu.make_async_remote_copy(
            src_ref=x_hbm.at[at], dst_ref=left_v.at[at], send_sem=right_sender, recv_sem=claim(),
            device_id=(dp, seq + 1), device_id_type=MESH,
        )
        for at in (pl.ds(0, tokens - fourth), pl.ds(tokens - fourth, fourth))
    ]

    def prepare_shares():
        for copy in params:
            copy.wait()
        low = [ref[...].astype(bf16).astype(f32) for ref in (gain_ref, shift_ref, skip_ref, bias_ref)]
        share_in[z, place] = jnp.concatenate(low + [jnp.zeros((1, 128 - 5 * ROWS), f32)], axis=1)
        for q in range(4):
            weight[q, z, y, x, c] = jnp.concatenate(
                [w_ref[:, 128 * q : 128 * q + 128], w_ref[:, channels + 128 * q : channels + 128 * q + 128]], axis=1
            ).astype(bf16)

    def prepare_taps():
        _, _, unit, _, _, _, coef = mode_terms(ldt_ref[...], lar_ref[...], ai_ref[...], cc_ref[...])
        steps, power = [], times(unit, unit)
        for _ in range(8):
            steps.append(power)
            power = times(power, power)
        for p in range(8):
            def row(value):
                return value[0][p : p + 1], value[1][p : p + 1]

            def table(factors):
                sub = lax.broadcasted_iota(jnp.int32, (8, 128), 0)
                tile = None
                for bit, factor in enumerate(factors):
                    on = lax.rem(lax.div(sub, 2**bit), 2) == 1
                    factor = tuple(jnp.where(on, part, rest) for part, rest in zip(row(factor), (1.0, 0.0)))
                    tile = factor if tile is None else times(tile, factor)
                return tile

            base = table(steps[:3])
            for step in steps[3:6]:
                more = times(base, row(step))
                base = tuple(jnp.concatenate([old, new], axis=0) for old, new in zip(base, more))
            leap = table([steps[6], steps[7], unit])
            leaps[p, 0], leaps[p, 1] = leap
            at = slice(256 * p, 256 * p + 256)
            high, low = split_low(jnp.concatenate(base, axis=1))
            base_high[:, at], base_low[:, at] = high, low
            lead = times(row(coef), leap)
            lead = jnp.concatenate([lead[0], -lead[1]], axis=1)
            first = lax.rem(lax.broadcasted_iota(jnp.int32, (8, 256), 1), 128) < 64
            lead = jnp.concatenate([jnp.where(first, lead, 0.0), jnp.where(first, 0.0, lead)], axis=0)
            lead_high, lead_low = split_low(lead)
            taps_of = dot_nt(
                jnp.concatenate([lead_high, lead_low, lead_high], axis=1), jnp.concatenate([high, high, low], axis=1)
            )
            taps_of = jnp.concatenate([taps_of, taps_of], axis=1)
            lines_f[8 * p : 8 * p + 8], lines_f[8 * p + 64 : 8 * p + 72] = taps_of[:8], taps_of[8:]
        own = jnp.concatenate([lines_f[pl.ds(m, ROWS, stride=8), :][:, :64] for m in range(8)], axis=1)
        kern[z, y, x, c] = (2.0 * own).astype(bf16)

    late = z == 3

    @pl.when(jnp.logical_not(late))
    def _():
        prepare_shares()
        prepare_taps()

    pl.semaphore_wait(barrier, len(peers))

    @pl.when(late)
    def _():
        prepare_shares()

    share_plane = same(share_in.at[z, place], plane_peers + other_peers, share_in.at[0, pl.ds(0, 7)])
    weight_x = same(weight.at[:, z, y, x, c], [x_peer], weight.at[:, 0, 0, 0, 0])

    @pl.when(seq < 3)
    def _():
        right_copies[0].start()

    @pl.when(late)
    def _():
        prepare_taps()

    kern_z = same(kern.at[z, y, x, c], z_peers, kern.at[three, 0, 0, 0])
    finish(share_plane)
    share_z = same(share_in.at[z], z_peers, share_in.at[three])
    finish(weight_x)

    def weight_to_z(q):
        return same(weight.at[q, z, y, :, c], z_peers, weight.at[q, three, 0, :, 0])

    def weight_to_y(q):
        finish(weight_z[q])
        piece = weight.at[q, :, y, :, c]
        same(piece, [core_peer], piece, core_recvs[q // 2])
        return same(piece, [y_peer], weight.at[q, :, 0, :, 0])

    def weight_to_core(q):
        finish(weight_y[q])
        piece = weight.at[q, :, flip_y, :, c]
        same(piece, [core_peer], piece, core_recvs[q // 2])

    core_recvs = [claim(), claim()]
    weight_core = [(sem, weight.at[pl.ds(2 * h, 2), :, :, :, 0]) for h, sem in enumerate(core_recvs)]
    weight_z = [weight_to_z(0)]
    last_y = same(weight.at[3, z, y, :, c], [y_peer], weight.at[3, 0, 0, :, 0])

    def last_to_z():
        finish(last_y)
        return same(weight.at[3, z, :, :, c], z_peers, weight.at[3, three, :, :, 0])

    def last_to_core():
        finish(last_z)
        same(weight.at[3, :, :, :, c], [core_peer], weight.at[3, :, :, :, 0], core_recvs[1])

    def normalise(source, hat, keep_std, begin, end):
        for first in range(begin, end, 32):
            at = slice(first, first + 32)
            value = source[at, :].astype(f32)
            centered = value - jnp.mean(value, axis=1, keepdims=True)
            scale = lax.rsqrt(jnp.mean(centered * centered, axis=1, keepdims=True) + EPS)
            put(hat, at, centered * scale)
            if keep_std:
                inv_std[at, :] = jnp.broadcast_to(scale, (32, 128))

    loads[0].wait()
    normalise(x_v, x_hat, True, 0, tokens)
    finish(kern_z)
    halves = [pl.ds(0, 2), pl.ds(2, 2)]
    kern_plane = [same(kern.at[at, y, x, c], plane_peers, dk_in2.at[:, at]) for at in halves]

    weight_z.append(weight_to_z(1))
    finish(share_z)
    weight_z.append(weight_to_z(2))
    last_z = last_to_z()

    @pl.when(seq < 3)
    def _():
        right_copies[1].start()

    load_all(10, (pick, mask))
    shares = share_in[...].reshape(32, 1, 128).reshape(32, 128).astype(bf16)
    spread = dot_nn(shares, pick[...]) * mask[...].astype(f32)
    spread = jnp.sum(spread, axis=0, keepdims=True)
    rows_f[...] = jnp.concatenate(
        [spread[:, channels * i : channels * (i + 1)] for i in range(5)] + [jnp.zeros((3, channels), f32)], axis=0
    )
    gain, shift = rows_f[0:1, :], rows_f[1:2, :]

    def every_other(i, parity):
        return pl.ds(128 * i + parity, 64, stride=2)

    def sixty_four(i):
        return pl.ds(pl.multiple_of(64 * i, 64), 64)

    def shifted(i, _):
        at = pl.ds(pl.multiple_of(i * 128, 128), 128)
        put(normed, at, take(x_hat, at) * gain + shift)
        for parity in range(2):
            own_b[parity, sixty_four(i)] = take(normed, every_other(i, parity)).astype(bf16)
        return 0

    lax.fori_loop(0, tokens // 128, shifted, 0)
    load_all(11, (fwd, fwd_most, fwd_rest, inv, turn))
    wide = 256

    def lanes(j):
        return pl.ds(pl.multiple_of(j * wide, wide), wide)

    few = 16

    def sign_of(r):
        return 1 if r < half // 2 else -1

    def turned(value, r, back):
        cosine, sine = (jnp.concatenate([turn[i, r : r + few]] * 2, axis=1) for i in range(2))
        return conj_times((cosine, sine), value) if back else times(value, (cosine, sine))

    def transform(block, exact):
        both = jnp.concatenate([block[0], block[1]], axis=1)
        if exact:
            return dot_nn(fwd[...], jnp.concatenate([both, both], axis=0))
        return dot_nn(fwd[:, :half], both)

    def joined(both, r):
        parts = both[r : r + few], both[half + r : half + r + few]
        even, odd = [part[:, :wide] for part in parts], turned([part[:, wide:] for part in parts], r, False)
        return tuple(a + b for a, b in zip(even, odd)), tuple(a - b for a, b in zip(even, odd))

    def places(r):
        return [pl.ds(first + r, few) for first in (0, taps, half, taps + half)]

    def keep(ref, at, r, pair):
        for lines, part in zip(places(r), pair[0] + pair[1]):
            ref[lines, at] = part

    def kept(ref, at, r):
        parts = [ref[lines, at] for lines in places(r)]
        return parts[:2], parts[2:]

    def signal(pair_at, exact):
        real, imag = [], []
        for r in range(0, half, few):
            a, b = pair_at(r)
            even = [x + y for x, y in zip(a, b)]
            odd = turned([x - y for x, y in zip(a, b)], r, True)
            for lines, x, y in zip((real, imag), even, odd):
                both = jnp.concatenate([x, y], axis=1)
                lines.append(split_low(both) if exact else (both.astype(bf16),))
        lines = real + imag
        if exact:
            high, low = (jnp.concatenate([line[i] for line in lines], axis=0) for i in range(2))
            return dot_nn(inv[...], jnp.concatenate([high, high, low], axis=0))
        return dot_nn(inv[:, : 2 * half], jnp.concatenate([line[0] for line in lines], axis=0))

    def each(function, pairs):
        return tuple(function(*values) for values in zip(*pairs))

    def swung(value, sign):
        return (value[1], -value[0]) if sign > 0 else (-value[1], value[0])

    def own_spectrum(j):
        at = lanes(j)
        both = transform((own_b[0, :, at], own_b[1, :, at]), True)
        for r in range(0, half, few):
            keep(u_spec, at, r, joined(both, r))

    own_spectrum(0)
    own_spectrum(1)
    weight_y = [weight_to_y(0)]

    def left_block(i):
        first, last = (0, 3) if i == 0 else (3, 4)
        right_copies[i].wait_recv()
        normalise(left_v, left_hat, False, 128 * first, 128 * last)
        for k in range(first, last):
            for parity in range(2):
                value = take(left_hat, pl.ds(128 * k + parity, 64, stride=2)) * gain + shift
                left_b[parity, 64 * k : 64 * k + 64] = value.astype(bf16)
        at = slice(64 * first, 64 * last)
        matrix = (fwd_most if i == 0 else fwd_rest)[...]
        for j in range(2):
            lane = slice(wide * j, wide * (j + 1))
            both = jnp.concatenate([left_b[0, at, lane], left_b[1, at, lane]], axis=1)
            both = dot_nn(matrix, jnp.concatenate([both, both], axis=0))
            lines = slice(taps * j, taps * (j + 1))
            if i == 0:
                d_spec[lines, :] = both
                continue
            both += d_spec[lines, :]
            for r in range(0, half, few):
                turns = [swung(value, -sign_of(r)) for value in joined(both, r)]
                old = kept(u_spec, lanes(j), r)
                keep(u_spec, lanes(j), r, tuple(tuple(a + b for a, b in zip(x, y)) for x, y in zip(old, turns)))

    @pl.when(seq > 0)
    def _():
        left_block(0)

    @pl.when(seq == 0)
    def _():
        left_hat[...] = jnp.zeros_like(left_hat)

    weight_y.append(weight_to_y(1))
    kern_core = []
    for arrival, at in zip(kern_plane, halves):
        finish(arrival)
        kern_core.append(same(kern.at[at, :, :, c], [core_peer], kern.at[at, :, :, 0]))

    def kernel_transform(j):
        rows = kern[2 * j : 2 * j + 2].reshape(wide, taps)
        rows = [jnp.concatenate([rows[:, at]] * 2, axis=1) for at in (slice(0, half), slice(half, taps))]
        return dot_nt(fwd[...], jnp.concatenate(rows, axis=0))

    def convolve(j, both):
        at = lanes(j)

        def product(r):
            k = joined(both, r)
            keep(k_spec, at, r, k)
            return each(times, (k, kept(u_spec, at, r)))

        both = signal(product, True)
        for parity in range(2):
            put(mixed, pl.ds(parity, half, stride=2), both[:, wide * parity : wide * (parity + 1)], 2 * j)

    def activate(j):
        for tile in (2 * j, 2 * j + 1):
            at = slice(128 * tile, 128 * tile + 128)
            for start_at in range(0, tokens, 128):
                lines = slice(start_at, start_at + 128)
                value = mixed[tile, lines, :] + rows_f[2:3, at] * normed[tile, lines, :]
                chance = 0.5 + 0.5 * lax.erf(value * (0.5**0.5))
                slope[lines, at] = chance + value * jnp.exp(value * value * -0.5 - 0.5 * float(np.log(2.0 * np.pi)))
                low = (value * chance).astype(bf16)
                activ[lines, at] = low
                activ_t[at, lines] = low.T

    for j in range(2):
        finish(kern_core[j])
        k_raw[j] = kernel_transform(j)
        if j == 0:
            weight_y.append(weight_to_y(2))

    @pl.when(seq > 0)
    def _():
        left_block(1)

    weight_to_core(0)
    convolve(0, k_raw[0])
    weight_to_core(1)
    last_to_core()
    convolve(1, k_raw[1])
    activate(0)
    activate(1)
    weight_to_core(2)
    loads[-1].wait()

    def matrix_of(h):
        return jnp.concatenate([weight[q].reshape(channels, 256) for q in (2 * h, 2 * h + 1)], axis=1)

    def gates(h, pre):
        lines_out = []
        sums = [jnp.zeros((32, 128), f32) for _ in range(4)]
        for start_at in range(0, tokens, 32):
            lines = slice(start_at, start_at + 32)
            low = []
            for i, q in enumerate((2 * h, 2 * h + 1)):
                at = slice(128 * q, 128 * q + 128)
                lin = pre[lines, 256 * i : 256 * i + 128] + rows_f[3:4, at]
                gate = 0.5 + 0.5 * jnp.tanh(0.5 * (pre[lines, 256 * i + 128 : 256 * i + 256] + rows_f[4:5, at]))
                grad = g_v[lines, at].astype(f32)
                product = lin * gate
                res_v[lines, at] = (x_v[lines, at].astype(f32) + product).astype(bf16)
                low += [(grad * gate).astype(bf16), (grad * (product - product * gate)).astype(bf16)]
            sums = [total + part.astype(f32) for total, part in zip(sums, low)]
            lines_out.append(jnp.concatenate(low, axis=1))
        for i, q in enumerate((2 * h, 2 * h + 1)):
            for k in range(2):
                rows_f[3 + k : 4 + k, 128 * q : 128 * q + 128] = jnp.sum(sums[2 * i + k], axis=0, keepdims=True)
        return jnp.concatenate(lines_out, axis=0)

    def weight_grad(h, low):
        grad = dot_nn(activ_t[...], low).astype(bf16)
        for i, q in enumerate((2 * h, 2 * h + 1)):
            dw_own[q] = grad[:, 256 * i : 256 * i + 256].reshape(4, 2, 2, 2, ROWS, 256)
            start([(dw_own.at[q, :, :, :, flip_c], dw_in1.at[q], core_peer)], dw_in1.at[q], dw_recvs[h])

    def mix_grad(d_act):
        total = jnp.zeros((32, channels), f32)
        for start_at in range(0, tokens, 32):
            lines = slice(start_at, start_at + 32)
            mix = (d_act[lines] * slope[lines, :]).astype(bf16).astype(f32)
            total += mix * take(normed, lines)
            put(mixed, lines, mix)
        rows_f[2:3, :] = jnp.sum(total, axis=0, keepdims=True)
        for parity in range(2):
            for start_at in range(0, half, 64):
                part = take(mixed, pl.ds(2 * start_at + parity, 64, stride=2))
                d_mix[parity, start_at : start_at + 64] = part.astype(bf16)

    def core_sum(q):
        if q % 2 == 0:
            arrive(dw_recvs[q // 2], dw_in1.at[pl.ds(q, 2)])
        dw_mid[q] = (dw_own[q, :, :, :, c].astype(f32) + dw_in1[q].astype(f32)).astype(bf16)

    def to_y(q):
        core_sum(q)
        return start([(dw_mid.at[q, :, flip_y], dw_in2.at[q], y_peer)], dw_in2.at[q])

    def end_to_z():
        core_sum(3)
        copies = [(dw_mid.at[3, peer[0]], end_in1.at[i], peer) for i, peer in enumerate(z_peers)]
        return start(copies, end_in1)

    def end_to_plane():
        finish(end_z)
        total = dw_mid[3, z].astype(f32)
        for i in range(3):
            total = total + end_in1[i].astype(f32)
        end_mid[...] = total.astype(bf16)
        copies = [(end_mid.at[peer[1], peer[2]], end_in2.at[i], peer) for i, peer in enumerate(plane_peers)]
        return start(copies, end_in2)

    def write_out(q, total):
        dw_ref[:, 128 * q : 128 * q + 128] = total[:, :128]
        dw_ref[:, channels + 128 * q : channels + 128 * q + 128] = total[:, 128:]

    def end_of_last():
        finish(end_plane)
        total = end_mid[y, x].astype(f32)
        for i in range(3):
            total = total + end_in2[i].astype(f32)
        write_out(3, total)

    def to_z(q):
        finish(dw_y[q])
        dw_low[q] = (dw_mid[q, :, y].astype(f32) + dw_in2[q].astype(f32)).astype(bf16)
        copies = [(dw_low.at[q, peer[0]], dw_in3.at[q, i], peer) for i, peer in enumerate(z_peers)]
        return start(copies, dw_in3.at[q])

    def to_x(q):
        finish(dw_z[q])
        total = dw_low[q, z].astype(f32)
        for i in range(3):
            total = total + dw_in3[q, i].astype(f32)
        dw_end[q] = total.astype(bf16)
        return start([(dw_end.at[q, flip_x], dw_in4.at[q], x_peer)], dw_in4.at[q])

    def to_end(q):
        finish(dw_x[q])
        write_out(q, dw_end[q, x].astype(f32) + dw_in4[q].astype(f32))

    skip = rows_f[2:3, :]
    dw_y, dw_z, dw_x = [], [], []
    phase[0], dw_recvs = "reduce", [claim(), claim()]
    finish(weight_core[0])
    first_low = gates(0, dot_nn(activ[...], matrix_of(0)))
    weight_grad(0, first_low)
    finish(weight_core[1])
    second_low = gates(1, dot_nn(activ[...], matrix_of(1)))
    weight_grad(1, second_low)
    dw_y.append(to_y(0))
    dw_y.append(to_y(1))
    d_act = dot_nt(
        jnp.concatenate([first_low, second_low], axis=1), jnp.concatenate([matrix_of(0), matrix_of(1)], axis=1)
    )
    mix_grad(d_act)
    left_copies = [
        pltpu.make_async_remote_copy(
            src_ref=d_mix.at[:, :, pl.ds(wide * j, wide)], dst_ref=right_v.at[j], send_sem=left_sender,
            recv_sem=claim(), device_id=(dp, seq - 1), device_id_type=MESH,
        )
        for j in range(2)
    ]

    @pl.when(seq > 0)
    def _():
        left_copies[0].start()

    dw_y.append(to_y(2))
    end_z = end_to_z()

    def mix_transform(j):
        at = lanes(j)
        return transform((d_mix[0, :, at], d_mix[1, :, at]), False)

    def kernel_grad(j, both):
        at = lanes(j)

        def product(r):
            d = joined(both, r)
            keep(d_spec, at, r, d)
            return each(conj_times, (kept(u_spec, at, r), d))

        both = signal(product, False)
        grad = jnp.concatenate([both[:, :wide].T, both[:, wide:].T], axis=1).reshape(2, 2, 2, 2, ROWS, taps)
        dk_own[2 * j : 2 * j + 2] = grad
        dk_low[2 * j : 2 * j + 2] = grad.astype(bf16)

    def kernel_middle():
        finish(dk_core)
        for i in range(4):
            total = dk_own[i, :, :, c] + dk_in1[i].astype(f32)
            dk_mid[i] = total
            dk_cut[i] = total.astype(bf16)
        return start([(dk_cut.at[:, peer[1], peer[2]], dk_in2.at[i], peer) for i, peer in enumerate(plane_peers)], dk_in2)

    def kernel_end():
        finish(dk_plane)
        for i in range(4):
            total = dk_mid[i, y, x]
            for k in range(3):
                total = total + dk_in2[k, i].astype(f32)
            dk_end[i] = total
            dk_out[i] = total.astype(bf16)
        return start([(dk_out.at[peer[0]], dk_in3.at[i], peer) for i, peer in enumerate(z_peers)], dk_in3)

    def own_grad(j):
        at = lanes(j)

        def product(r):
            return each(conj_times, (kept(k_spec, at, r), kept(d_spec, at, r)))

        def shifted_product(r):
            return tuple(swung(value, sign_of(r)) for value in product(r))

        own, back = signal(product, False), signal(shifted_product, False)
        d_gain, d_shift = jnp.zeros((1, wide), f32), jnp.zeros((1, wide), f32)
        for parity in range(2):
            lines = pl.ds(parity, half, stride=2)
            columns = slice(wide * parity, wide * (parity + 1))
            grad = own[:, columns] + rows_f[5:6, at] * d_mix[parity, :, at].astype(f32)
            put(d_norm, lines, grad, 2 * j)
            before = jnp.where(seq > 0, back[:, columns], 0.0)
            d_gain += jnp.sum(
                grad * take(x_hat, lines, 2 * j, 2) + before * take(left_hat, lines, 2 * j, 2), axis=0, keepdims=True
            )
            d_shift += jnp.sum(grad + before, axis=0, keepdims=True)
        rows_f[6:7, at], rows_f[7:8, at] = d_gain, d_shift

    def right_grad(j):
        at = lanes(j)
        both = transform((right_v[j, 0], right_v[j, 1]), False)

        def product(r):
            turns = [swung(value, sign_of(r)) for value in joined(both, r)]
            return each(conj_times, (kept(k_spec, at, r), turns))

        both = signal(product, False)
        for parity in range(2):
            lines = pl.ds(parity, half, stride=2)
            more = both[:, wide * parity : wide * (parity + 1)]
            put(d_norm, lines, take(d_norm, lines, 2 * j, 2) + more, 2 * j)

    rows_f[5:6, :] = skip
    first_half, second_half = mix_transform(0), mix_transform(1)
    kernel_grad(0, first_half)
    kernel_grad(1, second_half)
    dk_core = start([(dk_low.at[:, :, :, flip_c], dk_in1, core_peer)], dk_in1)
    own_grad(0)
    own_grad(1)
    dk_plane = kernel_middle()

    @pl.when(seq > 0)
    def _():
        left_copies[1].start()

    dw_z.append(to_z(0))
    dw_z.append(to_z(1))
    vector = jnp.concatenate([rows_f[6:7, :], rows_f[7:8, :], rows_f[2:3, :], rows_f[3:4, :], rows_f[4:5, :]], axis=1)
    high, low = split_low(jnp.broadcast_to(vector, mask.shape) * mask[...].astype(f32))
    shares = dot_nt(high, pick[...]) + dot_nt(low, pick[...])
    share_out[...] = shares.reshape(32, 1, 128).reshape(4, 8, 1, 128)
    copies = [(share_out.at[peer[0]], share_in1.at[i], peer) for i, peer in enumerate(z_peers)]
    share_z = start(copies, share_in1)
    @pl.when(seq < 3)
    def _():
        left_copies[0].wait_recv()
        right_grad(0)

    dw_z.append(to_z(2))
    end_plane = end_to_plane()
    dk_z = kernel_end()
    dw_x.append(to_x(0))
    dw_x.append(to_x(1))
    finish(share_z)
    share_mid[...] = share_out[z] + share_in1[0] + share_in1[1] + share_in1[2]
    copies = [
        (share_mid.at[(peer[1] * 2 + peer[2]) * 2 + peer[3]], share_in2.at[i], peer)
        for i, peer in enumerate(plane_peers + other_peers)
    ]
    share_plane = start(copies, share_in2)

    @pl.when(seq < 3)
    def _():
        left_copies[1].wait_recv()
        right_grad(1)

    dw_x.append(to_x(2))

    @pl.when(seq < 3)
    def _():
        arrive(right_sender, x_v)

    @pl.when(seq > 0)
    def _():
        arrive(left_sender, d_mix)

    for first in range(0, tokens, 32):
        at = slice(first, first + 32)
        hat = [x_hat[i, at, :] for i in range(4)]
        grad = [d_norm[i, at, :] * rows_f[0:1, 128 * i : 128 * i + 128] for i in range(4)]
        mean = jnp.sum(sum(grad[1:], grad[0]), axis=1, keepdims=True) * (1.0 / channels)
        along = [one * other for one, other in zip(grad, hat)]
        along = jnp.sum(sum(along[1:], along[0]), axis=1, keepdims=True) * (1.0 / channels)
        for i in range(4):
            lane = slice(128 * i, 128 * i + 128)
            inner = inv_std[at, :] * (grad[i] - mean - hat[i] * along)
            gin_v[at, lane] = (inner + g_v[at, lane].astype(f32)).astype(bf16)
    dt, a, unit, norm_sq, ratio, coef, scaled = mode_terms(ldt_ref[...], lar_ref[...], ai_ref[...], cc_ref[...])
    inverse_a = (a[0] / norm_sq, -a[1] / norm_sq)
    finish(dk_z)
    d_kernel = dk_end[z]
    for k in range(3):
        d_kernel = d_kernel + dk_in3[k].astype(f32)

    for m in range(8):
        block = d_kernel[:, 64 * m : 64 * m + 64]
        lines_f[pl.ds(m, ROWS, stride=8), :] = jnp.concatenate([block, block], axis=1)
    plain = lines_f[...][:, :64]
    ramp = plain * (2 * lax.broadcasted_iota(jnp.int32, (8 * ROWS, 64), 1)).astype(f32)
    high, low = split_low(jnp.concatenate([plain, ramp], axis=0))
    table = jnp.concatenate([base_high[...], base_low[...], base_high[...]], axis=0)
    sums = dot_nn(jnp.concatenate([high, high, low], axis=1), table)
    at_row = lax.broadcasted_iota(jnp.int32, (8, 128), 0)
    first = lax.broadcasted_iota(jnp.int32, (8, 128), 1) < 64
    leap_of = (128 * lax.rem(at_row, 4) + lax.div(at_row, 4)).astype(f32)
    zero = jnp.zeros((8, 128), f32)
    s0, s1 = [zero, zero], [zero, zero]
    for p in range(8):
        def pair(start, part):
            block = sums[start : start + 128, 256 * p + 128 * part : 256 * p + 128 * part + 128]
            return jnp.where(first, block[8 * p : 8 * p + 8], block[8 * p + 64 : 8 * p + 72])

        value, slope_of = [pair(0, part) for part in range(2)], [pair(128, part) for part in range(2)]
        leap = (leaps[p, 0], leaps[p, 1])
        slope_of = [one + leap_of * other for one, other in zip(slope_of, value)]
        for total, terms in ((s0, value), (s1, slope_of)):
            for part, product in enumerate(times(leap, terms)):
                total[part] = jnp.where(at_row == p, jnp.sum(product, axis=0, keepdims=True), total[part])
    d_coef = times(s0, ratio)
    half_g = times(times(coef, s0), times(unit, inverse_a))
    ramp_part = times(scaled, s1)
    half_g = (half_g[0] + ramp_part[0], half_g[1] + ramp_part[1])
    back = times(times(scaled, s0), inverse_a)
    q = (half_g[0] * dt - back[0], half_g[1] * dt - back[1])
    d_dt = 2.0 * dt * times(half_g, a)[0]
    dldt_ref[...] = row_of(jnp.sum(unpair_lanes(d_dt), axis=1, keepdims=True))[0]
    dlar_ref[...] = unpair_lanes(2.0 * q[0] * a[0])
    dai_ref[...] = unpair_lanes(-2.0 * q[1])
    dcc_ref[...] = jnp.concatenate([unpair_lanes(2.0 * d_coef[0]), unpair_lanes(-2.0 * d_coef[1])], axis=1)

    end_of_last()
    for q in range(3):
        to_end(q)
    finish(share_plane)
    small = share_mid[place]
    for i in range(7):
        small = small + share_in2[i]
    for i, target in enumerate([dgain_ref, dshift_ref, dskip_ref]):
        target[...] = small[0, ROWS * i : ROWS * (i + 1)]
    dbias_ref[...] = small[0, 3 * ROWS : 5 * ROWS]
    arrive(sends.at[0], u_spec.at[pl.ds(0, sent["gather"] // (4 * channels)), :])
    arrive(sends.at[1], u_spec.at[pl.ds(0, sent["reduce"] // (4 * channels)), :])
    arrive(sends.at[2], vector_rows.at[pl.ds(0, sent["vector"] // 512)])


def finish_kernel(*refs):
    count = len(refs) // 2
    sems = refs[-1]
    copies = [pltpu.make_async_copy(refs[i], refs[count + i], sems.at[i]) for i in range(count)]
    for copy in copies:
        copy.start()
    for copy in copies:
        copy.wait()


def kernel_body(
    inputs, grad_out, ln_gain, ln_bias, skip_scale, w_glu, b_glu, log_dt, log_a_real, a_imag, c_coef
):
    _, tokens, channels = inputs.shape
    taps = KTAPS
    glu = w_glu.shape[1]
    f32, bf16 = jnp.float32, jnp.bfloat16
    order = np.concatenate([np.arange(0, taps // 2, 2), np.arange(1, taps // 2, 2)]) + 0.5
    angle = np.outer(order, np.arange(taps // 2)) * (2 * np.pi / taps)
    matrix = np.concatenate([np.cos(angle), -np.sin(angle)], axis=0)
    high = matrix.astype(bf16)
    low = (matrix - high.astype(np.float64)).astype(bf16)
    forward = np.concatenate([high, low], axis=1)
    cut = 3 * taps // 8
    most, rest = (np.concatenate([part[:, at] for part in (high, low)], axis=1) for at in (slice(0, cut), slice(cut, None)))
    scale = np.asarray(1.0 / taps, bf16)
    inverse = np.concatenate([high.T, low.T, high.T], axis=1) * scale
    turns = np.stack([np.cos(order * (np.pi / taps)), -np.sin(order * (np.pi / taps))])
    turns = np.ascontiguousarray(np.broadcast_to(turns[:, :, None], (2, taps // 2, 128))).astype(np.float32)
    device_at, lane = np.arange(32)[:, None], np.arange(channels)[None, :]
    bias_lane = np.arange(2 * channels)[None, :]
    row = np.arange(128)[:, None]
    pick = np.concatenate(
        [row == i * ROWS + lane % ROWS for i in range(3)] + [row == 3 * ROWS + bias_lane % (2 * ROWS)], axis=1
    ).astype(bf16)
    mask = np.concatenate(
        [device_at == lane // ROWS] * 3 + [device_at == bias_lane // (2 * ROWS)], axis=1
    ).astype(bf16)
    hbm, vmem = pl.BlockSpec(memory_space=pl.ANY), pl.BlockSpec(memory_space=pltpu.VMEM)
    block = (tokens, channels)
    spec, tall = (2 * taps, channels), (channels // 128, tokens, 128)

    def space(*dims, kind=f32):
        return pltpu.VMEM(dims, kind)

    results = (
        (block, bf16), (block, bf16), ((ROWS,), f32), ((ROWS,), f32), ((ROWS,), f32), (w_glu.shape, f32),
        ((2 * ROWS,), f32), ((ROWS,), f32), (log_a_real.shape, f32), (a_imag.shape, f32), (c_coef.shape, f32),
    )
    outs = pl.pallas_call(
        layer_kernel,
        name="layer",
        out_shape=tuple(pltpu.VMEM(dims, kind) for dims, kind in results),
        in_specs=[hbm] * 18,
        out_specs=(vmem,) * len(results),
        scratch_shapes=[
            space(*w_glu.shape), space(1, ROWS), space(1, ROWS), space(1, ROWS), space(1, 2 * ROWS), space(1, ROWS),
            space(*log_a_real.shape), space(*a_imag.shape), space(*c_coef.shape),
            space(*block, kind=bf16), space(*block, kind=bf16), space(*block, kind=bf16),
            space(*forward.shape, kind=bf16), space(*most.shape, kind=bf16), space(*rest.shape, kind=bf16),
            space(*inverse.shape, kind=bf16),
            space(*pick.shape, kind=bf16), space(*mask.shape, kind=bf16), space(*turns.shape),
            space(4, 2, 2, 2, ROWS, taps, kind=bf16), space(4, 4, 2, 2, 2, ROWS, 256, kind=bf16),
            space(64, 2048, kind=bf16), space(64, 2048, kind=bf16), space(8, 2, 8, 128), space(8 * ROWS, 128),
            space(4, 8, 1, 128), space(4, 8, 1, 128), space(3, 8, 1, 128), space(8, 1, 128), space(7, 1, 128),
            space(64, 1, 128),
            space(8, channels),
            space(*tall), space(tokens, 128), space(*tall), space(*tall),
            space(2, tokens // 2, channels, kind=bf16), space(2, tokens // 2, channels, kind=bf16),
            space(2, taps, taps), space(*spec), space(*spec), space(*tall), space(*block),
            space(*block, kind=bf16), space(channels, tokens, kind=bf16),
            space(2, tokens // 2, channels, kind=bf16), space(2, 2, tokens // 2, 256, kind=bf16),
            space(*spec), space(*tall),
            space(4, 4, 2, 2, 2, ROWS, 256, kind=bf16), space(4, 4, 2, 2, ROWS, 256, kind=bf16),
            space(4, 4, 2, 2, ROWS, 256, kind=bf16), space(4, 4, 2, ROWS, 256, kind=bf16),
            space(4, 4, 2, ROWS, 256, kind=bf16), space(4, 3, 2, ROWS, 256, kind=bf16),
            space(4, 2, ROWS, 256, kind=bf16), space(4, ROWS, 256, kind=bf16),
            space(3, 2, 2, ROWS, 256, kind=bf16), space(2, 2, ROWS, 256, kind=bf16), space(3, ROWS, 256, kind=bf16),
            space(4, 2, 2, 2, ROWS, taps), space(4, 2, 2, 2, ROWS, taps, kind=bf16), space(4, 2, 2, ROWS, taps, kind=bf16),
            space(4, 2, 2, ROWS, taps), space(4, 2, 2, ROWS, taps, kind=bf16), space(3, 4, ROWS, taps, kind=bf16),
            space(4, ROWS, taps), space(4, ROWS, taps, kind=bf16), space(3, ROWS, taps, kind=bf16),
            pltpu.SemaphoreType.DMA((13,)), pltpu.SemaphoreType.DMA((5,)), pltpu.SemaphoreType.DMA((40,)),
        ],
        compiler_params=pltpu.CompilerParams(
            collective_id=0, has_side_effects=True, vmem_limit_bytes=48 * 2**20
        ),
    )(*[
        pltpu.with_memory_space_constraint(value, pltpu.HBM)
        for value in (
            inputs.reshape(block), grad_out.reshape(block), forward, most, rest, inverse, pick, mask, turns, w_glu,
            ln_gain.reshape(1, -1), ln_bias.reshape(1, -1), skip_scale.reshape(1, -1), b_glu.reshape(1, -1),
            log_dt.reshape(1, -1), log_a_real, a_imag, c_coef,
        )
    ])
    ended = pl.pallas_call(
        finish_kernel,
        name="finish",
        out_shape=tuple(jax.ShapeDtypeStruct(dims, kind) for dims, kind in results),
        in_specs=[vmem] * len(results),
        out_specs=(hbm,) * len(results),
        scratch_shapes=[pltpu.SemaphoreType.DMA((len(results),))],
    )(*[pltpu.with_memory_space_constraint(value, pltpu.VMEM) for value in outs])
    return (ended[0].reshape(inputs.shape), ended[1].reshape(inputs.shape)) + tuple(ended[2:])


def solution(mesh):
    in_specs = (
        P("dp", "seq", None),
        P("dp", "seq", None),
        P(("dp", "seq")),
        P(("dp", "seq")),
        P(("dp", "seq")),
        P(("dp", "seq"), None),
        P(("dp", "seq")),
        P(("dp", "seq")),
        P(("dp", "seq"), None),
        P(("dp", "seq"), None),
        P(("dp", "seq"), None),
    )
    out_specs = (
        P("dp", "seq", None),
        P("dp", "seq", None),
        P(("dp", "seq")),
        P(("dp", "seq")),
        P(("dp", "seq")),
        P(("dp", "seq"), None),
        P(("dp", "seq")),
        P(("dp", "seq")),
        P(("dp", "seq"), None),
        P(("dp", "seq"), None),
        P(("dp", "seq"), None),
    )
    quick = mesh.shape["dp"] == 8 and mesh.shape["seq"] == 4
    return jax.shard_map(kernel_body if quick else body, mesh=mesh, in_specs=in_specs, out_specs=out_specs, check_vma=False)
```

```python
import math
from functools import partial

import jax
import jax.numpy as jnp
import numpy as np
from jax import lax
from jax.experimental import pallas as pl
from jax.experimental.pallas import tpu as pltpu
from jax.sharding import PartitionSpec as P

KTAPS = 512


EPS = 1e-05


def passed_along(value, axis, steps):
    count = lax.axis_size(axis)
    first, last = (max(0, -steps), min(count, count - steps))
    return lax.ppermute(value, axis, [(source, source + steps) for source in range(first, last)])


def kernel_block(log_dt, log_a_real, a_imag, c_coef, start, count):
    mode_count = log_a_real.shape[1]
    step_size = jnp.exp(log_dt)[:, None]
    a_real = -jnp.exp(log_a_real)
    decay = a_real * step_size
    turn = a_imag * step_size
    growth = jnp.exp(decay)
    ex_re = growth * jnp.cos(turn) - 1.0
    ex_im = growth * jnp.sin(turn)
    norm_sq = a_real * a_real + a_imag * a_imag
    ratio_re = (ex_re * a_real + ex_im * a_imag) / norm_sq
    ratio_im = (ex_im * a_real - ex_re * a_imag) / norm_sq
    c_re = c_coef[:, :mode_count]
    c_im = c_coef[:, mode_count:]
    coef_re = c_re * ratio_re - c_im * ratio_im
    coef_im = c_re * ratio_im + c_im * ratio_re
    places = (start + jnp.arange(count)).astype(jnp.float32)
    phase = turn[:, :, None] * places
    damping = jnp.exp(decay[:, :, None] * places)
    terms = damping * (coef_re[:, :, None] * jnp.cos(phase) - coef_im[:, :, None] * jnp.sin(phase))
    return 2.0 * jnp.sum(terms, axis=1)


def transforms(taps):
    angle = np.outer(np.arange(taps) + 0.5, np.arange(taps)) * (np.pi / taps)
    forward = np.concatenate([np.cos(angle), -np.sin(angle)], axis=0)
    inverse = forward.T / taps
    return forward.astype(jnp.bfloat16), inverse.astype(jnp.bfloat16)


def body(
    inputs, grad_out, ln_gain, ln_bias, skip_scale, w_glu, b_glu, log_dt, log_a_real, a_imag, c_coef
):
    seq_count, own_len, channels = inputs.shape
    gain_low = ln_gain.astype(jnp.bfloat16)
    shift_low = ln_bias.astype(jnp.bfloat16)
    skip_low = skip_scale.astype(jnp.bfloat16)
    weight_low = w_glu.astype(jnp.bfloat16)
    bias_low = b_glu.astype(jnp.bfloat16)
    mode_own = (log_dt, log_a_real, a_imag, c_coef)
    own_kernel = kernel_block(*mode_own, 0, KTAPS).astype(jnp.bfloat16)
    gathered = (
        lax.all_gather(gain_low, ("dp", "seq"), axis=0, tiled=True),
        lax.all_gather(shift_low, ("dp", "seq"), axis=0, tiled=True),
        lax.all_gather(skip_low, ("dp", "seq"), axis=0, tiled=True),
        lax.all_gather(weight_low, ("dp", "seq"), axis=0, tiled=True),
        lax.all_gather(bias_low, ("dp", "seq"), axis=0, tiled=True),
        lax.all_gather(own_kernel, ("dp", "seq"), axis=0, tiled=True),
    )
    kernel_b = gathered[5]
    taps = own_len
    forward, inverse = transforms(taps)
    sign = jnp.where(jnp.arange(taps) % 2 == 0, 1.0, -1.0).astype(jnp.float32)[:, None]

    def to_spectrum(block):
        both = jnp.dot(forward, block, preferred_element_type=jnp.float32)
        return both[:taps], both[taps:]

    def from_spectrum(real, imag):
        both = jnp.concatenate([real, imag], axis=0).astype(jnp.bfloat16)
        return jnp.dot(inverse, both, preferred_element_type=jnp.float32)

    kernel_re, kernel_im = to_spectrum(kernel_b.T)
    gain_full = gathered[0].astype(jnp.float32)
    shift_full = gathered[1].astype(jnp.float32)
    skip_full = gathered[2].astype(jnp.float32)
    weight_b = gathered[3]
    glu_bias = gathered[4].astype(jnp.float32)
    x_float = inputs.astype(jnp.float32)
    row_mean = jnp.mean(x_float, axis=-1, keepdims=True)
    centered = x_float - row_mean
    row_var = jnp.mean(centered * centered, axis=-1, keepdims=True)
    inv_std = lax.rsqrt(row_var + EPS)
    x_hat = centered * inv_std
    normed = x_hat * gain_full + shift_full
    normed_b = normed.astype(jnp.bfloat16)
    own_re, own_im = to_spectrum(normed_b[0])
    left_re, left_im = to_spectrum(passed_along(normed_b, "seq", 1)[0])
    source_re = own_re - sign * left_im
    source_im = own_im + sign * left_re
    conv = from_spectrum(
        kernel_re * source_re - kernel_im * source_im,
        kernel_re * source_im + kernel_im * source_re,
    )
    mixed_pre = conv[None] + skip_full * normed
    activ, gelu_pull = jax.vjp(partial(jax.nn.gelu, approximate=False), mixed_pre)
    activ_b = activ.astype(jnp.bfloat16)
    glu_pre = (
        jnp.einsum("slh,hg->slg", activ_b, weight_b, preferred_element_type=jnp.float32) + glu_bias
    )
    half_dim = glu_pre.shape[-1] // 2
    lin_part = glu_pre[..., :half_dim]
    gate_sig = jax.nn.sigmoid(glu_pre[..., half_dim:])
    result = (x_float + lin_part * gate_sig).astype(jnp.bfloat16)
    grad_f = grad_out.astype(jnp.float32)
    d_pre = jnp.concatenate(
        [grad_f * gate_sig, grad_f * lin_part * gate_sig * (1.0 - gate_sig)], axis=-1
    ).astype(jnp.bfloat16)
    d_weight = jnp.einsum("slh,slg->hg", activ_b, d_pre, preferred_element_type=jnp.float32)
    d_glu_bias = jnp.sum(d_pre.astype(jnp.float32), axis=(0, 1))
    d_act = jnp.einsum("slg,hg->slh", d_pre, weight_b, preferred_element_type=jnp.float32)
    d_mix = gelu_pull(d_act)[0].astype(jnp.bfloat16)
    d_mix_f = d_mix.astype(jnp.float32)
    d_skip = jnp.sum(d_mix_f * normed, axis=(0, 1))
    mix_re, mix_im = to_spectrum(d_mix[0])
    d_kernel = from_spectrum(
        source_re * mix_re + source_im * mix_im, source_re * mix_im - source_im * mix_re
    ).T
    right_re, right_im = to_spectrum(passed_along(d_mix, "seq", -1)[0])
    sum_re = mix_re + sign * right_im
    sum_im = mix_im - sign * right_re
    d_conv = from_spectrum(
        kernel_re * sum_re + kernel_im * sum_im, kernel_re * sum_im - kernel_im * sum_re
    )[None]
    d_normed = d_conv + skip_full * d_mix_f
    d_gain = jnp.sum(d_normed * x_hat, axis=(0, 1))
    d_shift = jnp.sum(d_normed, axis=(0, 1))
    scaled = d_normed * gain_full
    d_input = (
        inv_std
        * (
            scaled
            - jnp.mean(scaled, axis=-1, keepdims=True)
            - x_hat * jnp.mean(scaled * x_hat, axis=-1, keepdims=True)
        )
        + grad_f
    )
    grad_in = d_input.astype(jnp.bfloat16)
    summed = (
        lax.psum_scatter(d_gain, ("dp", "seq"), scatter_dimension=0, tiled=True),
        lax.psum_scatter(d_shift, ("dp", "seq"), scatter_dimension=0, tiled=True),
        lax.psum_scatter(d_skip, ("dp", "seq"), scatter_dimension=0, tiled=True),
        lax.psum_scatter(d_weight, ("dp", "seq"), scatter_dimension=0, tiled=True),
        lax.psum_scatter(d_glu_bias, ("dp", "seq"), scatter_dimension=0, tiled=True),
        lax.psum_scatter(d_kernel, ("dp", "seq"), scatter_dimension=0, tiled=True),
    )
    _, own_pull = jax.vjp(partial(kernel_block, start=0, count=KTAPS), *mode_own)
    mode_grads = own_pull(summed[5])
    return (
        result,
        grad_in,
        summed[0],
        summed[1],
        summed[2],
        summed[3],
        summed[4],
        mode_grads[0],
        mode_grads[1],
        mode_grads[2],
        mode_grads[3],
    )


MESH = pl.DeviceIdType.MESH
ROWS = 16


def pair_lanes(value):
    return jnp.concatenate([value[:8], value[8:]], axis=1)


def unpair_lanes(value):
    half = value.shape[1] // 2
    return jnp.concatenate([value[:, :half], value[:, half:]], axis=0)


def column_of(row):
    n = row.shape[1]
    at = lax.broadcasted_iota(jnp.int32, (n, n), 0) == lax.broadcasted_iota(jnp.int32, (n, n), 1)
    return jnp.sum(jnp.where(at, jnp.broadcast_to(row, (n, n)), 0.0), axis=1, keepdims=True)


def row_of(column):
    n = column.shape[0]
    at = lax.broadcasted_iota(jnp.int32, (n, n), 0) == lax.broadcasted_iota(jnp.int32, (n, n), 1)
    return jnp.sum(jnp.where(at, jnp.broadcast_to(column, (n, n)), 0.0), axis=0, keepdims=True)


def mode_terms(ldt, lar, ai, cc):
    n_modes = lar.shape[1]
    dt = column_of(jnp.exp(ldt))
    dt = jnp.concatenate(
        [jnp.broadcast_to(dt[:8], (8, n_modes)), jnp.broadcast_to(dt[8:], (8, n_modes))], axis=1
    )
    a_re, a_im = -jnp.exp(pair_lanes(lar)), pair_lanes(ai)
    decay, turn = a_re * dt, a_im * dt
    growth = jnp.exp(decay)
    z_re, z_im = growth * jnp.cos(turn), growth * jnp.sin(turn)
    ex_re, ex_im = z_re - 1.0, z_im
    norm_sq = a_re * a_re + a_im * a_im
    r_re = (ex_re * a_re + ex_im * a_im) / norm_sq
    r_im = (ex_im * a_re - ex_re * a_im) / norm_sq
    c_re, c_im = pair_lanes(cc[:, :n_modes]), pair_lanes(cc[:, n_modes:])
    w_re, w_im = c_re * r_re - c_im * r_im, c_re * r_im + c_im * r_re
    return dt, (a_re, a_im), (z_re, z_im), norm_sq, (r_re, r_im), (c_re, c_im), (w_re, w_im)


def times(a, b):
    return a[0] * b[0] - a[1] * b[1], a[0] * b[1] + a[1] * b[0]


def conj_times(a, b):
    return a[0] * b[0] + a[1] * b[1], a[0] * b[1] - a[1] * b[0]


def split_low(value):
    high = value.astype(jnp.bfloat16)
    return high, (value - high.astype(jnp.float32)).astype(jnp.bfloat16)


def dot_nn(a, b):
    return lax.dot_general(a, b, (((1,), (0,)), ((), ())), preferred_element_type=jnp.float32)


def dot_nt(a, b):
    return lax.dot_general(a, b, (((1,), (1,)), ((), ())), preferred_element_type=jnp.float32)


def layer_kernel(
    x_hbm, g_hbm, fwd_hbm, most_hbm, rest_hbm, inv_hbm, pick_hbm, mask_hbm, turn_hbm,
    w_hbm, gain_hbm, shift_hbm, skip_hbm, bias_hbm, ldt_hbm, lar_hbm, ai_hbm, cc_hbm,
    res_v, gin_v, dgain_ref, dshift_ref, dskip_ref, dw_ref, dbias_ref, dldt_ref, dlar_ref, dai_ref, dcc_ref,
    w_ref, gain_ref, shift_ref, skip_ref, bias_ref, ldt_ref, lar_ref, ai_ref, cc_ref,
    x_v, g_v, left_v, fwd, fwd_most, fwd_rest, inv, pick, mask, turn, kern, weight, base_high, base_low, leaps, lines_f,
    share_in, share_out, share_in1, share_mid, share_in2, vector_rows, rows_f, x_hat, inv_std, left_hat, normed, own_b, left_b,
    k_raw, k_spec, u_spec, mixed, slope, activ, activ_t, d_mix, right_v, d_spec, d_norm,
    dw_own, dw_in1, dw_mid, dw_in2, dw_low, dw_in3, dw_end, dw_in4, end_in1, end_mid, end_in2,
    dk_own, dk_low, dk_in1, dk_mid, dk_cut, dk_in2, dk_end, dk_out, dk_in3,
    local, sends, recvs,
):
    f32, bf16 = jnp.float32, jnp.bfloat16
    tokens, channels = x_v.shape
    taps = KTAPS
    half, fourth = taps // 2, taps // 4
    dp, seq = lax.axis_index("dp"), lax.axis_index("seq")
    index = dp * 4 + seq
    z, y, x, c = lax.div(dp, 2), lax.rem(dp, 2), lax.div(seq, 2), lax.rem(seq, 2)
    flip_y, flip_x, flip_c = 1 - y, 1 - x, 1 - c

    def device(z, y, x, c):
        return (z * 2 + y, x * 2 + c)

    z_peers = [(lax.rem(z + k, 4), y, x, c) for k in (1, 2, 3)]
    plane_peers = [
        (z, lax.rem(y + k // 2, 2), lax.rem(x + k % 2, 2), c) for k in (1, 2, 3)
    ]
    x_peer, y_peer, core_peer = (z, y, flip_x, c), (z, flip_y, x, c), (z, y, x, flip_c)
    other_peers = [core_peer] + [(peer[0], peer[1], peer[2], flip_c) for peer in plane_peers]
    groups = ("gather", "reduce", "vector")
    sent = dict.fromkeys(groups, 0)
    phase, used = ["gather"], [0]

    def claim():
        used[0] += 1
        return recvs.at[used[0] - 1]

    def size_of(ref):
        return math.prod(ref.shape) * jnp.dtype(ref.dtype).itemsize

    def arrive(semaphore, total):
        pltpu.make_async_copy(total, total, semaphore).wait()

    def start(copies, total, recv_sem=None):
        if recv_sem is None:
            recv_sem = claim()
        group = "vector" if copies[0][0].shape[-2:] == (1, 128) else phase[0]
        for source, target, peer in copies:
            sent[group] += size_of(source)
            pltpu.make_async_remote_copy(
                src_ref=source, dst_ref=target, send_sem=sends.at[groups.index(group)], recv_sem=recv_sem,
                device_id=device(*peer), device_id_type=MESH,
            ).start()
        return recv_sem, total

    def finish(arrival):
        arrive(*arrival)

    def load(copies):
        for copy in copies:
            copy.start()
        return copies

    def take(ref, lines, first=0, count=4):
        return jnp.concatenate([ref[first + i, lines, :] for i in range(count)], axis=1)

    def put(ref, lines, value, first=0):
        for i in range(value.shape[1] // 128):
            ref[first + i, lines, :] = value[:, 128 * i : 128 * (i + 1)]

    barrier = pltpu.get_barrier_semaphore()
    peers = z_peers + plane_peers + other_peers
    for peer in peers:
        pl.semaphore_signal(barrier, inc=1, device_id=device(*peer), device_id_type=MESH)
    def fetch(pairs, numbers):
        return load([pltpu.make_async_copy(source, target, local.at[i]) for i, (source, target) in zip(numbers, pairs)])

    params = fetch([
        (gain_hbm, gain_ref), (shift_hbm, shift_ref), (skip_hbm, skip_ref), (bias_hbm, bias_ref), (w_hbm, w_ref),
        (ldt_hbm, ldt_ref), (lar_hbm, lar_ref), (ai_hbm, ai_ref), (cc_hbm, cc_ref),
    ], range(9))
    loads = fetch([
        (x_hbm, x_v), (pick_hbm, pick), (mask_hbm, mask), (fwd_hbm, fwd), (most_hbm, fwd_most), (rest_hbm, fwd_rest),
        (inv_hbm, inv), (turn_hbm, turn), (g_hbm, g_v),
    ], (9, 10, 10, 11, 11, 11, 11, 11, 12))
    three, place = pl.ds(0, 3), (y * 2 + x) * 2 + c

    def same(ref, peers, total, recv_sem=None):
        return start([(ref, ref, peer) for peer in peers], total, recv_sem)

    def load_all(number, refs):
        arrive(local.at[number], u_spec.at[pl.ds(0, sum(size_of(ref) for ref in refs) // (4 * channels)), :])

    right_sender, left_sender = sends.at[3], sends.at[4]
    right_copies = [
        pltpu.make_async_remote_copy(
            src_ref=x_hbm.at[at], dst_ref=left_v.at[at], send_sem=right_sender, recv_sem=claim(),
            device_id=(dp, seq + 1), device_id_type=MESH,
        )
        for at in (pl.ds(0, tokens - fourth), pl.ds(tokens - fourth, fourth))
    ]

    def prepare_shares():
        for copy in params:
            copy.wait()
        low = [ref[...].astype(bf16).astype(f32) for ref in (gain_ref, shift_ref, skip_ref, bias_ref)]
        share_in[z, place] = jnp.concatenate(low + [jnp.zeros((1, 128 - 5 * ROWS), f32)], axis=1)
        for q in range(4):
            weight[q, z, y, x, c] = jnp.concatenate(
                [w_ref[:, 128 * q : 128 * q + 128], w_ref[:, channels + 128 * q : channels + 128 * q + 128]], axis=1
            ).astype(bf16)

    def prepare_taps():
        _, _, unit, _, _, _, coef = mode_terms(ldt_ref[...], lar_ref[...], ai_ref[...], cc_ref[...])
        steps, power = [], times(unit, unit)
        for _ in range(8):
            steps.append(power)
            power = times(power, power)
        for p in range(8):
            def row(value):
                return value[0][p : p + 1], value[1][p : p + 1]

            def table(factors):
                sub = lax.broadcasted_iota(jnp.int32, (8, 128), 0)
                tile = None
                for bit, factor in enumerate(factors):
                    on = lax.rem(lax.div(sub, 2**bit), 2) == 1
                    factor = tuple(jnp.where(on, part, rest) for part, rest in zip(row(factor), (1.0, 0.0)))
                    tile = factor if tile is None else times(tile, factor)
                return tile

            base = table(steps[:3])
            for step in steps[3:6]:
                more = times(base, row(step))
                base = tuple(jnp.concatenate([old, new], axis=0) for old, new in zip(base, more))
            leap = table([steps[6], steps[7], unit])
            leaps[p, 0], leaps[p, 1] = leap
            at = slice(256 * p, 256 * p + 256)
            high, low = split_low(jnp.concatenate(base, axis=1))
            base_high[:, at], base_low[:, at] = high, low
            lead = times(row(coef), leap)
            lead = jnp.concatenate([lead[0], -lead[1]], axis=1)
            first = lax.rem(lax.broadcasted_iota(jnp.int32, (8, 256), 1), 128) < 64
            lead = jnp.concatenate([jnp.where(first, lead, 0.0), jnp.where(first, 0.0, lead)], axis=0)
            lead_high, lead_low = split_low(lead)
            taps_of = dot_nt(
                jnp.concatenate([lead_high, lead_low, lead_high], axis=1), jnp.concatenate([high, high, low], axis=1)
            )
            taps_of = jnp.concatenate([taps_of, taps_of], axis=1)
            lines_f[8 * p : 8 * p + 8], lines_f[8 * p + 64 : 8 * p + 72] = taps_of[:8], taps_of[8:]
        own = jnp.concatenate([lines_f[pl.ds(m, ROWS, stride=8), :][:, :64] for m in range(8)], axis=1)
        kern[z, y, x, c] = (2.0 * own).astype(bf16)

    late = z == 3

    @pl.when(jnp.logical_not(late))
    def _():
        prepare_shares()
        prepare_taps()

    pl.semaphore_wait(barrier, len(peers))

    @pl.when(late)
    def _():
        prepare_shares()

    share_plane = same(share_in.at[z, place], plane_peers + other_peers, share_in.at[0, pl.ds(0, 7)])
    weight_x = same(weight.at[:, z, y, x, c], [x_peer], weight.at[:, 0, 0, 0, 0])

    @pl.when(seq < 3)
    def _():
        right_copies[0].start()

    @pl.when(late)
    def _():
        prepare_taps()

    kern_z = same(kern.at[z, y, x, c], z_peers, kern.at[three, 0, 0, 0])
    finish(share_plane)
    share_z = same(share_in.at[z], z_peers, share_in.at[three])
    finish(weight_x)

    def weight_to_z(q):
        return same(weight.at[q, z, y, :, c], z_peers, weight.at[q, three, 0, :, 0])

    def weight_to_y(q):
        finish(weight_z[q])
        piece = weight.at[q, :, y, :, c]
        same(piece, [core_peer], piece, core_recvs[half_of[q]])
        return same(piece, [y_peer], weight.at[q, :, 0, :, 0])

    def weight_to_core(q):
        finish(weight_y[q])
        piece = weight.at[q, :, flip_y, :, c]
        same(piece, [core_peer], piece, core_recvs[half_of[q]])

    pairs, half_of = ((0, 3), (1, 2)), (0, 1, 1, 0)
    core_recvs = [claim(), claim()]
    weight_core = [(sem, weight.at[pl.ds(0, 2), :, :, :, 0]) for sem in core_recvs]
    weight_z = [weight_to_z(0)]
    last_y = same(weight.at[3, z, y, :, c], [y_peer], weight.at[3, 0, 0, :, 0])

    def last_to_z():
        finish(last_y)
        return same(weight.at[3, z, :, :, c], z_peers, weight.at[3, three, :, :, 0])

    def last_to_core():
        finish(last_z)
        same(weight.at[3, :, :, :, c], [core_peer], weight.at[3, :, :, :, 0], core_recvs[half_of[3]])

    def normalise(source, hat, keep_std, begin, end):
        for first in range(begin, end, 32):
            at = slice(first, first + 32)
            value = source[at, :].astype(f32)
            centered = value - jnp.mean(value, axis=1, keepdims=True)
            scale = lax.rsqrt(jnp.mean(centered * centered, axis=1, keepdims=True) + EPS)
            put(hat, at, centered * scale)
            if keep_std:
                inv_std[at, :] = jnp.broadcast_to(scale, (32, 128))

    loads[0].wait()
    normalise(x_v, x_hat, True, 0, tokens)
    finish(kern_z)
    halves = [pl.ds(0, 2), pl.ds(2, 2)]
    kern_plane = [same(kern.at[at, y, x, c], plane_peers, dk_in2.at[:, at]) for at in halves]

    weight_z.append(weight_to_z(1))
    finish(share_z)
    weight_z.append(weight_to_z(2))
    last_z = last_to_z()

    @pl.when(seq < 3)
    def _():
        right_copies[1].start()

    load_all(10, (pick, mask))
    shares = share_in[...].reshape(32, 1, 128).reshape(32, 128).astype(bf16)
    spread = dot_nn(shares, pick[...]) * mask[...].astype(f32)
    spread = jnp.sum(spread, axis=0, keepdims=True)
    rows_f[...] = jnp.concatenate(
        [spread[:, channels * i : channels * (i + 1)] for i in range(5)] + [jnp.zeros((3, channels), f32)], axis=0
    )
    gain, shift = rows_f[0:1, :], rows_f[1:2, :]

    def every_other(i, parity):
        return pl.ds(128 * i + parity, 64, stride=2)

    def sixty_four(i):
        return pl.ds(pl.multiple_of(64 * i, 64), 64)

    def shifted(i, _):
        at = pl.ds(pl.multiple_of(i * 128, 128), 128)
        put(normed, at, take(x_hat, at) * gain + shift)
        for parity in range(2):
            own_b[parity, sixty_four(i)] = take(normed, every_other(i, parity)).astype(bf16)
        return 0

    lax.fori_loop(0, tokens // 128, shifted, 0)
    load_all(11, (fwd, fwd_most, fwd_rest, inv, turn))
    wide = 256

    def lanes(j):
        return pl.ds(pl.multiple_of(j * wide, wide), wide)

    few = 16

    def sign_of(r):
        return 1 if r < half // 2 else -1

    def turned(value, r, back):
        copies = value[0].shape[1] // 128
        cosine, sine = (jnp.concatenate([turn[i, r : r + few]] * copies, axis=1) for i in range(2))
        return conj_times((cosine, sine), value) if back else times(value, (cosine, sine))

    def transform(block, exact):
        both = jnp.concatenate([block[0], block[1]], axis=1)
        if exact:
            return dot_nn(fwd[...], jnp.concatenate([both, both], axis=0))
        return dot_nn(fwd[:, :half], both)

    def joined(both, r):
        parts = both[r : r + few], both[half + r : half + r + few]
        width = both.shape[1] // 2
        even, odd = [part[:, :width] for part in parts], turned([part[:, width:] for part in parts], r, False)
        return tuple(a + b for a, b in zip(even, odd)), tuple(a - b for a, b in zip(even, odd))

    def places(r):
        return [pl.ds(first + r, few) for first in (0, taps, half, taps + half)]

    def keep(ref, at, r, pair):
        for lines, part in zip(places(r), pair[0] + pair[1]):
            ref[lines, at] = part

    def kept(ref, at, r):
        parts = [ref[lines, at] for lines in places(r)]
        return parts[:2], parts[2:]

    def signal(pair_at, exact):
        real, imag = [], []
        for r in range(0, half, few):
            a, b = pair_at(r)
            even = [x + y for x, y in zip(a, b)]
            odd = turned([x - y for x, y in zip(a, b)], r, True)
            for lines, x, y in zip((real, imag), even, odd):
                both = jnp.concatenate([x, y], axis=1)
                lines.append(split_low(both) if exact else (both.astype(bf16),))
        lines = real + imag
        if exact:
            high, low = (jnp.concatenate([line[i] for line in lines], axis=0) for i in range(2))
            return dot_nn(inv[...], jnp.concatenate([high, high, low], axis=0))
        return dot_nn(inv[:, : 2 * half], jnp.concatenate([line[0] for line in lines], axis=0))

    def each(function, pairs):
        return tuple(function(*values) for values in zip(*pairs))

    def swung(value, sign):
        return (value[1], -value[0]) if sign > 0 else (-value[1], value[0])

    def own_spectrum(j):
        at = lanes(j)
        both = transform((own_b[0, :, at], own_b[1, :, at]), True)
        for r in range(0, half, few):
            keep(u_spec, at, r, joined(both, r))

    own_spectrum(0)
    own_spectrum(1)
    weight_y = [weight_to_y(0)]

    def left_block(i):
        first, last = (0, 3) if i == 0 else (3, 4)
        right_copies[i].wait_recv()
        normalise(left_v, left_hat, False, 128 * first, 128 * last)
        for k in range(first, last):
            for parity in range(2):
                value = take(left_hat, pl.ds(128 * k + parity, 64, stride=2)) * gain + shift
                left_b[parity, 64 * k : 64 * k + 64] = value.astype(bf16)
        at = slice(64 * first, 64 * last)
        matrix = (fwd_most if i == 0 else fwd_rest)[...]
        for j in range(2):
            lane = slice(wide * j, wide * (j + 1))
            both = jnp.concatenate([left_b[0, at, lane], left_b[1, at, lane]], axis=1)
            both = dot_nn(matrix, jnp.concatenate([both, both], axis=0))
            lines = slice(taps * j, taps * (j + 1))
            if i == 0:
                d_spec[lines, :] = both
                continue
            both += d_spec[lines, :]
            for r in range(0, half, few):
                turns = [swung(value, -sign_of(r)) for value in joined(both, r)]
                old = kept(u_spec, lanes(j), r)
                keep(u_spec, lanes(j), r, tuple(tuple(a + b for a, b in zip(x, y)) for x, y in zip(old, turns)))

    @pl.when(seq > 0)
    def _():
        left_block(0)

    @pl.when(seq == 0)
    def _():
        left_hat[...] = jnp.zeros_like(left_hat)

    weight_y.append(weight_to_y(1))
    kern_core = []
    for arrival, at in zip(kern_plane, halves):
        finish(arrival)
        kern_core.append(same(kern.at[at, :, :, c], [core_peer], kern.at[at, :, :, 0]))

    def kernel_transform(j):
        rows = kern[2 * j : 2 * j + 2].reshape(wide, taps)
        rows = [jnp.concatenate([rows[:, at]] * 2, axis=1) for at in (slice(0, half), slice(half, taps))]
        return dot_nt(fwd[...], jnp.concatenate(rows, axis=0))

    def convolve(j, both):
        at = lanes(j)

        def product(r):
            k = joined(both, r)
            keep(k_spec, at, r, k)
            return each(times, (k, kept(u_spec, at, r)))

        both = signal(product, True)
        for parity in range(2):
            put(mixed, pl.ds(parity, half, stride=2), both[:, wide * parity : wide * (parity + 1)], 2 * j)

    def activate(j):
        for tile in (2 * j, 2 * j + 1):
            at = slice(128 * tile, 128 * tile + 128)
            for start_at in range(0, tokens, 128):
                lines = slice(start_at, start_at + 128)
                value = mixed[tile, lines, :] + rows_f[2:3, at] * normed[tile, lines, :]
                chance = 0.5 + 0.5 * lax.erf(value * (0.5**0.5))
                slope[lines, at] = chance + value * jnp.exp(value * value * -0.5 - 0.5 * float(np.log(2.0 * np.pi)))
                low = (value * chance).astype(bf16)
                activ[lines, at] = low
                activ_t[at, lines] = low.T

    for j in range(2):
        finish(kern_core[j])
        k_raw[j] = kernel_transform(j)
        if j == 0:
            weight_y.append(weight_to_y(2))

    @pl.when(seq > 0)
    def _():
        left_block(1)

    weight_to_core(0)
    convolve(0, k_raw[0])
    weight_to_core(1)
    last_to_core()
    convolve(1, k_raw[1])
    activate(0)
    activate(1)
    weight_to_core(2)
    loads[-1].wait()

    def matrix_of(h):
        return jnp.concatenate([weight[q].reshape(channels, 256) for q in pairs[h]], axis=1)

    def gates(h, pre):
        lines_out = []
        sums = [jnp.zeros((32, 128), f32) for _ in range(4)]
        for start_at in range(0, tokens, 32):
            lines = slice(start_at, start_at + 32)
            low = []
            for i, q in enumerate(pairs[h]):
                at = slice(128 * q, 128 * q + 128)
                lin = pre[lines, 256 * i : 256 * i + 128] + rows_f[3:4, at]
                gate = 0.5 + 0.5 * jnp.tanh(0.5 * (pre[lines, 256 * i + 128 : 256 * i + 256] + rows_f[4:5, at]))
                grad = g_v[lines, at].astype(f32)
                product = lin * gate
                res_v[lines, at] = (x_v[lines, at].astype(f32) + product).astype(bf16)
                low += [(grad * gate).astype(bf16), (grad * (product - product * gate)).astype(bf16)]
            sums = [total + part.astype(f32) for total, part in zip(sums, low)]
            lines_out.append(jnp.concatenate(low, axis=1))
        for i, q in enumerate(pairs[h]):
            for k in range(2):
                rows_f[3 + k : 4 + k, 128 * q : 128 * q + 128] = jnp.sum(sums[2 * i + k], axis=0, keepdims=True)
        return jnp.concatenate(lines_out, axis=0)

    def weight_grad(h, low):
        grad = dot_nn(activ_t[...], low).astype(bf16)
        for i, q in enumerate(pairs[h]):
            dw_own[q] = grad[:, 256 * i : 256 * i + 256].reshape(4, 2, 2, 2, ROWS, 256)
            start([(dw_own.at[q, :, :, :, flip_c], dw_in1.at[q], core_peer)], dw_in1.at[q], dw_recvs[h])

    def mix_grad(d_act):
        total = jnp.zeros((32, channels), f32)
        for start_at in range(0, tokens, 32):
            lines = slice(start_at, start_at + 32)
            mix = (d_act[lines] * slope[lines, :]).astype(bf16).astype(f32)
            total += mix * take(normed, lines)
            put(mixed, lines, mix)
        rows_f[2:3, :] = jnp.sum(total, axis=0, keepdims=True)
        for parity in range(2):
            for start_at in range(0, half, 64):
                part = take(mixed, pl.ds(2 * start_at + parity, 64, stride=2))
                d_mix[parity, start_at : start_at + 64] = part.astype(bf16)

    def core_sum(q):
        if half_of[q] not in summed:
            summed.add(half_of[q])
            arrive(dw_recvs[half_of[q]], dw_in1.at[pl.ds(0, 2)])
        dw_mid[q] = (dw_own[q, :, :, :, c].astype(f32) + dw_in1[q].astype(f32)).astype(bf16)

    def to_y(q):
        core_sum(q)
        dw_y[q] = start([(dw_mid.at[q, :, flip_y], dw_in2.at[q], y_peer)], dw_in2.at[q])

    def end_to_z(q):
        core_sum(q)
        copies = [(dw_mid.at[q, peer[0]], end_in1.at[q, i], peer) for i, peer in enumerate(z_peers)]
        end_z[q] = start(copies, end_in1.at[q])

    def end_to_plane(q):
        finish(end_z[q])
        total = dw_mid[q, z].astype(f32)
        for i in range(3):
            total = total + end_in1[q, i].astype(f32)
        end_mid[q] = total.astype(bf16)
        copies = [(end_mid.at[q, peer[1], peer[2]], end_in2.at[q, i], peer) for i, peer in enumerate(plane_peers)]
        end_plane[q] = start(copies, end_in2.at[q])

    def write_out(q, total):
        dw_ref[:, 128 * q : 128 * q + 128] = total[:, :128]
        dw_ref[:, channels + 128 * q : channels + 128 * q + 128] = total[:, 128:]

    def end_of(q):
        finish(end_plane[q])
        total = end_mid[q, y, x].astype(f32)
        for i in range(3):
            total = total + end_in2[q, i].astype(f32)
        write_out(q, total)

    def to_z(q):
        finish(dw_y[q])
        dw_low[q] = (dw_mid[q, :, y].astype(f32) + dw_in2[q].astype(f32)).astype(bf16)
        copies = [(dw_low.at[q, peer[0]], dw_in3.at[q, i], peer) for i, peer in enumerate(z_peers)]
        dw_z[q] = start(copies, dw_in3.at[q])

    def to_x(q):
        finish(dw_z[q])
        total = dw_low[q, z].astype(f32)
        for i in range(3):
            total = total + dw_in3[q, i].astype(f32)
        dw_end[q] = total.astype(bf16)
        dw_x[q] = start([(dw_end.at[q, flip_x], dw_in4.at[q], x_peer)], dw_in4.at[q])

    def to_end(q):
        finish(dw_x[q])
        write_out(q, dw_end[q, x].astype(f32) + dw_in4[q].astype(f32))

    skip = rows_f[2:3, :]
    dw_y, dw_z, dw_x, end_z, end_plane, summed = {}, {}, {}, {}, {}, set()
    phase[0], dw_recvs = "reduce", [claim(), claim()]
    finish(weight_core[0])
    first_low = gates(0, dot_nn(activ[...], matrix_of(0)))
    weight_grad(0, first_low)
    finish(weight_core[1])
    second_low = gates(1, dot_nn(activ[...], matrix_of(1)))
    d_act = dot_nt(
        jnp.concatenate([first_low, second_low], axis=1), jnp.concatenate([matrix_of(0), matrix_of(1)], axis=1)
    )
    mix_grad(d_act)
    left_pieces = ((0, 256), (256, 256))
    left_copies = [
        pltpu.make_async_remote_copy(
            src_ref=d_mix.at[:, :, pl.ds(first, width)], dst_ref=right_v.at[:, :, pl.ds(first, width)], send_sem=left_sender,
            recv_sem=claim(), device_id=(dp, seq - 1), device_id_type=MESH,
        )
        for first, width in left_pieces
    ]

    @pl.when(seq > 0)
    def _():
        for copy in left_copies[:1]:
            copy.start()

    to_y(0)
    end_to_z(3)
    weight_grad(1, second_low)

    def mix_transform(j):
        at = lanes(j)
        return transform((d_mix[0, :, at], d_mix[1, :, at]), False)

    def kernel_grad(j, both):
        at = lanes(j)

        def product(r):
            d = joined(both, r)
            keep(d_spec, at, r, d)
            return each(conj_times, (kept(u_spec, at, r), d))

        both = signal(product, False)
        grad = jnp.concatenate([both[:, :wide].T, both[:, wide:].T], axis=1).reshape(2, 2, 2, 2, ROWS, taps)
        dk_own[2 * j : 2 * j + 2] = grad
        dk_low[2 * j : 2 * j + 2] = grad.astype(bf16)

    def kernel_middle():
        finish(dk_core)
        for i in range(4):
            total = dk_own[i, :, :, c] + dk_in1[i].astype(f32)
            dk_mid[i] = total
            dk_cut[i] = total.astype(bf16)
        return start([(dk_cut.at[:, peer[1], peer[2]], dk_in2.at[i], peer) for i, peer in enumerate(plane_peers)], dk_in2)

    def kernel_end():
        finish(dk_plane)
        for i in range(4):
            total = dk_mid[i, y, x]
            for k in range(3):
                total = total + dk_in2[k, i].astype(f32)
            dk_end[i] = total
            dk_out[i] = total.astype(bf16)
        return start([(dk_out.at[peer[0]], dk_in3.at[i], peer) for i, peer in enumerate(z_peers)], dk_in3)

    def own_grad(j):
        at = lanes(j)

        def product(r):
            return each(conj_times, (kept(k_spec, at, r), kept(d_spec, at, r)))

        def shifted_product(r):
            return tuple(swung(value, sign_of(r)) for value in product(r))

        own, back = signal(product, False), signal(shifted_product, False)
        d_gain, d_shift = jnp.zeros((1, wide), f32), jnp.zeros((1, wide), f32)
        for parity in range(2):
            lines = pl.ds(parity, half, stride=2)
            columns = slice(wide * parity, wide * (parity + 1))
            grad = own[:, columns] + rows_f[5:6, at] * d_mix[parity, :, at].astype(f32)
            put(d_norm, lines, grad, 2 * j)
            before = jnp.where(seq > 0, back[:, columns], 0.0)
            d_gain += jnp.sum(
                grad * take(x_hat, lines, 2 * j, 2) + before * take(left_hat, lines, 2 * j, 2), axis=0, keepdims=True
            )
            d_shift += jnp.sum(grad + before, axis=0, keepdims=True)
        rows_f[6:7, at], rows_f[7:8, at] = d_gain, d_shift

    def right_grad(i):
        first, width = left_pieces[i]
        at = slice(first, first + width)
        left_copies[i].wait_recv()
        both = transform((right_v[0, :, at], right_v[1, :, at]), False)

        def product(r):
            turns = [swung(value, sign_of(r)) for value in joined(both, r)]
            return each(conj_times, (kept(k_spec, at, r), turns))

        both = signal(product, False)
        for parity in range(2):
            lines = pl.ds(parity, half, stride=2)
            more = both[:, width * parity : width * (parity + 1)]
            put(d_norm, lines, take(d_norm, lines, first // 128, width // 128) + more, first // 128)

    rows_f[5:6, :] = skip
    first_half, second_half = mix_transform(0), mix_transform(1)
    kernel_grad(0, first_half)
    kernel_grad(1, second_half)
    dk_core = start([(dk_low.at[:, :, :, flip_c], dk_in1, core_peer)], dk_in1)
    end_to_z(1)
    to_y(2)
    own_grad(0)
    dk_plane = kernel_middle()

    @pl.when(seq > 0)
    def _():
        for copy in left_copies[1:]:
            copy.start()

    own_grad(1)
    to_z(0)
    vector = jnp.concatenate([rows_f[6:7, :], rows_f[7:8, :], rows_f[2:3, :], rows_f[3:4, :], rows_f[4:5, :]], axis=1)
    high, low = split_low(jnp.broadcast_to(vector, mask.shape) * mask[...].astype(f32))
    shares = dot_nt(high, pick[...]) + dot_nt(low, pick[...])
    share_out[...] = shares.reshape(32, 1, 128).reshape(4, 8, 1, 128)
    copies = [(share_out.at[peer[0]], share_in1.at[i], peer) for i, peer in enumerate(z_peers)]
    share_z = start(copies, share_in1)
    @pl.when(seq < 3)
    def _():
        right_grad(0)

    to_z(2)
    end_to_plane(3)
    dk_z = kernel_end()
    end_to_plane(1)
    to_x(0)
    finish(share_z)
    share_mid[...] = share_out[z] + share_in1[0] + share_in1[1] + share_in1[2]
    copies = [
        (share_mid.at[(peer[1] * 2 + peer[2]) * 2 + peer[3]], share_in2.at[i], peer)
        for i, peer in enumerate(plane_peers + other_peers)
    ]
    share_plane = start(copies, share_in2)

    @pl.when(seq < 3)
    def _():
        for i in range(1, len(left_pieces)):
            right_grad(i)

    to_x(2)

    @pl.when(seq < 3)
    def _():
        arrive(right_sender, x_v)

    @pl.when(seq > 0)
    def _():
        arrive(left_sender, d_mix)

    for first in range(0, tokens, 32):
        at = slice(first, first + 32)
        hat = [x_hat[i, at, :] for i in range(4)]
        grad = [d_norm[i, at, :] * rows_f[0:1, 128 * i : 128 * i + 128] for i in range(4)]
        mean = jnp.sum(sum(grad[1:], grad[0]), axis=1, keepdims=True) * (1.0 / channels)
        along = [one * other for one, other in zip(grad, hat)]
        along = jnp.sum(sum(along[1:], along[0]), axis=1, keepdims=True) * (1.0 / channels)
        for i in range(4):
            lane = slice(128 * i, 128 * i + 128)
            inner = inv_std[at, :] * (grad[i] - mean - hat[i] * along)
            gin_v[at, lane] = (inner + g_v[at, lane].astype(f32)).astype(bf16)
    dt, a, unit, norm_sq, ratio, coef, scaled = mode_terms(ldt_ref[...], lar_ref[...], ai_ref[...], cc_ref[...])
    inverse_a = (a[0] / norm_sq, -a[1] / norm_sq)
    end_of(3)
    end_of(1)
    to_end(0)
    finish(dk_z)
    d_kernel = dk_end[z]
    for k in range(3):
        d_kernel = d_kernel + dk_in3[k].astype(f32)

    for m in range(8):
        block = d_kernel[:, 64 * m : 64 * m + 64]
        block = jnp.concatenate([block, block], axis=1)
        for k in range(2):
            lines_f[pl.ds(8 * k + m, 8, stride=16), :] = block[8 * k : 8 * k + 8]
    at_row = lax.broadcasted_iota(jnp.int32, (8, 128), 0)
    first = lax.broadcasted_iota(jnp.int32, (8, 128), 1) < 64
    leap_of = (128 * lax.rem(at_row, 4) + lax.div(at_row, 4)).astype(f32)
    ramp = (2 * lax.broadcasted_iota(jnp.int32, (32, 64), 1)).astype(f32)
    sums = []
    for pair in range(4):
        plain = lines_f[32 * pair : 32 * pair + 32, :][:, :64]
        high, low = split_low(jnp.concatenate([plain, plain * ramp], axis=0))
        at = slice(512 * pair, 512 * pair + 512)
        table = jnp.concatenate([base_high[:, at], base_low[:, at], base_high[:, at]], axis=0)
        sums.append(dot_nn(jnp.concatenate([high, high, low], axis=1), table))
    zero = jnp.zeros((8, 128), f32)
    s0, s1 = [zero, zero], [zero, zero]
    for p in range(8):
        def part_of(begin, part):
            lane = 256 * (p % 2) + 128 * part
            block = sums[p // 2][begin + 16 * (p % 2) : begin + 16 * (p % 2) + 16, lane : lane + 128]
            return jnp.where(first, block[:8], block[8:])

        value, slope_of = [part_of(0, part) for part in range(2)], [part_of(32, part) for part in range(2)]
        leap = (leaps[p, 0], leaps[p, 1])
        slope_of = [one + leap_of * other for one, other in zip(slope_of, value)]
        for total, terms in ((s0, value), (s1, slope_of)):
            for part, product in enumerate(times(leap, terms)):
                total[part] = jnp.where(at_row == p, jnp.sum(product, axis=0, keepdims=True), total[part])
    d_coef = times(s0, ratio)
    half_g = times(times(coef, s0), times(unit, inverse_a))
    ramp_part = times(scaled, s1)
    half_g = (half_g[0] + ramp_part[0], half_g[1] + ramp_part[1])
    back = times(times(scaled, s0), inverse_a)
    q = (half_g[0] * dt - back[0], half_g[1] * dt - back[1])
    d_dt = 2.0 * dt * times(half_g, a)[0]
    dldt_ref[...] = row_of(jnp.sum(unpair_lanes(d_dt), axis=1, keepdims=True))[0]
    dlar_ref[...] = unpair_lanes(2.0 * q[0] * a[0])
    dai_ref[...] = unpair_lanes(-2.0 * q[1])
    dcc_ref[...] = jnp.concatenate([unpair_lanes(2.0 * d_coef[0]), unpair_lanes(-2.0 * d_coef[1])], axis=1)

    to_end(2)
    finish(share_plane)
    small = share_mid[place]
    for i in range(7):
        small = small + share_in2[i]
    for i, target in enumerate([dgain_ref, dshift_ref, dskip_ref]):
        target[...] = small[0, ROWS * i : ROWS * (i + 1)]
    dbias_ref[...] = small[0, 3 * ROWS : 5 * ROWS]
    arrive(sends.at[0], u_spec.at[pl.ds(0, sent["gather"] // (4 * channels)), :])
    arrive(sends.at[1], u_spec.at[pl.ds(0, sent["reduce"] // (4 * channels)), :])
    arrive(sends.at[2], vector_rows.at[pl.ds(0, sent["vector"] // 512)])


def finish_kernel(*refs):
    count = len(refs) // 2
    sems = refs[-1]
    copies = [pltpu.make_async_copy(refs[i], refs[count + i], sems.at[i]) for i in range(count)]
    for copy in copies:
        copy.start()
    for copy in copies:
        copy.wait()


def kernel_body(
    inputs, grad_out, ln_gain, ln_bias, skip_scale, w_glu, b_glu, log_dt, log_a_real, a_imag, c_coef
):
    _, tokens, channels = inputs.shape
    taps = KTAPS
    glu = w_glu.shape[1]
    f32, bf16 = jnp.float32, jnp.bfloat16
    order = np.concatenate([np.arange(0, taps // 2, 2), np.arange(1, taps // 2, 2)]) + 0.5
    angle = np.outer(order, np.arange(taps // 2)) * (2 * np.pi / taps)
    matrix = np.concatenate([np.cos(angle), -np.sin(angle)], axis=0)
    high = matrix.astype(bf16)
    low = (matrix - high.astype(np.float64)).astype(bf16)
    forward = np.concatenate([high, low], axis=1)
    cut = 3 * taps // 8
    most, rest = (np.concatenate([part[:, at] for part in (high, low)], axis=1) for at in (slice(0, cut), slice(cut, None)))
    scale = np.asarray(1.0 / taps, bf16)
    inverse = np.concatenate([high.T, low.T, high.T], axis=1) * scale
    turns = np.stack([np.cos(order * (np.pi / taps)), -np.sin(order * (np.pi / taps))])
    turns = np.ascontiguousarray(np.broadcast_to(turns[:, :, None], (2, taps // 2, 128))).astype(np.float32)
    device_at, lane = np.arange(32)[:, None], np.arange(channels)[None, :]
    bias_lane = np.arange(2 * channels)[None, :]
    row = np.arange(128)[:, None]
    pick = np.concatenate(
        [row == i * ROWS + lane % ROWS for i in range(3)] + [row == 3 * ROWS + bias_lane % (2 * ROWS)], axis=1
    ).astype(bf16)
    mask = np.concatenate(
        [device_at == lane // ROWS] * 3 + [device_at == bias_lane // (2 * ROWS)], axis=1
    ).astype(bf16)
    hbm, vmem = pl.BlockSpec(memory_space=pl.ANY), pl.BlockSpec(memory_space=pltpu.VMEM)
    block = (tokens, channels)
    spec, tall = (2 * taps, channels), (channels // 128, tokens, 128)

    def space(*dims, kind=f32):
        return pltpu.VMEM(dims, kind)

    results = (
        (block, bf16), (block, bf16), ((ROWS,), f32), ((ROWS,), f32), ((ROWS,), f32), (w_glu.shape, f32),
        ((2 * ROWS,), f32), ((ROWS,), f32), (log_a_real.shape, f32), (a_imag.shape, f32), (c_coef.shape, f32),
    )
    outs = pl.pallas_call(
        layer_kernel,
        name="layer",
        out_shape=tuple(pltpu.VMEM(dims, kind) for dims, kind in results),
        in_specs=[hbm] * 18,
        out_specs=(vmem,) * len(results),
        scratch_shapes=[
            space(*w_glu.shape), space(1, ROWS), space(1, ROWS), space(1, ROWS), space(1, 2 * ROWS), space(1, ROWS),
            space(*log_a_real.shape), space(*a_imag.shape), space(*c_coef.shape),
            space(*block, kind=bf16), space(*block, kind=bf16), space(*block, kind=bf16),
            space(*forward.shape, kind=bf16), space(*most.shape, kind=bf16), space(*rest.shape, kind=bf16),
            space(*inverse.shape, kind=bf16),
            space(*pick.shape, kind=bf16), space(*mask.shape, kind=bf16), space(*turns.shape),
            space(4, 2, 2, 2, ROWS, taps, kind=bf16), space(4, 4, 2, 2, 2, ROWS, 256, kind=bf16),
            space(64, 2048, kind=bf16), space(64, 2048, kind=bf16), space(8, 2, 8, 128), space(8 * ROWS, 128),
            space(4, 8, 1, 128), space(4, 8, 1, 128), space(3, 8, 1, 128), space(8, 1, 128), space(7, 1, 128),
            space(64, 1, 128),
            space(8, channels),
            space(*tall), space(tokens, 128), space(*tall), space(*tall),
            space(2, tokens // 2, channels, kind=bf16), space(2, tokens // 2, channels, kind=bf16),
            space(2, taps, taps), space(*spec), space(*spec), space(*tall), space(*block),
            space(*block, kind=bf16), space(channels, tokens, kind=bf16),
            space(2, tokens // 2, channels, kind=bf16), space(2, tokens // 2, channels, kind=bf16),
            space(*spec), space(*tall),
            space(4, 4, 2, 2, 2, ROWS, 256, kind=bf16), space(4, 4, 2, 2, ROWS, 256, kind=bf16),
            space(4, 4, 2, 2, ROWS, 256, kind=bf16), space(4, 4, 2, ROWS, 256, kind=bf16),
            space(4, 4, 2, ROWS, 256, kind=bf16), space(4, 3, 2, ROWS, 256, kind=bf16),
            space(4, 2, ROWS, 256, kind=bf16), space(4, ROWS, 256, kind=bf16),
            space(4, 3, 2, 2, ROWS, 256, kind=bf16), space(4, 2, 2, ROWS, 256, kind=bf16), space(4, 3, ROWS, 256, kind=bf16),
            space(4, 2, 2, 2, ROWS, taps), space(4, 2, 2, 2, ROWS, taps, kind=bf16), space(4, 2, 2, ROWS, taps, kind=bf16),
            space(4, 2, 2, ROWS, taps), space(4, 2, 2, ROWS, taps, kind=bf16), space(3, 4, ROWS, taps, kind=bf16),
            space(4, ROWS, taps), space(4, ROWS, taps, kind=bf16), space(3, ROWS, taps, kind=bf16),
            pltpu.SemaphoreType.DMA((13,)), pltpu.SemaphoreType.DMA((5,)), pltpu.SemaphoreType.DMA((39,)),
        ],
        compiler_params=pltpu.CompilerParams(
            collective_id=0, has_side_effects=True, vmem_limit_bytes=48 * 2**20
        ),
    )(*[
        pltpu.with_memory_space_constraint(value, pltpu.HBM)
        for value in (
            inputs.reshape(block), grad_out.reshape(block), forward, most, rest, inverse, pick, mask, turns, w_glu,
            ln_gain.reshape(1, -1), ln_bias.reshape(1, -1), skip_scale.reshape(1, -1), b_glu.reshape(1, -1),
            log_dt.reshape(1, -1), log_a_real, a_imag, c_coef,
        )
    ])
    ended = pl.pallas_call(
        finish_kernel,
        name="finish",
        out_shape=tuple(jax.ShapeDtypeStruct(dims, kind) for dims, kind in results),
        in_specs=[vmem] * len(results),
        out_specs=(hbm,) * len(results),
        scratch_shapes=[pltpu.SemaphoreType.DMA((len(results),))],
    )(*[pltpu.with_memory_space_constraint(value, pltpu.VMEM) for value in outs])
    return (ended[0].reshape(inputs.shape), ended[1].reshape(inputs.shape)) + tuple(ended[2:])


def solution(mesh):
    in_specs = (
        P("dp", "seq", None),
        P("dp", "seq", None),
        P(("dp", "seq")),
        P(("dp", "seq")),
        P(("dp", "seq")),
        P(("dp", "seq"), None),
        P(("dp", "seq")),
        P(("dp", "seq")),
        P(("dp", "seq"), None),
        P(("dp", "seq"), None),
        P(("dp", "seq"), None),
    )
    out_specs = (
        P("dp", "seq", None),
        P("dp", "seq", None),
        P(("dp", "seq")),
        P(("dp", "seq")),
        P(("dp", "seq")),
        P(("dp", "seq"), None),
        P(("dp", "seq")),
        P(("dp", "seq")),
        P(("dp", "seq"), None),
        P(("dp", "seq"), None),
        P(("dp", "seq"), None),
    )
    quick = mesh.shape["dp"] == 8 and mesh.shape["seq"] == 4
    return jax.shard_map(kernel_body if quick else body, mesh=mesh, in_specs=in_specs, out_specs=out_specs, check_vma=False)
```

```python
import math
from functools import partial

import jax
import jax.numpy as jnp
import numpy as np
from jax import lax
from jax.experimental import pallas as pl
from jax.experimental.pallas import tpu as pltpu
from jax.sharding import PartitionSpec as P

KTAPS = 512


EPS = 1e-05


def passed_along(value, axis, steps):
    count = lax.axis_size(axis)
    first, last = (max(0, -steps), min(count, count - steps))
    return lax.ppermute(value, axis, [(source, source + steps) for source in range(first, last)])


def kernel_block(log_dt, log_a_real, a_imag, c_coef, start, count):
    mode_count = log_a_real.shape[1]
    step_size = jnp.exp(log_dt)[:, None]
    a_real = -jnp.exp(log_a_real)
    decay = a_real * step_size
    turn = a_imag * step_size
    growth = jnp.exp(decay)
    ex_re = growth * jnp.cos(turn) - 1.0
    ex_im = growth * jnp.sin(turn)
    norm_sq = a_real * a_real + a_imag * a_imag
    ratio_re = (ex_re * a_real + ex_im * a_imag) / norm_sq
    ratio_im = (ex_im * a_real - ex_re * a_imag) / norm_sq
    c_re = c_coef[:, :mode_count]
    c_im = c_coef[:, mode_count:]
    coef_re = c_re * ratio_re - c_im * ratio_im
    coef_im = c_re * ratio_im + c_im * ratio_re
    places = (start + jnp.arange(count)).astype(jnp.float32)
    phase = turn[:, :, None] * places
    damping = jnp.exp(decay[:, :, None] * places)
    terms = damping * (coef_re[:, :, None] * jnp.cos(phase) - coef_im[:, :, None] * jnp.sin(phase))
    return 2.0 * jnp.sum(terms, axis=1)


def transforms(taps):
    angle = np.outer(np.arange(taps) + 0.5, np.arange(taps)) * (np.pi / taps)
    forward = np.concatenate([np.cos(angle), -np.sin(angle)], axis=0)
    inverse = forward.T / taps
    return forward.astype(jnp.bfloat16), inverse.astype(jnp.bfloat16)


def body(
    inputs, grad_out, ln_gain, ln_bias, skip_scale, w_glu, b_glu, log_dt, log_a_real, a_imag, c_coef
):
    seq_count, own_len, channels = inputs.shape
    gain_low = ln_gain.astype(jnp.bfloat16)
    shift_low = ln_bias.astype(jnp.bfloat16)
    skip_low = skip_scale.astype(jnp.bfloat16)
    weight_low = w_glu.astype(jnp.bfloat16)
    bias_low = b_glu.astype(jnp.bfloat16)
    mode_own = (log_dt, log_a_real, a_imag, c_coef)
    own_kernel = kernel_block(*mode_own, 0, KTAPS).astype(jnp.bfloat16)
    gathered = (
        lax.all_gather(gain_low, ("dp", "seq"), axis=0, tiled=True),
        lax.all_gather(shift_low, ("dp", "seq"), axis=0, tiled=True),
        lax.all_gather(skip_low, ("dp", "seq"), axis=0, tiled=True),
        lax.all_gather(weight_low, ("dp", "seq"), axis=0, tiled=True),
        lax.all_gather(bias_low, ("dp", "seq"), axis=0, tiled=True),
        lax.all_gather(own_kernel, ("dp", "seq"), axis=0, tiled=True),
    )
    kernel_b = gathered[5]
    taps = own_len
    forward, inverse = transforms(taps)
    sign = jnp.where(jnp.arange(taps) % 2 == 0, 1.0, -1.0).astype(jnp.float32)[:, None]

    def to_spectrum(block):
        both = jnp.dot(forward, block, preferred_element_type=jnp.float32)
        return both[:taps], both[taps:]

    def from_spectrum(real, imag):
        both = jnp.concatenate([real, imag], axis=0).astype(jnp.bfloat16)
        return jnp.dot(inverse, both, preferred_element_type=jnp.float32)

    kernel_re, kernel_im = to_spectrum(kernel_b.T)
    gain_full = gathered[0].astype(jnp.float32)
    shift_full = gathered[1].astype(jnp.float32)
    skip_full = gathered[2].astype(jnp.float32)
    weight_b = gathered[3]
    glu_bias = gathered[4].astype(jnp.float32)
    x_float = inputs.astype(jnp.float32)
    row_mean = jnp.mean(x_float, axis=-1, keepdims=True)
    centered = x_float - row_mean
    row_var = jnp.mean(centered * centered, axis=-1, keepdims=True)
    inv_std = lax.rsqrt(row_var + EPS)
    x_hat = centered * inv_std
    normed = x_hat * gain_full + shift_full
    normed_b = normed.astype(jnp.bfloat16)
    own_re, own_im = to_spectrum(normed_b[0])
    left_re, left_im = to_spectrum(passed_along(normed_b, "seq", 1)[0])
    source_re = own_re - sign * left_im
    source_im = own_im + sign * left_re
    conv = from_spectrum(
        kernel_re * source_re - kernel_im * source_im,
        kernel_re * source_im + kernel_im * source_re,
    )
    mixed_pre = conv[None] + skip_full * normed
    activ, gelu_pull = jax.vjp(partial(jax.nn.gelu, approximate=False), mixed_pre)
    activ_b = activ.astype(jnp.bfloat16)
    glu_pre = (
        jnp.einsum("slh,hg->slg", activ_b, weight_b, preferred_element_type=jnp.float32) + glu_bias
    )
    half_dim = glu_pre.shape[-1] // 2
    lin_part = glu_pre[..., :half_dim]
    gate_sig = jax.nn.sigmoid(glu_pre[..., half_dim:])
    result = (x_float + lin_part * gate_sig).astype(jnp.bfloat16)
    grad_f = grad_out.astype(jnp.float32)
    d_pre = jnp.concatenate(
        [grad_f * gate_sig, grad_f * lin_part * gate_sig * (1.0 - gate_sig)], axis=-1
    ).astype(jnp.bfloat16)
    d_weight = jnp.einsum("slh,slg->hg", activ_b, d_pre, preferred_element_type=jnp.float32)
    d_glu_bias = jnp.sum(d_pre.astype(jnp.float32), axis=(0, 1))
    d_act = jnp.einsum("slg,hg->slh", d_pre, weight_b, preferred_element_type=jnp.float32)
    d_mix = gelu_pull(d_act)[0].astype(jnp.bfloat16)
    d_mix_f = d_mix.astype(jnp.float32)
    d_skip = jnp.sum(d_mix_f * normed, axis=(0, 1))
    mix_re, mix_im = to_spectrum(d_mix[0])
    d_kernel = from_spectrum(
        source_re * mix_re + source_im * mix_im, source_re * mix_im - source_im * mix_re
    ).T
    right_re, right_im = to_spectrum(passed_along(d_mix, "seq", -1)[0])
    sum_re = mix_re + sign * right_im
    sum_im = mix_im - sign * right_re
    d_conv = from_spectrum(
        kernel_re * sum_re + kernel_im * sum_im, kernel_re * sum_im - kernel_im * sum_re
    )[None]
    d_normed = d_conv + skip_full * d_mix_f
    d_gain = jnp.sum(d_normed * x_hat, axis=(0, 1))
    d_shift = jnp.sum(d_normed, axis=(0, 1))
    scaled = d_normed * gain_full
    d_input = (
        inv_std
        * (
            scaled
            - jnp.mean(scaled, axis=-1, keepdims=True)
            - x_hat * jnp.mean(scaled * x_hat, axis=-1, keepdims=True)
        )
        + grad_f
    )
    grad_in = d_input.astype(jnp.bfloat16)
    summed = (
        lax.psum_scatter(d_gain, ("dp", "seq"), scatter_dimension=0, tiled=True),
        lax.psum_scatter(d_shift, ("dp", "seq"), scatter_dimension=0, tiled=True),
        lax.psum_scatter(d_skip, ("dp", "seq"), scatter_dimension=0, tiled=True),
        lax.psum_scatter(d_weight, ("dp", "seq"), scatter_dimension=0, tiled=True),
        lax.psum_scatter(d_glu_bias, ("dp", "seq"), scatter_dimension=0, tiled=True),
        lax.psum_scatter(d_kernel, ("dp", "seq"), scatter_dimension=0, tiled=True),
    )
    _, own_pull = jax.vjp(partial(kernel_block, start=0, count=KTAPS), *mode_own)
    mode_grads = own_pull(summed[5])
    return (
        result,
        grad_in,
        summed[0],
        summed[1],
        summed[2],
        summed[3],
        summed[4],
        mode_grads[0],
        mode_grads[1],
        mode_grads[2],
        mode_grads[3],
    )


MESH = pl.DeviceIdType.MESH
ROWS = 16


def pair_lanes(value):
    return jnp.concatenate([value[:8], value[8:]], axis=1)


def unpair_lanes(value):
    half = value.shape[1] // 2
    return jnp.concatenate([value[:, :half], value[:, half:]], axis=0)


def column_of(row):
    n = row.shape[1]
    at = lax.broadcasted_iota(jnp.int32, (n, n), 0) == lax.broadcasted_iota(jnp.int32, (n, n), 1)
    return jnp.sum(jnp.where(at, jnp.broadcast_to(row, (n, n)), 0.0), axis=1, keepdims=True)


def row_of(column):
    n = column.shape[0]
    at = lax.broadcasted_iota(jnp.int32, (n, n), 0) == lax.broadcasted_iota(jnp.int32, (n, n), 1)
    return jnp.sum(jnp.where(at, jnp.broadcast_to(column, (n, n)), 0.0), axis=0, keepdims=True)


def mode_terms(ldt, lar, ai, cc):
    n_modes = lar.shape[1]
    dt = column_of(jnp.exp(ldt))
    dt = jnp.concatenate(
        [jnp.broadcast_to(dt[:8], (8, n_modes)), jnp.broadcast_to(dt[8:], (8, n_modes))], axis=1
    )
    a_re, a_im = -jnp.exp(pair_lanes(lar)), pair_lanes(ai)
    decay, turn = a_re * dt, a_im * dt
    growth = jnp.exp(decay)
    z_re, z_im = growth * jnp.cos(turn), growth * jnp.sin(turn)
    ex_re, ex_im = z_re - 1.0, z_im
    norm_sq = a_re * a_re + a_im * a_im
    r_re = (ex_re * a_re + ex_im * a_im) / norm_sq
    r_im = (ex_im * a_re - ex_re * a_im) / norm_sq
    c_re, c_im = pair_lanes(cc[:, :n_modes]), pair_lanes(cc[:, n_modes:])
    w_re, w_im = c_re * r_re - c_im * r_im, c_re * r_im + c_im * r_re
    return dt, (a_re, a_im), (z_re, z_im), norm_sq, (r_re, r_im), (c_re, c_im), (w_re, w_im)


def times(a, b):
    return a[0] * b[0] - a[1] * b[1], a[0] * b[1] + a[1] * b[0]


def conj_times(a, b):
    return a[0] * b[0] + a[1] * b[1], a[0] * b[1] - a[1] * b[0]


def split_low(value):
    high = value.astype(jnp.bfloat16)
    return high, (value - high.astype(jnp.float32)).astype(jnp.bfloat16)


def dot_nn(a, b):
    return lax.dot_general(a, b, (((1,), (0,)), ((), ())), preferred_element_type=jnp.float32)


def dot_nt(a, b):
    return lax.dot_general(a, b, (((1,), (1,)), ((), ())), preferred_element_type=jnp.float32)


def layer_kernel(
    x_hbm, g_hbm, fwd_hbm, most_hbm, rest_hbm, inv_hbm, pick_hbm, mask_hbm,
    w_hbm, gain_hbm, shift_hbm, skip_hbm, bias_hbm, ldt_hbm, lar_hbm, ai_hbm, cc_hbm,
    res_v, gin_v, dgain_ref, dshift_ref, dskip_ref, dw_ref, dbias_ref, dldt_ref, dlar_ref, dai_ref, dcc_ref,
    w_ref, gain_ref, shift_ref, skip_ref, bias_ref, ldt_ref, lar_ref, ai_ref, cc_ref,
    x_v, g_v, left_v, fwd, fwd_most, fwd_rest, inv, pick, mask, kern, weight, base_high, base_low, leaps, lines_f,
    share_in, share_out, share_in1, share_mid, share_in2, vector_rows, rows_f, x_hat, inv_std, left_hat, normed, own_b, left_b,
    k_raw, k_spec, u_spec, mixed, slope, activ, activ_t, d_mix, right_v, d_spec, d_norm,
    dw_own, dw_in1, dw_mid, dw_in2, dw_low, dw_in3, dw_end, dw_in4, end_in1, end_mid, end_in2,
    dk_own, dk_low, dk_in1, dk_mid, dk_cut, dk_in2, dk_end, dk_out, dk_in3,
    local, sends, recvs,
):
    f32, bf16 = jnp.float32, jnp.bfloat16
    tokens, channels = x_v.shape
    taps = KTAPS
    half, fourth = taps // 2, taps // 4
    dp, seq = lax.axis_index("dp"), lax.axis_index("seq")
    index = dp * 4 + seq
    z, y, x, c = lax.div(dp, 2), lax.rem(dp, 2), lax.div(seq, 2), lax.rem(seq, 2)
    flip_y, flip_x, flip_c = 1 - y, 1 - x, 1 - c

    def device(z, y, x, c):
        return (z * 2 + y, x * 2 + c)

    z_peers = [(lax.rem(z + k, 4), y, x, c) for k in (1, 2, 3)]
    plane_peers = [
        (z, lax.rem(y + k // 2, 2), lax.rem(x + k % 2, 2), c) for k in (1, 2, 3)
    ]
    x_peer, y_peer, core_peer = (z, y, flip_x, c), (z, flip_y, x, c), (z, y, x, flip_c)
    other_peers = [core_peer] + [(peer[0], peer[1], peer[2], flip_c) for peer in plane_peers]
    groups = ("gather", "reduce", "vector")
    sent = dict.fromkeys(groups, 0)
    phase, used = ["gather"], [0]

    def claim():
        used[0] += 1
        return recvs.at[used[0] - 1]

    def size_of(ref):
        return math.prod(ref.shape) * jnp.dtype(ref.dtype).itemsize

    def arrive(semaphore, total):
        pltpu.make_async_copy(total, total, semaphore).wait()

    def start(copies, total, recv_sem=None):
        if recv_sem is None:
            recv_sem = claim()
        group = "vector" if copies[0][0].shape[-2:] == (1, 128) else phase[0]
        for source, target, peer in copies:
            sent[group] += size_of(source)
            pltpu.make_async_remote_copy(
                src_ref=source, dst_ref=target, send_sem=sends.at[groups.index(group)], recv_sem=recv_sem,
                device_id=device(*peer), device_id_type=MESH,
            ).start()
        return recv_sem, total

    def finish(arrival):
        arrive(*arrival)

    def load(copies):
        for copy in copies:
            copy.start()
        return copies

    def take(ref, lines, first=0, count=4):
        return jnp.concatenate([ref[first + i, lines, :] for i in range(count)], axis=1)

    def put(ref, lines, value, first=0):
        for i in range(value.shape[1] // 128):
            ref[first + i, lines, :] = value[:, 128 * i : 128 * (i + 1)]

    barrier = pltpu.get_barrier_semaphore()
    peers = z_peers + plane_peers + other_peers
    for peer in peers:
        pl.semaphore_signal(barrier, inc=1, device_id=device(*peer), device_id_type=MESH)
    def fetch(pairs, numbers):
        return load([pltpu.make_async_copy(source, target, local.at[i]) for i, (source, target) in zip(numbers, pairs)])

    params = fetch([
        (gain_hbm, gain_ref), (shift_hbm, shift_ref), (skip_hbm, skip_ref), (bias_hbm, bias_ref), (w_hbm, w_ref),
        (ldt_hbm, ldt_ref), (lar_hbm, lar_ref), (ai_hbm, ai_ref), (cc_hbm, cc_ref),
    ], range(9))
    loads = fetch([
        (x_hbm, x_v), (pick_hbm, pick), (mask_hbm, mask), (fwd_hbm, fwd), (most_hbm, fwd_most), (rest_hbm, fwd_rest),
        (inv_hbm, inv), (g_hbm, g_v),
    ], (9, 10, 10, 11, 11, 11, 12, 13))
    three, place = pl.ds(0, 3), (y * 2 + x) * 2 + c

    def same(ref, peers, total, recv_sem=None):
        return start([(ref, ref, peer) for peer in peers], total, recv_sem)

    def load_all(number, refs):
        arrive(local.at[number], u_spec.at[pl.ds(0, sum(size_of(ref) for ref in refs) // (4 * channels)), :])

    right_sender, left_sender = sends.at[3], sends.at[4]
    right_copies = [
        pltpu.make_async_remote_copy(
            src_ref=x_hbm.at[at], dst_ref=left_v.at[at], send_sem=right_sender, recv_sem=claim(),
            device_id=(dp, seq + 1), device_id_type=MESH,
        )
        for at in (pl.ds(0, tokens - fourth), pl.ds(tokens - fourth, fourth))
    ]

    def prepare_shares():
        for copy in params:
            copy.wait()
        low = [ref[...].astype(bf16).astype(f32) for ref in (gain_ref, shift_ref, skip_ref, bias_ref)]
        share_in[z, place] = jnp.concatenate(low + [jnp.zeros((1, 128 - 5 * ROWS), f32)], axis=1)
        for q in range(4):
            weight[q, z, y, x, c] = jnp.concatenate(
                [w_ref[:, 128 * q : 128 * q + 128], w_ref[:, channels + 128 * q : channels + 128 * q + 128]], axis=1
            ).astype(bf16)

    def prepare_taps():
        _, _, unit, _, _, _, coef = mode_terms(ldt_ref[...], lar_ref[...], ai_ref[...], cc_ref[...])
        steps, power = [], times(unit, unit)
        for _ in range(8):
            steps.append(power)
            power = times(power, power)
        for p in range(8):
            def row(value):
                return value[0][p : p + 1], value[1][p : p + 1]

            def table(factors):
                sub = lax.broadcasted_iota(jnp.int32, (8, 128), 0)
                tile = None
                for bit, factor in enumerate(factors):
                    on = lax.rem(lax.div(sub, 2**bit), 2) == 1
                    factor = tuple(jnp.where(on, part, rest) for part, rest in zip(row(factor), (1.0, 0.0)))
                    tile = factor if tile is None else times(tile, factor)
                return tile

            base = table(steps[:3])
            for step in steps[3:6]:
                more = times(base, row(step))
                base = tuple(jnp.concatenate([old, new], axis=0) for old, new in zip(base, more))
            leap = table([steps[6], steps[7], unit])
            leaps[p, 0], leaps[p, 1] = leap
            at = slice(256 * p, 256 * p + 256)
            high, low = split_low(jnp.concatenate(base, axis=1))
            base_high[:, at], base_low[:, at] = high, low
            lead = times(row(coef), leap)
            lead = jnp.concatenate([lead[0], -lead[1]], axis=1)
            first = lax.rem(lax.broadcasted_iota(jnp.int32, (8, 256), 1), 128) < 64
            lead = jnp.concatenate([jnp.where(first, lead, 0.0), jnp.where(first, 0.0, lead)], axis=0)
            lead_high, lead_low = split_low(lead)
            taps_of = dot_nt(
                jnp.concatenate([lead_high, lead_low, lead_high], axis=1), jnp.concatenate([high, high, low], axis=1)
            )
            taps_of = jnp.concatenate([taps_of, taps_of], axis=1)
            lines_f[8 * p : 8 * p + 8], lines_f[8 * p + 64 : 8 * p + 72] = taps_of[:8], taps_of[8:]
        own = jnp.concatenate([lines_f[pl.ds(m, ROWS, stride=8), :][:, :64] for m in range(8)], axis=1)
        kern[z, y, x, c] = (2.0 * own).astype(bf16)

    late = z == 3

    @pl.when(jnp.logical_not(late))
    def _():
        prepare_shares()
        prepare_taps()

    pl.semaphore_wait(barrier, len(peers))

    @pl.when(late)
    def _():
        prepare_shares()

    share_plane = same(share_in.at[z, place], plane_peers + other_peers, share_in.at[0, pl.ds(0, 7)])
    weight_x = same(weight.at[:, z, y, x, c], [x_peer], weight.at[:, 0, 0, 0, 0])

    @pl.when(seq < 3)
    def _():
        right_copies[0].start()

    @pl.when(late)
    def _():
        prepare_taps()

    kern_z = same(kern.at[z, y, x, c], z_peers, kern.at[three, 0, 0, 0])
    finish(share_plane)
    share_z = same(share_in.at[z], z_peers, share_in.at[three])
    finish(weight_x)

    def weight_to_z(q):
        return same(weight.at[q, z, y, :, c], z_peers, weight.at[q, three, 0, :, 0])

    def weight_to_y(q):
        finish(weight_z[q])
        piece = weight.at[q, :, y, :, c]
        same(piece, [core_peer], piece, core_recvs[half_of[q]])
        return same(piece, [y_peer], weight.at[q, :, 0, :, 0])

    def weight_to_core(q):
        finish(weight_y[q])
        piece = weight.at[q, :, flip_y, :, c]
        same(piece, [core_peer], piece, core_recvs[half_of[q]])

    pairs, half_of = ((0, 3), (1, 2)), (0, 1, 1, 0)
    core_recvs = [claim(), claim()]
    weight_core = [(sem, weight.at[pl.ds(0, 2), :, :, :, 0]) for sem in core_recvs]
    weight_z = [weight_to_z(0)]
    last_y = same(weight.at[3, z, y, :, c], [y_peer], weight.at[3, 0, 0, :, 0])

    def last_to_z():
        finish(last_y)
        return same(weight.at[3, z, :, :, c], z_peers, weight.at[3, three, :, :, 0])

    def last_to_core():
        finish(last_z)
        same(weight.at[3, :, :, :, c], [core_peer], weight.at[3, :, :, :, 0], core_recvs[half_of[3]])

    def normalise(source, hat, keep_std, begin, end):
        for first in range(begin, end, 32):
            at = slice(first, first + 32)
            value = source[at, :].astype(f32)
            centered = value - jnp.mean(value, axis=1, keepdims=True)
            scale = lax.rsqrt(jnp.mean(centered * centered, axis=1, keepdims=True) + EPS)
            put(hat, at, centered * scale)
            if keep_std:
                inv_std[at, :] = jnp.broadcast_to(scale, (32, 128))

    loads[0].wait()
    normalise(x_v, x_hat, True, 0, tokens)
    finish(kern_z)
    halves = [pl.ds(0, 2), pl.ds(2, 2)]
    kern_plane = [same(kern.at[at, y, x, c], plane_peers, dk_in2.at[:, at]) for at in halves]

    weight_z.append(weight_to_z(1))
    finish(share_z)
    weight_z.append(weight_to_z(2))
    last_z = last_to_z()

    @pl.when(seq < 3)
    def _():
        right_copies[1].start()

    load_all(10, (pick, mask))
    shares = share_in[...].reshape(32, 1, 128).reshape(32, 128).astype(bf16)
    spread = dot_nn(shares, pick[...]) * mask[...].astype(f32)
    spread = jnp.sum(spread, axis=0, keepdims=True)
    rows_f[...] = jnp.concatenate(
        [spread[:, channels * i : channels * (i + 1)] for i in range(5)] + [jnp.zeros((3, channels), f32)], axis=0
    )
    gain, shift = rows_f[0:1, :], rows_f[1:2, :]

    def every_other(i, parity):
        return pl.ds(128 * i + parity, 64, stride=2)

    def sixty_four(i):
        return pl.ds(pl.multiple_of(64 * i, 64), 64)

    def shifted(i, _):
        at = pl.ds(pl.multiple_of(i * 128, 128), 128)
        put(normed, at, take(x_hat, at) * gain + shift)
        for parity in range(2):
            own_b[parity, sixty_four(i)] = take(normed, every_other(i, parity)).astype(bf16)
        return 0

    lax.fori_loop(0, tokens // 128, shifted, 0)
    load_all(11, (fwd, fwd_most, fwd_rest))
    load_all(12, (inv,))
    wide = 256

    def lanes(j):
        return pl.ds(pl.multiple_of(j * wide, wide), wide)

    few = 16

    def sign_of(r):
        return 1 if r < half // 2 else -1

    def transform(block, exact):
        both = []
        for parity, rows in enumerate(block):
            if exact:
                both.append(dot_nn(fwd[parity], jnp.concatenate([rows, rows], axis=0)))
            else:
                both.append(dot_nn(fwd[parity, :, :half], rows))
        return jnp.concatenate(both, axis=1)

    def joined(both, r):
        parts = both[r : r + few], both[half + r : half + r + few]
        width = both.shape[1] // 2
        even, odd = [part[:, :width] for part in parts], [part[:, width:] for part in parts]
        return tuple(a + b for a, b in zip(even, odd)), tuple(a - b for a, b in zip(even, odd))

    def places(r):
        return [pl.ds(first + r, few) for first in (0, taps, half, taps + half)]

    def keep(ref, at, r, pair):
        for lines, part in zip(places(r), pair[0] + pair[1]):
            ref[lines, at] = part

    def kept(ref, at, r):
        parts = [ref[lines, at] for lines in places(r)]
        return parts[:2], parts[2:]

    def signals(pairs_at, exact):
        lines = None
        for r in range(0, half, few):
            pairs = pairs_at(r)
            lines = lines or [[[[], []] for _ in range(2)] for _ in pairs]
            for (a, b), parities in zip(pairs, lines):
                for k, (x, y) in enumerate(zip(a, b)):
                    for parity, value in enumerate((x + y, x - y)):
                        parities[parity][k].append(split_low(value) if exact else (value.astype(bf16),))
        results = []
        for parities in lines:
            both = []
            for parity, (real, imag) in enumerate(parities):
                parts = [jnp.concatenate([line[i] for line in real + imag], axis=0) for i in range(2 if exact else 1)]
                if exact:
                    high, low = parts
                    both.append(dot_nn(inv[parity], jnp.concatenate([high, high, low], axis=0)))
                else:
                    both.append(dot_nn(inv[parity, :, : 2 * half], parts[0]))
            results.append(jnp.concatenate(both, axis=1))
        return results

    def signal(pair_at, exact):
        return signals(lambda r: (pair_at(r),), exact)[0]

    def each(function, pairs):
        return tuple(function(*values) for values in zip(*pairs))

    def swung(value, sign):
        return (value[1], -value[0]) if sign > 0 else (-value[1], value[0])

    def own_spectrum(j):
        at = lanes(j)
        both = transform((own_b[0, :, at], own_b[1, :, at]), True)
        for r in range(0, half, few):
            keep(u_spec, at, r, joined(both, r))

    own_spectrum(0)
    own_spectrum(1)
    weight_y = [weight_to_y(0)]

    def left_block(i):
        first, last = (0, 3) if i == 0 else (3, 4)
        right_copies[i].wait_recv()
        normalise(left_v, left_hat, False, 128 * first, 128 * last)
        for k in range(first, last):
            for parity in range(2):
                value = take(left_hat, pl.ds(128 * k + parity, 64, stride=2)) * gain + shift
                left_b[parity, 64 * k : 64 * k + 64] = value.astype(bf16)
        at = slice(64 * first, 64 * last)
        matrix = (fwd_most if i == 0 else fwd_rest)[...]
        for j in range(2):
            lane = slice(wide * j, wide * (j + 1))
            both = [left_b[parity, at, lane] for parity in range(2)]
            both = [dot_nn(matrix[k], jnp.concatenate([rows, rows], axis=0)) for k, rows in enumerate(both)]
            both = jnp.concatenate(both, axis=1)
            lines = slice(taps * j, taps * (j + 1))
            if i == 0:
                d_spec[lines, :] = both
                continue
            both += d_spec[lines, :]
            for r in range(0, half, few):
                turns = [swung(value, -sign_of(r)) for value in joined(both, r)]
                old = kept(u_spec, lanes(j), r)
                keep(u_spec, lanes(j), r, tuple(tuple(a + b for a, b in zip(x, y)) for x, y in zip(old, turns)))

    @pl.when(seq > 0)
    def _():
        left_block(0)

    @pl.when(seq == 0)
    def _():
        left_hat[...] = jnp.zeros_like(left_hat)

    weight_y.append(weight_to_y(1))
    kern_core = []
    for arrival, at in zip(kern_plane, halves):
        finish(arrival)
        kern_core.append(same(kern.at[at, :, :, c], [core_peer], kern.at[at, :, :, 0]))

    def kernel_transform(j):
        rows = kern[2 * j : 2 * j + 2].reshape(wide, taps)
        rows = [jnp.concatenate([rows[:, at]] * 2, axis=1) for at in (slice(0, half), slice(half, taps))]
        return jnp.concatenate([dot_nt(fwd[parity], part) for parity, part in enumerate(rows)], axis=1)

    def convolve(j, both):
        at = lanes(j)

        def product(r):
            k = joined(both, r)
            keep(k_spec, at, r, k)
            return each(times, (k, kept(u_spec, at, r)))

        both = signal(product, True)
        for parity in range(2):
            put(mixed, pl.ds(parity, half, stride=2), both[:, wide * parity : wide * (parity + 1)], 2 * j)

    def activate(j):
        for tile in (2 * j, 2 * j + 1):
            at = slice(128 * tile, 128 * tile + 128)
            for start_at in range(0, tokens, 128):
                lines = slice(start_at, start_at + 128)
                value = mixed[tile, lines, :] + rows_f[2:3, at] * normed[tile, lines, :]
                chance = 0.5 + 0.5 * lax.erf(value * (0.5**0.5))
                slope[lines, at] = chance + value * jnp.exp(value * value * -0.5 - 0.5 * float(np.log(2.0 * np.pi)))
                low = (value * chance).astype(bf16)
                activ[lines, at] = low
                activ_t[at, lines] = low.T

    for j in range(2):
        finish(kern_core[j])
        k_raw[j] = kernel_transform(j)
        if j == 0:
            weight_y.append(weight_to_y(2))

    @pl.when(seq > 0)
    def _():
        left_block(1)

    weight_to_core(0)
    convolve(0, k_raw[0])
    weight_to_core(1)
    last_to_core()
    convolve(1, k_raw[1])
    activate(0)
    activate(1)
    weight_to_core(2)
    loads[-1].wait()

    def matrix_of(h):
        return jnp.concatenate([weight[q].reshape(channels, 256) for q in pairs[h]], axis=1)

    def gates(h, pre):
        lines_out = []
        sums = [jnp.zeros((32, 128), f32) for _ in range(4)]
        for start_at in range(0, tokens, 32):
            lines = slice(start_at, start_at + 32)
            low = []
            for i, q in enumerate(pairs[h]):
                at = slice(128 * q, 128 * q + 128)
                lin = pre[lines, 256 * i : 256 * i + 128] + rows_f[3:4, at]
                gate = 0.5 + 0.5 * jnp.tanh(0.5 * (pre[lines, 256 * i + 128 : 256 * i + 256] + rows_f[4:5, at]))
                grad = g_v[lines, at].astype(f32)
                product = lin * gate
                res_v[lines, at] = (x_v[lines, at].astype(f32) + product).astype(bf16)
                low += [(grad * gate).astype(bf16), (grad * (product - product * gate)).astype(bf16)]
            sums = [total + part.astype(f32) for total, part in zip(sums, low)]
            lines_out.append(jnp.concatenate(low, axis=1))
        for i, q in enumerate(pairs[h]):
            for k in range(2):
                rows_f[3 + k : 4 + k, 128 * q : 128 * q + 128] = jnp.sum(sums[2 * i + k], axis=0, keepdims=True)
        return jnp.concatenate(lines_out, axis=0)

    def weight_grad(h, low):
        grad = dot_nn(activ_t[...], low).astype(bf16)
        for i, q in enumerate(pairs[h]):
            dw_own[q] = grad[:, 256 * i : 256 * i + 256].reshape(4, 2, 2, 2, ROWS, 256)
            start([(dw_own.at[q, :, :, :, flip_c], dw_in1.at[q], core_peer)], dw_in1.at[q], dw_recvs[h])

    def mix_grad(d_act):
        total = jnp.zeros((32, channels), f32)
        for start_at in range(0, tokens, 32):
            lines = slice(start_at, start_at + 32)
            mix = (d_act[lines] * slope[lines, :]).astype(bf16).astype(f32)
            total += mix * take(normed, lines)
            put(mixed, lines, mix)
        rows_f[2:3, :] = jnp.sum(total, axis=0, keepdims=True)
        for parity in range(2):
            for start_at in range(0, half, 64):
                part = take(mixed, pl.ds(2 * start_at + parity, 64, stride=2))
                d_mix[parity, start_at : start_at + 64] = part.astype(bf16)

    def core_sum(q):
        if half_of[q] not in summed:
            summed.add(half_of[q])
            arrive(dw_recvs[half_of[q]], dw_in1.at[pl.ds(0, 2)])
        dw_mid[q] = (dw_own[q, :, :, :, c].astype(f32) + dw_in1[q].astype(f32)).astype(bf16)

    def to_y(q):
        core_sum(q)
        dw_y[q] = start([(dw_mid.at[q, :, flip_y], dw_in2.at[q], y_peer)], dw_in2.at[q])

    def end_to_z(q):
        core_sum(q)
        copies = [(dw_mid.at[q, peer[0]], end_in1.at[q, i], peer) for i, peer in enumerate(z_peers)]
        end_z[q] = start(copies, end_in1.at[q])

    def end_to_plane(q):
        finish(end_z[q])
        total = dw_mid[q, z].astype(f32)
        for i in range(3):
            total = total + end_in1[q, i].astype(f32)
        end_mid[q] = total.astype(bf16)
        copies = [(end_mid.at[q, peer[1], peer[2]], end_in2.at[q, i], peer) for i, peer in enumerate(plane_peers)]
        end_plane[q] = start(copies, end_in2.at[q])

    def write_out(q, total):
        dw_ref[:, 128 * q : 128 * q + 128] = total[:, :128]
        dw_ref[:, channels + 128 * q : channels + 128 * q + 128] = total[:, 128:]

    def end_of(q):
        finish(end_plane[q])
        total = end_mid[q, y, x].astype(f32)
        for i in range(3):
            total = total + end_in2[q, i].astype(f32)
        write_out(q, total)

    def to_z(q):
        finish(dw_y[q])
        dw_low[q] = (dw_mid[q, :, y].astype(f32) + dw_in2[q].astype(f32)).astype(bf16)
        copies = [(dw_low.at[q, peer[0]], dw_in3.at[q, i], peer) for i, peer in enumerate(z_peers)]
        dw_z[q] = start(copies, dw_in3.at[q])

    def to_x(q):
        finish(dw_z[q])
        total = dw_low[q, z].astype(f32)
        for i in range(3):
            total = total + dw_in3[q, i].astype(f32)
        dw_end[q] = total.astype(bf16)
        dw_x[q] = start([(dw_end.at[q, flip_x], dw_in4.at[q], x_peer)], dw_in4.at[q])

    def to_end(q):
        finish(dw_x[q])
        write_out(q, dw_end[q, x].astype(f32) + dw_in4[q].astype(f32))

    skip = rows_f[2:3, :]
    dw_y, dw_z, dw_x, end_z, end_plane, summed = {}, {}, {}, {}, {}, set()
    phase[0], dw_recvs = "reduce", [claim(), claim()]
    finish(weight_core[0])
    first_low = gates(0, dot_nn(activ[...], matrix_of(0)))
    weight_grad(0, first_low)
    finish(weight_core[1])
    second_low = gates(1, dot_nn(activ[...], matrix_of(1)))
    d_act = dot_nt(
        jnp.concatenate([first_low, second_low], axis=1), jnp.concatenate([matrix_of(0), matrix_of(1)], axis=1)
    )
    mix_grad(d_act)
    left_pieces = ((0, 256), (256, 256))
    left_copies = [
        pltpu.make_async_remote_copy(
            src_ref=d_mix.at[:, :, pl.ds(first, width)], dst_ref=right_v.at[:, :, pl.ds(first, width)], send_sem=left_sender,
            recv_sem=claim(), device_id=(dp, seq - 1), device_id_type=MESH,
        )
        for first, width in left_pieces
    ]

    @pl.when(seq > 0)
    def _():
        for copy in left_copies[:1]:
            copy.start()

    to_y(0)
    end_to_z(3)
    weight_grad(1, second_low)

    def mix_transform(j):
        at = lanes(j)
        return transform((d_mix[0, :, at], d_mix[1, :, at]), False)

    def kernel_grad(j, both):
        at = lanes(j)

        def product(r):
            d = joined(both, r)
            keep(d_spec, at, r, d)
            return each(conj_times, (kept(u_spec, at, r), d))

        both = signal(product, False)
        grad = jnp.concatenate([both[:, :wide].T, both[:, wide:].T], axis=1).reshape(2, 2, 2, 2, ROWS, taps)
        dk_own[2 * j : 2 * j + 2] = grad
        dk_low[2 * j : 2 * j + 2] = grad.astype(bf16)

    def kernel_middle():
        finish(dk_core)
        for i in range(4):
            total = dk_own[i, :, :, c] + dk_in1[i].astype(f32)
            dk_mid[i] = total
            dk_cut[i] = total.astype(bf16)
        return start([(dk_cut.at[:, peer[1], peer[2]], dk_in2.at[i], peer) for i, peer in enumerate(plane_peers)], dk_in2)

    def kernel_end():
        finish(dk_plane)
        for i in range(4):
            total = dk_mid[i, y, x]
            for k in range(3):
                total = total + dk_in2[k, i].astype(f32)
            dk_end[i] = total
            dk_out[i] = total.astype(bf16)
        return start([(dk_out.at[peer[0]], dk_in3.at[i], peer) for i, peer in enumerate(z_peers)], dk_in3)

    def own_grad(j):
        at = lanes(j)

        def product(r):
            return each(conj_times, (kept(k_spec, at, r), kept(d_spec, at, r)))

        def products(r):
            pair = product(r)
            return pair, tuple(swung(value, sign_of(r)) for value in pair)

        own, back = signals(products, False)
        d_gain, d_shift = jnp.zeros((1, wide), f32), jnp.zeros((1, wide), f32)
        for parity in range(2):
            lines = pl.ds(parity, half, stride=2)
            columns = slice(wide * parity, wide * (parity + 1))
            grad = own[:, columns] + rows_f[5:6, at] * d_mix[parity, :, at].astype(f32)
            put(d_norm, lines, grad, 2 * j)
            before = jnp.where(seq > 0, back[:, columns], 0.0)
            d_gain += jnp.sum(
                grad * take(x_hat, lines, 2 * j, 2) + before * take(left_hat, lines, 2 * j, 2), axis=0, keepdims=True
            )
            d_shift += jnp.sum(grad + before, axis=0, keepdims=True)
        rows_f[6:7, at], rows_f[7:8, at] = d_gain, d_shift

    def right_grad(i):
        first, width = left_pieces[i]
        at = slice(first, first + width)
        left_copies[i].wait_recv()
        both = transform((right_v[0, :, at], right_v[1, :, at]), False)

        def product(r):
            turns = [swung(value, sign_of(r)) for value in joined(both, r)]
            return each(conj_times, (kept(k_spec, at, r), turns))

        both = signal(product, False)
        for parity in range(2):
            lines = pl.ds(parity, half, stride=2)
            more = both[:, width * parity : width * (parity + 1)]
            put(d_norm, lines, take(d_norm, lines, first // 128, width // 128) + more, first // 128)

    rows_f[5:6, :] = skip
    first_half, second_half = mix_transform(0), mix_transform(1)
    kernel_grad(0, first_half)
    kernel_grad(1, second_half)
    dk_core = start([(dk_low.at[:, :, :, flip_c], dk_in1, core_peer)], dk_in1)
    end_to_z(1)
    to_y(2)
    own_grad(0)
    dk_plane = kernel_middle()

    @pl.when(seq > 0)
    def _():
        for copy in left_copies[1:]:
            copy.start()

    own_grad(1)
    to_z(0)
    vector = jnp.concatenate([rows_f[6:7, :], rows_f[7:8, :], rows_f[2:3, :], rows_f[3:4, :], rows_f[4:5, :]], axis=1)
    high, low = split_low(jnp.broadcast_to(vector, mask.shape) * mask[...].astype(f32))
    shares = dot_nt(high, pick[...]) + dot_nt(low, pick[...])
    share_out[...] = shares.reshape(32, 1, 128).reshape(4, 8, 1, 128)
    copies = [(share_out.at[peer[0]], share_in1.at[i], peer) for i, peer in enumerate(z_peers)]
    share_z = start(copies, share_in1)
    @pl.when(seq < 3)
    def _():
        right_grad(0)

    to_z(2)
    end_to_plane(3)
    dk_z = kernel_end()
    end_to_plane(1)
    to_x(0)
    finish(share_z)
    share_mid[...] = share_out[z] + share_in1[0] + share_in1[1] + share_in1[2]
    copies = [
        (share_mid.at[(peer[1] * 2 + peer[2]) * 2 + peer[3]], share_in2.at[i], peer)
        for i, peer in enumerate(plane_peers + other_peers)
    ]
    share_plane = start(copies, share_in2)

    @pl.when(seq < 3)
    def _():
        for i in range(1, len(left_pieces)):
            right_grad(i)

    to_x(2)

    @pl.when(seq < 3)
    def _():
        arrive(right_sender, x_v)

    @pl.when(seq > 0)
    def _():
        arrive(left_sender, d_mix)

    for first in range(0, tokens, 32):
        at = slice(first, first + 32)
        hat = [x_hat[i, at, :] for i in range(4)]
        grad = [d_norm[i, at, :] * rows_f[0:1, 128 * i : 128 * i + 128] for i in range(4)]
        mean = jnp.sum(sum(grad[1:], grad[0]), axis=1, keepdims=True) * (1.0 / channels)
        along = [one * other for one, other in zip(grad, hat)]
        along = jnp.sum(sum(along[1:], along[0]), axis=1, keepdims=True) * (1.0 / channels)
        for i in range(4):
            lane = slice(128 * i, 128 * i + 128)
            inner = inv_std[at, :] * (grad[i] - mean - hat[i] * along)
            gin_v[at, lane] = (inner + g_v[at, lane].astype(f32)).astype(bf16)
    dt, a, unit, norm_sq, ratio, coef, scaled = mode_terms(ldt_ref[...], lar_ref[...], ai_ref[...], cc_ref[...])
    inverse_a = (a[0] / norm_sq, -a[1] / norm_sq)
    end_of(3)
    end_of(1)
    to_end(0)
    finish(dk_z)
    d_kernel = dk_end[z]
    for k in range(3):
        d_kernel = d_kernel + dk_in3[k].astype(f32)

    for m in range(8):
        block = d_kernel[:, 64 * m : 64 * m + 64]
        block = jnp.concatenate([block, block], axis=1)
        for k in range(2):
            lines_f[pl.ds(8 * k + m, 8, stride=16), :] = block[8 * k : 8 * k + 8]
    at_row = lax.broadcasted_iota(jnp.int32, (8, 128), 0)
    first = lax.broadcasted_iota(jnp.int32, (8, 128), 1) < 64
    leap_of = (128 * lax.rem(at_row, 4) + lax.div(at_row, 4)).astype(f32)
    ramp = (2 * lax.broadcasted_iota(jnp.int32, (32, 64), 1)).astype(f32)
    sums = []
    for pair in range(4):
        plain = lines_f[32 * pair : 32 * pair + 32, :][:, :64]
        high, low = split_low(jnp.concatenate([plain, plain * ramp], axis=0))
        at = slice(512 * pair, 512 * pair + 512)
        table = jnp.concatenate([base_high[:, at], base_low[:, at], base_high[:, at]], axis=0)
        sums.append(dot_nn(jnp.concatenate([high, high, low], axis=1), table))
    zero = jnp.zeros((8, 128), f32)
    s0, s1 = [zero, zero], [zero, zero]
    for p in range(8):
        def part_of(begin, part):
            lane = 256 * (p % 2) + 128 * part
            block = sums[p // 2][begin + 16 * (p % 2) : begin + 16 * (p % 2) + 16, lane : lane + 128]
            return jnp.where(first, block[:8], block[8:])

        value, slope_of = [part_of(0, part) for part in range(2)], [part_of(32, part) for part in range(2)]
        leap = (leaps[p, 0], leaps[p, 1])
        slope_of = [one + leap_of * other for one, other in zip(slope_of, value)]
        for total, terms in ((s0, value), (s1, slope_of)):
            for part, product in enumerate(times(leap, terms)):
                total[part] = jnp.where(at_row == p, jnp.sum(product, axis=0, keepdims=True), total[part])
    d_coef = times(s0, ratio)
    half_g = times(times(coef, s0), times(unit, inverse_a))
    ramp_part = times(scaled, s1)
    half_g = (half_g[0] + ramp_part[0], half_g[1] + ramp_part[1])
    back = times(times(scaled, s0), inverse_a)
    q = (half_g[0] * dt - back[0], half_g[1] * dt - back[1])
    d_dt = 2.0 * dt * times(half_g, a)[0]
    dldt_ref[...] = row_of(jnp.sum(unpair_lanes(d_dt), axis=1, keepdims=True))[0]
    dlar_ref[...] = unpair_lanes(2.0 * q[0] * a[0])
    dai_ref[...] = unpair_lanes(-2.0 * q[1])
    dcc_ref[...] = jnp.concatenate([unpair_lanes(2.0 * d_coef[0]), unpair_lanes(-2.0 * d_coef[1])], axis=1)

    to_end(2)
    finish(share_plane)
    small = share_mid[place]
    for i in range(7):
        small = small + share_in2[i]
    for i, target in enumerate([dgain_ref, dshift_ref, dskip_ref]):
        target[...] = small[0, ROWS * i : ROWS * (i + 1)]
    dbias_ref[...] = small[0, 3 * ROWS : 5 * ROWS]
    arrive(sends.at[0], u_spec.at[pl.ds(0, sent["gather"] // (4 * channels)), :])
    arrive(sends.at[1], u_spec.at[pl.ds(0, sent["reduce"] // (4 * channels)), :])
    arrive(sends.at[2], vector_rows.at[pl.ds(0, sent["vector"] // 512)])


def finish_kernel(*refs):
    count = len(refs) // 2
    sems = refs[-1]
    copies = [pltpu.make_async_copy(refs[i], refs[count + i], sems.at[i]) for i in range(count)]
    for copy in copies:
        copy.start()
    for copy in copies:
        copy.wait()


def kernel_body(
    inputs, grad_out, ln_gain, ln_bias, skip_scale, w_glu, b_glu, log_dt, log_a_real, a_imag, c_coef
):
    _, tokens, channels = inputs.shape
    taps = KTAPS
    glu = w_glu.shape[1]
    f32, bf16 = jnp.float32, jnp.bfloat16
    order = np.concatenate([np.arange(0, taps // 2, 2), np.arange(1, taps // 2, 2)]) + 0.5
    forward, inverse = [], []
    for parity in range(2):
        angle = np.outer(order, 2 * np.arange(taps // 2) + parity) * (np.pi / taps)
        matrix = np.concatenate([np.cos(angle), -np.sin(angle)], axis=0)
        high = matrix.astype(bf16)
        low = (matrix - high.astype(np.float64)).astype(bf16)
        forward.append(np.concatenate([high, low], axis=1))
        inverse.append(np.concatenate([high.T, low.T, high.T], axis=1) * np.asarray(1.0 / taps, bf16))
    forward, inverse = np.stack(forward), np.stack(inverse)
    cut, end = 3 * taps // 8, taps // 2
    most, rest = (
        np.concatenate([forward[:, :, a:b], forward[:, :, end + a : end + b]], axis=2) for a, b in ((0, cut), (cut, end))
    )
    device_at, lane = np.arange(32)[:, None], np.arange(channels)[None, :]
    bias_lane = np.arange(2 * channels)[None, :]
    row = np.arange(128)[:, None]
    pick = np.concatenate(
        [row == i * ROWS + lane % ROWS for i in range(3)] + [row == 3 * ROWS + bias_lane % (2 * ROWS)], axis=1
    ).astype(bf16)
    mask = np.concatenate(
        [device_at == lane // ROWS] * 3 + [device_at == bias_lane // (2 * ROWS)], axis=1
    ).astype(bf16)
    hbm, vmem = pl.BlockSpec(memory_space=pl.ANY), pl.BlockSpec(memory_space=pltpu.VMEM)
    block = (tokens, channels)
    spec, tall = (2 * taps, channels), (channels // 128, tokens, 128)

    def space(*dims, kind=f32):
        return pltpu.VMEM(dims, kind)

    results = (
        (block, bf16), (block, bf16), ((ROWS,), f32), ((ROWS,), f32), ((ROWS,), f32), (w_glu.shape, f32),
        ((2 * ROWS,), f32), ((ROWS,), f32), (log_a_real.shape, f32), (a_imag.shape, f32), (c_coef.shape, f32),
    )
    outs = pl.pallas_call(
        layer_kernel,
        name="layer",
        out_shape=tuple(pltpu.VMEM(dims, kind) for dims, kind in results),
        in_specs=[hbm] * 17,
        out_specs=(vmem,) * len(results),
        scratch_shapes=[
            space(*w_glu.shape), space(1, ROWS), space(1, ROWS), space(1, ROWS), space(1, 2 * ROWS), space(1, ROWS),
            space(*log_a_real.shape), space(*a_imag.shape), space(*c_coef.shape),
            space(*block, kind=bf16), space(*block, kind=bf16), space(*block, kind=bf16),
            space(*forward.shape, kind=bf16), space(*most.shape, kind=bf16), space(*rest.shape, kind=bf16),
            space(*inverse.shape, kind=bf16),
            space(*pick.shape, kind=bf16), space(*mask.shape, kind=bf16),
            space(4, 2, 2, 2, ROWS, taps, kind=bf16), space(4, 4, 2, 2, 2, ROWS, 256, kind=bf16),
            space(64, 2048, kind=bf16), space(64, 2048, kind=bf16), space(8, 2, 8, 128), space(8 * ROWS, 128),
            space(4, 8, 1, 128), space(4, 8, 1, 128), space(3, 8, 1, 128), space(8, 1, 128), space(7, 1, 128),
            space(64, 1, 128),
            space(8, channels),
            space(*tall), space(tokens, 128), space(*tall), space(*tall),
            space(2, tokens // 2, channels, kind=bf16), space(2, tokens // 2, channels, kind=bf16),
            space(2, taps, taps), space(*spec), space(*spec), space(*tall), space(*block),
            space(*block, kind=bf16), space(channels, tokens, kind=bf16),
            space(2, tokens // 2, channels, kind=bf16), space(2, tokens // 2, channels, kind=bf16),
            space(*spec), space(*tall),
            space(4, 4, 2, 2, 2, ROWS, 256, kind=bf16), space(4, 4, 2, 2, ROWS, 256, kind=bf16),
            space(4, 4, 2, 2, ROWS, 256, kind=bf16), space(4, 4, 2, ROWS, 256, kind=bf16),
            space(4, 4, 2, ROWS, 256, kind=bf16), space(4, 3, 2, ROWS, 256, kind=bf16),
            space(4, 2, ROWS, 256, kind=bf16), space(4, ROWS, 256, kind=bf16),
            space(4, 3, 2, 2, ROWS, 256, kind=bf16), space(4, 2, 2, ROWS, 256, kind=bf16), space(4, 3, ROWS, 256, kind=bf16),
            space(4, 2, 2, 2, ROWS, taps), space(4, 2, 2, 2, ROWS, taps, kind=bf16), space(4, 2, 2, ROWS, taps, kind=bf16),
            space(4, 2, 2, ROWS, taps), space(4, 2, 2, ROWS, taps, kind=bf16), space(3, 4, ROWS, taps, kind=bf16),
            space(4, ROWS, taps), space(4, ROWS, taps, kind=bf16), space(3, ROWS, taps, kind=bf16),
            pltpu.SemaphoreType.DMA((14,)), pltpu.SemaphoreType.DMA((5,)), pltpu.SemaphoreType.DMA((39,)),
        ],
        compiler_params=pltpu.CompilerParams(
            collective_id=0, has_side_effects=True, vmem_limit_bytes=48 * 2**20
        ),
    )(*[
        pltpu.with_memory_space_constraint(value, pltpu.HBM)
        for value in (
            inputs.reshape(block), grad_out.reshape(block), forward, most, rest, inverse, pick, mask, w_glu,
            ln_gain.reshape(1, -1), ln_bias.reshape(1, -1), skip_scale.reshape(1, -1), b_glu.reshape(1, -1),
            log_dt.reshape(1, -1), log_a_real, a_imag, c_coef,
        )
    ])
    ended = pl.pallas_call(
        finish_kernel,
        name="finish",
        out_shape=tuple(jax.ShapeDtypeStruct(dims, kind) for dims, kind in results),
        in_specs=[vmem] * len(results),
        out_specs=(hbm,) * len(results),
        scratch_shapes=[pltpu.SemaphoreType.DMA((len(results),))],
    )(*[pltpu.with_memory_space_constraint(value, pltpu.VMEM) for value in outs])
    return (ended[0].reshape(inputs.shape), ended[1].reshape(inputs.shape)) + tuple(ended[2:])


def solution(mesh):
    in_specs = (
        P("dp", "seq", None),
        P("dp", "seq", None),
        P(("dp", "seq")),
        P(("dp", "seq")),
        P(("dp", "seq")),
        P(("dp", "seq"), None),
        P(("dp", "seq")),
        P(("dp", "seq")),
        P(("dp", "seq"), None),
        P(("dp", "seq"), None),
        P(("dp", "seq"), None),
    )
    out_specs = (
        P("dp", "seq", None),
        P("dp", "seq", None),
        P(("dp", "seq")),
        P(("dp", "seq")),
        P(("dp", "seq")),
        P(("dp", "seq"), None),
        P(("dp", "seq")),
        P(("dp", "seq")),
        P(("dp", "seq"), None),
        P(("dp", "seq"), None),
        P(("dp", "seq"), None),
    )
    quick = mesh.shape["dp"] == 8 and mesh.shape["seq"] == 4
    return jax.shard_map(kernel_body if quick else body, mesh=mesh, in_specs=in_specs, out_specs=out_specs, check_vma=False)
```

```python
import math
from functools import partial

import jax
import jax.numpy as jnp
import numpy as np
from jax import lax
from jax.experimental import pallas as pl
from jax.experimental.pallas import tpu as pltpu
from jax.sharding import PartitionSpec as P

KTAPS = 512


EPS = 1e-05


def passed_along(value, axis, steps):
    count = lax.axis_size(axis)
    first, last = (max(0, -steps), min(count, count - steps))
    return lax.ppermute(value, axis, [(source, source + steps) for source in range(first, last)])


def kernel_block(log_dt, log_a_real, a_imag, c_coef, start, count):
    mode_count = log_a_real.shape[1]
    step_size = jnp.exp(log_dt)[:, None]
    a_real = -jnp.exp(log_a_real)
    decay = a_real * step_size
    turn = a_imag * step_size
    growth = jnp.exp(decay)
    ex_re = growth * jnp.cos(turn) - 1.0
    ex_im = growth * jnp.sin(turn)
    norm_sq = a_real * a_real + a_imag * a_imag
    ratio_re = (ex_re * a_real + ex_im * a_imag) / norm_sq
    ratio_im = (ex_im * a_real - ex_re * a_imag) / norm_sq
    c_re = c_coef[:, :mode_count]
    c_im = c_coef[:, mode_count:]
    coef_re = c_re * ratio_re - c_im * ratio_im
    coef_im = c_re * ratio_im + c_im * ratio_re
    places = (start + jnp.arange(count)).astype(jnp.float32)
    phase = turn[:, :, None] * places
    damping = jnp.exp(decay[:, :, None] * places)
    terms = damping * (coef_re[:, :, None] * jnp.cos(phase) - coef_im[:, :, None] * jnp.sin(phase))
    return 2.0 * jnp.sum(terms, axis=1)


def transforms(taps):
    angle = np.outer(np.arange(taps) + 0.5, np.arange(taps)) * (np.pi / taps)
    forward = np.concatenate([np.cos(angle), -np.sin(angle)], axis=0)
    inverse = forward.T / taps
    return forward.astype(jnp.bfloat16), inverse.astype(jnp.bfloat16)


def body(
    inputs, grad_out, ln_gain, ln_bias, skip_scale, w_glu, b_glu, log_dt, log_a_real, a_imag, c_coef
):
    seq_count, own_len, channels = inputs.shape
    gain_low = ln_gain.astype(jnp.bfloat16)
    shift_low = ln_bias.astype(jnp.bfloat16)
    skip_low = skip_scale.astype(jnp.bfloat16)
    weight_low = w_glu.astype(jnp.bfloat16)
    bias_low = b_glu.astype(jnp.bfloat16)
    mode_own = (log_dt, log_a_real, a_imag, c_coef)
    own_kernel = kernel_block(*mode_own, 0, KTAPS).astype(jnp.bfloat16)
    gathered = (
        lax.all_gather(gain_low, ("dp", "seq"), axis=0, tiled=True),
        lax.all_gather(shift_low, ("dp", "seq"), axis=0, tiled=True),
        lax.all_gather(skip_low, ("dp", "seq"), axis=0, tiled=True),
        lax.all_gather(weight_low, ("dp", "seq"), axis=0, tiled=True),
        lax.all_gather(bias_low, ("dp", "seq"), axis=0, tiled=True),
        lax.all_gather(own_kernel, ("dp", "seq"), axis=0, tiled=True),
    )
    kernel_b = gathered[5]
    taps = own_len
    forward, inverse = transforms(taps)
    sign = jnp.where(jnp.arange(taps) % 2 == 0, 1.0, -1.0).astype(jnp.float32)[:, None]

    def to_spectrum(block):
        both = jnp.dot(forward, block, preferred_element_type=jnp.float32)
        return both[:taps], both[taps:]

    def from_spectrum(real, imag):
        both = jnp.concatenate([real, imag], axis=0).astype(jnp.bfloat16)
        return jnp.dot(inverse, both, preferred_element_type=jnp.float32)

    kernel_re, kernel_im = to_spectrum(kernel_b.T)
    gain_full = gathered[0].astype(jnp.float32)
    shift_full = gathered[1].astype(jnp.float32)
    skip_full = gathered[2].astype(jnp.float32)
    weight_b = gathered[3]
    glu_bias = gathered[4].astype(jnp.float32)
    x_float = inputs.astype(jnp.float32)
    row_mean = jnp.mean(x_float, axis=-1, keepdims=True)
    centered = x_float - row_mean
    row_var = jnp.mean(centered * centered, axis=-1, keepdims=True)
    inv_std = lax.rsqrt(row_var + EPS)
    x_hat = centered * inv_std
    normed = x_hat * gain_full + shift_full
    normed_b = normed.astype(jnp.bfloat16)
    own_re, own_im = to_spectrum(normed_b[0])
    left_re, left_im = to_spectrum(passed_along(normed_b, "seq", 1)[0])
    source_re = own_re - sign * left_im
    source_im = own_im + sign * left_re
    conv = from_spectrum(
        kernel_re * source_re - kernel_im * source_im,
        kernel_re * source_im + kernel_im * source_re,
    )
    mixed_pre = conv[None] + skip_full * normed
    activ, gelu_pull = jax.vjp(partial(jax.nn.gelu, approximate=False), mixed_pre)
    activ_b = activ.astype(jnp.bfloat16)
    glu_pre = (
        jnp.einsum("slh,hg->slg", activ_b, weight_b, preferred_element_type=jnp.float32) + glu_bias
    )
    half_dim = glu_pre.shape[-1] // 2
    lin_part = glu_pre[..., :half_dim]
    gate_sig = jax.nn.sigmoid(glu_pre[..., half_dim:])
    result = (x_float + lin_part * gate_sig).astype(jnp.bfloat16)
    grad_f = grad_out.astype(jnp.float32)
    d_pre = jnp.concatenate(
        [grad_f * gate_sig, grad_f * lin_part * gate_sig * (1.0 - gate_sig)], axis=-1
    ).astype(jnp.bfloat16)
    d_weight = jnp.einsum("slh,slg->hg", activ_b, d_pre, preferred_element_type=jnp.float32)
    d_glu_bias = jnp.sum(d_pre.astype(jnp.float32), axis=(0, 1))
    d_act = jnp.einsum("slg,hg->slh", d_pre, weight_b, preferred_element_type=jnp.float32)
    d_mix = gelu_pull(d_act)[0].astype(jnp.bfloat16)
    d_mix_f = d_mix.astype(jnp.float32)
    d_skip = jnp.sum(d_mix_f * normed, axis=(0, 1))
    mix_re, mix_im = to_spectrum(d_mix[0])
    d_kernel = from_spectrum(
        source_re * mix_re + source_im * mix_im, source_re * mix_im - source_im * mix_re
    ).T
    right_re, right_im = to_spectrum(passed_along(d_mix, "seq", -1)[0])
    sum_re = mix_re + sign * right_im
    sum_im = mix_im - sign * right_re
    d_conv = from_spectrum(
        kernel_re * sum_re + kernel_im * sum_im, kernel_re * sum_im - kernel_im * sum_re
    )[None]
    d_normed = d_conv + skip_full * d_mix_f
    d_gain = jnp.sum(d_normed * x_hat, axis=(0, 1))
    d_shift = jnp.sum(d_normed, axis=(0, 1))
    scaled = d_normed * gain_full
    d_input = (
        inv_std
        * (
            scaled
            - jnp.mean(scaled, axis=-1, keepdims=True)
            - x_hat * jnp.mean(scaled * x_hat, axis=-1, keepdims=True)
        )
        + grad_f
    )
    grad_in = d_input.astype(jnp.bfloat16)
    summed = (
        lax.psum_scatter(d_gain, ("dp", "seq"), scatter_dimension=0, tiled=True),
        lax.psum_scatter(d_shift, ("dp", "seq"), scatter_dimension=0, tiled=True),
        lax.psum_scatter(d_skip, ("dp", "seq"), scatter_dimension=0, tiled=True),
        lax.psum_scatter(d_weight, ("dp", "seq"), scatter_dimension=0, tiled=True),
        lax.psum_scatter(d_glu_bias, ("dp", "seq"), scatter_dimension=0, tiled=True),
        lax.psum_scatter(d_kernel, ("dp", "seq"), scatter_dimension=0, tiled=True),
    )
    _, own_pull = jax.vjp(partial(kernel_block, start=0, count=KTAPS), *mode_own)
    mode_grads = own_pull(summed[5])
    return (
        result,
        grad_in,
        summed[0],
        summed[1],
        summed[2],
        summed[3],
        summed[4],
        mode_grads[0],
        mode_grads[1],
        mode_grads[2],
        mode_grads[3],
    )


MESH = pl.DeviceIdType.MESH
ROWS = 16


def pair_lanes(value):
    return jnp.concatenate([value[:8], value[8:]], axis=1)


def unpair_lanes(value):
    half = value.shape[1] // 2
    return jnp.concatenate([value[:, :half], value[:, half:]], axis=0)


def column_of(row):
    n = row.shape[1]
    at = lax.broadcasted_iota(jnp.int32, (n, n), 0) == lax.broadcasted_iota(jnp.int32, (n, n), 1)
    return jnp.sum(jnp.where(at, jnp.broadcast_to(row, (n, n)), 0.0), axis=1, keepdims=True)


def row_of(column):
    n = column.shape[0]
    at = lax.broadcasted_iota(jnp.int32, (n, n), 0) == lax.broadcasted_iota(jnp.int32, (n, n), 1)
    return jnp.sum(jnp.where(at, jnp.broadcast_to(column, (n, n)), 0.0), axis=0, keepdims=True)


def mode_terms(ldt, lar, ai, cc):
    n_modes = lar.shape[1]
    dt = column_of(jnp.exp(ldt))
    dt = jnp.concatenate(
        [jnp.broadcast_to(dt[:8], (8, n_modes)), jnp.broadcast_to(dt[8:], (8, n_modes))], axis=1
    )
    a_re, a_im = -jnp.exp(pair_lanes(lar)), pair_lanes(ai)
    decay, turn = a_re * dt, a_im * dt
    growth = jnp.exp(decay)
    z_re, z_im = growth * jnp.cos(turn), growth * jnp.sin(turn)
    ex_re, ex_im = z_re - 1.0, z_im
    norm_sq = a_re * a_re + a_im * a_im
    r_re = (ex_re * a_re + ex_im * a_im) / norm_sq
    r_im = (ex_im * a_re - ex_re * a_im) / norm_sq
    c_re, c_im = pair_lanes(cc[:, :n_modes]), pair_lanes(cc[:, n_modes:])
    w_re, w_im = c_re * r_re - c_im * r_im, c_re * r_im + c_im * r_re
    return dt, (a_re, a_im), (z_re, z_im), norm_sq, (r_re, r_im), (c_re, c_im), (w_re, w_im)


def times(a, b):
    return a[0] * b[0] - a[1] * b[1], a[0] * b[1] + a[1] * b[0]


def conj_times(a, b):
    return a[0] * b[0] + a[1] * b[1], a[0] * b[1] - a[1] * b[0]


def split_low(value):
    high = value.astype(jnp.bfloat16)
    return high, (value - high.astype(jnp.float32)).astype(jnp.bfloat16)


def dot_nn(a, b):
    return lax.dot_general(a, b, (((1,), (0,)), ((), ())), preferred_element_type=jnp.float32)


def dot_nt(a, b):
    return lax.dot_general(a, b, (((1,), (1,)), ((), ())), preferred_element_type=jnp.float32)


def layer_kernel(
    x_hbm, g_hbm, fwd_hbm, most_hbm, rest_hbm, inv_hbm, pick_hbm, mask_hbm,
    w_hbm, gain_hbm, shift_hbm, skip_hbm, bias_hbm, ldt_hbm, lar_hbm, ai_hbm, cc_hbm,
    res_v, gin_v, dgain_ref, dshift_ref, dskip_ref, dw_ref, dbias_ref, dldt_ref, dlar_ref, dai_ref, dcc_ref,
    w_ref, gain_ref, shift_ref, skip_ref, bias_ref, ldt_ref, lar_ref, ai_ref, cc_ref,
    x_v, g_v, left_v, fwd, fwd_most, fwd_rest, inv, pick, mask, kern, weight, base_high, base_low, leaps, lines_f,
    share_in, share_out, share_in1, share_mid, share_in2, vector_rows, rows_f, x_hat, inv_std, left_hat, normed, own_b, left_b,
    k_raw, k_spec, u_spec, mixed, slope, activ, activ_t, d_mix, right_v, d_spec, d_norm,
    dw_own, dw_in1, dw_mid, dw_in2, dw_low, dw_in3, dw_end, dw_in4, end_in1, end_mid, end_in2,
    dk_own, dk_low, dk_in1, dk_mid, dk_cut, dk_in2, dk_end, dk_out, dk_in3,
    local, sends, recvs,
):
    f32, bf16 = jnp.float32, jnp.bfloat16
    tokens, channels = x_v.shape
    taps = KTAPS
    half, fourth = taps // 2, taps // 4
    dp, seq = lax.axis_index("dp"), lax.axis_index("seq")
    index = dp * 4 + seq
    z, y, x, c = lax.div(dp, 2), lax.rem(dp, 2), lax.div(seq, 2), lax.rem(seq, 2)
    flip_y, flip_x, flip_c = 1 - y, 1 - x, 1 - c

    def device(z, y, x, c):
        return (z * 2 + y, x * 2 + c)

    z_peers = [(lax.rem(z + k, 4), y, x, c) for k in (1, 2, 3)]
    plane_peers = [
        (z, lax.rem(y + k // 2, 2), lax.rem(x + k % 2, 2), c) for k in (1, 2, 3)
    ]
    x_peer, y_peer, core_peer = (z, y, flip_x, c), (z, flip_y, x, c), (z, y, x, flip_c)
    other_peers = [core_peer] + [(peer[0], peer[1], peer[2], flip_c) for peer in plane_peers]
    groups = ("gather", "reduce", "vector")
    sent = dict.fromkeys(groups, 0)
    phase, used = ["gather"], [0]

    def claim():
        used[0] += 1
        return recvs.at[used[0] - 1]

    def size_of(ref):
        return math.prod(ref.shape) * jnp.dtype(ref.dtype).itemsize

    def arrive(semaphore, total):
        pltpu.make_async_copy(total, total, semaphore).wait()

    def start(copies, total, recv_sem=None):
        if recv_sem is None:
            recv_sem = claim()
        group = "vector" if copies[0][0].shape[-2:] == (1, 128) else phase[0]
        for source, target, peer in copies:
            sent[group] += size_of(source)
            pltpu.make_async_remote_copy(
                src_ref=source, dst_ref=target, send_sem=sends.at[groups.index(group)], recv_sem=recv_sem,
                device_id=device(*peer), device_id_type=MESH,
            ).start()
        return recv_sem, total

    def finish(arrival):
        arrive(*arrival)

    def load(copies):
        for copy in copies:
            copy.start()
        return copies

    def take(ref, lines, first=0, count=4):
        return jnp.concatenate([ref[first + i, lines, :] for i in range(count)], axis=1)

    def put(ref, lines, value, first=0):
        for i in range(value.shape[1] // 128):
            ref[first + i, lines, :] = value[:, 128 * i : 128 * (i + 1)]

    barrier = pltpu.get_barrier_semaphore()
    peers = z_peers + plane_peers + other_peers
    for peer in peers:
        pl.semaphore_signal(barrier, inc=1, device_id=device(*peer), device_id_type=MESH)
    def fetch(pairs, numbers):
        return load([pltpu.make_async_copy(source, target, local.at[i]) for i, (source, target) in zip(numbers, pairs)])

    params = fetch([
        (gain_hbm, gain_ref), (shift_hbm, shift_ref), (skip_hbm, skip_ref), (bias_hbm, bias_ref), (w_hbm, w_ref),
        (ldt_hbm, ldt_ref), (lar_hbm, lar_ref), (ai_hbm, ai_ref), (cc_hbm, cc_ref),
    ], range(9))
    loads = fetch([
        (x_hbm, x_v), (pick_hbm, pick), (mask_hbm, mask), (fwd_hbm, fwd), (most_hbm, fwd_most), (rest_hbm, fwd_rest),
        (inv_hbm, inv), (g_hbm, g_v),
    ], (9, 10, 10, 11, 11, 11, 12, 13))
    three, place = pl.ds(0, 3), (y * 2 + x) * 2 + c

    def same(ref, peers, total, recv_sem=None):
        return start([(ref, ref, peer) for peer in peers], total, recv_sem)

    def load_all(number, refs):
        arrive(local.at[number], u_spec.at[pl.ds(0, sum(size_of(ref) for ref in refs) // (4 * channels)), :])

    right_sender, left_sender = sends.at[3], sends.at[4]
    right_copies = [
        pltpu.make_async_remote_copy(
            src_ref=x_hbm.at[at], dst_ref=left_v.at[at], send_sem=right_sender, recv_sem=claim(),
            device_id=(dp, seq + 1), device_id_type=MESH,
        )
        for at in (pl.ds(0, tokens - fourth), pl.ds(tokens - fourth, fourth))
    ]

    def prepare_shares():
        for copy in params:
            copy.wait()
        low = [ref[...].astype(bf16).astype(f32) for ref in (gain_ref, shift_ref, skip_ref, bias_ref)]
        share_in[z, place] = jnp.concatenate(low + [jnp.zeros((1, 128 - 5 * ROWS), f32)], axis=1)
        for q in range(4):
            weight[q, z, y, x, c] = jnp.concatenate(
                [w_ref[:, 128 * q : 128 * q + 128], w_ref[:, channels + 128 * q : channels + 128 * q + 128]], axis=1
            ).astype(bf16)

    def prepare_taps():
        _, _, unit, _, _, _, coef = mode_terms(ldt_ref[...], lar_ref[...], ai_ref[...], cc_ref[...])
        steps, power = [], times(unit, unit)
        for _ in range(8):
            steps.append(power)
            power = times(power, power)
        for p in range(8):
            def row(value):
                return value[0][p : p + 1], value[1][p : p + 1]

            def table(factors):
                sub = lax.broadcasted_iota(jnp.int32, (8, 128), 0)
                tile = None
                for bit, factor in enumerate(factors):
                    on = lax.rem(lax.div(sub, 2**bit), 2) == 1
                    factor = tuple(jnp.where(on, part, rest) for part, rest in zip(row(factor), (1.0, 0.0)))
                    tile = factor if tile is None else times(tile, factor)
                return tile

            base = table(steps[:3])
            for step in steps[3:6]:
                more = times(base, row(step))
                base = tuple(jnp.concatenate([old, new], axis=0) for old, new in zip(base, more))
            leap = table([steps[6], steps[7], unit])
            leaps[p, 0], leaps[p, 1] = leap
            at = slice(256 * p, 256 * p + 256)
            high, low = split_low(jnp.concatenate(base, axis=1))
            base_high[:, at], base_low[:, at] = high, low
            lead = times(row(coef), leap)
            lead = jnp.concatenate([lead[0], -lead[1]], axis=1)
            first = lax.rem(lax.broadcasted_iota(jnp.int32, (8, 256), 1), 128) < 64
            lead = jnp.concatenate([jnp.where(first, lead, 0.0), jnp.where(first, 0.0, lead)], axis=0)
            lead_high, lead_low = split_low(lead)
            taps_of = dot_nt(
                jnp.concatenate([lead_high, lead_low, lead_high], axis=1), jnp.concatenate([high, high, low], axis=1)
            )
            taps_of = jnp.concatenate([taps_of, taps_of], axis=1)
            lines_f[8 * p : 8 * p + 8], lines_f[8 * p + 64 : 8 * p + 72] = taps_of[:8], taps_of[8:]
        own = jnp.concatenate([lines_f[pl.ds(m, ROWS, stride=8), :][:, :64] for m in range(8)], axis=1)
        kern[z, y, x, c] = (2.0 * own).astype(bf16)

    late = z == 3

    @pl.when(jnp.logical_not(late))
    def _():
        prepare_shares()
        prepare_taps()

    pl.semaphore_wait(barrier, len(peers))

    @pl.when(late)
    def _():
        prepare_shares()

    share_plane = same(share_in.at[z, place], plane_peers + other_peers, share_in.at[0, pl.ds(0, 7)])
    weight_x = same(weight.at[:, z, y, x, c], [x_peer], weight.at[:, 0, 0, 0, 0])

    @pl.when(seq < 3)
    def _():
        right_copies[0].start()

    @pl.when(late)
    def _():
        prepare_taps()

    kern_z = same(kern.at[z, y, x, c], z_peers, kern.at[three, 0, 0, 0])
    finish(share_plane)
    share_z = same(share_in.at[z], z_peers, share_in.at[three])
    finish(weight_x)

    def weight_to_z(q):
        return same(weight.at[q, z, y, :, c], z_peers, weight.at[q, three, 0, :, 0])

    def weight_to_y(q):
        finish(weight_z[q])
        piece = weight.at[q, :, y, :, c]
        same(piece, [core_peer], piece, core_recvs[half_of[q]])
        return same(piece, [y_peer], weight.at[q, :, 0, :, 0])

    def weight_to_core(q):
        finish(weight_y[q])
        piece = weight.at[q, :, flip_y, :, c]
        same(piece, [core_peer], piece, core_recvs[half_of[q]])

    pairs, half_of = ((0, 3), (1, 2)), (0, 1, 1, 0)
    core_recvs = [claim(), claim()]
    weight_core = [(sem, weight.at[pl.ds(0, 2), :, :, :, 0]) for sem in core_recvs]
    weight_z = [weight_to_z(0)]
    last_y = same(weight.at[3, z, y, :, c], [y_peer], weight.at[3, 0, 0, :, 0])

    def last_to_z():
        finish(last_y)
        return same(weight.at[3, z, :, :, c], z_peers, weight.at[3, three, :, :, 0])

    def last_to_core():
        finish(last_z)
        same(weight.at[3, :, :, :, c], [core_peer], weight.at[3, :, :, :, 0], core_recvs[half_of[3]])

    def normalise(source, hat, keep_std, begin, end):
        for first in range(begin, end, 32):
            at = slice(first, first + 32)
            value = source[at, :].astype(f32)
            centered = value - jnp.mean(value, axis=1, keepdims=True)
            scale = lax.rsqrt(jnp.mean(centered * centered, axis=1, keepdims=True) + EPS)
            put(hat, at, centered * scale)
            if keep_std:
                inv_std[at, :] = jnp.broadcast_to(scale, (32, 128))

    loads[0].wait()
    normalise(x_v, x_hat, True, 0, tokens)
    finish(kern_z)
    halves = [pl.ds(0, 2), pl.ds(2, 2)]
    kern_plane = [same(kern.at[at, y, x, c], plane_peers, dk_in2.at[:, at]) for at in halves]

    weight_z.append(weight_to_z(1))
    weight_z.append(weight_to_z(2))
    finish(share_z)

    @pl.when(seq < 3)
    def _():
        right_copies[1].start()

    load_all(10, (pick, mask))
    shares = share_in[...].reshape(32, 1, 128).reshape(32, 128).astype(bf16)
    spread = dot_nn(shares, pick[...]) * mask[...].astype(f32)
    spread = jnp.sum(spread, axis=0, keepdims=True)
    rows_f[...] = jnp.concatenate(
        [spread[:, channels * i : channels * (i + 1)] for i in range(5)] + [jnp.zeros((3, channels), f32)], axis=0
    )
    gain, shift = rows_f[0:1, :], rows_f[1:2, :]

    def every_other(i, parity):
        return pl.ds(128 * i + parity, 64, stride=2)

    def sixty_four(i):
        return pl.ds(pl.multiple_of(64 * i, 64), 64)

    def shifted(i, _):
        at = pl.ds(pl.multiple_of(i * 128, 128), 128)
        put(normed, at, take(x_hat, at) * gain + shift)
        for parity in range(2):
            own_b[parity, sixty_four(i)] = take(normed, every_other(i, parity)).astype(bf16)
        return 0

    lax.fori_loop(0, tokens // 128, shifted, 0)
    load_all(11, (fwd, fwd_most, fwd_rest))
    load_all(12, (inv,))
    wide = 256

    def lanes(j):
        return pl.ds(pl.multiple_of(j * wide, wide), wide)

    few = 16

    def sign_of(r):
        return 1 if r < half // 2 else -1

    def transform(block, exact):
        both = []
        for parity, rows in enumerate(block):
            if exact:
                both.append(dot_nn(fwd[parity], jnp.concatenate([rows, rows], axis=0)))
            else:
                both.append(dot_nn(fwd[parity, :, :half], rows))
        return jnp.concatenate(both, axis=1)

    def joined(both, r):
        parts = both[r : r + few], both[half + r : half + r + few]
        width = both.shape[1] // 2
        even, odd = [part[:, :width] for part in parts], [part[:, width:] for part in parts]
        return tuple(a + b for a, b in zip(even, odd)), tuple(a - b for a, b in zip(even, odd))

    def places(r):
        return [pl.ds(first + r, few) for first in (0, taps, half, taps + half)]

    def keep(ref, at, r, pair):
        for lines, part in zip(places(r), pair[0] + pair[1]):
            ref[lines, at] = part

    def kept(ref, at, r):
        parts = [ref[lines, at] for lines in places(r)]
        return parts[:2], parts[2:]

    def signals(pairs_at, exact):
        lines = None
        for r in range(0, half, few):
            pairs = pairs_at(r)
            lines = lines or [[[[], []] for _ in range(2)] for _ in pairs]
            for (a, b), parities in zip(pairs, lines):
                for k, (x, y) in enumerate(zip(a, b)):
                    for parity, value in enumerate((x + y, x - y)):
                        parities[parity][k].append(split_low(value) if exact else (value.astype(bf16),))
        results = []
        for parities in lines:
            both = []
            for parity, (real, imag) in enumerate(parities):
                parts = [jnp.concatenate([line[i] for line in real + imag], axis=0) for i in range(2 if exact else 1)]
                if exact:
                    high, low = parts
                    both.append(dot_nn(inv[parity], jnp.concatenate([high, high, low], axis=0)))
                else:
                    both.append(dot_nn(inv[parity, :, : 2 * half], parts[0]))
            results.append(jnp.concatenate(both, axis=1))
        return results

    def signal(pair_at, exact):
        return signals(lambda r: (pair_at(r),), exact)[0]

    def each(function, pairs):
        return tuple(function(*values) for values in zip(*pairs))

    def swung(value, sign):
        return (value[1], -value[0]) if sign > 0 else (-value[1], value[0])

    def own_spectrum(j):
        at = lanes(j)
        both = transform((own_b[0, :, at], own_b[1, :, at]), True)
        for r in range(0, half, few):
            keep(u_spec, at, r, joined(both, r))

    own_spectrum(0)
    own_spectrum(1)
    last_z = last_to_z()
    weight_y = [weight_to_y(0)]

    def left_block(i):
        first, last = (0, 3) if i == 0 else (3, 4)
        right_copies[i].wait_recv()
        normalise(left_v, left_hat, False, 128 * first, 128 * last)
        for k in range(first, last):
            for parity in range(2):
                value = take(left_hat, pl.ds(128 * k + parity, 64, stride=2)) * gain + shift
                left_b[parity, 64 * k : 64 * k + 64] = value.astype(bf16)
        at = slice(64 * first, 64 * last)
        matrix = (fwd_most if i == 0 else fwd_rest)[...]
        for j in range(2):
            lane = slice(wide * j, wide * (j + 1))
            both = [left_b[parity, at, lane] for parity in range(2)]
            both = [dot_nn(matrix[k], jnp.concatenate([rows, rows], axis=0)) for k, rows in enumerate(both)]
            both = jnp.concatenate(both, axis=1)
            lines = slice(taps * j, taps * (j + 1))
            if i == 0:
                d_spec[lines, :] = both
                continue
            both += d_spec[lines, :]
            for r in range(0, half, few):
                turns = [swung(value, -sign_of(r)) for value in joined(both, r)]
                old = kept(u_spec, lanes(j), r)
                keep(u_spec, lanes(j), r, tuple(tuple(a + b for a, b in zip(x, y)) for x, y in zip(old, turns)))

    @pl.when(seq > 0)
    def _():
        left_block(0)

    @pl.when(seq == 0)
    def _():
        left_hat[...] = jnp.zeros_like(left_hat)

    weight_y.append(weight_to_y(1))
    kern_core = []
    for arrival, at in zip(kern_plane, halves):
        finish(arrival)
        kern_core.append(same(kern.at[at, :, :, c], [core_peer], kern.at[at, :, :, 0]))

    def kernel_transform(j):
        rows = kern[2 * j : 2 * j + 2].reshape(wide, taps)
        rows = [jnp.concatenate([rows[:, at]] * 2, axis=1) for at in (slice(0, half), slice(half, taps))]
        return jnp.concatenate([dot_nt(fwd[parity], part) for parity, part in enumerate(rows)], axis=1)

    def convolve(j, both):
        at = lanes(j)

        def product(r):
            k = joined(both, r)
            keep(k_spec, at, r, k)
            return each(times, (k, kept(u_spec, at, r)))

        both = signal(product, True)
        for parity in range(2):
            put(mixed, pl.ds(parity, half, stride=2), both[:, wide * parity : wide * (parity + 1)], 2 * j)

    def activate(j):
        for tile in (2 * j, 2 * j + 1):
            at = slice(128 * tile, 128 * tile + 128)
            for start_at in range(0, tokens, 128):
                lines = slice(start_at, start_at + 128)
                value = mixed[tile, lines, :] + rows_f[2:3, at] * normed[tile, lines, :]
                chance = 0.5 + 0.5 * lax.erf(value * (0.5**0.5))
                slope[lines, at] = chance + value * jnp.exp(value * value * -0.5 - 0.5 * float(np.log(2.0 * np.pi)))
                low = (value * chance).astype(bf16)
                activ[lines, at] = low
                activ_t[at, lines] = low.T

    finish(kern_core[0])
    k_raw[0] = kernel_transform(0)
    weight_y.append(weight_to_y(2))

    @pl.when(seq > 0)
    def _():
        left_block(1)

    weight_to_core(0)
    finish(kern_core[1])
    second_half = kernel_transform(1)
    convolve(0, k_raw[0])
    weight_to_core(1)
    last_to_core()
    convolve(1, second_half)
    activate(0)
    activate(1)
    weight_to_core(2)
    loads[-1].wait()

    def matrix_of(h):
        return jnp.concatenate([weight[q].reshape(channels, 256) for q in pairs[h]], axis=1)

    def gates(h, pre):
        lines_out = []
        sums = [jnp.zeros((32, 128), f32) for _ in range(4)]
        for start_at in range(0, tokens, 32):
            lines = slice(start_at, start_at + 32)
            low = []
            for i, q in enumerate(pairs[h]):
                at = slice(128 * q, 128 * q + 128)
                lin = pre[lines, 256 * i : 256 * i + 128] + rows_f[3:4, at]
                gate = 0.5 + 0.5 * jnp.tanh(0.5 * (pre[lines, 256 * i + 128 : 256 * i + 256] + rows_f[4:5, at]))
                grad = g_v[lines, at].astype(f32)
                product = lin * gate
                res_v[lines, at] = (x_v[lines, at].astype(f32) + product).astype(bf16)
                low += [(grad * gate).astype(bf16), (grad * (product - product * gate)).astype(bf16)]
            sums = [total + part.astype(f32) for total, part in zip(sums, low)]
            lines_out.append(jnp.concatenate(low, axis=1))
        for i, q in enumerate(pairs[h]):
            for k in range(2):
                rows_f[3 + k : 4 + k, 128 * q : 128 * q + 128] = jnp.sum(sums[2 * i + k], axis=0, keepdims=True)
        return jnp.concatenate(lines_out, axis=0)

    def weight_grad(h, low):
        grad = dot_nn(activ_t[...], low).astype(bf16)
        for i, q in enumerate(pairs[h]):
            dw_own[q] = grad[:, 256 * i : 256 * i + 256].reshape(4, 2, 2, 2, ROWS, 256)
            start([(dw_own.at[q, :, :, :, flip_c], dw_in1.at[q], core_peer)], dw_in1.at[q], dw_recvs[h])

    def mix_grad(d_act):
        total = jnp.zeros((32, channels), f32)
        for start_at in range(0, tokens, 32):
            lines = slice(start_at, start_at + 32)
            mix = (d_act[lines] * slope[lines, :]).astype(bf16).astype(f32)
            total += mix * take(normed, lines)
            put(mixed, lines, mix)
        rows_f[2:3, :] = jnp.sum(total, axis=0, keepdims=True)
        for parity in range(2):
            for start_at in range(0, half, 64):
                part = take(mixed, pl.ds(2 * start_at + parity, 64, stride=2))
                d_mix[parity, start_at : start_at + 64] = part.astype(bf16)

    def core_sum(q):
        if half_of[q] not in summed:
            summed.add(half_of[q])
            arrive(dw_recvs[half_of[q]], dw_in1.at[pl.ds(0, 2)])
        dw_mid[q] = (dw_own[q, :, :, :, c].astype(f32) + dw_in1[q].astype(f32)).astype(bf16)

    def to_y(q):
        core_sum(q)
        dw_y[q] = start([(dw_mid.at[q, :, flip_y], dw_in2.at[q], y_peer)], dw_in2.at[q])

    def end_to_z(q):
        core_sum(q)
        copies = [(dw_mid.at[q, peer[0]], end_in1.at[q, i], peer) for i, peer in enumerate(z_peers)]
        end_z[q] = start(copies, end_in1.at[q])

    def end_to_plane(q):
        finish(end_z[q])
        total = dw_mid[q, z].astype(f32)
        for i in range(3):
            total = total + end_in1[q, i].astype(f32)
        end_mid[q] = total.astype(bf16)
        copies = [(end_mid.at[q, peer[1], peer[2]], end_in2.at[q, i], peer) for i, peer in enumerate(plane_peers)]
        end_plane[q] = start(copies, end_in2.at[q])

    def write_out(q, total):
        dw_ref[:, 128 * q : 128 * q + 128] = total[:, :128]
        dw_ref[:, channels + 128 * q : channels + 128 * q + 128] = total[:, 128:]

    def end_of(q):
        finish(end_plane[q])
        total = end_mid[q, y, x].astype(f32)
        for i in range(3):
            total = total + end_in2[q, i].astype(f32)
        write_out(q, total)

    def to_z(q):
        finish(dw_y[q])
        dw_low[q] = (dw_mid[q, :, y].astype(f32) + dw_in2[q].astype(f32)).astype(bf16)
        copies = [(dw_low.at[q, peer[0]], dw_in3.at[q, i], peer) for i, peer in enumerate(z_peers)]
        dw_z[q] = start(copies, dw_in3.at[q])

    def to_x(q):
        finish(dw_z[q])
        total = dw_low[q, z].astype(f32)
        for i in range(3):
            total = total + dw_in3[q, i].astype(f32)
        dw_end[q] = total.astype(bf16)
        dw_x[q] = start([(dw_end.at[q, flip_x], dw_in4.at[q], x_peer)], dw_in4.at[q])

    def to_end(q):
        finish(dw_x[q])
        write_out(q, dw_end[q, x].astype(f32) + dw_in4[q].astype(f32))

    skip = rows_f[2:3, :]
    dw_y, dw_z, dw_x, end_z, end_plane, summed = {}, {}, {}, {}, {}, set()
    phase[0], dw_recvs = "reduce", [claim(), claim()]
    finish(weight_core[0])
    first_low = gates(0, dot_nn(activ[...], matrix_of(0)))
    weight_grad(0, first_low)
    finish(weight_core[1])
    second_low = gates(1, dot_nn(activ[...], matrix_of(1)))
    d_act = dot_nt(
        jnp.concatenate([first_low, second_low], axis=1), jnp.concatenate([matrix_of(0), matrix_of(1)], axis=1)
    )
    mix_grad(d_act)
    left_pieces = ((0, 256), (256, 256))
    left_copies = [
        pltpu.make_async_remote_copy(
            src_ref=d_mix.at[:, :, pl.ds(first, width)], dst_ref=right_v.at[:, :, pl.ds(first, width)], send_sem=left_sender,
            recv_sem=claim(), device_id=(dp, seq - 1), device_id_type=MESH,
        )
        for first, width in left_pieces
    ]

    @pl.when(seq > 0)
    def _():
        for copy in left_copies[:1]:
            copy.start()

    to_y(0)
    end_to_z(3)
    weight_grad(1, second_low)

    def mix_transform(j):
        at = lanes(j)
        return transform((d_mix[0, :, at], d_mix[1, :, at]), False)

    def kernel_grad(j, both):
        at = lanes(j)

        def product(r):
            d = joined(both, r)
            keep(d_spec, at, r, d)
            return each(conj_times, (kept(u_spec, at, r), d))

        both = signal(product, False)
        grad = jnp.concatenate([both[:, :wide].T, both[:, wide:].T], axis=1).reshape(2, 2, 2, 2, ROWS, taps)
        dk_own[2 * j : 2 * j + 2] = grad
        dk_low[2 * j : 2 * j + 2] = grad.astype(bf16)

    def kernel_middle():
        finish(dk_core)
        for i in range(4):
            total = dk_own[i, :, :, c] + dk_in1[i].astype(f32)
            dk_mid[i] = total
            dk_cut[i] = total.astype(bf16)
        return start([(dk_cut.at[:, peer[1], peer[2]], dk_in2.at[i], peer) for i, peer in enumerate(plane_peers)], dk_in2)

    def kernel_end():
        finish(dk_plane)
        for i in range(4):
            total = dk_mid[i, y, x]
            for k in range(3):
                total = total + dk_in2[k, i].astype(f32)
            dk_end[i] = total
            dk_out[i] = total.astype(bf16)
        return start([(dk_out.at[peer[0]], dk_in3.at[i], peer) for i, peer in enumerate(z_peers)], dk_in3)

    def own_grad(j):
        at = lanes(j)

        def product(r):
            return each(conj_times, (kept(k_spec, at, r), kept(d_spec, at, r)))

        def products(r):
            pair = product(r)
            return pair, tuple(swung(value, sign_of(r)) for value in pair)

        own, back = signals(products, False)
        d_gain, d_shift = jnp.zeros((1, wide), f32), jnp.zeros((1, wide), f32)
        for parity in range(2):
            lines = pl.ds(parity, half, stride=2)
            columns = slice(wide * parity, wide * (parity + 1))
            grad = own[:, columns] + rows_f[5:6, at] * d_mix[parity, :, at].astype(f32)
            put(d_norm, lines, grad, 2 * j)
            before = jnp.where(seq > 0, back[:, columns], 0.0)
            d_gain += jnp.sum(
                grad * take(x_hat, lines, 2 * j, 2) + before * take(left_hat, lines, 2 * j, 2), axis=0, keepdims=True
            )
            d_shift += jnp.sum(grad + before, axis=0, keepdims=True)
        rows_f[6:7, at], rows_f[7:8, at] = d_gain, d_shift

    def right_grad(i):
        first, width = left_pieces[i]
        at = slice(first, first + width)
        left_copies[i].wait_recv()
        both = transform((right_v[0, :, at], right_v[1, :, at]), False)

        def product(r):
            turns = [swung(value, sign_of(r)) for value in joined(both, r)]
            return each(conj_times, (kept(k_spec, at, r), turns))

        both = signal(product, False)
        for parity in range(2):
            lines = pl.ds(parity, half, stride=2)
            more = both[:, width * parity : width * (parity + 1)]
            put(d_norm, lines, take(d_norm, lines, first // 128, width // 128) + more, first // 128)

    rows_f[5:6, :] = skip
    first_half, second_half = mix_transform(0), mix_transform(1)
    kernel_grad(0, first_half)
    kernel_grad(1, second_half)
    dk_core = start([(dk_low.at[:, :, :, flip_c], dk_in1, core_peer)], dk_in1)
    end_to_z(1)
    to_y(2)
    own_grad(0)
    dk_plane = kernel_middle()

    @pl.when(seq > 0)
    def _():
        for copy in left_copies[1:]:
            copy.start()

    own_grad(1)
    to_z(0)
    vector = jnp.concatenate([rows_f[6:7, :], rows_f[7:8, :], rows_f[2:3, :], rows_f[3:4, :], rows_f[4:5, :]], axis=1)
    high, low = split_low(jnp.broadcast_to(vector, mask.shape) * mask[...].astype(f32))
    shares = dot_nt(high, pick[...]) + dot_nt(low, pick[...])
    share_out[...] = shares.reshape(32, 1, 128).reshape(4, 8, 1, 128)
    copies = [(share_out.at[peer[0]], share_in1.at[i], peer) for i, peer in enumerate(z_peers)]
    share_z = start(copies, share_in1)
    @pl.when(seq < 3)
    def _():
        right_grad(0)

    to_z(2)
    end_to_plane(3)
    dk_z = kernel_end()
    end_to_plane(1)
    to_x(0)
    finish(share_z)
    share_mid[...] = share_out[z] + share_in1[0] + share_in1[1] + share_in1[2]
    copies = [
        (share_mid.at[(peer[1] * 2 + peer[2]) * 2 + peer[3]], share_in2.at[i], peer)
        for i, peer in enumerate(plane_peers + other_peers)
    ]
    share_plane = start(copies, share_in2)

    to_x(2)

    @pl.when(seq < 3)
    def _():
        for i in range(1, len(left_pieces)):
            right_grad(i)


    @pl.when(seq < 3)
    def _():
        arrive(right_sender, x_v)

    @pl.when(seq > 0)
    def _():
        arrive(left_sender, d_mix)

    for first in range(0, tokens, 32):
        at = slice(first, first + 32)
        hat = [x_hat[i, at, :] for i in range(4)]
        grad = [d_norm[i, at, :] * rows_f[0:1, 128 * i : 128 * i + 128] for i in range(4)]
        mean = jnp.sum(sum(grad[1:], grad[0]), axis=1, keepdims=True) * (1.0 / channels)
        along = [one * other for one, other in zip(grad, hat)]
        along = jnp.sum(sum(along[1:], along[0]), axis=1, keepdims=True) * (1.0 / channels)
        for i in range(4):
            lane = slice(128 * i, 128 * i + 128)
            inner = inv_std[at, :] * (grad[i] - mean - hat[i] * along)
            gin_v[at, lane] = (inner + g_v[at, lane].astype(f32)).astype(bf16)
    dt, a, unit, norm_sq, ratio, coef, scaled = mode_terms(ldt_ref[...], lar_ref[...], ai_ref[...], cc_ref[...])
    inverse_a = (a[0] / norm_sq, -a[1] / norm_sq)
    end_of(3)
    end_of(1)
    finish(dk_z)
    d_kernel = dk_end[z]
    for k in range(3):
        d_kernel = d_kernel + dk_in3[k].astype(f32)

    for m in range(8):
        block = d_kernel[:, 64 * m : 64 * m + 64]
        block = jnp.concatenate([block, block], axis=1)
        for k in range(2):
            lines_f[pl.ds(8 * k + m, 8, stride=16), :] = block[8 * k : 8 * k + 8]
    at_row = lax.broadcasted_iota(jnp.int32, (8, 128), 0)
    first = lax.broadcasted_iota(jnp.int32, (8, 128), 1) < 64
    leap_of = (128 * lax.rem(at_row, 4) + lax.div(at_row, 4)).astype(f32)
    ramp = (2 * lax.broadcasted_iota(jnp.int32, (32, 64), 1)).astype(f32)
    sums = []
    for pair in range(4):
        plain = lines_f[32 * pair : 32 * pair + 32, :][:, :64]
        high, low = split_low(jnp.concatenate([plain, plain * ramp], axis=0))
        at = slice(512 * pair, 512 * pair + 512)
        table = jnp.concatenate([base_high[:, at], base_low[:, at], base_high[:, at]], axis=0)
        sums.append(dot_nn(jnp.concatenate([high, high, low], axis=1), table))
    zero = jnp.zeros((8, 128), f32)
    s0, s1 = [zero, zero], [zero, zero]
    for p in range(8):
        def part_of(begin, part):
            lane = 256 * (p % 2) + 128 * part
            block = sums[p // 2][begin + 16 * (p % 2) : begin + 16 * (p % 2) + 16, lane : lane + 128]
            return jnp.where(first, block[:8], block[8:])

        value, slope_of = [part_of(0, part) for part in range(2)], [part_of(32, part) for part in range(2)]
        leap = (leaps[p, 0], leaps[p, 1])
        slope_of = [one + leap_of * other for one, other in zip(slope_of, value)]
        for total, terms in ((s0, value), (s1, slope_of)):
            for part, product in enumerate(times(leap, terms)):
                total[part] = jnp.where(at_row == p, jnp.sum(product, axis=0, keepdims=True), total[part])
    d_coef = times(s0, ratio)
    half_g = times(times(coef, s0), times(unit, inverse_a))
    ramp_part = times(scaled, s1)
    half_g = (half_g[0] + ramp_part[0], half_g[1] + ramp_part[1])
    back = times(times(scaled, s0), inverse_a)
    q = (half_g[0] * dt - back[0], half_g[1] * dt - back[1])
    d_dt = 2.0 * dt * times(half_g, a)[0]
    dldt_ref[...] = row_of(jnp.sum(unpair_lanes(d_dt), axis=1, keepdims=True))[0]
    dlar_ref[...] = unpair_lanes(2.0 * q[0] * a[0])
    dai_ref[...] = unpair_lanes(-2.0 * q[1])
    dcc_ref[...] = jnp.concatenate([unpair_lanes(2.0 * d_coef[0]), unpair_lanes(-2.0 * d_coef[1])], axis=1)

    to_end(0)
    to_end(2)
    finish(share_plane)
    small = share_mid[place]
    for i in range(7):
        small = small + share_in2[i]
    for i, target in enumerate([dgain_ref, dshift_ref, dskip_ref]):
        target[...] = small[0, ROWS * i : ROWS * (i + 1)]
    dbias_ref[...] = small[0, 3 * ROWS : 5 * ROWS]
    arrive(sends.at[0], u_spec.at[pl.ds(0, sent["gather"] // (4 * channels)), :])
    arrive(sends.at[1], u_spec.at[pl.ds(0, sent["reduce"] // (4 * channels)), :])
    arrive(sends.at[2], vector_rows.at[pl.ds(0, sent["vector"] // 512)])


def finish_kernel(*refs):
    count = len(refs) // 2
    sems = refs[-1]
    copies = [pltpu.make_async_copy(refs[i], refs[count + i], sems.at[i]) for i in range(count)]
    for copy in copies:
        copy.start()
    for copy in copies:
        copy.wait()


def kernel_body(
    inputs, grad_out, ln_gain, ln_bias, skip_scale, w_glu, b_glu, log_dt, log_a_real, a_imag, c_coef
):
    _, tokens, channels = inputs.shape
    taps = KTAPS
    glu = w_glu.shape[1]
    f32, bf16 = jnp.float32, jnp.bfloat16
    order = np.concatenate([np.arange(0, taps // 2, 2), np.arange(1, taps // 2, 2)]) + 0.5
    forward, inverse = [], []
    for parity in range(2):
        angle = np.outer(order, 2 * np.arange(taps // 2) + parity) * (np.pi / taps)
        matrix = np.concatenate([np.cos(angle), -np.sin(angle)], axis=0)
        high = matrix.astype(bf16)
        low = (matrix - high.astype(np.float64)).astype(bf16)
        forward.append(np.concatenate([high, low], axis=1))
        inverse.append(np.concatenate([high.T, low.T, high.T], axis=1) * np.asarray(1.0 / taps, bf16))
    forward, inverse = np.stack(forward), np.stack(inverse)
    cut, end = 3 * taps // 8, taps // 2
    most, rest = (
        np.concatenate([forward[:, :, a:b], forward[:, :, end + a : end + b]], axis=2) for a, b in ((0, cut), (cut, end))
    )
    device_at, lane = np.arange(32)[:, None], np.arange(channels)[None, :]
    bias_lane = np.arange(2 * channels)[None, :]
    row = np.arange(128)[:, None]
    pick = np.concatenate(
        [row == i * ROWS + lane % ROWS for i in range(3)] + [row == 3 * ROWS + bias_lane % (2 * ROWS)], axis=1
    ).astype(bf16)
    mask = np.concatenate(
        [device_at == lane // ROWS] * 3 + [device_at == bias_lane // (2 * ROWS)], axis=1
    ).astype(bf16)
    hbm, vmem = pl.BlockSpec(memory_space=pl.ANY), pl.BlockSpec(memory_space=pltpu.VMEM)
    block = (tokens, channels)
    spec, tall = (2 * taps, channels), (channels // 128, tokens, 128)

    def space(*dims, kind=f32):
        return pltpu.VMEM(dims, kind)

    results = (
        (block, bf16), (block, bf16), ((ROWS,), f32), ((ROWS,), f32), ((ROWS,), f32), (w_glu.shape, f32),
        ((2 * ROWS,), f32), ((ROWS,), f32), (log_a_real.shape, f32), (a_imag.shape, f32), (c_coef.shape, f32),
    )
    outs = pl.pallas_call(
        layer_kernel,
        name="layer",
        out_shape=tuple(pltpu.VMEM(dims, kind) for dims, kind in results),
        in_specs=[hbm] * 17,
        out_specs=(vmem,) * len(results),
        scratch_shapes=[
            space(*w_glu.shape), space(1, ROWS), space(1, ROWS), space(1, ROWS), space(1, 2 * ROWS), space(1, ROWS),
            space(*log_a_real.shape), space(*a_imag.shape), space(*c_coef.shape),
            space(*block, kind=bf16), space(*block, kind=bf16), space(*block, kind=bf16),
            space(*forward.shape, kind=bf16), space(*most.shape, kind=bf16), space(*rest.shape, kind=bf16),
            space(*inverse.shape, kind=bf16),
            space(*pick.shape, kind=bf16), space(*mask.shape, kind=bf16),
            space(4, 2, 2, 2, ROWS, taps, kind=bf16), space(4, 4, 2, 2, 2, ROWS, 256, kind=bf16),
            space(64, 2048, kind=bf16), space(64, 2048, kind=bf16), space(8, 2, 8, 128), space(8 * ROWS, 128),
            space(4, 8, 1, 128), space(4, 8, 1, 128), space(3, 8, 1, 128), space(8, 1, 128), space(7, 1, 128),
            space(64, 1, 128),
            space(8, channels),
            space(*tall), space(tokens, 128), space(*tall), space(*tall),
            space(2, tokens // 2, channels, kind=bf16), space(2, tokens // 2, channels, kind=bf16),
            space(2, taps, taps), space(*spec), space(*spec), space(*tall), space(*block),
            space(*block, kind=bf16), space(channels, tokens, kind=bf16),
            space(2, tokens // 2, channels, kind=bf16), space(2, tokens // 2, channels, kind=bf16),
            space(*spec), space(*tall),
            space(4, 4, 2, 2, 2, ROWS, 256, kind=bf16), space(4, 4, 2, 2, ROWS, 256, kind=bf16),
            space(4, 4, 2, 2, ROWS, 256, kind=bf16), space(4, 4, 2, ROWS, 256, kind=bf16),
            space(4, 4, 2, ROWS, 256, kind=bf16), space(4, 3, 2, ROWS, 256, kind=bf16),
            space(4, 2, ROWS, 256, kind=bf16), space(4, ROWS, 256, kind=bf16),
            space(4, 3, 2, 2, ROWS, 256, kind=bf16), space(4, 2, 2, ROWS, 256, kind=bf16), space(4, 3, ROWS, 256, kind=bf16),
            space(4, 2, 2, 2, ROWS, taps), space(4, 2, 2, 2, ROWS, taps, kind=bf16), space(4, 2, 2, ROWS, taps, kind=bf16),
            space(4, 2, 2, ROWS, taps), space(4, 2, 2, ROWS, taps, kind=bf16), space(3, 4, ROWS, taps, kind=bf16),
            space(4, ROWS, taps), space(4, ROWS, taps, kind=bf16), space(3, ROWS, taps, kind=bf16),
            pltpu.SemaphoreType.DMA((14,)), pltpu.SemaphoreType.DMA((5,)), pltpu.SemaphoreType.DMA((39,)),
        ],
        compiler_params=pltpu.CompilerParams(
            collective_id=0, has_side_effects=True, vmem_limit_bytes=48 * 2**20
        ),
    )(*[
        pltpu.with_memory_space_constraint(value, pltpu.HBM)
        for value in (
            inputs.reshape(block), grad_out.reshape(block), forward, most, rest, inverse, pick, mask, w_glu,
            ln_gain.reshape(1, -1), ln_bias.reshape(1, -1), skip_scale.reshape(1, -1), b_glu.reshape(1, -1),
            log_dt.reshape(1, -1), log_a_real, a_imag, c_coef,
        )
    ])
    ended = pl.pallas_call(
        finish_kernel,
        name="finish",
        out_shape=tuple(jax.ShapeDtypeStruct(dims, kind) for dims, kind in results),
        in_specs=[vmem] * len(results),
        out_specs=(hbm,) * len(results),
        scratch_shapes=[pltpu.SemaphoreType.DMA((len(results),))],
    )(*[pltpu.with_memory_space_constraint(value, pltpu.VMEM) for value in outs])
    return (ended[0].reshape(inputs.shape), ended[1].reshape(inputs.shape)) + tuple(ended[2:])


def solution(mesh):
    in_specs = (
        P("dp", "seq", None),
        P("dp", "seq", None),
        P(("dp", "seq")),
        P(("dp", "seq")),
        P(("dp", "seq")),
        P(("dp", "seq"), None),
        P(("dp", "seq")),
        P(("dp", "seq")),
        P(("dp", "seq"), None),
        P(("dp", "seq"), None),
        P(("dp", "seq"), None),
    )
    out_specs = (
        P("dp", "seq", None),
        P("dp", "seq", None),
        P(("dp", "seq")),
        P(("dp", "seq")),
        P(("dp", "seq")),
        P(("dp", "seq"), None),
        P(("dp", "seq")),
        P(("dp", "seq")),
        P(("dp", "seq"), None),
        P(("dp", "seq"), None),
        P(("dp", "seq"), None),
    )
    quick = mesh.shape["dp"] == 8 and mesh.shape["seq"] == 4
    return jax.shard_map(kernel_body if quick else body, mesh=mesh, in_specs=in_specs, out_specs=out_specs, check_vma=False)
```

```python
import math
from functools import partial

import jax
import jax.numpy as jnp
import numpy as np
from jax import lax
from jax.experimental import pallas as pl
from jax.experimental.pallas import tpu as pltpu
from jax.sharding import PartitionSpec as P

KTAPS = 512


EPS = 1e-05


def passed_along(value, axis, steps):
    count = lax.axis_size(axis)
    first, last = (max(0, -steps), min(count, count - steps))
    return lax.ppermute(value, axis, [(source, source + steps) for source in range(first, last)])


def kernel_block(log_dt, log_a_real, a_imag, c_coef, start, count):
    mode_count = log_a_real.shape[1]
    step_size = jnp.exp(log_dt)[:, None]
    a_real = -jnp.exp(log_a_real)
    decay = a_real * step_size
    turn = a_imag * step_size
    growth = jnp.exp(decay)
    ex_re = growth * jnp.cos(turn) - 1.0
    ex_im = growth * jnp.sin(turn)
    norm_sq = a_real * a_real + a_imag * a_imag
    ratio_re = (ex_re * a_real + ex_im * a_imag) / norm_sq
    ratio_im = (ex_im * a_real - ex_re * a_imag) / norm_sq
    c_re = c_coef[:, :mode_count]
    c_im = c_coef[:, mode_count:]
    coef_re = c_re * ratio_re - c_im * ratio_im
    coef_im = c_re * ratio_im + c_im * ratio_re
    places = (start + jnp.arange(count)).astype(jnp.float32)
    phase = turn[:, :, None] * places
    damping = jnp.exp(decay[:, :, None] * places)
    terms = damping * (coef_re[:, :, None] * jnp.cos(phase) - coef_im[:, :, None] * jnp.sin(phase))
    return 2.0 * jnp.sum(terms, axis=1)


def transforms(taps):
    angle = np.outer(np.arange(taps) + 0.5, np.arange(taps)) * (np.pi / taps)
    forward = np.concatenate([np.cos(angle), -np.sin(angle)], axis=0)
    inverse = forward.T / taps
    return forward.astype(jnp.bfloat16), inverse.astype(jnp.bfloat16)


def body(
    inputs, grad_out, ln_gain, ln_bias, skip_scale, w_glu, b_glu, log_dt, log_a_real, a_imag, c_coef
):
    seq_count, own_len, channels = inputs.shape
    gain_low = ln_gain.astype(jnp.bfloat16)
    shift_low = ln_bias.astype(jnp.bfloat16)
    skip_low = skip_scale.astype(jnp.bfloat16)
    weight_low = w_glu.astype(jnp.bfloat16)
    bias_low = b_glu.astype(jnp.bfloat16)
    mode_own = (log_dt, log_a_real, a_imag, c_coef)
    own_kernel = kernel_block(*mode_own, 0, KTAPS).astype(jnp.bfloat16)
    gathered = (
        lax.all_gather(gain_low, ("dp", "seq"), axis=0, tiled=True),
        lax.all_gather(shift_low, ("dp", "seq"), axis=0, tiled=True),
        lax.all_gather(skip_low, ("dp", "seq"), axis=0, tiled=True),
        lax.all_gather(weight_low, ("dp", "seq"), axis=0, tiled=True),
        lax.all_gather(bias_low, ("dp", "seq"), axis=0, tiled=True),
        lax.all_gather(own_kernel, ("dp", "seq"), axis=0, tiled=True),
    )
    kernel_b = gathered[5]
    taps = own_len
    forward, inverse = transforms(taps)
    sign = jnp.where(jnp.arange(taps) % 2 == 0, 1.0, -1.0).astype(jnp.float32)[:, None]

    def to_spectrum(block):
        both = jnp.dot(forward, block, preferred_element_type=jnp.float32)
        return both[:taps], both[taps:]

    def from_spectrum(real, imag):
        both = jnp.concatenate([real, imag], axis=0).astype(jnp.bfloat16)
        return jnp.dot(inverse, both, preferred_element_type=jnp.float32)

    kernel_re, kernel_im = to_spectrum(kernel_b.T)
    gain_full = gathered[0].astype(jnp.float32)
    shift_full = gathered[1].astype(jnp.float32)
    skip_full = gathered[2].astype(jnp.float32)
    weight_b = gathered[3]
    glu_bias = gathered[4].astype(jnp.float32)
    x_float = inputs.astype(jnp.float32)
    row_mean = jnp.mean(x_float, axis=-1, keepdims=True)
    centered = x_float - row_mean
    row_var = jnp.mean(centered * centered, axis=-1, keepdims=True)
    inv_std = lax.rsqrt(row_var + EPS)
    x_hat = centered * inv_std
    normed = x_hat * gain_full + shift_full
    normed_b = normed.astype(jnp.bfloat16)
    own_re, own_im = to_spectrum(normed_b[0])
    left_re, left_im = to_spectrum(passed_along(normed_b, "seq", 1)[0])
    source_re = own_re - sign * left_im
    source_im = own_im + sign * left_re
    conv = from_spectrum(
        kernel_re * source_re - kernel_im * source_im,
        kernel_re * source_im + kernel_im * source_re,
    )
    mixed_pre = conv[None] + skip_full * normed
    activ, gelu_pull = jax.vjp(partial(jax.nn.gelu, approximate=False), mixed_pre)
    activ_b = activ.astype(jnp.bfloat16)
    glu_pre = (
        jnp.einsum("slh,hg->slg", activ_b, weight_b, preferred_element_type=jnp.float32) + glu_bias
    )
    half_dim = glu_pre.shape[-1] // 2
    lin_part = glu_pre[..., :half_dim]
    gate_sig = jax.nn.sigmoid(glu_pre[..., half_dim:])
    result = (x_float + lin_part * gate_sig).astype(jnp.bfloat16)
    grad_f = grad_out.astype(jnp.float32)
    d_pre = jnp.concatenate(
        [grad_f * gate_sig, grad_f * lin_part * gate_sig * (1.0 - gate_sig)], axis=-1
    ).astype(jnp.bfloat16)
    d_weight = jnp.einsum("slh,slg->hg", activ_b, d_pre, preferred_element_type=jnp.float32)
    d_glu_bias = jnp.sum(d_pre.astype(jnp.float32), axis=(0, 1))
    d_act = jnp.einsum("slg,hg->slh", d_pre, weight_b, preferred_element_type=jnp.float32)
    d_mix = gelu_pull(d_act)[0].astype(jnp.bfloat16)
    d_mix_f = d_mix.astype(jnp.float32)
    d_skip = jnp.sum(d_mix_f * normed, axis=(0, 1))
    mix_re, mix_im = to_spectrum(d_mix[0])
    d_kernel = from_spectrum(
        source_re * mix_re + source_im * mix_im, source_re * mix_im - source_im * mix_re
    ).T
    right_re, right_im = to_spectrum(passed_along(d_mix, "seq", -1)[0])
    sum_re = mix_re + sign * right_im
    sum_im = mix_im - sign * right_re
    d_conv = from_spectrum(
        kernel_re * sum_re + kernel_im * sum_im, kernel_re * sum_im - kernel_im * sum_re
    )[None]
    d_normed = d_conv + skip_full * d_mix_f
    d_gain = jnp.sum(d_normed * x_hat, axis=(0, 1))
    d_shift = jnp.sum(d_normed, axis=(0, 1))
    scaled = d_normed * gain_full
    d_input = (
        inv_std
        * (
            scaled
            - jnp.mean(scaled, axis=-1, keepdims=True)
            - x_hat * jnp.mean(scaled * x_hat, axis=-1, keepdims=True)
        )
        + grad_f
    )
    grad_in = d_input.astype(jnp.bfloat16)
    summed = (
        lax.psum_scatter(d_gain, ("dp", "seq"), scatter_dimension=0, tiled=True),
        lax.psum_scatter(d_shift, ("dp", "seq"), scatter_dimension=0, tiled=True),
        lax.psum_scatter(d_skip, ("dp", "seq"), scatter_dimension=0, tiled=True),
        lax.psum_scatter(d_weight, ("dp", "seq"), scatter_dimension=0, tiled=True),
        lax.psum_scatter(d_glu_bias, ("dp", "seq"), scatter_dimension=0, tiled=True),
        lax.psum_scatter(d_kernel, ("dp", "seq"), scatter_dimension=0, tiled=True),
    )
    _, own_pull = jax.vjp(partial(kernel_block, start=0, count=KTAPS), *mode_own)
    mode_grads = own_pull(summed[5])
    return (
        result,
        grad_in,
        summed[0],
        summed[1],
        summed[2],
        summed[3],
        summed[4],
        mode_grads[0],
        mode_grads[1],
        mode_grads[2],
        mode_grads[3],
    )


MESH = pl.DeviceIdType.MESH
ROWS = 16


def pair_lanes(value):
    return jnp.concatenate([value[:8], value[8:]], axis=1)


def unpair_lanes(value):
    half = value.shape[1] // 2
    return jnp.concatenate([value[:, :half], value[:, half:]], axis=0)


def column_of(row):
    n = row.shape[1]
    at = lax.broadcasted_iota(jnp.int32, (n, n), 0) == lax.broadcasted_iota(jnp.int32, (n, n), 1)
    return jnp.sum(jnp.where(at, jnp.broadcast_to(row, (n, n)), 0.0), axis=1, keepdims=True)


def row_of(column):
    n = column.shape[0]
    at = lax.broadcasted_iota(jnp.int32, (n, n), 0) == lax.broadcasted_iota(jnp.int32, (n, n), 1)
    return jnp.sum(jnp.where(at, jnp.broadcast_to(column, (n, n)), 0.0), axis=0, keepdims=True)


def mode_terms(ldt, lar, ai, cc):
    n_modes = lar.shape[1]
    dt = column_of(jnp.exp(ldt))
    dt = jnp.concatenate(
        [jnp.broadcast_to(dt[:8], (8, n_modes)), jnp.broadcast_to(dt[8:], (8, n_modes))], axis=1
    )
    a_re, a_im = -jnp.exp(pair_lanes(lar)), pair_lanes(ai)
    decay, turn = a_re * dt, a_im * dt
    growth = jnp.exp(decay)
    z_re, z_im = growth * jnp.cos(turn), growth * jnp.sin(turn)
    ex_re, ex_im = z_re - 1.0, z_im
    norm_sq = a_re * a_re + a_im * a_im
    r_re = (ex_re * a_re + ex_im * a_im) / norm_sq
    r_im = (ex_im * a_re - ex_re * a_im) / norm_sq
    c_re, c_im = pair_lanes(cc[:, :n_modes]), pair_lanes(cc[:, n_modes:])
    w_re, w_im = c_re * r_re - c_im * r_im, c_re * r_im + c_im * r_re
    return dt, (a_re, a_im), (z_re, z_im), norm_sq, (r_re, r_im), (c_re, c_im), (w_re, w_im)


def times(a, b):
    return a[0] * b[0] - a[1] * b[1], a[0] * b[1] + a[1] * b[0]


def conj_times(a, b):
    return a[0] * b[0] + a[1] * b[1], a[0] * b[1] - a[1] * b[0]


def split_low(value):
    high = value.astype(jnp.bfloat16)
    return high, (value - high.astype(jnp.float32)).astype(jnp.bfloat16)


def dot_nn(a, b):
    return lax.dot_general(a, b, (((1,), (0,)), ((), ())), preferred_element_type=jnp.float32)


def dot_nt(a, b):
    return lax.dot_general(a, b, (((1,), (1,)), ((), ())), preferred_element_type=jnp.float32)


def layer_kernel(
    x_hbm, g_hbm, fwd_hbm, most_hbm, rest_hbm, inv_hbm, pick_hbm, mask_hbm,
    w_hbm, gain_hbm, shift_hbm, skip_hbm, bias_hbm, ldt_hbm, lar_hbm, ai_hbm, cc_hbm,
    res_v, gin_v, dgain_ref, dshift_ref, dskip_ref, dw_ref, dbias_ref, dldt_ref, dlar_ref, dai_ref, dcc_ref,
    w_ref, gain_ref, shift_ref, skip_ref, bias_ref, ldt_ref, lar_ref, ai_ref, cc_ref,
    x_v, g_v, left_v, fwd, fwd_most, fwd_rest, inv, pick, mask, kern, weight, base_high, base_low, leaps, lines_f,
    share_in, share_out, share_in1, share_mid, share_in2, vector_rows, rows_f, x_hat, inv_std, left_hat, normed, own_b, left_b,
    k_raw, k_spec, u_spec, mixed, slope, activ, activ_t, d_mix, right_v, d_spec, d_norm,
    dw_own, dw_in1, dw_mid, dw_in2, dw_low, dw_in3, dw_end, dw_in4, end_in1, end_mid, end_in2,
    dk_own, dk_low, dk_in1, dk_mid, dk_cut, dk_in2, dk_end, dk_out, dk_in3,
    local, sends, recvs,
):
    f32, bf16 = jnp.float32, jnp.bfloat16
    tokens, channels = x_v.shape
    taps = KTAPS
    half, fourth = taps // 2, taps // 4
    dp, seq = lax.axis_index("dp"), lax.axis_index("seq")
    index = dp * 4 + seq
    z, y, x, c = lax.div(dp, 2), lax.rem(dp, 2), lax.div(seq, 2), lax.rem(seq, 2)
    flip_y, flip_x, flip_c = 1 - y, 1 - x, 1 - c

    def device(z, y, x, c):
        return (z * 2 + y, x * 2 + c)

    z_peers = [(lax.rem(z + k, 4), y, x, c) for k in (1, 2, 3)]
    plane_peers = [
        (z, lax.rem(y + k // 2, 2), lax.rem(x + k % 2, 2), c) for k in (1, 2, 3)
    ]
    x_peer, y_peer, core_peer = (z, y, flip_x, c), (z, flip_y, x, c), (z, y, x, flip_c)
    other_peers = [core_peer] + [(peer[0], peer[1], peer[2], flip_c) for peer in plane_peers]
    groups = ("gather", "reduce", "vector")
    sent = dict.fromkeys(groups, 0)
    phase, used = ["gather"], [0]

    def claim():
        used[0] += 1
        return recvs.at[used[0] - 1]

    def size_of(ref):
        return math.prod(ref.shape) * jnp.dtype(ref.dtype).itemsize

    def arrive(semaphore, total):
        pltpu.make_async_copy(total, total, semaphore).wait()

    def start(copies, total, recv_sem=None):
        if recv_sem is None:
            recv_sem = claim()
        group = "vector" if copies[0][0].shape[-2:] == (1, 128) else phase[0]
        for source, target, peer in copies:
            sent[group] += size_of(source)
            pltpu.make_async_remote_copy(
                src_ref=source, dst_ref=target, send_sem=sends.at[groups.index(group)], recv_sem=recv_sem,
                device_id=device(*peer), device_id_type=MESH,
            ).start()
        return recv_sem, total

    def finish(arrival):
        arrive(*arrival)

    def load(copies):
        for copy in copies:
            copy.start()
        return copies

    def take(ref, lines, first=0, count=4):
        return jnp.concatenate([ref[first + i, lines, :] for i in range(count)], axis=1)

    def put(ref, lines, value, first=0):
        for i in range(value.shape[1] // 128):
            ref[first + i, lines, :] = value[:, 128 * i : 128 * (i + 1)]

    barrier = pltpu.get_barrier_semaphore()
    peers = z_peers + plane_peers + other_peers
    for peer in peers:
        pl.semaphore_signal(barrier, inc=1, device_id=device(*peer), device_id_type=MESH)
    def fetch(pairs, numbers):
        return load([pltpu.make_async_copy(source, target, local.at[i]) for i, (source, target) in zip(numbers, pairs)])

    params = fetch([
        (gain_hbm, gain_ref), (shift_hbm, shift_ref), (skip_hbm, skip_ref), (bias_hbm, bias_ref), (w_hbm, w_ref),
        (ldt_hbm, ldt_ref), (lar_hbm, lar_ref), (ai_hbm, ai_ref), (cc_hbm, cc_ref),
    ], range(9))
    loads = fetch([
        (x_hbm, x_v), (pick_hbm, pick), (mask_hbm, mask), (fwd_hbm, fwd), (most_hbm, fwd_most), (rest_hbm, fwd_rest),
        (inv_hbm, inv), (g_hbm, g_v),
    ], (9, 10, 10, 11, 11, 11, 12, 13))
    three, place = pl.ds(0, 3), (y * 2 + x) * 2 + c

    def same(ref, peers, total, recv_sem=None):
        return start([(ref, ref, peer) for peer in peers], total, recv_sem)

    def load_all(number, refs):
        arrive(local.at[number], u_spec.at[pl.ds(0, sum(size_of(ref) for ref in refs) // (4 * channels)), :])

    right_sender, left_sender = sends.at[3], sends.at[4]
    right_copies = [
        pltpu.make_async_remote_copy(
            src_ref=x_hbm.at[at], dst_ref=left_v.at[at], send_sem=right_sender, recv_sem=claim(),
            device_id=(dp, seq + 1), device_id_type=MESH,
        )
        for at in (pl.ds(0, tokens - fourth), pl.ds(tokens - fourth, fourth))
    ]

    def prepare_shares():
        for copy in params:
            copy.wait()
        low = [ref[...].astype(bf16).astype(f32) for ref in (gain_ref, shift_ref, skip_ref, bias_ref)]
        share_in[z, place] = jnp.concatenate(low + [jnp.zeros((1, 128 - 5 * ROWS), f32)], axis=1)
        for q in range(4):
            weight[q, z, y, x, c] = jnp.concatenate(
                [w_ref[:, 128 * q : 128 * q + 128], w_ref[:, channels + 128 * q : channels + 128 * q + 128]], axis=1
            ).astype(bf16)

    def prepare_taps():
        _, _, unit, _, _, _, coef = mode_terms(ldt_ref[...], lar_ref[...], ai_ref[...], cc_ref[...])
        steps, power = [], times(unit, unit)
        for _ in range(8):
            steps.append(power)
            power = times(power, power)
        for p in range(8):
            def row(value):
                return value[0][p : p + 1], value[1][p : p + 1]

            def table(factors):
                sub = lax.broadcasted_iota(jnp.int32, (8, 128), 0)
                tile = None
                for bit, factor in enumerate(factors):
                    on = lax.rem(lax.div(sub, 2**bit), 2) == 1
                    factor = tuple(jnp.where(on, part, rest) for part, rest in zip(row(factor), (1.0, 0.0)))
                    tile = factor if tile is None else times(tile, factor)
                return tile

            base = table(steps[:3])
            for step in steps[3:6]:
                more = times(base, row(step))
                base = tuple(jnp.concatenate([old, new], axis=0) for old, new in zip(base, more))
            leap = table([steps[6], steps[7], unit])
            leaps[p, 0], leaps[p, 1] = leap
            at = slice(256 * p, 256 * p + 256)
            high, low = split_low(jnp.concatenate(base, axis=1))
            base_high[:, at], base_low[:, at] = high, low
            lead = times(row(coef), leap)
            lead = jnp.concatenate([lead[0], -lead[1]], axis=1)
            first = lax.rem(lax.broadcasted_iota(jnp.int32, (8, 256), 1), 128) < 64
            lead = jnp.concatenate([jnp.where(first, lead, 0.0), jnp.where(first, 0.0, lead)], axis=0)
            lead_high, lead_low = split_low(lead)
            taps_of = dot_nt(
                jnp.concatenate([lead_high, lead_low, lead_high], axis=1), jnp.concatenate([high, high, low], axis=1)
            )
            taps_of = jnp.concatenate([taps_of, taps_of], axis=1)
            lines_f[8 * p : 8 * p + 8], lines_f[8 * p + 64 : 8 * p + 72] = taps_of[:8], taps_of[8:]
        own = jnp.concatenate([lines_f[pl.ds(m, ROWS, stride=8), :][:, :64] for m in range(8)], axis=1)
        kern[z, y, x, c] = (2.0 * own).astype(bf16)

    late = z == 3

    @pl.when(jnp.logical_not(late))
    def _():
        prepare_shares()
        prepare_taps()

    pl.semaphore_wait(barrier, len(peers))

    @pl.when(late)
    def _():
        prepare_shares()

    share_plane = same(share_in.at[z, place], plane_peers + other_peers, share_in.at[0, pl.ds(0, 7)])
    weight_x = same(weight.at[:, z, y, x, c], [x_peer], weight.at[:, 0, 0, 0, 0])

    @pl.when(seq < 3)
    def _():
        right_copies[0].start()

    @pl.when(late)
    def _():
        prepare_taps()

    kern_z = same(kern.at[z, y, x, c], z_peers, kern.at[three, 0, 0, 0])
    finish(share_plane)
    share_z = same(share_in.at[z], z_peers, share_in.at[three])
    finish(weight_x)

    def weight_to_z(q):
        return same(weight.at[q, z, y, :, c], z_peers, weight.at[q, three, 0, :, 0])

    def weight_to_y(q):
        finish(weight_z[q])
        piece = weight.at[q, :, y, :, c]
        same(piece, [core_peer], piece, core_recvs[half_of[q]])
        return same(piece, [y_peer], weight.at[q, :, 0, :, 0])

    def weight_to_core(q):
        finish(weight_y[q])
        piece = weight.at[q, :, flip_y, :, c]
        same(piece, [core_peer], piece, core_recvs[half_of[q]])

    pairs, half_of = ((0, 3), (1, 2)), (0, 1, 1, 0)
    core_recvs = [claim(), claim()]
    weight_core = [(sem, weight.at[pl.ds(0, 2), :, :, :, 0]) for sem in core_recvs]
    weight_z = [weight_to_z(0)]
    last_y = same(weight.at[3, z, y, :, c], [y_peer], weight.at[3, 0, 0, :, 0])

    def last_to_z():
        finish(last_y)
        return same(weight.at[3, z, :, :, c], z_peers, weight.at[3, three, :, :, 0])

    def last_to_core():
        finish(last_z)
        same(weight.at[3, :, :, :, c], [core_peer], weight.at[3, :, :, :, 0], core_recvs[half_of[3]])

    def normalise(source, hat, keep_std, begin, end):
        for first in range(begin, end, 32):
            at = slice(first, first + 32)
            value = source[at, :].astype(f32)
            centered = value - jnp.mean(value, axis=1, keepdims=True)
            scale = lax.rsqrt(jnp.mean(centered * centered, axis=1, keepdims=True) + EPS)
            put(hat, at, centered * scale)
            if keep_std:
                inv_std[at, :] = jnp.broadcast_to(scale, (32, 128))

    loads[0].wait()
    normalise(x_v, x_hat, True, 0, tokens)
    finish(kern_z)
    halves = [pl.ds(0, 2), pl.ds(2, 2)]
    kern_plane = [same(kern.at[at, y, x, c], plane_peers, dk_in2.at[:, at]) for at in halves]

    weight_z.append(weight_to_z(1))
    weight_z.append(weight_to_z(2))
    finish(share_z)

    @pl.when(seq < 3)
    def _():
        right_copies[1].start()

    load_all(10, (pick, mask))
    shares = share_in[...].reshape(32, 1, 128).reshape(32, 128).astype(bf16)
    spread = dot_nn(shares, pick[...]) * mask[...].astype(f32)
    spread = jnp.sum(spread, axis=0, keepdims=True)
    rows_f[...] = jnp.concatenate(
        [spread[:, channels * i : channels * (i + 1)] for i in range(5)] + [jnp.zeros((3, channels), f32)], axis=0
    )
    gain, shift = rows_f[0:1, :], rows_f[1:2, :]

    def every_other(i, parity):
        return pl.ds(128 * i + parity, 64, stride=2)

    def sixty_four(i):
        return pl.ds(pl.multiple_of(64 * i, 64), 64)

    def shifted(i, _):
        at = pl.ds(pl.multiple_of(i * 128, 128), 128)
        put(normed, at, take(x_hat, at) * gain + shift)
        for parity in range(2):
            own_b[parity, sixty_four(i)] = take(normed, every_other(i, parity)).astype(bf16)
        return 0

    lax.fori_loop(0, tokens // 128, shifted, 0)
    load_all(11, (fwd, fwd_most, fwd_rest))
    load_all(12, (inv,))
    wide = 256

    def lanes(j):
        return pl.ds(pl.multiple_of(j * wide, wide), wide)

    few = 16

    def sign_of(r):
        return 1 if r < half // 2 else -1

    def transform(block, exact):
        both = []
        for parity, rows in enumerate(block):
            if exact:
                both.append(dot_nn(fwd[parity], jnp.concatenate([rows, rows], axis=0)))
            else:
                both.append(dot_nn(fwd[parity, :, :half], rows))
        return jnp.concatenate(both, axis=1)

    def joined(both, r):
        parts = both[r : r + few], both[half + r : half + r + few]
        width = both.shape[1] // 2
        even, odd = [part[:, :width] for part in parts], [part[:, width:] for part in parts]
        return tuple(a + b for a, b in zip(even, odd)), tuple(a - b for a, b in zip(even, odd))

    def places(r):
        return [pl.ds(first + r, few) for first in (0, taps, half, taps + half)]

    def keep(ref, at, r, pair):
        for lines, part in zip(places(r), pair[0] + pair[1]):
            ref[lines, at] = part

    def kept(ref, at, r):
        parts = [ref[lines, at] for lines in places(r)]
        return parts[:2], parts[2:]

    def signals(pairs_at, exact):
        lines = None
        for r in range(0, half, few):
            pairs = pairs_at(r)
            lines = lines or [[[[], []] for _ in range(2)] for _ in pairs]
            for (a, b), parities in zip(pairs, lines):
                for k, (x, y) in enumerate(zip(a, b)):
                    for parity, value in enumerate((x + y, x - y)):
                        parities[parity][k].append(split_low(value) if exact else (value.astype(bf16),))
        results = []
        for parities in lines:
            both = []
            for parity, (real, imag) in enumerate(parities):
                parts = [jnp.concatenate([line[i] for line in real + imag], axis=0) for i in range(2 if exact else 1)]
                if exact:
                    high, low = parts
                    both.append(dot_nn(inv[parity], jnp.concatenate([high, high, low], axis=0)))
                else:
                    both.append(dot_nn(inv[parity, :, : 2 * half], parts[0]))
            results.append(jnp.concatenate(both, axis=1))
        return results

    def signal(pair_at, exact):
        return signals(lambda r: (pair_at(r),), exact)[0]

    def each(function, pairs):
        return tuple(function(*values) for values in zip(*pairs))

    def swung(value, sign):
        return (value[1], -value[0]) if sign > 0 else (-value[1], value[0])

    def own_spectrum(j):
        at = lanes(j)
        both = transform((own_b[0, :, at], own_b[1, :, at]), True)
        for r in range(0, half, few):
            keep(u_spec, at, r, joined(both, r))

    own_spectrum(0)
    own_spectrum(1)
    last_z = last_to_z()
    weight_y = [weight_to_y(0)]

    def left_block(i):
        first, last = (0, 3) if i == 0 else (3, 4)
        right_copies[i].wait_recv()
        normalise(left_v, left_hat, False, 128 * first, 128 * last)
        for k in range(first, last):
            for parity in range(2):
                value = take(left_hat, pl.ds(128 * k + parity, 64, stride=2)) * gain + shift
                left_b[parity, 64 * k : 64 * k + 64] = value.astype(bf16)
        at = slice(64 * first, 64 * last)
        matrix = (fwd_most if i == 0 else fwd_rest)[...]
        for j in range(2):
            lane = slice(wide * j, wide * (j + 1))
            both = [left_b[parity, at, lane] for parity in range(2)]
            both = [dot_nn(matrix[k], jnp.concatenate([rows, rows], axis=0)) for k, rows in enumerate(both)]
            both = jnp.concatenate(both, axis=1)
            lines = slice(taps * j, taps * (j + 1))
            if i == 0:
                d_spec[lines, :] = both
                continue
            both += d_spec[lines, :]
            for r in range(0, half, few):
                turns = [swung(value, -sign_of(r)) for value in joined(both, r)]
                old = kept(u_spec, lanes(j), r)
                keep(u_spec, lanes(j), r, tuple(tuple(a + b for a, b in zip(x, y)) for x, y in zip(old, turns)))

    @pl.when(seq > 0)
    def _():
        left_block(0)

    @pl.when(seq == 0)
    def _():
        left_hat[...] = jnp.zeros_like(left_hat)

    weight_y.append(weight_to_y(1))
    kern_core = []
    for arrival, at in zip(kern_plane, halves):
        finish(arrival)
        kern_core.append(same(kern.at[at, :, :, c], [core_peer], kern.at[at, :, :, 0]))

    def kernel_transform(j):
        rows = kern[2 * j : 2 * j + 2].reshape(wide, taps)
        rows = [jnp.concatenate([rows[:, at]] * 2, axis=1) for at in (slice(0, half), slice(half, taps))]
        return jnp.concatenate([dot_nt(fwd[parity], part) for parity, part in enumerate(rows)], axis=1)

    def convolve(j, both):
        at = lanes(j)

        def product(r):
            k = joined(both, r)
            keep(k_spec, at, r, k)
            return each(times, (k, kept(u_spec, at, r)))

        both = signal(product, True)
        for parity in range(2):
            put(mixed, pl.ds(parity, half, stride=2), both[:, wide * parity : wide * (parity + 1)], 2 * j)

    def activate(j):
        for tile in (2 * j, 2 * j + 1):
            at = slice(128 * tile, 128 * tile + 128)
            for start_at in range(0, tokens, 128):
                lines = slice(start_at, start_at + 128)
                value = mixed[tile, lines, :] + rows_f[2:3, at] * normed[tile, lines, :]
                chance = 0.5 + 0.5 * lax.erf(value * (0.5**0.5))
                slope[lines, at] = chance + value * jnp.exp(value * value * -0.5 - 0.5 * float(np.log(2.0 * np.pi)))
                low = (value * chance).astype(bf16)
                activ[lines, at] = low
                activ_t[at, lines] = low.T

    finish(kern_core[0])
    k_raw[0] = kernel_transform(0)
    weight_y.append(weight_to_y(2))

    @pl.when(seq > 0)
    def _():
        left_block(1)

    weight_to_core(0)
    finish(kern_core[1])
    second_half = kernel_transform(1)
    convolve(0, k_raw[0])
    weight_to_core(1)
    last_to_core()
    convolve(1, second_half)
    activate(0)
    activate(1)
    weight_to_core(2)
    loads[-1].wait()

    def matrix_of(h):
        return jnp.concatenate([weight[q].reshape(channels, 256) for q in pairs[h]], axis=1)

    def gates(h, pre):
        lines_out = []
        sums = [jnp.zeros((32, 128), f32) for _ in range(4)]
        for start_at in range(0, tokens, 32):
            lines = slice(start_at, start_at + 32)
            low = []
            for i, q in enumerate(pairs[h]):
                at = slice(128 * q, 128 * q + 128)
                lin = pre[lines, 256 * i : 256 * i + 128] + rows_f[3:4, at]
                gate = 0.5 + 0.5 * jnp.tanh(0.5 * (pre[lines, 256 * i + 128 : 256 * i + 256] + rows_f[4:5, at]))
                grad = g_v[lines, at].astype(f32)
                product = lin * gate
                res_v[lines, at] = (x_v[lines, at].astype(f32) + product).astype(bf16)
                low += [(grad * gate).astype(bf16), (grad * (product - product * gate)).astype(bf16)]
            sums = [total + part.astype(f32) for total, part in zip(sums, low)]
            lines_out.append(jnp.concatenate(low, axis=1))
        for i, q in enumerate(pairs[h]):
            for k in range(2):
                rows_f[3 + k : 4 + k, 128 * q : 128 * q + 128] = jnp.sum(sums[2 * i + k], axis=0, keepdims=True)
        return jnp.concatenate(lines_out, axis=0)

    def weight_grad(h, low):
        grad = dot_nn(activ_t[...], low).astype(bf16)
        for i, q in enumerate(pairs[h]):
            dw_own[q] = grad[:, 256 * i : 256 * i + 256].reshape(4, 2, 2, 2, ROWS, 256)
            start([(dw_own.at[q, :, :, :, flip_c], dw_in1.at[q], core_peer)], dw_in1.at[q], dw_recvs[h])

    def mix_grad(d_act):
        total = jnp.zeros((32, channels), f32)
        for start_at in range(0, tokens, 32):
            lines = slice(start_at, start_at + 32)
            mix = (d_act[lines] * slope[lines, :]).astype(bf16).astype(f32)
            total += mix * take(normed, lines)
            put(mixed, lines, mix)
        rows_f[2:3, :] = jnp.sum(total, axis=0, keepdims=True)
        for parity in range(2):
            for start_at in range(0, half, 64):
                part = take(mixed, pl.ds(2 * start_at + parity, 64, stride=2))
                d_mix[parity, start_at : start_at + 64] = part.astype(bf16)

    def core_sum(q):
        if half_of[q] not in summed:
            summed.add(half_of[q])
            arrive(dw_recvs[half_of[q]], dw_in1.at[pl.ds(0, 2)])
        dw_mid[q] = (dw_own[q, :, :, :, c].astype(f32) + dw_in1[q].astype(f32)).astype(bf16)

    def to_y(q):
        core_sum(q)
        dw_y[q] = start([(dw_mid.at[q, :, flip_y], dw_in2.at[q], y_peer)], dw_in2.at[q])

    def end_to_z(q):
        core_sum(q)
        copies = [(dw_mid.at[q, peer[0]], end_in1.at[q, i], peer) for i, peer in enumerate(z_peers)]
        end_z[q] = start(copies, end_in1.at[q])

    def end_to_plane(q):
        finish(end_z[q])
        total = dw_mid[q, z].astype(f32)
        for i in range(3):
            total = total + end_in1[q, i].astype(f32)
        end_mid[q] = total.astype(bf16)
        copies = [(end_mid.at[q, peer[1], peer[2]], end_in2.at[q, i], peer) for i, peer in enumerate(plane_peers)]
        end_plane[q] = start(copies, end_in2.at[q])

    def write_out(q, total):
        dw_ref[:, 128 * q : 128 * q + 128] = total[:, :128]
        dw_ref[:, channels + 128 * q : channels + 128 * q + 128] = total[:, 128:]

    def end_of(q):
        finish(end_plane[q])
        total = end_mid[q, y, x].astype(f32)
        for i in range(3):
            total = total + end_in2[q, i].astype(f32)
        write_out(q, total)

    def to_z(q):
        finish(dw_y[q])
        dw_low[q] = (dw_mid[q, :, y].astype(f32) + dw_in2[q].astype(f32)).astype(bf16)
        copies = [(dw_low.at[q, peer[0]], dw_in3.at[q, i], peer) for i, peer in enumerate(z_peers)]
        dw_z[q] = start(copies, dw_in3.at[q])

    def to_x(q):
        finish(dw_z[q])
        total = dw_low[q, z].astype(f32)
        for i in range(3):
            total = total + dw_in3[q, i].astype(f32)
        dw_end[q] = total.astype(bf16)
        dw_x[q] = start([(dw_end.at[q, flip_x], dw_in4.at[q], x_peer)], dw_in4.at[q])

    def to_end(q):
        finish(dw_x[q])
        write_out(q, dw_end[q, x].astype(f32) + dw_in4[q].astype(f32))

    skip = rows_f[2:3, :]
    dw_y, dw_z, dw_x, end_z, end_plane, summed = {}, {}, {}, {}, {}, set()
    phase[0], dw_recvs = "reduce", [claim(), claim()]
    finish(weight_core[0])
    first_low = gates(0, dot_nn(activ[...], matrix_of(0)))
    weight_grad(0, first_low)
    finish(weight_core[1])
    second_low = gates(1, dot_nn(activ[...], matrix_of(1)))
    d_act = dot_nt(
        jnp.concatenate([first_low, second_low], axis=1), jnp.concatenate([matrix_of(0), matrix_of(1)], axis=1)
    )
    to_y(0)
    end_to_z(3)
    mix_grad(d_act)
    left_pieces = ((0, 256), (256, 256))
    left_copies = [
        pltpu.make_async_remote_copy(
            src_ref=d_mix.at[:, :, pl.ds(first, width)], dst_ref=right_v.at[:, :, pl.ds(first, width)], send_sem=left_sender,
            recv_sem=claim(), device_id=(dp, seq - 1), device_id_type=MESH,
        )
        for first, width in left_pieces
    ]

    @pl.when(seq > 0)
    def _():
        for copy in left_copies[:1]:
            copy.start()

    weight_grad(1, second_low)

    def mix_transform(j):
        at = lanes(j)
        return transform((d_mix[0, :, at], d_mix[1, :, at]), False)

    def kernel_grad(j, both):
        at = lanes(j)

        def product(r):
            d = joined(both, r)
            keep(d_spec, at, r, d)
            return each(conj_times, (kept(u_spec, at, r), d))

        both = signal(product, False)
        grad = jnp.concatenate([both[:, :wide].T, both[:, wide:].T], axis=1).reshape(2, 2, 2, 2, ROWS, taps)
        dk_own[2 * j : 2 * j + 2] = grad
        dk_low[2 * j : 2 * j + 2] = grad.astype(bf16)

    def kernel_middle():
        finish(dk_core)
        for i in range(4):
            total = dk_own[i, :, :, c] + dk_in1[i].astype(f32)
            dk_mid[i] = total
            dk_cut[i] = total.astype(bf16)
        return start([(dk_cut.at[:, peer[1], peer[2]], dk_in2.at[i], peer) for i, peer in enumerate(plane_peers)], dk_in2)

    def kernel_end():
        finish(dk_plane)
        for i in range(4):
            total = dk_mid[i, y, x]
            for k in range(3):
                total = total + dk_in2[k, i].astype(f32)
            dk_end[i] = total
            dk_out[i] = total.astype(bf16)
        return start([(dk_out.at[peer[0]], dk_in3.at[i], peer) for i, peer in enumerate(z_peers)], dk_in3)

    def own_grad(j):
        at = lanes(j)

        def product(r):
            return each(conj_times, (kept(k_spec, at, r), kept(d_spec, at, r)))

        def products(r):
            pair = product(r)
            return pair, tuple(swung(value, sign_of(r)) for value in pair)

        own, back = signals(products, False)
        d_gain, d_shift = jnp.zeros((1, wide), f32), jnp.zeros((1, wide), f32)
        for parity in range(2):
            lines = pl.ds(parity, half, stride=2)
            columns = slice(wide * parity, wide * (parity + 1))
            grad = own[:, columns] + rows_f[5:6, at] * d_mix[parity, :, at].astype(f32)
            put(d_norm, lines, grad, 2 * j)
            before = jnp.where(seq > 0, back[:, columns], 0.0)
            d_gain += jnp.sum(
                grad * take(x_hat, lines, 2 * j, 2) + before * take(left_hat, lines, 2 * j, 2), axis=0, keepdims=True
            )
            d_shift += jnp.sum(grad + before, axis=0, keepdims=True)
        rows_f[6:7, at], rows_f[7:8, at] = d_gain, d_shift

    def right_grad(i):
        first, width = left_pieces[i]
        at = slice(first, first + width)
        left_copies[i].wait_recv()
        both = transform((right_v[0, :, at], right_v[1, :, at]), False)

        def product(r):
            turns = [swung(value, sign_of(r)) for value in joined(both, r)]
            return each(conj_times, (kept(k_spec, at, r), turns))

        both = signal(product, False)
        for parity in range(2):
            lines = pl.ds(parity, half, stride=2)
            more = both[:, width * parity : width * (parity + 1)]
            put(d_norm, lines, take(d_norm, lines, first // 128, width // 128) + more, first // 128)

    rows_f[5:6, :] = skip
    first_half, second_half = mix_transform(0), mix_transform(1)
    kernel_grad(0, first_half)
    kernel_grad(1, second_half)
    dk_core = start([(dk_low.at[:, :, :, flip_c], dk_in1, core_peer)], dk_in1)
    end_to_z(1)
    to_y(2)
    own_grad(0)
    dk_plane = kernel_middle()

    @pl.when(seq > 0)
    def _():
        for copy in left_copies[1:]:
            copy.start()

    own_grad(1)
    to_z(0)
    vector = jnp.concatenate([rows_f[6:7, :], rows_f[7:8, :], rows_f[2:3, :], rows_f[3:4, :], rows_f[4:5, :]], axis=1)
    high, low = split_low(jnp.broadcast_to(vector, mask.shape) * mask[...].astype(f32))
    shares = dot_nt(high, pick[...]) + dot_nt(low, pick[...])
    share_out[...] = shares.reshape(32, 1, 128).reshape(4, 8, 1, 128)
    copies = [(share_out.at[peer[0]], share_in1.at[i], peer) for i, peer in enumerate(z_peers)]
    share_z = start(copies, share_in1)
    @pl.when(seq < 3)
    def _():
        right_grad(0)

    to_z(2)
    end_to_plane(3)
    dk_z = kernel_end()
    end_to_plane(1)
    to_x(0)
    finish(share_z)
    share_mid[...] = share_out[z] + share_in1[0] + share_in1[1] + share_in1[2]
    copies = [
        (share_mid.at[(peer[1] * 2 + peer[2]) * 2 + peer[3]], share_in2.at[i], peer)
        for i, peer in enumerate(plane_peers + other_peers)
    ]
    share_plane = start(copies, share_in2)

    to_x(2)

    @pl.when(seq < 3)
    def _():
        for i in range(1, len(left_pieces)):
            right_grad(i)


    @pl.when(seq < 3)
    def _():
        arrive(right_sender, x_v)

    @pl.when(seq > 0)
    def _():
        arrive(left_sender, d_mix)

    for first in range(0, tokens, 32):
        at = slice(first, first + 32)
        hat = [x_hat[i, at, :] for i in range(4)]
        grad = [d_norm[i, at, :] * rows_f[0:1, 128 * i : 128 * i + 128] for i in range(4)]
        mean = jnp.sum(sum(grad[1:], grad[0]), axis=1, keepdims=True) * (1.0 / channels)
        along = [one * other for one, other in zip(grad, hat)]
        along = jnp.sum(sum(along[1:], along[0]), axis=1, keepdims=True) * (1.0 / channels)
        for i in range(4):
            lane = slice(128 * i, 128 * i + 128)
            inner = inv_std[at, :] * (grad[i] - mean - hat[i] * along)
            gin_v[at, lane] = (inner + g_v[at, lane].astype(f32)).astype(bf16)
    dt, a, unit, norm_sq, ratio, coef, scaled = mode_terms(ldt_ref[...], lar_ref[...], ai_ref[...], cc_ref[...])
    inverse_a = (a[0] / norm_sq, -a[1] / norm_sq)
    end_of(3)
    end_of(1)
    finish(dk_z)
    d_kernel = dk_end[z]
    for k in range(3):
        d_kernel = d_kernel + dk_in3[k].astype(f32)

    for m in range(8):
        block = d_kernel[:, 64 * m : 64 * m + 64]
        block = jnp.concatenate([block, block], axis=1)
        for k in range(2):
            lines_f[pl.ds(8 * k + m, 8, stride=16), :] = block[8 * k : 8 * k + 8]
    at_row = lax.broadcasted_iota(jnp.int32, (8, 128), 0)
    first = lax.broadcasted_iota(jnp.int32, (8, 128), 1) < 64
    leap_of = (128 * lax.rem(at_row, 4) + lax.div(at_row, 4)).astype(f32)
    ramp = (2 * lax.broadcasted_iota(jnp.int32, (32, 64), 1)).astype(f32)
    sums = []
    for pair in range(4):
        plain = lines_f[32 * pair : 32 * pair + 32, :][:, :64]
        high, low = split_low(jnp.concatenate([plain, plain * ramp], axis=0))
        at = slice(512 * pair, 512 * pair + 512)
        table = jnp.concatenate([base_high[:, at], base_low[:, at], base_high[:, at]], axis=0)
        sums.append(dot_nn(jnp.concatenate([high, high, low], axis=1), table))
    zero = jnp.zeros((8, 128), f32)
    s0, s1 = [zero, zero], [zero, zero]
    for p in range(8):
        def part_of(begin, part):
            lane = 256 * (p % 2) + 128 * part
            block = sums[p // 2][begin + 16 * (p % 2) : begin + 16 * (p % 2) + 16, lane : lane + 128]
            return jnp.where(first, block[:8], block[8:])

        value, slope_of = [part_of(0, part) for part in range(2)], [part_of(32, part) for part in range(2)]
        leap = (leaps[p, 0], leaps[p, 1])
        slope_of = [one + leap_of * other for one, other in zip(slope_of, value)]
        for total, terms in ((s0, value), (s1, slope_of)):
            for part, product in enumerate(times(leap, terms)):
                total[part] = jnp.where(at_row == p, jnp.sum(product, axis=0, keepdims=True), total[part])
    d_coef = times(s0, ratio)
    half_g = times(times(coef, s0), times(unit, inverse_a))
    ramp_part = times(scaled, s1)
    half_g = (half_g[0] + ramp_part[0], half_g[1] + ramp_part[1])
    back = times(times(scaled, s0), inverse_a)
    q = (half_g[0] * dt - back[0], half_g[1] * dt - back[1])
    d_dt = 2.0 * dt * times(half_g, a)[0]
    dldt_ref[...] = row_of(jnp.sum(unpair_lanes(d_dt), axis=1, keepdims=True))[0]
    dlar_ref[...] = unpair_lanes(2.0 * q[0] * a[0])
    dai_ref[...] = unpair_lanes(-2.0 * q[1])
    dcc_ref[...] = jnp.concatenate([unpair_lanes(2.0 * d_coef[0]), unpair_lanes(-2.0 * d_coef[1])], axis=1)

    to_end(0)
    to_end(2)
    finish(share_plane)
    small = share_mid[place]
    for i in range(7):
        small = small + share_in2[i]
    for i, target in enumerate([dgain_ref, dshift_ref, dskip_ref]):
        target[...] = small[0, ROWS * i : ROWS * (i + 1)]
    dbias_ref[...] = small[0, 3 * ROWS : 5 * ROWS]
    arrive(sends.at[0], u_spec.at[pl.ds(0, sent["gather"] // (4 * channels)), :])
    arrive(sends.at[1], u_spec.at[pl.ds(0, sent["reduce"] // (4 * channels)), :])
    arrive(sends.at[2], vector_rows.at[pl.ds(0, sent["vector"] // 512)])


def finish_kernel(*refs):
    count = len(refs) // 2
    sems = refs[-1]
    copies = [pltpu.make_async_copy(refs[i], refs[count + i], sems.at[i]) for i in range(count)]
    for copy in copies:
        copy.start()
    for copy in copies:
        copy.wait()


def kernel_body(
    inputs, grad_out, ln_gain, ln_bias, skip_scale, w_glu, b_glu, log_dt, log_a_real, a_imag, c_coef
):
    _, tokens, channels = inputs.shape
    taps = KTAPS
    glu = w_glu.shape[1]
    f32, bf16 = jnp.float32, jnp.bfloat16
    order = np.concatenate([np.arange(0, taps // 2, 2), np.arange(1, taps // 2, 2)]) + 0.5
    forward, inverse = [], []
    for parity in range(2):
        angle = np.outer(order, 2 * np.arange(taps // 2) + parity) * (np.pi / taps)
        matrix = np.concatenate([np.cos(angle), -np.sin(angle)], axis=0)
        high = matrix.astype(bf16)
        low = (matrix - high.astype(np.float64)).astype(bf16)
        forward.append(np.concatenate([high, low], axis=1))
        inverse.append(np.concatenate([high.T, low.T, high.T], axis=1) * np.asarray(1.0 / taps, bf16))
    forward, inverse = np.stack(forward), np.stack(inverse)
    cut, end = 3 * taps // 8, taps // 2
    most, rest = (
        np.concatenate([forward[:, :, a:b], forward[:, :, end + a : end + b]], axis=2) for a, b in ((0, cut), (cut, end))
    )
    device_at, lane = np.arange(32)[:, None], np.arange(channels)[None, :]
    bias_lane = np.arange(2 * channels)[None, :]
    row = np.arange(128)[:, None]
    pick = np.concatenate(
        [row == i * ROWS + lane % ROWS for i in range(3)] + [row == 3 * ROWS + bias_lane % (2 * ROWS)], axis=1
    ).astype(bf16)
    mask = np.concatenate(
        [device_at == lane // ROWS] * 3 + [device_at == bias_lane // (2 * ROWS)], axis=1
    ).astype(bf16)
    hbm, vmem = pl.BlockSpec(memory_space=pl.ANY), pl.BlockSpec(memory_space=pltpu.VMEM)
    block = (tokens, channels)
    spec, tall = (2 * taps, channels), (channels // 128, tokens, 128)

    def space(*dims, kind=f32):
        return pltpu.VMEM(dims, kind)

    results = (
        (block, bf16), (block, bf16), ((ROWS,), f32), ((ROWS,), f32), ((ROWS,), f32), (w_glu.shape, f32),
        ((2 * ROWS,), f32), ((ROWS,), f32), (log_a_real.shape, f32), (a_imag.shape, f32), (c_coef.shape, f32),
    )
    outs = pl.pallas_call(
        layer_kernel,
        name="layer",
        out_shape=tuple(pltpu.VMEM(dims, kind) for dims, kind in results),
        in_specs=[hbm] * 17,
        out_specs=(vmem,) * len(results),
        scratch_shapes=[
            space(*w_glu.shape), space(1, ROWS), space(1, ROWS), space(1, ROWS), space(1, 2 * ROWS), space(1, ROWS),
            space(*log_a_real.shape), space(*a_imag.shape), space(*c_coef.shape),
            space(*block, kind=bf16), space(*block, kind=bf16), space(*block, kind=bf16),
            space(*forward.shape, kind=bf16), space(*most.shape, kind=bf16), space(*rest.shape, kind=bf16),
            space(*inverse.shape, kind=bf16),
            space(*pick.shape, kind=bf16), space(*mask.shape, kind=bf16),
            space(4, 2, 2, 2, ROWS, taps, kind=bf16), space(4, 4, 2, 2, 2, ROWS, 256, kind=bf16),
            space(64, 2048, kind=bf16), space(64, 2048, kind=bf16), space(8, 2, 8, 128), space(8 * ROWS, 128),
            space(4, 8, 1, 128), space(4, 8, 1, 128), space(3, 8, 1, 128), space(8, 1, 128), space(7, 1, 128),
            space(64, 1, 128),
            space(8, channels),
            space(*tall), space(tokens, 128), space(*tall), space(*tall),
            space(2, tokens // 2, channels, kind=bf16), space(2, tokens // 2, channels, kind=bf16),
            space(2, taps, taps), space(*spec), space(*spec), space(*tall), space(*block),
            space(*block, kind=bf16), space(channels, tokens, kind=bf16),
            space(2, tokens // 2, channels, kind=bf16), space(2, tokens // 2, channels, kind=bf16),
            space(*spec), space(*tall),
            space(4, 4, 2, 2, 2, ROWS, 256, kind=bf16), space(4, 4, 2, 2, ROWS, 256, kind=bf16),
            space(4, 4, 2, 2, ROWS, 256, kind=bf16), space(4, 4, 2, ROWS, 256, kind=bf16),
            space(4, 4, 2, ROWS, 256, kind=bf16), space(4, 3, 2, ROWS, 256, kind=bf16),
            space(4, 2, ROWS, 256, kind=bf16), space(4, ROWS, 256, kind=bf16),
            space(4, 3, 2, 2, ROWS, 256, kind=bf16), space(4, 2, 2, ROWS, 256, kind=bf16), space(4, 3, ROWS, 256, kind=bf16),
            space(4, 2, 2, 2, ROWS, taps), space(4, 2, 2, 2, ROWS, taps, kind=bf16), space(4, 2, 2, ROWS, taps, kind=bf16),
            space(4, 2, 2, ROWS, taps), space(4, 2, 2, ROWS, taps, kind=bf16), space(3, 4, ROWS, taps, kind=bf16),
            space(4, ROWS, taps), space(4, ROWS, taps, kind=bf16), space(3, ROWS, taps, kind=bf16),
            pltpu.SemaphoreType.DMA((14,)), pltpu.SemaphoreType.DMA((5,)), pltpu.SemaphoreType.DMA((39,)),
        ],
        compiler_params=pltpu.CompilerParams(
            collective_id=0, has_side_effects=True, vmem_limit_bytes=48 * 2**20
        ),
    )(*[
        pltpu.with_memory_space_constraint(value, pltpu.HBM)
        for value in (
            inputs.reshape(block), grad_out.reshape(block), forward, most, rest, inverse, pick, mask, w_glu,
            ln_gain.reshape(1, -1), ln_bias.reshape(1, -1), skip_scale.reshape(1, -1), b_glu.reshape(1, -1),
            log_dt.reshape(1, -1), log_a_real, a_imag, c_coef,
        )
    ])
    ended = pl.pallas_call(
        finish_kernel,
        name="finish",
        out_shape=tuple(jax.ShapeDtypeStruct(dims, kind) for dims, kind in results),
        in_specs=[vmem] * len(results),
        out_specs=(hbm,) * len(results),
        scratch_shapes=[pltpu.SemaphoreType.DMA((len(results),))],
    )(*[pltpu.with_memory_space_constraint(value, pltpu.VMEM) for value in outs])
    return (ended[0].reshape(inputs.shape), ended[1].reshape(inputs.shape)) + tuple(ended[2:])


def solution(mesh):
    in_specs = (
        P("dp", "seq", None),
        P("dp", "seq", None),
        P(("dp", "seq")),
        P(("dp", "seq")),
        P(("dp", "seq")),
        P(("dp", "seq"), None),
        P(("dp", "seq")),
        P(("dp", "seq")),
        P(("dp", "seq"), None),
        P(("dp", "seq"), None),
        P(("dp", "seq"), None),
    )
    out_specs = (
        P("dp", "seq", None),
        P("dp", "seq", None),
        P(("dp", "seq")),
        P(("dp", "seq")),
        P(("dp", "seq")),
        P(("dp", "seq"), None),
        P(("dp", "seq")),
        P(("dp", "seq")),
        P(("dp", "seq"), None),
        P(("dp", "seq"), None),
        P(("dp", "seq"), None),
    )
    quick = mesh.shape["dp"] == 8 and mesh.shape["seq"] == 4
    return jax.shard_map(kernel_body if quick else body, mesh=mesh, in_specs=in_specs, out_specs=out_specs, check_vma=False)
```

```python
import math
from functools import partial

import jax
import jax.numpy as jnp
import numpy as np
from jax import lax
from jax.experimental import pallas as pl
from jax.experimental.pallas import tpu as pltpu
from jax.sharding import PartitionSpec as P

KTAPS = 512


EPS = 1e-05


def passed_along(value, axis, steps):
    count = lax.axis_size(axis)
    first, last = (max(0, -steps), min(count, count - steps))
    return lax.ppermute(value, axis, [(source, source + steps) for source in range(first, last)])


def kernel_block(log_dt, log_a_real, a_imag, c_coef, start, count):
    mode_count = log_a_real.shape[1]
    step_size = jnp.exp(log_dt)[:, None]
    a_real = -jnp.exp(log_a_real)
    decay = a_real * step_size
    turn = a_imag * step_size
    growth = jnp.exp(decay)
    ex_re = growth * jnp.cos(turn) - 1.0
    ex_im = growth * jnp.sin(turn)
    norm_sq = a_real * a_real + a_imag * a_imag
    ratio_re = (ex_re * a_real + ex_im * a_imag) / norm_sq
    ratio_im = (ex_im * a_real - ex_re * a_imag) / norm_sq
    c_re = c_coef[:, :mode_count]
    c_im = c_coef[:, mode_count:]
    coef_re = c_re * ratio_re - c_im * ratio_im
    coef_im = c_re * ratio_im + c_im * ratio_re
    places = (start + jnp.arange(count)).astype(jnp.float32)
    phase = turn[:, :, None] * places
    damping = jnp.exp(decay[:, :, None] * places)
    terms = damping * (coef_re[:, :, None] * jnp.cos(phase) - coef_im[:, :, None] * jnp.sin(phase))
    return 2.0 * jnp.sum(terms, axis=1)


def transforms(taps):
    angle = np.outer(np.arange(taps) + 0.5, np.arange(taps)) * (np.pi / taps)
    forward = np.concatenate([np.cos(angle), -np.sin(angle)], axis=0)
    inverse = forward.T / taps
    return forward.astype(jnp.bfloat16), inverse.astype(jnp.bfloat16)


def body(
    inputs, grad_out, ln_gain, ln_bias, skip_scale, w_glu, b_glu, log_dt, log_a_real, a_imag, c_coef
):
    seq_count, own_len, channels = inputs.shape
    gain_low = ln_gain.astype(jnp.bfloat16)
    shift_low = ln_bias.astype(jnp.bfloat16)
    skip_low = skip_scale.astype(jnp.bfloat16)
    weight_low = w_glu.astype(jnp.bfloat16)
    bias_low = b_glu.astype(jnp.bfloat16)
    mode_own = (log_dt, log_a_real, a_imag, c_coef)
    own_kernel = kernel_block(*mode_own, 0, KTAPS).astype(jnp.bfloat16)
    gathered = (
        lax.all_gather(gain_low, ("dp", "seq"), axis=0, tiled=True),
        lax.all_gather(shift_low, ("dp", "seq"), axis=0, tiled=True),
        lax.all_gather(skip_low, ("dp", "seq"), axis=0, tiled=True),
        lax.all_gather(weight_low, ("dp", "seq"), axis=0, tiled=True),
        lax.all_gather(bias_low, ("dp", "seq"), axis=0, tiled=True),
        lax.all_gather(own_kernel, ("dp", "seq"), axis=0, tiled=True),
    )
    kernel_b = gathered[5]
    taps = own_len
    forward, inverse = transforms(taps)
    sign = jnp.where(jnp.arange(taps) % 2 == 0, 1.0, -1.0).astype(jnp.float32)[:, None]

    def to_spectrum(block):
        both = jnp.dot(forward, block, preferred_element_type=jnp.float32)
        return both[:taps], both[taps:]

    def from_spectrum(real, imag):
        both = jnp.concatenate([real, imag], axis=0).astype(jnp.bfloat16)
        return jnp.dot(inverse, both, preferred_element_type=jnp.float32)

    kernel_re, kernel_im = to_spectrum(kernel_b.T)
    gain_full = gathered[0].astype(jnp.float32)
    shift_full = gathered[1].astype(jnp.float32)
    skip_full = gathered[2].astype(jnp.float32)
    weight_b = gathered[3]
    glu_bias = gathered[4].astype(jnp.float32)
    x_float = inputs.astype(jnp.float32)
    row_mean = jnp.mean(x_float, axis=-1, keepdims=True)
    centered = x_float - row_mean
    row_var = jnp.mean(centered * centered, axis=-1, keepdims=True)
    inv_std = lax.rsqrt(row_var + EPS)
    x_hat = centered * inv_std
    normed = x_hat * gain_full + shift_full
    normed_b = normed.astype(jnp.bfloat16)
    own_re, own_im = to_spectrum(normed_b[0])
    left_re, left_im = to_spectrum(passed_along(normed_b, "seq", 1)[0])
    source_re = own_re - sign * left_im
    source_im = own_im + sign * left_re
    conv = from_spectrum(
        kernel_re * source_re - kernel_im * source_im,
        kernel_re * source_im + kernel_im * source_re,
    )
    mixed_pre = conv[None] + skip_full * normed
    activ, gelu_pull = jax.vjp(partial(jax.nn.gelu, approximate=False), mixed_pre)
    activ_b = activ.astype(jnp.bfloat16)
    glu_pre = (
        jnp.einsum("slh,hg->slg", activ_b, weight_b, preferred_element_type=jnp.float32) + glu_bias
    )
    half_dim = glu_pre.shape[-1] // 2
    lin_part = glu_pre[..., :half_dim]
    gate_sig = jax.nn.sigmoid(glu_pre[..., half_dim:])
    result = (x_float + lin_part * gate_sig).astype(jnp.bfloat16)
    grad_f = grad_out.astype(jnp.float32)
    d_pre = jnp.concatenate(
        [grad_f * gate_sig, grad_f * lin_part * gate_sig * (1.0 - gate_sig)], axis=-1
    ).astype(jnp.bfloat16)
    d_weight = jnp.einsum("slh,slg->hg", activ_b, d_pre, preferred_element_type=jnp.float32)
    d_glu_bias = jnp.sum(d_pre.astype(jnp.float32), axis=(0, 1))
    d_act = jnp.einsum("slg,hg->slh", d_pre, weight_b, preferred_element_type=jnp.float32)
    d_mix = gelu_pull(d_act)[0].astype(jnp.bfloat16)
    d_mix_f = d_mix.astype(jnp.float32)
    d_skip = jnp.sum(d_mix_f * normed, axis=(0, 1))
    mix_re, mix_im = to_spectrum(d_mix[0])
    d_kernel = from_spectrum(
        source_re * mix_re + source_im * mix_im, source_re * mix_im - source_im * mix_re
    ).T
    right_re, right_im = to_spectrum(passed_along(d_mix, "seq", -1)[0])
    sum_re = mix_re + sign * right_im
    sum_im = mix_im - sign * right_re
    d_conv = from_spectrum(
        kernel_re * sum_re + kernel_im * sum_im, kernel_re * sum_im - kernel_im * sum_re
    )[None]
    d_normed = d_conv + skip_full * d_mix_f
    d_gain = jnp.sum(d_normed * x_hat, axis=(0, 1))
    d_shift = jnp.sum(d_normed, axis=(0, 1))
    scaled = d_normed * gain_full
    d_input = (
        inv_std
        * (
            scaled
            - jnp.mean(scaled, axis=-1, keepdims=True)
            - x_hat * jnp.mean(scaled * x_hat, axis=-1, keepdims=True)
        )
        + grad_f
    )
    grad_in = d_input.astype(jnp.bfloat16)
    summed = (
        lax.psum_scatter(d_gain, ("dp", "seq"), scatter_dimension=0, tiled=True),
        lax.psum_scatter(d_shift, ("dp", "seq"), scatter_dimension=0, tiled=True),
        lax.psum_scatter(d_skip, ("dp", "seq"), scatter_dimension=0, tiled=True),
        lax.psum_scatter(d_weight, ("dp", "seq"), scatter_dimension=0, tiled=True),
        lax.psum_scatter(d_glu_bias, ("dp", "seq"), scatter_dimension=0, tiled=True),
        lax.psum_scatter(d_kernel, ("dp", "seq"), scatter_dimension=0, tiled=True),
    )
    _, own_pull = jax.vjp(partial(kernel_block, start=0, count=KTAPS), *mode_own)
    mode_grads = own_pull(summed[5])
    return (
        result,
        grad_in,
        summed[0],
        summed[1],
        summed[2],
        summed[3],
        summed[4],
        mode_grads[0],
        mode_grads[1],
        mode_grads[2],
        mode_grads[3],
    )


MESH = pl.DeviceIdType.MESH
ROWS = 16


def pair_lanes(value):
    return jnp.concatenate([value[:8], value[8:]], axis=1)


def unpair_lanes(value):
    half = value.shape[1] // 2
    return jnp.concatenate([value[:, :half], value[:, half:]], axis=0)


def column_of(row):
    n = row.shape[1]
    at = lax.broadcasted_iota(jnp.int32, (n, n), 0) == lax.broadcasted_iota(jnp.int32, (n, n), 1)
    return jnp.sum(jnp.where(at, jnp.broadcast_to(row, (n, n)), 0.0), axis=1, keepdims=True)


def row_of(column):
    n = column.shape[0]
    at = lax.broadcasted_iota(jnp.int32, (n, n), 0) == lax.broadcasted_iota(jnp.int32, (n, n), 1)
    return jnp.sum(jnp.where(at, jnp.broadcast_to(column, (n, n)), 0.0), axis=0, keepdims=True)


def mode_terms(ldt, lar, ai, cc):
    n_modes = lar.shape[1]
    dt = column_of(jnp.exp(ldt))
    dt = jnp.concatenate(
        [jnp.broadcast_to(dt[:8], (8, n_modes)), jnp.broadcast_to(dt[8:], (8, n_modes))], axis=1
    )
    a_re, a_im = -jnp.exp(pair_lanes(lar)), pair_lanes(ai)
    decay, turn = a_re * dt, a_im * dt
    growth = jnp.exp(decay)
    z_re, z_im = growth * jnp.cos(turn), growth * jnp.sin(turn)
    ex_re, ex_im = z_re - 1.0, z_im
    norm_sq = a_re * a_re + a_im * a_im
    r_re = (ex_re * a_re + ex_im * a_im) / norm_sq
    r_im = (ex_im * a_re - ex_re * a_im) / norm_sq
    c_re, c_im = pair_lanes(cc[:, :n_modes]), pair_lanes(cc[:, n_modes:])
    w_re, w_im = c_re * r_re - c_im * r_im, c_re * r_im + c_im * r_re
    return dt, (a_re, a_im), (z_re, z_im), norm_sq, (r_re, r_im), (c_re, c_im), (w_re, w_im)


def times(a, b):
    return a[0] * b[0] - a[1] * b[1], a[0] * b[1] + a[1] * b[0]


def conj_times(a, b):
    return a[0] * b[0] + a[1] * b[1], a[0] * b[1] - a[1] * b[0]


def split_low(value):
    high = value.astype(jnp.bfloat16)
    return high, (value - high.astype(jnp.float32)).astype(jnp.bfloat16)


def dot_nn(a, b):
    return lax.dot_general(a, b, (((1,), (0,)), ((), ())), preferred_element_type=jnp.float32)


def dot_nt(a, b):
    return lax.dot_general(a, b, (((1,), (1,)), ((), ())), preferred_element_type=jnp.float32)


def layer_kernel(
    x_hbm, g_hbm, fwd_hbm, most_hbm, rest_hbm, inv_hbm, pick_hbm, mask_hbm,
    w_hbm, gain_hbm, shift_hbm, skip_hbm, bias_hbm, ldt_hbm, lar_hbm, ai_hbm, cc_hbm,
    res_v, gin_v, dgain_ref, dshift_ref, dskip_ref, dw_ref, dbias_ref, dldt_ref, dlar_ref, dai_ref, dcc_ref,
    w_ref, gain_ref, shift_ref, skip_ref, bias_ref, ldt_ref, lar_ref, ai_ref, cc_ref,
    x_v, g_v, left_v, fwd, fwd_most, fwd_rest, inv, pick, mask, kern, weight, base_high, base_low, leaps, lines_f,
    share_in, share_out, share_in1, share_mid, share_in2, vector_rows, rows_f, x_hat, inv_std, left_hat, normed, own_b, left_b,
    k_raw, k_spec, u_spec, mixed, slope, activ, activ_t, d_mix, right_v, d_spec, d_norm,
    dw_own, dw_in1, dw_mid, dw_in2, dw_low, dw_in3, dw_end, dw_in4, end_in1, end_mid, end_in2,
    dk_own, dk_low, dk_in1, dk_mid, dk_cut, dk_in2, dk_end, dk_out, dk_in3,
    local, sends, recvs,
):
    f32, bf16 = jnp.float32, jnp.bfloat16
    tokens, channels = x_v.shape
    taps = KTAPS
    half, fourth = taps // 2, taps // 4
    dp, seq = lax.axis_index("dp"), lax.axis_index("seq")
    index = dp * 4 + seq
    z, y, x, c = lax.div(dp, 2), lax.rem(dp, 2), lax.div(seq, 2), lax.rem(seq, 2)
    flip_y, flip_x, flip_c = 1 - y, 1 - x, 1 - c

    def device(z, y, x, c):
        return (z * 2 + y, x * 2 + c)

    z_peers = [(lax.rem(z + k, 4), y, x, c) for k in (1, 2, 3)]
    plane_peers = [
        (z, lax.rem(y + k // 2, 2), lax.rem(x + k % 2, 2), c) for k in (1, 2, 3)
    ]
    x_peer, y_peer, core_peer = (z, y, flip_x, c), (z, flip_y, x, c), (z, y, x, flip_c)
    other_peers = [core_peer] + [(peer[0], peer[1], peer[2], flip_c) for peer in plane_peers]
    groups = ("gather", "reduce", "vector")
    sent = dict.fromkeys(groups, 0)
    phase, used = ["gather"], [0]

    def claim():
        used[0] += 1
        return recvs.at[used[0] - 1]

    def size_of(ref):
        return math.prod(ref.shape) * jnp.dtype(ref.dtype).itemsize

    def arrive(semaphore, total):
        pltpu.make_async_copy(total, total, semaphore).wait()

    def start(copies, total, recv_sem=None):
        if recv_sem is None:
            recv_sem = claim()
        group = "vector" if copies[0][0].shape[-2:] == (1, 128) else phase[0]
        for source, target, peer in copies:
            sent[group] += size_of(source)
            pltpu.make_async_remote_copy(
                src_ref=source, dst_ref=target, send_sem=sends.at[groups.index(group)], recv_sem=recv_sem,
                device_id=device(*peer), device_id_type=MESH,
            ).start()
        return recv_sem, total

    def finish(arrival):
        arrive(*arrival)

    def load(copies):
        for copy in copies:
            copy.start()
        return copies

    def take(ref, lines, first=0, count=4):
        return jnp.concatenate([ref[first + i, lines, :] for i in range(count)], axis=1)

    def put(ref, lines, value, first=0):
        for i in range(value.shape[1] // 128):
            ref[first + i, lines, :] = value[:, 128 * i : 128 * (i + 1)]

    barrier = pltpu.get_barrier_semaphore()
    peers = z_peers + plane_peers + other_peers
    for peer in peers:
        pl.semaphore_signal(barrier, inc=1, device_id=device(*peer), device_id_type=MESH)
    def fetch(pairs, numbers):
        return load([pltpu.make_async_copy(source, target, local.at[i]) for i, (source, target) in zip(numbers, pairs)])

    params = fetch([
        (gain_hbm, gain_ref), (shift_hbm, shift_ref), (skip_hbm, skip_ref), (bias_hbm, bias_ref), (w_hbm, w_ref),
        (ldt_hbm, ldt_ref), (lar_hbm, lar_ref), (ai_hbm, ai_ref), (cc_hbm, cc_ref),
    ], range(9))
    loads = fetch([
        (x_hbm, x_v), (pick_hbm, pick), (mask_hbm, mask), (fwd_hbm, fwd), (most_hbm, fwd_most), (rest_hbm, fwd_rest),
        (inv_hbm, inv), (g_hbm, g_v),
    ], (9, 10, 10, 11, 11, 11, 12, 13))
    three, place = pl.ds(0, 3), (y * 2 + x) * 2 + c

    def same(ref, peers, total, recv_sem=None):
        return start([(ref, ref, peer) for peer in peers], total, recv_sem)

    def load_all(number, refs):
        arrive(local.at[number], u_spec.at[pl.ds(0, sum(size_of(ref) for ref in refs) // (4 * channels)), :])

    right_sender, left_sender = sends.at[3], sends.at[4]
    right_copies = [
        pltpu.make_async_remote_copy(
            src_ref=x_hbm.at[at], dst_ref=left_v.at[at], send_sem=right_sender, recv_sem=claim(),
            device_id=(dp, seq + 1), device_id_type=MESH,
        )
        for at in (pl.ds(0, tokens - fourth), pl.ds(tokens - fourth, fourth))
    ]

    def prepare_shares():
        for copy in params:
            copy.wait()
        low = [ref[...].astype(bf16).astype(f32) for ref in (gain_ref, shift_ref, skip_ref, bias_ref)]
        share_in[z, place] = jnp.concatenate(low + [jnp.zeros((1, 128 - 5 * ROWS), f32)], axis=1)
        for q in range(4):
            weight[q, z, y, x, c] = jnp.concatenate(
                [w_ref[:, 128 * q : 128 * q + 128], w_ref[:, channels + 128 * q : channels + 128 * q + 128]], axis=1
            ).astype(bf16)

    def prepare_taps():
        _, _, unit, _, _, _, coef = mode_terms(ldt_ref[...], lar_ref[...], ai_ref[...], cc_ref[...])
        steps, power = [], times(unit, unit)
        for _ in range(8):
            steps.append(power)
            power = times(power, power)
        for p in range(8):
            def row(value):
                return value[0][p : p + 1], value[1][p : p + 1]

            def table(factors):
                sub = lax.broadcasted_iota(jnp.int32, (8, 128), 0)
                tile = None
                for bit, factor in enumerate(factors):
                    on = lax.rem(lax.div(sub, 2**bit), 2) == 1
                    factor = tuple(jnp.where(on, part, rest) for part, rest in zip(row(factor), (1.0, 0.0)))
                    tile = factor if tile is None else times(tile, factor)
                return tile

            base = table(steps[:3])
            for step in steps[3:6]:
                more = times(base, row(step))
                base = tuple(jnp.concatenate([old, new], axis=0) for old, new in zip(base, more))
            leap = table([steps[6], steps[7], unit])
            leaps[p, 0], leaps[p, 1] = leap
            at = slice(256 * p, 256 * p + 256)
            high, low = split_low(jnp.concatenate(base, axis=1))
            base_high[:, at], base_low[:, at] = high, low
            lead = times(row(coef), leap)
            lead = jnp.concatenate([lead[0], -lead[1]], axis=1)
            first = lax.rem(lax.broadcasted_iota(jnp.int32, (8, 256), 1), 128) < 64
            lead = jnp.concatenate([jnp.where(first, lead, 0.0), jnp.where(first, 0.0, lead)], axis=0)
            lead_high, lead_low = split_low(lead)
            taps_of = dot_nt(
                jnp.concatenate([lead_high, lead_low, lead_high], axis=1), jnp.concatenate([high, high, low], axis=1)
            )
            taps_of = jnp.concatenate([taps_of, taps_of], axis=1)
            lines_f[8 * p : 8 * p + 8], lines_f[8 * p + 64 : 8 * p + 72] = taps_of[:8], taps_of[8:]
        own = jnp.concatenate([lines_f[pl.ds(m, ROWS, stride=8), :][:, :64] for m in range(8)], axis=1)
        kern[z, y, x, c] = (2.0 * own).astype(bf16)

    late = z == 3

    @pl.when(jnp.logical_not(late))
    def _():
        prepare_shares()
        prepare_taps()

    pl.semaphore_wait(barrier, len(peers))

    @pl.when(late)
    def _():
        prepare_shares()

    share_plane = same(share_in.at[z, place], plane_peers + other_peers, share_in.at[0, pl.ds(0, 7)])
    weight_x = same(weight.at[:, z, y, x, c], [x_peer], weight.at[:, 0, 0, 0, 0])

    @pl.when(seq < 3)
    def _():
        right_copies[0].start()

    @pl.when(late)
    def _():
        prepare_taps()

    kern_z = same(kern.at[z, y, x, c], z_peers, kern.at[three, 0, 0, 0])
    finish(share_plane)
    share_z = same(share_in.at[z], z_peers, share_in.at[three])
    finish(weight_x)

    def weight_to_z(q):
        return same(weight.at[q, z, y, :, c], z_peers, weight.at[q, three, 0, :, 0])

    def weight_to_y(q):
        finish(weight_z[q])
        piece = weight.at[q, :, y, :, c]
        same(piece, [core_peer], piece, core_recvs[half_of[q]])
        return same(piece, [y_peer], weight.at[q, :, 0, :, 0])

    def weight_to_core(q):
        finish(weight_y[q])
        piece = weight.at[q, :, flip_y, :, c]
        same(piece, [core_peer], piece, core_recvs[half_of[q]])

    pairs, half_of = ((0, 3), (1, 2)), (0, 1, 1, 0)
    core_recvs = [claim(), claim()]
    weight_core = [(sem, weight.at[pl.ds(0, 2), :, :, :, 0]) for sem in core_recvs]
    weight_z = [weight_to_z(0)]
    last_y = same(weight.at[3, z, y, :, c], [y_peer], weight.at[3, 0, 0, :, 0])

    def last_to_z():
        finish(last_y)
        return same(weight.at[3, z, :, :, c], z_peers, weight.at[3, three, :, :, 0])

    def last_to_core():
        finish(last_z)
        same(weight.at[3, :, :, :, c], [core_peer], weight.at[3, :, :, :, 0], core_recvs[half_of[3]])

    def normalise(source, hat, keep_std, begin, end):
        for first in range(begin, end, 32):
            at = slice(first, first + 32)
            value = source[at, :].astype(f32)
            centered = value - jnp.mean(value, axis=1, keepdims=True)
            scale = lax.rsqrt(jnp.mean(centered * centered, axis=1, keepdims=True) + EPS)
            put(hat, at, centered * scale)
            if keep_std:
                inv_std[at, :] = jnp.broadcast_to(scale, (32, 128))

    loads[0].wait()
    normalise(x_v, x_hat, True, 0, tokens)
    finish(kern_z)
    halves = [pl.ds(0, 2), pl.ds(2, 2)]
    kern_plane = [same(kern.at[at, y, x, c], plane_peers, dk_in2.at[:, at]) for at in halves]

    weight_z.append(weight_to_z(1))
    weight_z.append(weight_to_z(2))
    finish(share_z)

    @pl.when(seq < 3)
    def _():
        right_copies[1].start()

    load_all(10, (pick, mask))
    shares = share_in[...].reshape(32, 1, 128).reshape(32, 128).astype(bf16)
    spread = dot_nn(shares, pick[...]) * mask[...].astype(f32)
    spread = jnp.sum(spread, axis=0, keepdims=True)
    rows_f[...] = jnp.concatenate(
        [spread[:, channels * i : channels * (i + 1)] for i in range(5)] + [jnp.zeros((3, channels), f32)], axis=0
    )
    gain, shift = rows_f[0:1, :], rows_f[1:2, :]

    def every_other(i, parity):
        return pl.ds(128 * i + parity, 64, stride=2)

    def sixty_four(i):
        return pl.ds(pl.multiple_of(64 * i, 64), 64)

    def shifted(i, _):
        at = pl.ds(pl.multiple_of(i * 128, 128), 128)
        put(normed, at, take(x_hat, at) * gain + shift)
        for parity in range(2):
            own_b[parity, sixty_four(i)] = take(normed, every_other(i, parity)).astype(bf16)
        return 0

    lax.fori_loop(0, tokens // 128, shifted, 0)
    load_all(11, (fwd, fwd_most, fwd_rest))
    load_all(12, (inv,))
    wide = 256

    def lanes(j):
        return pl.ds(pl.multiple_of(j * wide, wide), wide)

    few = 16

    def sign_of(r):
        return 1 if r < half // 2 else -1

    def transform(block, exact):
        both = []
        for parity, rows in enumerate(block):
            if exact:
                both.append(dot_nn(fwd[parity], jnp.concatenate([rows, rows], axis=0)))
            else:
                both.append(dot_nn(fwd[parity, :, :half], rows))
        return jnp.concatenate(both, axis=1)

    def joined(both, r):
        parts = both[r : r + few], both[half + r : half + r + few]
        width = both.shape[1] // 2
        even, odd = [part[:, :width] for part in parts], [part[:, width:] for part in parts]
        return tuple(a + b for a, b in zip(even, odd)), tuple(a - b for a, b in zip(even, odd))

    def places(r):
        return [pl.ds(first + r, few) for first in (0, taps, half, taps + half)]

    def keep(ref, at, r, pair):
        for lines, part in zip(places(r), pair[0] + pair[1]):
            ref[lines, at] = part

    def kept(ref, at, r):
        parts = [ref[lines, at] for lines in places(r)]
        return parts[:2], parts[2:]

    def signals(pairs_at, exact):
        lines = None
        for r in range(0, half, few):
            pairs = pairs_at(r)
            lines = lines or [[[[], []] for _ in range(2)] for _ in pairs]
            for (a, b), parities in zip(pairs, lines):
                for k, (x, y) in enumerate(zip(a, b)):
                    for parity, value in enumerate((x + y, x - y)):
                        parities[parity][k].append(split_low(value) if exact else (value.astype(bf16),))
        results = []
        for parities in lines:
            both = []
            for parity, (real, imag) in enumerate(parities):
                parts = [jnp.concatenate([line[i] for line in real + imag], axis=0) for i in range(2 if exact else 1)]
                if exact:
                    high, low = parts
                    both.append(dot_nn(inv[parity], jnp.concatenate([high, high, low], axis=0)))
                else:
                    both.append(dot_nn(inv[parity, :, : 2 * half], parts[0]))
            results.append(jnp.concatenate(both, axis=1))
        return results

    def signal(pair_at, exact):
        return signals(lambda r: (pair_at(r),), exact)[0]

    def each(function, pairs):
        return tuple(function(*values) for values in zip(*pairs))

    def swung(value, sign):
        return (value[1], -value[0]) if sign > 0 else (-value[1], value[0])

    def own_spectrum(j):
        at = lanes(j)
        both = transform((own_b[0, :, at], own_b[1, :, at]), True)
        for r in range(0, half, few):
            keep(u_spec, at, r, joined(both, r))

    own_spectrum(0)
    own_spectrum(1)
    last_z = last_to_z()
    weight_y = [weight_to_y(0)]

    def left_block(i):
        first, last = (0, 3) if i == 0 else (3, 4)
        right_copies[i].wait_recv()
        normalise(left_v, left_hat, False, 128 * first, 128 * last)
        for k in range(first, last):
            for parity in range(2):
                value = take(left_hat, pl.ds(128 * k + parity, 64, stride=2)) * gain + shift
                left_b[parity, 64 * k : 64 * k + 64] = value.astype(bf16)
        at = slice(64 * first, 64 * last)
        matrix = (fwd_most if i == 0 else fwd_rest)[...]
        for j in range(2):
            lane = slice(wide * j, wide * (j + 1))
            both = [left_b[parity, at, lane] for parity in range(2)]
            both = [dot_nn(matrix[k], jnp.concatenate([rows, rows], axis=0)) for k, rows in enumerate(both)]
            both = jnp.concatenate(both, axis=1)
            lines = slice(taps * j, taps * (j + 1))
            if i == 0:
                d_spec[lines, :] = both
                continue
            both += d_spec[lines, :]
            for r in range(0, half, few):
                turns = [swung(value, -sign_of(r)) for value in joined(both, r)]
                old = kept(u_spec, lanes(j), r)
                keep(u_spec, lanes(j), r, tuple(tuple(a + b for a, b in zip(x, y)) for x, y in zip(old, turns)))

    @pl.when(seq > 0)
    def _():
        left_block(0)

    @pl.when(seq == 0)
    def _():
        left_hat[...] = jnp.zeros_like(left_hat)

    weight_y.append(weight_to_y(1))
    kern_core = []
    for arrival, at in zip(kern_plane, halves):
        finish(arrival)
        kern_core.append(same(kern.at[at, :, :, c], [core_peer], kern.at[at, :, :, 0]))

    def kernel_transform(j):
        rows = kern[2 * j : 2 * j + 2].reshape(wide, taps)
        rows = [jnp.concatenate([rows[:, at]] * 2, axis=1) for at in (slice(0, half), slice(half, taps))]
        return jnp.concatenate([dot_nt(fwd[parity], part) for parity, part in enumerate(rows)], axis=1)

    def convolve(j, both):
        at = lanes(j)

        def product(r):
            k = joined(both, r)
            keep(k_spec, at, r, k)
            return each(times, (k, kept(u_spec, at, r)))

        both = signal(product, True)
        for parity in range(2):
            put(mixed, pl.ds(parity, half, stride=2), both[:, wide * parity : wide * (parity + 1)], 2 * j)

    def activate(j):
        for tile in (2 * j, 2 * j + 1):
            at = slice(128 * tile, 128 * tile + 128)
            for start_at in range(0, tokens, 128):
                lines = slice(start_at, start_at + 128)
                value = mixed[tile, lines, :] + rows_f[2:3, at] * normed[tile, lines, :]
                chance = 0.5 + 0.5 * lax.erf(value * (0.5**0.5))
                slope[lines, at] = chance + value * jnp.exp(value * value * -0.5 - 0.5 * float(np.log(2.0 * np.pi)))
                low = (value * chance).astype(bf16)
                activ[lines, at] = low
                activ_t[at, lines] = low.T

    finish(kern_core[0])
    k_raw[0] = kernel_transform(0)
    weight_y.append(weight_to_y(2))

    @pl.when(seq > 0)
    def _():
        left_block(1)

    weight_to_core(0)
    finish(kern_core[1])
    second_half = kernel_transform(1)
    convolve(0, k_raw[0])
    weight_to_core(1)
    last_to_core()
    convolve(1, second_half)
    activate(0)
    activate(1)
    weight_to_core(2)
    loads[-1].wait()

    def matrix_of(h):
        return jnp.concatenate([weight[q].reshape(channels, 256) for q in pairs[h]], axis=1)

    def gates(h, pre):
        lines_out = []
        sums = [jnp.zeros((32, 128), f32) for _ in range(4)]
        for start_at in range(0, tokens, 32):
            lines = slice(start_at, start_at + 32)
            low = []
            for i, q in enumerate(pairs[h]):
                at = slice(128 * q, 128 * q + 128)
                lin = pre[lines, 256 * i : 256 * i + 128] + rows_f[3:4, at]
                gate = 0.5 + 0.5 * jnp.tanh(0.5 * (pre[lines, 256 * i + 128 : 256 * i + 256] + rows_f[4:5, at]))
                grad = g_v[lines, at].astype(f32)
                product = lin * gate
                res_v[lines, at] = (x_v[lines, at].astype(f32) + product).astype(bf16)
                low += [(grad * gate).astype(bf16), (grad * (product - product * gate)).astype(bf16)]
            sums = [total + part.astype(f32) for total, part in zip(sums, low)]
            lines_out.append(jnp.concatenate(low, axis=1))
        for i, q in enumerate(pairs[h]):
            for k in range(2):
                rows_f[3 + k : 4 + k, 128 * q : 128 * q + 128] = jnp.sum(sums[2 * i + k], axis=0, keepdims=True)
        return jnp.concatenate(lines_out, axis=0)

    def weight_grad(h, low):
        grad = dot_nn(activ_t[...], low).astype(bf16)
        for i, q in enumerate(pairs[h]):
            dw_own[q] = grad[:, 256 * i : 256 * i + 256].reshape(4, 2, 2, 2, ROWS, 256)
            start([(dw_own.at[q, :, :, :, flip_c], dw_in1.at[q], core_peer)], dw_in1.at[q], dw_recvs[h])

    def mix_grad(d_act):
        total = jnp.zeros((32, channels), f32)
        for start_at in range(0, tokens, 32):
            lines = slice(start_at, start_at + 32)
            mix = (d_act[lines] * slope[lines, :]).astype(bf16).astype(f32)
            total += mix * take(normed, lines)
            put(mixed, lines, mix)
        rows_f[2:3, :] = jnp.sum(total, axis=0, keepdims=True)
        for parity in range(2):
            for start_at in range(0, half, 64):
                part = take(mixed, pl.ds(2 * start_at + parity, 64, stride=2))
                d_mix[parity, start_at : start_at + 64] = part.astype(bf16)

    def core_sum(q):
        if half_of[q] not in summed:
            summed.add(half_of[q])
            arrive(dw_recvs[half_of[q]], dw_in1.at[pl.ds(0, 2)])
        dw_mid[q] = (dw_own[q, :, :, :, c].astype(f32) + dw_in1[q].astype(f32)).astype(bf16)

    def to_y(q):
        core_sum(q)
        dw_y[q] = start([(dw_mid.at[q, :, flip_y], dw_in2.at[q], y_peer)], dw_in2.at[q])

    def end_to_z(q):
        core_sum(q)
        copies = [(dw_mid.at[q, peer[0]], end_in1.at[q, i], peer) for i, peer in enumerate(z_peers)]
        end_z[q] = start(copies, end_in1.at[q])

    def end_to_plane(q):
        finish(end_z[q])
        total = dw_mid[q, z].astype(f32)
        for i in range(3):
            total = total + end_in1[q, i].astype(f32)
        end_mid[q] = total.astype(bf16)
        copies = [(end_mid.at[q, peer[1], peer[2]], end_in2.at[q, i], peer) for i, peer in enumerate(plane_peers)]
        end_plane[q] = start(copies, end_in2.at[q])

    def write_out(q, total):
        dw_ref[:, 128 * q : 128 * q + 128] = total[:, :128]
        dw_ref[:, channels + 128 * q : channels + 128 * q + 128] = total[:, 128:]

    def end_of(q):
        finish(end_plane[q])
        total = end_mid[q, y, x].astype(f32)
        for i in range(3):
            total = total + end_in2[q, i].astype(f32)
        write_out(q, total)

    def to_z(q):
        finish(dw_y[q])
        dw_low[q] = (dw_mid[q, :, y].astype(f32) + dw_in2[q].astype(f32)).astype(bf16)
        copies = [(dw_low.at[q, peer[0]], dw_in3.at[q, i], peer) for i, peer in enumerate(z_peers)]
        dw_z[q] = start(copies, dw_in3.at[q])

    def to_x(q):
        finish(dw_z[q])
        total = dw_low[q, z].astype(f32)
        for i in range(3):
            total = total + dw_in3[q, i].astype(f32)
        dw_end[q] = total.astype(bf16)
        dw_x[q] = start([(dw_end.at[q, flip_x], dw_in4.at[q], x_peer)], dw_in4.at[q])

    def to_end(q):
        finish(dw_x[q])
        write_out(q, dw_end[q, x].astype(f32) + dw_in4[q].astype(f32))

    skip = rows_f[2:3, :]
    dw_y, dw_z, dw_x, end_z, end_plane, summed = {}, {}, {}, {}, {}, set()
    phase[0], dw_recvs = "reduce", [claim(), claim()]
    finish(weight_core[0])
    first_low = gates(0, dot_nn(activ[...], matrix_of(0)))
    weight_grad(0, first_low)
    finish(weight_core[1])
    second_low = gates(1, dot_nn(activ[...], matrix_of(1)))
    d_act = dot_nt(
        jnp.concatenate([first_low, second_low], axis=1), jnp.concatenate([matrix_of(0), matrix_of(1)], axis=1)
    )
    to_y(0)
    end_to_z(3)
    mix_grad(d_act)
    left_pieces = ((0, 256), (256, 256))
    left_copies = [
        pltpu.make_async_remote_copy(
            src_ref=d_mix.at[:, :, pl.ds(first, width)], dst_ref=right_v.at[:, :, pl.ds(first, width)], send_sem=left_sender,
            recv_sem=claim(), device_id=(dp, seq - 1), device_id_type=MESH,
        )
        for first, width in left_pieces
    ]

    @pl.when(seq > 0)
    def _():
        for copy in left_copies[:1]:
            copy.start()

    weight_grad(1, second_low)

    def mix_transform(j):
        at = lanes(j)
        return transform((d_mix[0, :, at], d_mix[1, :, at]), False)

    def kernel_grad(j, both):
        at = lanes(j)

        def product(r):
            d = joined(both, r)
            keep(d_spec, at, r, d)
            return each(conj_times, (kept(u_spec, at, r), d))

        both = signal(product, False)
        grad = jnp.concatenate([both[:, :wide].T, both[:, wide:].T], axis=1).reshape(2, 2, 2, 2, ROWS, taps)
        dk_own[2 * j : 2 * j + 2] = grad
        dk_low[2 * j : 2 * j + 2] = grad.astype(bf16)

    def kernel_middle():
        finish(dk_core)
        for i in range(4):
            total = dk_own[i, :, :, c] + dk_in1[i].astype(f32)
            dk_mid[i] = total
            dk_cut[i] = total.astype(bf16)
        return start([(dk_cut.at[:, peer[1], peer[2]], dk_in2.at[i], peer) for i, peer in enumerate(plane_peers)], dk_in2)

    def kernel_end():
        finish(dk_plane)
        for i in range(4):
            total = dk_mid[i, y, x]
            for k in range(3):
                total = total + dk_in2[k, i].astype(f32)
            dk_end[i] = total
            dk_out[i] = total.astype(bf16)
        return start([(dk_out.at[peer[0]], dk_in3.at[i], peer) for i, peer in enumerate(z_peers)], dk_in3)

    def own_grad(j):
        at = lanes(j)

        def product(r):
            return each(conj_times, (kept(k_spec, at, r), kept(d_spec, at, r)))

        def products(r):
            pair = product(r)
            return pair, tuple(swung(value, sign_of(r)) for value in pair)

        own, back = signals(products, False)
        d_gain, d_shift = jnp.zeros((1, wide), f32), jnp.zeros((1, wide), f32)
        for parity in range(2):
            lines = pl.ds(parity, half, stride=2)
            columns = slice(wide * parity, wide * (parity + 1))
            grad = own[:, columns] + rows_f[5:6, at] * d_mix[parity, :, at].astype(f32)
            put(d_norm, lines, grad, 2 * j)
            before = jnp.where(seq > 0, back[:, columns], 0.0)
            d_gain += jnp.sum(
                grad * take(x_hat, lines, 2 * j, 2) + before * take(left_hat, lines, 2 * j, 2), axis=0, keepdims=True
            )
            d_shift += jnp.sum(grad + before, axis=0, keepdims=True)
        rows_f[6:7, at], rows_f[7:8, at] = d_gain, d_shift

    def right_grad(i):
        first, width = left_pieces[i]
        at = slice(first, first + width)
        left_copies[i].wait_recv()
        both = transform((right_v[0, :, at], right_v[1, :, at]), False)

        def product(r):
            turns = [swung(value, sign_of(r)) for value in joined(both, r)]
            return each(conj_times, (kept(k_spec, at, r), turns))

        both = signal(product, False)
        for parity in range(2):
            lines = pl.ds(parity, half, stride=2)
            more = both[:, width * parity : width * (parity + 1)]
            put(d_norm, lines, take(d_norm, lines, first // 128, width // 128) + more, first // 128)

    rows_f[5:6, :] = skip
    first_half, second_half = mix_transform(0), mix_transform(1)
    kernel_grad(0, first_half)
    kernel_grad(1, second_half)
    dk_core = start([(dk_low.at[:, :, :, flip_c], dk_in1, core_peer)], dk_in1)
    end_to_z(1)
    to_y(2)
    own_grad(0)
    dk_plane = kernel_middle()

    @pl.when(seq > 0)
    def _():
        for copy in left_copies[1:]:
            copy.start()

    own_grad(1)
    to_z(0)
    vector = jnp.concatenate([rows_f[6:7, :], rows_f[7:8, :], rows_f[2:3, :], rows_f[3:4, :], rows_f[4:5, :]], axis=1)
    high, low = split_low(jnp.broadcast_to(vector, mask.shape) * mask[...].astype(f32))
    shares = dot_nt(high, pick[...]) + dot_nt(low, pick[...])
    share_out[...] = shares.reshape(32, 1, 128).reshape(4, 8, 1, 128)
    copies = [(share_out.at[peer[0]], share_in1.at[i], peer) for i, peer in enumerate(z_peers)]
    share_z = start(copies, share_in1)
    @pl.when(seq < 3)
    def _():
        right_grad(0)

    to_z(2)
    end_to_plane(3)
    dk_z = kernel_end()
    end_to_plane(1)
    to_x(0)
    finish(share_z)
    share_mid[...] = share_out[z] + share_in1[0] + share_in1[1] + share_in1[2]
    copies = [
        (share_mid.at[(peer[1] * 2 + peer[2]) * 2 + peer[3]], share_in2.at[i], peer)
        for i, peer in enumerate(plane_peers + other_peers)
    ]
    share_plane = start(copies, share_in2)

    to_x(2)

    @pl.when(seq < 3)
    def _():
        for i in range(1, len(left_pieces)):
            right_grad(i)


    @pl.when(seq < 3)
    def _():
        arrive(right_sender, x_v)

    @pl.when(seq > 0)
    def _():
        arrive(left_sender, d_mix)

    for first in range(0, tokens, 32):
        at = slice(first, first + 32)
        hat = [x_hat[i, at, :] for i in range(4)]
        grad = [d_norm[i, at, :] * rows_f[0:1, 128 * i : 128 * i + 128] for i in range(4)]
        mean = jnp.sum(sum(grad[1:], grad[0]), axis=1, keepdims=True) * (1.0 / channels)
        along = [one * other for one, other in zip(grad, hat)]
        along = jnp.sum(sum(along[1:], along[0]), axis=1, keepdims=True) * (1.0 / channels)
        for i in range(4):
            lane = slice(128 * i, 128 * i + 128)
            inner = inv_std[at, :] * (grad[i] - mean - hat[i] * along)
            gin_v[at, lane] = (inner + g_v[at, lane].astype(f32)).astype(bf16)
    dt, a, unit, norm_sq, ratio, coef, scaled = mode_terms(ldt_ref[...], lar_ref[...], ai_ref[...], cc_ref[...])
    inverse_a = (a[0] / norm_sq, -a[1] / norm_sq)
    end_of(3)
    end_of(1)
    finish(dk_z)
    d_kernel = dk_end[z]
    for k in range(3):
        d_kernel = d_kernel + dk_in3[k].astype(f32)

    for m in range(8):
        block = d_kernel[:, 64 * m : 64 * m + 64]
        block = jnp.concatenate([block, block], axis=1)
        for k in range(2):
            lines_f[pl.ds(8 * k + m, 8, stride=16), :] = block[8 * k : 8 * k + 8]
    at_row = lax.broadcasted_iota(jnp.int32, (8, 128), 0)
    first = lax.broadcasted_iota(jnp.int32, (8, 128), 1) < 64
    leap_of = (128 * lax.rem(at_row, 4) + lax.div(at_row, 4)).astype(f32)
    ramp = (2 * lax.broadcasted_iota(jnp.int32, (32, 64), 1)).astype(f32)
    sums = []
    for pair in range(4):
        plain = lines_f[32 * pair : 32 * pair + 32, :][:, :64]
        high, low = split_low(jnp.concatenate([plain, plain * ramp], axis=0))
        at = slice(512 * pair, 512 * pair + 512)
        table = jnp.concatenate([base_high[:, at], base_low[:, at], base_high[:, at]], axis=0)
        sums.append(dot_nn(jnp.concatenate([high, high, low], axis=1), table))
    zero = jnp.zeros((8, 128), f32)
    s0, s1 = [zero, zero], [zero, zero]
    for p in range(8):
        def part_of(begin, part):
            lane = 256 * (p % 2) + 128 * part
            block = sums[p // 2][begin + 16 * (p % 2) : begin + 16 * (p % 2) + 16, lane : lane + 128]
            return jnp.where(first, block[:8], block[8:])

        value, slope_of = [part_of(0, part) for part in range(2)], [part_of(32, part) for part in range(2)]
        leap = (leaps[p, 0], leaps[p, 1])
        slope_of = [one + leap_of * other for one, other in zip(slope_of, value)]
        for total, terms in ((s0, value), (s1, slope_of)):
            for part, product in enumerate(times(leap, terms)):
                total[part] = jnp.where(at_row == p, jnp.sum(product, axis=0, keepdims=True), total[part])
    d_coef = times(s0, ratio)
    half_g = times(times(coef, s0), times(unit, inverse_a))
    ramp_part = times(scaled, s1)
    half_g = (half_g[0] + ramp_part[0], half_g[1] + ramp_part[1])
    back = times(times(scaled, s0), inverse_a)
    q = (half_g[0] * dt - back[0], half_g[1] * dt - back[1])
    d_dt = 2.0 * dt * times(half_g, a)[0]
    dldt_ref[...] = row_of(jnp.sum(unpair_lanes(d_dt), axis=1, keepdims=True))[0]
    dlar_ref[...] = unpair_lanes(2.0 * q[0] * a[0])
    dai_ref[...] = unpair_lanes(-2.0 * q[1])
    dcc_ref[...] = jnp.concatenate([unpair_lanes(2.0 * d_coef[0]), unpair_lanes(-2.0 * d_coef[1])], axis=1)

    to_end(0)
    to_end(2)
    finish(share_plane)
    small = share_mid[place]
    for i in range(7):
        small = small + share_in2[i]
    for i, target in enumerate([dgain_ref, dshift_ref, dskip_ref]):
        target[...] = small[0, ROWS * i : ROWS * (i + 1)]
    dbias_ref[...] = small[0, 3 * ROWS : 5 * ROWS]
    arrive(sends.at[0], u_spec.at[pl.ds(0, sent["gather"] // (4 * channels)), :])
    arrive(sends.at[1], u_spec.at[pl.ds(0, sent["reduce"] // (4 * channels)), :])
    arrive(sends.at[2], vector_rows.at[pl.ds(0, sent["vector"] // 512)])


def finish_kernel(*refs):
    count = len(refs) // 2
    sems = refs[-1]
    copies = [pltpu.make_async_copy(refs[i], refs[count + i], sems.at[i]) for i in range(count)]
    for copy in copies:
        copy.start()
    for copy in copies:
        copy.wait()


def kernel_body(
    inputs, grad_out, ln_gain, ln_bias, skip_scale, w_glu, b_glu, log_dt, log_a_real, a_imag, c_coef
):
    _, tokens, channels = inputs.shape
    taps = KTAPS
    glu = w_glu.shape[1]
    f32, bf16 = jnp.float32, jnp.bfloat16
    order = np.concatenate([np.arange(0, taps // 2, 2), np.arange(1, taps // 2, 2)]) + 0.5
    forward, inverse = [], []
    for parity in range(2):
        angle = np.outer(order, 2 * np.arange(taps // 2) + parity) * (np.pi / taps)
        matrix = np.concatenate([np.cos(angle), -np.sin(angle)], axis=0)
        high = matrix.astype(bf16)
        low = (matrix - high.astype(np.float64)).astype(bf16)
        forward.append(np.concatenate([high, low], axis=1))
        inverse.append(np.concatenate([high.T, low.T, high.T], axis=1) * np.asarray(1.0 / taps, bf16))
    forward, inverse = np.stack(forward), np.stack(inverse)
    cut, end = 3 * taps // 8, taps // 2
    most, rest = (
        np.concatenate([forward[:, :, a:b], forward[:, :, end + a : end + b]], axis=2) for a, b in ((0, cut), (cut, end))
    )
    device_at, lane = np.arange(32)[:, None], np.arange(channels)[None, :]
    bias_lane = np.arange(2 * channels)[None, :]
    row = np.arange(128)[:, None]
    pick = np.concatenate(
        [row == i * ROWS + lane % ROWS for i in range(3)] + [row == 3 * ROWS + bias_lane % (2 * ROWS)], axis=1
    ).astype(bf16)
    mask = np.concatenate(
        [device_at == lane // ROWS] * 3 + [device_at == bias_lane // (2 * ROWS)], axis=1
    ).astype(bf16)
    hbm, vmem = pl.BlockSpec(memory_space=pl.ANY), pl.BlockSpec(memory_space=pltpu.VMEM)
    block = (tokens, channels)
    spec, tall = (2 * taps, channels), (channels // 128, tokens + 8, 128)

    def space(*dims, kind=f32):
        return pltpu.VMEM(dims, kind)

    results = (
        (block, bf16), (block, bf16), ((ROWS,), f32), ((ROWS,), f32), ((ROWS,), f32), (w_glu.shape, f32),
        ((2 * ROWS,), f32), ((ROWS,), f32), (log_a_real.shape, f32), (a_imag.shape, f32), (c_coef.shape, f32),
    )
    outs = pl.pallas_call(
        layer_kernel,
        name="layer",
        out_shape=tuple(pltpu.VMEM(dims, kind) for dims, kind in results),
        in_specs=[hbm] * 17,
        out_specs=(vmem,) * len(results),
        scratch_shapes=[
            space(*w_glu.shape), space(1, ROWS), space(1, ROWS), space(1, ROWS), space(1, 2 * ROWS), space(1, ROWS),
            space(*log_a_real.shape), space(*a_imag.shape), space(*c_coef.shape),
            space(*block, kind=bf16), space(*block, kind=bf16), space(*block, kind=bf16),
            space(*forward.shape, kind=bf16), space(*most.shape, kind=bf16), space(*rest.shape, kind=bf16),
            space(*inverse.shape, kind=bf16),
            space(*pick.shape, kind=bf16), space(*mask.shape, kind=bf16),
            space(4, 2, 2, 2, ROWS, taps, kind=bf16), space(4, 4, 2, 2, 2, ROWS, 256, kind=bf16),
            space(64, 2048, kind=bf16), space(64, 2048, kind=bf16), space(8, 2, 8, 128), space(8 * ROWS, 128),
            space(4, 8, 1, 128), space(4, 8, 1, 128), space(3, 8, 1, 128), space(8, 1, 128), space(7, 1, 128),
            space(64, 1, 128),
            space(8, channels),
            space(*tall), space(tokens, 128), space(*tall), space(*tall),
            space(2, tokens // 2, channels, kind=bf16), space(2, tokens // 2, channels, kind=bf16),
            space(2, taps, taps), space(*spec), space(*spec), space(*tall), space(*block),
            space(*block, kind=bf16), space(channels, tokens, kind=bf16),
            space(2, tokens // 2, channels, kind=bf16), space(2, tokens // 2, channels, kind=bf16),
            space(*spec), space(*tall),
            space(4, 4, 2, 2, 2, ROWS, 256, kind=bf16), space(4, 4, 2, 2, ROWS, 256, kind=bf16),
            space(4, 4, 2, 2, ROWS, 256, kind=bf16), space(4, 4, 2, ROWS, 256, kind=bf16),
            space(4, 4, 2, ROWS, 256, kind=bf16), space(4, 3, 2, ROWS, 256, kind=bf16),
            space(4, 2, ROWS, 256, kind=bf16), space(4, ROWS, 256, kind=bf16),
            space(4, 3, 2, 2, ROWS, 256, kind=bf16), space(4, 2, 2, ROWS, 256, kind=bf16), space(4, 3, ROWS, 256, kind=bf16),
            space(4, 2, 2, 2, ROWS, taps), space(4, 2, 2, 2, ROWS, taps, kind=bf16), space(4, 2, 2, ROWS, taps, kind=bf16),
            space(4, 2, 2, ROWS, taps), space(4, 2, 2, ROWS, taps, kind=bf16), space(3, 4, ROWS, taps, kind=bf16),
            space(4, ROWS, taps), space(4, ROWS, taps, kind=bf16), space(3, ROWS, taps, kind=bf16),
            pltpu.SemaphoreType.DMA((14,)), pltpu.SemaphoreType.DMA((5,)), pltpu.SemaphoreType.DMA((39,)),
        ],
        compiler_params=pltpu.CompilerParams(
            collective_id=0, has_side_effects=True, vmem_limit_bytes=48 * 2**20
        ),
    )(*[
        pltpu.with_memory_space_constraint(value, pltpu.HBM)
        for value in (
            inputs.reshape(block), grad_out.reshape(block), forward, most, rest, inverse, pick, mask, w_glu,
            ln_gain.reshape(1, -1), ln_bias.reshape(1, -1), skip_scale.reshape(1, -1), b_glu.reshape(1, -1),
            log_dt.reshape(1, -1), log_a_real, a_imag, c_coef,
        )
    ])
    ended = pl.pallas_call(
        finish_kernel,
        name="finish",
        out_shape=tuple(jax.ShapeDtypeStruct(dims, kind) for dims, kind in results),
        in_specs=[vmem] * len(results),
        out_specs=(hbm,) * len(results),
        scratch_shapes=[pltpu.SemaphoreType.DMA((len(results),))],
    )(*[pltpu.with_memory_space_constraint(value, pltpu.VMEM) for value in outs])
    return (ended[0].reshape(inputs.shape), ended[1].reshape(inputs.shape)) + tuple(ended[2:])


def solution(mesh):
    in_specs = (
        P("dp", "seq", None),
        P("dp", "seq", None),
        P(("dp", "seq")),
        P(("dp", "seq")),
        P(("dp", "seq")),
        P(("dp", "seq"), None),
        P(("dp", "seq")),
        P(("dp", "seq")),
        P(("dp", "seq"), None),
        P(("dp", "seq"), None),
        P(("dp", "seq"), None),
    )
    out_specs = (
        P("dp", "seq", None),
        P("dp", "seq", None),
        P(("dp", "seq")),
        P(("dp", "seq")),
        P(("dp", "seq")),
        P(("dp", "seq"), None),
        P(("dp", "seq")),
        P(("dp", "seq")),
        P(("dp", "seq"), None),
        P(("dp", "seq"), None),
        P(("dp", "seq"), None),
    )
    quick = mesh.shape["dp"] == 8 and mesh.shape["seq"] == 4
    return jax.shard_map(kernel_body if quick else body, mesh=mesh, in_specs=in_specs, out_specs=out_specs, check_vma=False)
```
